32 devices in a mesh: seq: 8 (over z, y), opt: 4 (over x, core).
Axes of the slice: x: 2, y: 2, z: 4, core: 2. Of those that a mesh axis runs over, the one named last changes fastest.
Arguments:
- inputs: bfloat16 [4, 1024, 512], P('opt', 'seq'), may hold values from -6 to 6
- cotangent: bfloat16 [4, 1024, 512], P('opt', 'seq'), may hold values from -6 to 6
- seq_lengths: int32 [4, 8], P('opt'), may hold values from 0 to 1024, as said below
- unit_slot: int32 [24], replicated, may hold values from 0 to 23, each once
- masters: float32 [24, 512, 512], P('opt', 'seq'), may hold values from -0.25 to 0.25
- first_moment: float32 [24, 512, 512], P('opt', 'seq'), may hold values from -6 to 6
- second_moment: float32 [24, 512, 512], P('opt', 'seq'), may hold values from 18.432 to 73.728
- bases: float32 [24, 2, 512, 512], P('opt', None, 'seq'), may hold values from -1 to 1, as said below
- stats: float32 [24, 2, 512, 512], P('opt', None, 'seq'), as said below
- vec_master: float32 [9216], P(('seq', 'opt')), may hold values from -1.5 to 1.5, as said below
- vec_first: float32 [9216], P(('seq', 'opt')), may hold values from -6 to 6
- vec_second: float32 [9216], P(('seq', 'opt')), may hold values from 20.48 to 81.92
Outputs:
- outputs: bfloat16 [4, 1024, 512], P('opt', 'seq')
- input_grad: float32 [4, 1024, 512], P('opt', 'seq')
- new_masters: float32 [24, 512, 512], P('opt', 'seq')
- new_first: float32 [24, 512, 512], P('opt', 'seq')
- new_second: float32 [24, 512, 512], P('opt', 'seq')
- new_bases: float32 [24, 2, 512, 512], P('opt', None, 'seq')
- new_stats: float32 [24, 2, 512, 512], P('opt', None, 'seq')
- new_vectors: float32 [9216], P(('seq', 'opt'))
- new_vec_first: float32 [9216], P(('seq', 'opt'))
- new_vec_second: float32 [9216], P(('seq', 'opt'))
The draws below stay inside these ranges and needn't reach their ends.
Inputs may be any that keep to these rules, and one draw needn't show every extreme that they name: seq_lengths[r, j] is the length of the sequence that starts at device j of row r, 0 where none starts; sequences cover a power of two of devices, start at a multiple of it, have 1024 tokens or more (one device at the least) and 1024 at the most, and fill the row; some sequence of every draw has 1024 tokens. `unit_slot`: slot s belongs to opt index s // 6. `bases`: every [512, 512] matrix is orthogonal. `stats`: every [512, 512] matrix is symmetric with a positive diagonal that exceeds each row's other entries in absolute sum. `vec_master`: the 4608 entries of a layer are g1, c1, g2, c2, b_up, b_down.
All inputs are finite; a program needn't handle non-finite values.
Results may differ from the reference program's by a relative error of at most 0.014.
Values may be sent and summed in bfloat16 or wider, within the bound.
No kernel may reach another device: no remote copies, remote signals or barrier semaphores. Data moves between devices by JAX's collectives and lax.ppermute only.
A program may use at most 192 MiB of HBM per device.

```python
import math
import jax
import jax.numpy as jnp
from jax import lax

D = 512
HEADS = 8
FF = 2048
BLOCK = 16
LAYERS = 2
STEP = 10
MIN_LEN = 1024
MAX_LEN = 4096
TOK_DEV = 128
ROW_TOK = 1024
TOKENS = 4096
LONG_LEN = 1024
UNITS = 24
VECS = 9216
N_SEQ = 8
N_OPT = 4


def draw_seq_lengths(key, part):
    key = jax.random.fold_in(key, 11)
    key_long, key_half, key_row, key_group = jax.random.split(key, 4)
    unit_devs = max(1, MIN_LEN // TOK_DEV)
    long_devs = min(max(MAX_LEN // TOK_DEV, 1), N_SEQ)
    half_devs = max(long_devs // 2, unit_devs)
    group_count = N_SEQ // long_devs
    devices = jnp.arange(N_SEQ, dtype=jnp.int32)
    group_of = devices // long_devs
    half_of = devices * 2 // long_devs
    long_on = jax.random.randint(key_long, (N_OPT, group_count), 0, 2) == 0
    half_on = jax.random.randint(key_half, (N_OPT, 2 * group_count), 0, 2) == 0
    forced_row = jax.random.randint(key_row, (), 0, N_OPT)
    forced_group = jax.random.randint(key_group, (), 0, group_count)
    row_ids = jnp.arange(N_OPT, dtype=jnp.int32)[:, None]
    group_ids = jnp.arange(group_count, dtype=jnp.int32)[None, :]
    long_on = long_on | (row_ids == forced_row) & (group_ids == forced_group)
    spans = jnp.where(long_on[:, group_of], long_devs, jnp.where(half_on[:, half_of], half_devs, unit_devs))
    starts = devices[None, :] % spans == 0
    return jnp.where(starts, spans * TOK_DEV, 0).astype(jnp.int32)


def draw_bases(key, part):
    key = jax.random.fold_in(key, 5)
    bit_count = D.bit_length() - 1
    result = jnp.broadcast_to(jnp.eye(D, dtype=jnp.float32), (UNITS, 2, D, D))
    for round_at in range(3):
        key_round = jax.random.fold_in(key, round_at)
        key_angle, key_order = jax.random.split(key_round)
        angles = jax.random.uniform(key_angle, (UNITS, 2, bit_count, D // 2), jnp.float32, -math.pi, math.pi)
        for bit_at in range(bit_count):
            width = 1 << bit_at
            shaped = result.reshape(UNITS, 2, D // (2 * width), 2, width, D)
            lower_rows = shaped[:, :, :, 0]
            upper_rows = shaped[:, :, :, 1]
            theta = angles[:, :, bit_at].reshape(UNITS, 2, D // (2 * width), width)[..., None]
            cosine = jnp.cos(theta)
            sine = jnp.sin(theta)
            new_lower = cosine * lower_rows - sine * upper_rows
            new_upper = sine * lower_rows + cosine * upper_rows
            result = jnp.stack([new_lower, new_upper], axis=3).reshape(UNITS, 2, D, D)
        if round_at < 2:
            order = jax.random.permutation(key_order, D)
            result = jnp.take(result, order, axis=2)
    return result


def draw_stats(key, part):
    key = jax.random.fold_in(key, 7)
    key_diag, key_size, key_sign = jax.random.split(key, 3)
    level_scale = 0.09 * D * TOKENS
    diagonal = jax.random.uniform(key_diag, (UNITS, 2, D), jnp.float32, 0.5, 2.0) * level_scale
    sizes = jax.random.uniform(key_size, (UNITS, 2, D, D), jnp.float32, 0.8, 1.0)
    block_signs = (2 * jax.random.randint(key_sign, (UNITS, 2, 8, 8), 0, 2) - 1).astype(jnp.float32)
    block_of = jnp.arange(D, dtype=jnp.int32) // (D // 8)
    sign_full = block_signs[:, :, block_of][:, :, :, block_of]
    raw = sizes * sign_full * (0.48 * level_scale / D)
    row_at = jnp.arange(D, dtype=jnp.int32)[:, None]
    col_at = jnp.arange(D, dtype=jnp.int32)[None, :]
    symmetric = jnp.where(row_at < col_at, raw, jnp.swapaxes(raw, -1, -2))
    return jnp.where(row_at == col_at, diagonal[..., None, :], symmetric)


def draw_vec_master(key, part):
    key = jax.random.fold_in(key, 3)
    key_gain, key_bias = jax.random.split(key)
    position = jnp.arange(VECS, dtype=jnp.int32) % (5 * D + FF)
    is_gain = (position < D) | (position >= 2 * D) & (position < 3 * D)
    gains = jax.random.uniform(key_gain, (VECS,), jnp.float32, 0.6, 1.4)
    biases = jnp.clip(0.3 * jax.random.normal(key_bias, (VECS,), jnp.float32), -1.5, 1.5)
    return jnp.where(is_gain, gains, biases)


def levels(stream_key, shape, shards, smallest, top_value):
    loudness, own = 1.0, jax.random.fold_in(stream_key, 6)
    for dim, blocks in shards:
        heights = jnp.exp(jax.random.uniform(jax.random.fold_in(own, dim), (blocks,), jnp.float32, smallest / len(shards), top_value / len(shards)))
        loudness = loudness * jnp.repeat(heights, shape[dim] // blocks).reshape([-1 if axis == dim else 1 for axis in range(len(shape))])
    return loudness


def noise(rng, extent, scale, limit, cuts=(), held_as=jnp.bfloat16):
    array = jax.random.normal(rng, extent, jnp.float32) * scale
    if len(cuts) > 0:
        array = levels(rng, extent, cuts, -0.22, 0.18) * array
    return jnp.clip(array, min=-limit, max=limit).astype(held_as)


def setup_inputs(seed: int = 0) -> dict:
    streams_of = jax.random.split(jax.random.key(seed), 13)
    return {
        "inputs": noise(streams_of[0], (N_OPT, ROW_TOK, D), 1.0, 6.0, ((0, 4), (1, 8))),
        "cotangent": noise(streams_of[1], (N_OPT, ROW_TOK, D), 1.0, 6.0, ((0, 4), (1, 8))),
        "seq_lengths": draw_seq_lengths(jax.random.fold_in(streams_of[12], 71), 0),
        "unit_slot": jax.random.permutation(streams_of[3], UNITS).astype(jnp.int32),
        "masters": noise(streams_of[4], (UNITS, D, D), D ** -0.5, 0.25, ((0, 4), (1, 8)), jnp.float32),
        "first_moment": noise(streams_of[5], (UNITS, D, D), (0.03 * TOKENS ** 0.5), 6.0, ((0, 4), (1, 8)), jnp.float32),
        "second_moment": jnp.clip(jnp.exp(math.log(73.728) - 1.3862944 * jax.random.uniform(streams_of[6], (UNITS, D, D), jnp.float32) ** levels(streams_of[6], (UNITS, D, D), ((0, 4), (1, 8)), -0.2, 0.2)), 18.432, 73.728),
        "bases": draw_bases(jax.random.fold_in(streams_of[12], 71), 0),
        "stats": draw_stats(jax.random.fold_in(streams_of[12], 71), 0),
        "vec_master": draw_vec_master(jax.random.fold_in(streams_of[12], 71), 0),
        "vec_first": noise(streams_of[10], (VECS,), (0.03 * TOKENS ** 0.5), 6.0, ((0, 32),), jnp.float32),
        "vec_second": jnp.clip(jnp.exp(math.log(81.92) - 1.3862944 * jax.random.uniform(streams_of[11], (VECS,), jnp.float32) ** levels(streams_of[11], (VECS,), ((0, 32),), -0.2, 0.2)), 20.48, 81.92),
    }


@jax.custom_vjp
def low(v):
    return lax.optimization_barrier(v.astype(jnp.bfloat16)).astype(jnp.float32)

@jax.custom_vjp
def low_back(v):
    return v

def low_keep(v):
    return (low(v), None)

def low_pass(kept, grad):
    return (grad,)

def back_keep(v):
    return (v, None)

def back_low(kept, grad):
    return (low(grad),)
low.defvjp(low_keep, low_pass)
low_back.defvjp(back_keep, back_low)
HIGH = lax.Precision.HIGHEST
LN_TWO = math.log(2.0)
NEG_FILL = -1e+30
NORM_EPS = 1e-05
ADAM_EPS = 1e-08
RATE_MATRIX = 0.03
RATE_VECTOR = 0.2
WEIGHT_DECAY = 0.01
BETA_ONE = 0.9
BETA_TWO = 0.95
BETA_STAT = 0.95

def pair_mean(values):
    shaped = values.reshape((values.shape[0] // 2, 2) + values.shape[1:])
    return 0.5 * (shaped[:, 0] + shaped[:, 1])

def flip_pairs(segments):
    shaped = segments.reshape((segments.shape[0] // 2, 2) + segments.shape[1:])
    return shaped[:, ::-1].reshape(segments.shape)

def seg_scores(queries, key_segs):
    seg_count = key_segs.shape[0]
    shaped = queries.reshape((seg_count, queries.shape[0] // seg_count) + queries.shape[1:])
    result = jnp.einsum('sqhe,skhe->sqhk', shaped, key_segs, precision=HIGH)
    return result.reshape(queries.shape[0], queries.shape[1], key_segs.shape[1])

def seg_apply(weights, value_segs):
    seg_count = value_segs.shape[0]
    shaped = weights.reshape((seg_count, weights.shape[0] // seg_count) + weights.shape[1:])
    result = jnp.einsum('sqhk,skhe->sqhe', shaped, value_segs, precision=HIGH)
    return result.reshape(weights.shape[0], weights.shape[1], value_segs.shape[3])

def layer_norm(values, gain_vec, bias_vec):
    centre = lax.optimization_barrier(jnp.mean(values, axis=-1, keepdims=True))
    centred = values - centre
    spread = lax.optimization_barrier(jnp.mean(centred * centred, axis=-1, keepdims=True))
    return centred * lax.rsqrt(spread + NORM_EPS) * gain_vec + bias_vec

def attention(queries, key_rows, value_rows, seq_len):
    row_count, head_count, head_size = queries.shape
    level_count = (LONG_LEN // BLOCK).bit_length() - 1
    score_scale = head_size ** (-0.5)
    key_levels = [key_rows]
    value_levels = [value_rows]
    for height in range(1, level_count):
        key_levels.append(low(pair_mean(key_levels[-1])))
        value_levels.append(low(pair_mean(value_levels[-1])))
    groups = [(key_rows.reshape(row_count // BLOCK, BLOCK, head_count, head_size), value_rows.reshape(row_count // BLOCK, BLOCK, head_count, head_size), 0.0, None)]
    for height in range(level_count):
        seg_count = key_levels[height].shape[0] // BLOCK
        groups.append((flip_pairs(key_levels[height].reshape(seg_count, BLOCK, head_count, head_size)), flip_pairs(value_levels[height].reshape(seg_count, BLOCK, head_count, head_size)), height * LN_TWO, seq_len >= 2 * BLOCK << height))
    parts = []
    for key_segs, value_segs, offset, counted in groups:
        piece = low_back(seg_scores(queries, key_segs) * score_scale + offset)
        if counted is not None:
            piece = jnp.where(counted[:, None, None], piece, NEG_FILL)
        parts.append(piece)
    scores = jnp.concatenate(parts, axis=2)
    highest = lax.optimization_barrier(jnp.max(scores, axis=2, keepdims=True))
    expo = jnp.exp(scores - highest)
    probs = low(expo / lax.optimization_barrier(jnp.sum(expo, axis=2, keepdims=True)))
    result = jnp.zeros(queries.shape, jnp.float32)
    for position, group in enumerate(groups):
        result = result + seg_apply(probs[:, :, BLOCK * position:BLOCK * (position + 1)], group[1])
    return result

def row_forward(hidden, units, vectors, seq_len):
    row_count, model_width = hidden.shape
    head_count = HEADS
    head_size = model_width // head_count
    ff_blocks = FF // model_width
    per_layer = 4 + 2 * ff_blocks
    vec_width = 5 * model_width + FF
    for layer_at in range(LAYERS):
        block_units = units[layer_at * per_layer:(layer_at + 1) * per_layer]
        w_qkv = block_units[0:3].transpose(1, 0, 2).reshape(model_width, 3 * model_width)
        w_out = block_units[3]
        w_up = block_units[4:4 + ff_blocks].transpose(1, 0, 2).reshape(model_width, FF)
        w_down = block_units[4 + ff_blocks:].reshape(FF, model_width)
        layer_vec = vectors[layer_at * vec_width:(layer_at + 1) * vec_width]
        gain_one = layer_vec[0:model_width]
        bias_one = layer_vec[model_width:2 * model_width]
        gain_two = layer_vec[2 * model_width:3 * model_width]
        bias_two = layer_vec[3 * model_width:4 * model_width]
        bias_up = layer_vec[4 * model_width:4 * model_width + FF]
        bias_down = layer_vec[4 * model_width + FF:]
        normed = low(layer_norm(hidden, gain_one, bias_one))
        qkv = jnp.dot(normed, w_qkv, precision=HIGH)
        queries = low_back(low(qkv[:, :model_width])).reshape(row_count, head_count, head_size)
        key_rows = low_back(low(qkv[:, model_width:2 * model_width])).reshape(row_count, head_count, head_size)
        value_rows = low_back(low(qkv[:, 2 * model_width:])).reshape(row_count, head_count, head_size)
        attended = attention(queries, key_rows, value_rows, seq_len)
        mixed = low_back(low(attended.reshape(row_count, model_width)))
        middle = hidden + low_back(jnp.dot(mixed, w_out, precision=HIGH))
        normed_two = low(layer_norm(middle, gain_two, bias_two))
        pre_act = low_back(jnp.dot(normed_two, w_up, precision=HIGH) + bias_up)
        activated = low(jax.nn.gelu(pre_act, approximate=False))
        hidden = middle + low_back(jnp.dot(activated, w_down, precision=HIGH)) + bias_down
    return hidden

def reference(inputs, cotangent, seq_lengths, unit_slot, masters, first_moment, second_moment, bases, stats, vec_master, vec_first, vec_second):
    row_tok = inputs.shape[1]
    dev_tok = row_tok // N_SEQ
    devices = jnp.arange(N_SEQ, dtype=jnp.int32)
    seq_bits = N_SEQ.bit_length() - 1

    def device_spans(length_row):
        spans = jnp.zeros((N_SEQ,), jnp.int32)
        for bit_at in range(seq_bits + 1):
            starts = devices >> bit_at << bit_at
            hits = length_row[starts] == dev_tok * (1 << bit_at)
            spans = jnp.where(hits, dev_tok * (1 << bit_at), spans)
        return jnp.repeat(spans, dev_tok)
    token_lengths = jnp.stack([device_spans(seq_lengths[row_at]) for row_at in range(N_OPT)])

    def forward(all_inputs, weights, vec_values):
        units = low(jnp.take(weights, unit_slot, axis=0))
        vec_low = low(vec_values)

        def one_row(pair_in):
            return row_forward(pair_in[0], units, vec_low, pair_in[1])
        return lax.map(jax.checkpoint(one_row), (all_inputs, token_lengths))
    result, pullback = jax.vjp(forward, inputs.astype(jnp.float32), masters, vec_master)
    input_grad, slot_grads, vec_grads = pullback(cotangent.astype(jnp.float32))
    left_basis = bases[:, 0]
    right_basis = bases[:, 1]
    rotated = jnp.einsum('sri,src->sic', left_basis, slot_grads, precision=HIGH)
    rotated = jnp.einsum('sic,scd->sid', rotated, right_basis, precision=HIGH)
    new_first = BETA_ONE * first_moment + (1.0 - BETA_ONE) * rotated
    new_second = BETA_TWO * second_moment + (1.0 - BETA_TWO) * rotated * rotated
    direction = new_first / (1.0 - BETA_ONE ** STEP) / (jnp.sqrt(new_second / (1.0 - BETA_TWO ** STEP)) + ADAM_EPS)
    turned = jnp.einsum('sid,scd->sic', direction, right_basis, precision=HIGH)
    update = jnp.einsum('sri,sic->src', left_basis, turned, precision=HIGH)
    new_masters = masters - RATE_MATRIX * (update + WEIGHT_DECAY * masters)
    left_stat = BETA_STAT * stats[:, 0] + (1.0 - BETA_STAT) * jnp.einsum('src,sqc->srq', slot_grads, slot_grads, precision=HIGH)
    right_stat = BETA_STAT * stats[:, 1] + (1.0 - BETA_STAT) * jnp.einsum('sqr,sqc->src', slot_grads, slot_grads, precision=HIGH)
    new_stats = jnp.stack([left_stat, right_stat], axis=1)
    product = jnp.einsum('sprq,spqc->sprc', new_stats, bases, precision=HIGH)
    gram = jnp.einsum('sprc,sprd->spcd', product, product, precision=HIGH)
    factor = jnp.linalg.cholesky(gram)
    solved = lax.linalg.triangular_solve(factor, jnp.swapaxes(product, -1, -2), left_side=True, lower=True)
    new_bases = jnp.swapaxes(solved, -1, -2)
    new_vec_first = BETA_ONE * vec_first + (1.0 - BETA_ONE) * vec_grads
    new_vec_second = BETA_TWO * vec_second + (1.0 - BETA_TWO) * vec_grads * vec_grads
    new_vectors = vec_master - RATE_VECTOR * (new_vec_first / (1.0 - BETA_ONE ** STEP)) / (jnp.sqrt(new_vec_second / (1.0 - BETA_TWO ** STEP)) + ADAM_EPS)
    return (result.astype(jnp.bfloat16), input_grad, new_masters, new_first, new_second, new_bases, new_stats, new_vectors, new_vec_first, new_vec_second)
```

```python
import functools
import math

import jax
import jax.numpy as jnp
from jax import lax
from jax.experimental import pallas as pl
from jax.experimental.pallas import tpu as pltpu
from jax.sharding import PartitionSpec as P

HEADS = 8
FF = 2048
BLOCK = 16
LAYERS = 2
STEP = 10
MAX_LEN = 4096


HIGH = lax.Precision.HIGHEST
LN_TWO = math.log(2.0)
NEG_FILL = -1e30
NORM_EPS = 1e-05
ADAM_EPS = 1e-08
RATE_MATRIX = 0.03
RATE_VECTOR = 0.2
WEIGHT_DECAY = 0.01
BETA_ONE = 0.9
BETA_TWO = 0.95
BETA_STAT = 0.95

PANEL = 8
DIAG = 128
VMEM_GRANT = 48 * 2**20
IN_VMEM = pl.BlockSpec(memory_space=pltpu.VMEM)
IN_SMEM = pl.BlockSpec(memory_space=pltpu.SMEM)


def contract(left, right, left_dim, right_dim, precision=None):
    return lax.dot_general(
        left,
        right,
        (((left_dim,), (right_dim,)), ((), ())),
        precision=precision,
        preferred_element_type=jnp.float32,
    )


def split_two(values):
    high = values.astype(jnp.bfloat16)
    return (high, (values - high.astype(jnp.float32)).astype(jnp.bfloat16))


def wide_left(left, right_low, left_dim, right_dim):
    high, rest = split_two(left)
    return contract(high, right_low, left_dim, right_dim) + contract(
        rest, right_low, left_dim, right_dim
    )


def wide_right(left_low, right, left_dim, right_dim):
    high, rest = split_two(right)
    return contract(left_low, high, left_dim, right_dim) + contract(
        left_low, rest, left_dim, right_dim
    )


def call_kernel(body, out_shapes, scratch, name, *operands, smem_count=0):
    return pl.pallas_call(
        body,
        out_shape=out_shapes,
        in_specs=[IN_SMEM] * smem_count + [IN_VMEM] * (len(operands) - smem_count),
        out_specs=jax.tree.map(lambda _: IN_VMEM, out_shapes),
        scratch_shapes=scratch,
        compiler_params=pltpu.CompilerParams(vmem_limit_bytes=VMEM_GRANT),
        name=name,
    )(*operands)


def eliminate(left_part, right_part, turn):
    width = left_part.shape[1]
    turned = pltpu.roll(left_part, turn, 1)
    row_at = lax.broadcasted_iota(jnp.int32, (PANEL, width), 0)
    columns = [
        jnp.broadcast_to(turned[:, i : i + 1], (PANEL, width)) for i in range(PANEL)
    ]
    pivots = jnp.ones((PANEL, width), jnp.float32)
    for i in range(PANEL):
        pivot = jnp.broadcast_to(columns[i][i : i + 1, :], (PANEL, width))
        factor = jnp.where(row_at > i, columns[i] * pltpu.reciprocal(pivot, approx=False), 0.0)
        pivots = jnp.where(row_at == i, pivot, pivots)
        left_part = left_part - factor * jnp.broadcast_to(left_part[i : i + 1, :], (PANEL, width))
        right_part = right_part - factor * jnp.broadcast_to(
            right_part[i : i + 1, :], (PANEL, width)
        )
        for j in range(i + 1, PANEL):
            columns[j] = columns[j] - factor * jnp.broadcast_to(
                columns[j][i : i + 1, :], (PANEL, width)
            )
    scale = lax.rsqrt(pivots)
    return (left_part * scale, right_part * scale)


def factorize(gram, upper, work, inverses):
    count, size, _ = gram.shape
    blocks = size // DIAG
    eye = (
        lax.broadcasted_iota(jnp.int32, (DIAG, DIAG), 0)
        == lax.broadcasted_iota(jnp.int32, (DIAG, DIAG), 1)
    ).astype(jnp.float32)
    for block_at in range(blocks):
        low, top = (block_at * DIAG, (block_at + 1) * DIAG)
        for m in range(count):
            work[m, :, 0:DIAG] = gram[m, low:top, low:top]
            work[m, :, DIAG:] = eye

        def panel(panel_at, carry):
            row = pl.multiple_of(panel_at * PANEL, PANEL)
            turn = lax.rem(DIAG - panel_at * PANEL, DIAG)
            for m in range(count):
                left_part, right_part = eliminate(
                    work[m, pl.ds(row, PANEL), 0:DIAG], work[m, pl.ds(row, PANEL), DIAG:], turn
                )
                inverses[m, block_at, pl.ds(row, PANEL), :] = right_part
                both = jnp.concatenate([left_part, right_part], axis=1)
                work[m] = work[m] - contract(left_part, both, 0, 0, HIGH)
            return carry

        lax.fori_loop(0, DIAG // PANEL, panel, 0)
        for m in range(count):
            if block_at + 1 < blocks:
                right_of = contract(inverses[m, block_at], gram[m, low:top, top:], 1, 0, HIGH)
                upper[m, low:top, top:] = right_of
                for other in range(block_at + 1, blocks):
                    skip = (other - block_at - 1) * DIAG
                    gram[m, other * DIAG : (other + 1) * DIAG, other * DIAG :] -= contract(
                        right_of[:, skip : skip + DIAG], right_of[:, skip:], 0, 0, HIGH
                    )


def renew_body(piece_count, *refs):
    offset_ref, stat_ref, basis_ref = refs[:3]
    piece_refs = refs[3 : 3 + piece_count]
    product, gram, upper, work, inverses = refs[3 + piece_count :]
    count, size, _ = stat_ref.shape
    for m in range(count):
        product[m] = wide_left(stat_ref[m], basis_ref[m], 1, 0)
        gram[m] = contract(product[m], product[m], 0, 0, HIGH)
    factorize(gram, upper, work, inverses)
    for low in range(0, size, DIAG):
        top = low + DIAG
        for m in range(count):
            rest = product[m, :, low:top]
            if low:
                rest = rest - contract(product[m, :, :low], upper[m, :low, low:top], 1, 0, HIGH)
            product[m, :, low:top] = contract(rest, inverses[m, low // DIAG], 1, 1, HIGH)
    rows = piece_refs[0].shape[1]
    for piece_at in range(piece_count):
        row = pl.multiple_of(offset_ref[piece_at], 8)
        piece_refs[piece_at][...] = product[:, pl.ds(row, rows), :].astype(jnp.bfloat16)


def renew_bases(offsets, new_stat, basis_low):
    count, size, _ = new_stat.shape
    piece_count = offsets.shape[0]
    square = pltpu.VMEM((count, size, size), jnp.float32)
    return call_kernel(
        functools.partial(renew_body, piece_count),
        [
            jax.ShapeDtypeStruct((count, size // piece_count, size), jnp.bfloat16)
            for _ in range(piece_count)
        ],
        [
            square,
            square,
            square,
            pltpu.VMEM((count, DIAG, 2 * DIAG), jnp.float32),
            pltpu.VMEM((count, size // DIAG, DIAG, DIAG), jnp.float32),
        ],
        "renew_bases",
        offsets,
        new_stat,
        basis_low,
        smem_count=1,
    )


def pack_body(slot_ref, stats, bases, first, second, *piece_refs):
    for piece_at, piece_ref in enumerate(piece_refs):
        slot = slot_ref[piece_at]
        piece_ref[0:2] = stats[slot].astype(jnp.bfloat16)
        piece_ref[2:4] = bases[slot].astype(jnp.bfloat16)
        piece_ref[4] = first[slot].astype(jnp.bfloat16)
        piece_ref[5] = second[slot].astype(jnp.bfloat16)


def rotate_body(piece_count, *refs):
    offset_ref, grad_ref = refs[:2]
    given = refs[2 : 2 + piece_count]
    sent = refs[2 + piece_count : 2 + 2 * piece_count]
    stat_ref, basis_ref, whole, results = refs[2 + 2 * piece_count :]
    rows = given[0].shape[1]
    for piece_at in range(piece_count):
        row = pl.multiple_of(offset_ref[piece_at], 8)
        whole[:, pl.ds(row, rows), :] = given[piece_at][...].astype(jnp.float32)
    grad = grad_ref[...]
    left = whole[2].astype(jnp.bfloat16)
    right = whole[3].astype(jnp.bfloat16)
    basis_ref[0] = left
    basis_ref[1] = right
    results[0] = contract(grad, grad, 1, 1)
    results[1] = contract(grad, grad, 0, 0)
    stat_ref[0] = BETA_STAT * whole[0] + (1.0 - BETA_STAT) * results[0]
    stat_ref[1] = BETA_STAT * whole[1] + (1.0 - BETA_STAT) * results[1]
    rotated = wide_left(contract(left, grad, 0, 0), right, 1, 0)
    results[2] = rotated
    new_first = BETA_ONE * whole[4] + (1.0 - BETA_ONE) * rotated
    new_second = BETA_TWO * whole[5] + (1.0 - BETA_TWO) * rotated * rotated
    direction = (
        new_first
        / (1.0 - BETA_ONE**STEP)
        / (jnp.sqrt(new_second / (1.0 - BETA_TWO**STEP)) + ADAM_EPS)
    )
    results[3] = wide_right(left, wide_left(direction, right, 1, 1), 1, 0)
    for piece_at in range(piece_count):
        row = pl.multiple_of(offset_ref[piece_at], 8)
        sent[piece_at][...] = results[:, pl.ds(row, rows), :].astype(jnp.bfloat16)


def rotate_slot(offsets, grad, pieces):
    size = grad.shape[0]
    piece_count = offsets.shape[0]
    return call_kernel(
        functools.partial(rotate_body, piece_count),
        [
            jax.ShapeDtypeStruct((4, size // piece_count, size), jnp.bfloat16)
            for _ in range(piece_count)
        ]
        + [
            jax.ShapeDtypeStruct((2, size, size), jnp.float32),
            jax.ShapeDtypeStruct((2, size, size), jnp.bfloat16),
        ],
        [
            pltpu.VMEM((6, size, size), jnp.float32),
            pltpu.VMEM((4, size, size), jnp.float32),
        ],
        "rotate_slot",
        offsets,
        grad,
        *pieces,
        smem_count=1,
    )


def finish_body(own_slots, piece_count, *refs):
    slot_ref, masters, first, second, stats = refs[:5]
    given = refs[5 : 5 + piece_count]
    new_masters, new_first, new_second, new_stats = refs[5 + piece_count :]
    for piece_at in range(piece_count):
        slot = slot_ref[piece_at]

        @pl.when(slot < own_slots)
        def _():
            piece = given[piece_at]
            rotated = piece[2].astype(jnp.float32)
            update = piece[3].astype(jnp.float32)
            new_first[slot] = BETA_ONE * first[slot] + (1.0 - BETA_ONE) * rotated
            new_second[slot] = BETA_TWO * second[slot] + (1.0 - BETA_TWO) * rotated * rotated
            new_masters[slot] = masters[slot] - RATE_MATRIX * (
                update + WEIGHT_DECAY * masters[slot]
            )
            new_stats[slot] = BETA_STAT * stats[slot] + (1.0 - BETA_STAT) * piece[
                0:2
            ].astype(jnp.float32)


def place_body(own_slots, slot_ref, *refs):
    new_bases = refs[-1]
    for piece_at, piece in enumerate(refs[:-1]):
        slot = slot_ref[piece_at]

        @pl.when(slot < own_slots)
        def _():
            new_bases[slot] = piece[...].astype(jnp.float32)


def swap_pieces(pieces, axis):
    device_count = lax.axis_size(axis)
    return [pieces[0]] + [
        lax.ppermute(pieces[k], axis, [(i, i ^ k) for i in range(device_count)])
        for k in range(1, device_count)
    ]


def to_owners(pieces, axis, by_permutes):
    if by_permutes:
        return swap_pieces(pieces, axis)
    stacked = jnp.stack(pieces)
    device_count = lax.axis_size(axis)
    padded = jnp.pad(stacked, [(0, device_count - len(pieces))] + [(0, 0)] * (stacked.ndim - 1))
    swapped = lax.all_to_all(padded, axis, 0, 0, tiled=True)
    kinds, _, width = pieces[0].shape
    return [jnp.swapaxes(swapped, 0, 1).reshape(kinds, -1, width)]


def to_homes(pieces, axis, by_permutes, own_slots):
    if by_permutes:
        return swap_pieces(pieces, axis)
    kinds, _, width = pieces[0].shape
    device_count = lax.axis_size(axis)
    shaped = jnp.swapaxes(pieces[0].reshape(kinds, device_count, -1, width), 0, 1)
    swapped = lax.all_to_all(shaped, axis, 0, 0, tiled=True)
    return [swapped[slot] for slot in range(own_slots)]


def partner(value, axis, apart):
    return lax.ppermute(value, axis, [(i, i ^ 1 << apart) for i in range(lax.axis_size(axis))])


def shortened(value):
    return jax.tree.map(lambda a: a.astype(jnp.bfloat16) if a.dtype == jnp.float32 else a, value)


def pair_mean(values):
    shaped = values.reshape((values.shape[0] // 2, 2) + values.shape[1:])
    return 0.5 * (shaped[:, 0] + shaped[:, 1])


def pair_spread(grads):
    return 0.5 * jnp.repeat(grads, 2, axis=0)


def flip_pairs(segments):
    shaped = segments.reshape((segments.shape[0] // 2, 2) + segments.shape[1:])
    return shaped[:, ::-1].reshape(segments.shape)


def seg_scores(queries, key_segs):
    seg_count = key_segs.shape[0]
    shaped = queries.reshape((seg_count, queries.shape[0] // seg_count) + queries.shape[1:])
    result = jnp.einsum("sqhe,skhe->sqhk", shaped, key_segs, preferred_element_type=jnp.float32)
    return result.reshape(queries.shape[0], queries.shape[1], key_segs.shape[1])


def seg_apply(weights, value_segs):
    seg_count = value_segs.shape[0]
    shaped = weights.reshape((seg_count, weights.shape[0] // seg_count) + weights.shape[1:])
    result = jnp.einsum("sqhk,skhe->sqhe", shaped, value_segs, preferred_element_type=jnp.float32)
    return result.reshape(weights.shape[0], weights.shape[1], value_segs.shape[3])


def seg_collect(weights, row_values, seg_count):
    w_shaped = weights.reshape((seg_count, weights.shape[0] // seg_count) + weights.shape[1:])
    r_shaped = row_values.reshape(
        (seg_count, row_values.shape[0] // seg_count) + row_values.shape[1:]
    )
    return jnp.einsum("sqhk,sqhe->skhe", w_shaped, r_shaped, preferred_element_type=jnp.float32)


def layer_norm(values, gain_vec, bias_vec):
    centre = jnp.mean(values, axis=-1, keepdims=True)
    centred = values - centre
    spread = jnp.mean(centred * centred, axis=-1, keepdims=True)
    return centred * lax.rsqrt(spread + NORM_EPS) * gain_vec + bias_vec


def gelu_exact(values):
    return jax.nn.gelu(values, approximate=False)


def make_groups(key_levels, value_levels, far_list, head_count, head_size, local_levels):

    def as_segs(row_values, seg_count):
        return row_values.reshape(seg_count, BLOCK, head_count, head_size)

    own_count = key_levels[0].shape[0] // BLOCK
    groups = [(as_segs(key_levels[0], own_count), as_segs(value_levels[0], own_count), 0.0, None)]
    for height in range(local_levels):
        seg_count = key_levels[height].shape[0] // BLOCK
        groups.append(
            (
                flip_pairs(as_segs(key_levels[height], seg_count)),
                flip_pairs(as_segs(value_levels[height], seg_count)),
                height * LN_TWO,
                None,
            )
        )
    for step_at, (far_keys, far_values, counted) in enumerate(far_list):
        groups.append(
            (
                as_segs(far_keys, 1),
                as_segs(far_values, 1),
                (local_levels + step_at) * LN_TWO,
                counted,
            )
        )
    return groups


def score_all(queries, groups, score_scale):
    parts = []
    for key_segs, value_segs, offset, counted in groups:
        piece = seg_scores(queries, key_segs) * score_scale + offset
        if counted is not None:
            piece = jnp.where(counted, piece, NEG_FILL)
        parts.append(piece)
    return jnp.concatenate(parts, axis=2)


def attend(queries, groups, score_scale):
    scores = score_all(queries, groups, score_scale)
    highest = jnp.max(scores, axis=2, keepdims=True)
    expo = jnp.exp(scores - highest)
    totals = jnp.sum(expo, axis=2, keepdims=True)
    probs = (expo / totals).astype(jnp.bfloat16)
    result = jnp.zeros(queries.shape, jnp.float32)
    for position, group in enumerate(groups):
        result = result + seg_apply(
            probs[:, :, BLOCK * position : BLOCK * (position + 1)], group[1]
        )
    return (result, highest[..., 0] + jnp.log(totals[..., 0]))


def attend_back(queries, groups, score_scale, log_total, out_grad):
    scores = score_all(queries, groups, score_scale)
    probs = jnp.exp(scores - log_total[..., None])
    prob_grad = jnp.concatenate([seg_scores(out_grad, group[1]) for group in groups], axis=2)
    inner = jnp.sum(probs * prob_grad, axis=2, keepdims=True)
    score_grad = (probs * (prob_grad - inner)).astype(jnp.bfloat16)
    probs_low = probs.astype(jnp.bfloat16)
    query_grad = jnp.zeros(queries.shape, jnp.float32)
    key_grads = []
    value_grads = []
    for position, (key_segs, value_segs, offset, counted) in enumerate(groups):
        piece = score_grad[:, :, BLOCK * position : BLOCK * (position + 1)]
        weights = probs_low[:, :, BLOCK * position : BLOCK * (position + 1)]
        query_grad = query_grad + seg_apply(piece, key_segs) * score_scale
        key_grads.append(seg_collect(piece, queries, key_segs.shape[0]) * score_scale)
        value_grads.append(seg_collect(weights, out_grad, key_segs.shape[0]))
    return (query_grad, key_grads, value_grads)


def coarse_up(near_keys, near_values, seq_index, tree_bits, span_bits):
    far_list = []
    own_keys, own_values = (near_keys, near_values)
    for bit_at in range(tree_bits):
        far_keys, far_values = partner((own_keys, own_values), "seq", bit_at)
        far_list.append((far_keys, far_values, bit_at + 1 <= span_bits))
        if bit_at + 1 < tree_bits:
            upper = seq_index >> bit_at & 1 == 1
            joined_keys = jnp.where(
                upper, jnp.concatenate([far_keys, own_keys]), jnp.concatenate([own_keys, far_keys])
            )
            joined_values = jnp.where(
                upper,
                jnp.concatenate([far_values, own_values]),
                jnp.concatenate([own_values, far_values]),
            )
            own_keys = pair_mean(joined_keys.astype(jnp.float32)).astype(jnp.bfloat16)
            own_values = pair_mean(joined_values.astype(jnp.float32)).astype(jnp.bfloat16)
    return far_list


def coarse_down(far_grads, seq_index, tree_bits, model_width):
    key_above = None
    value_above = None
    for bit_at in reversed(range(tree_bits)):
        upper = seq_index >> bit_at & 1 == 1
        if key_above is None:
            own_key = jnp.zeros((BLOCK, model_width), jnp.float32)
            other_key = own_key
            own_value = own_key
            other_value = own_key
        else:
            spread_keys = pair_spread(key_above)
            spread_values = pair_spread(value_above)
            own_key = jnp.where(upper, spread_keys[BLOCK:], spread_keys[:BLOCK])
            other_key = jnp.where(upper, spread_keys[:BLOCK], spread_keys[BLOCK:])
            own_value = jnp.where(upper, spread_values[BLOCK:], spread_values[:BLOCK])
            other_value = jnp.where(upper, spread_values[:BLOCK], spread_values[BLOCK:])
        back_key, back_value = partner(
            (
                shortened(other_key + far_grads[bit_at][0]),
                shortened(other_value + far_grads[bit_at][1]),
            ),
            "seq",
            bit_at,
        )
        key_above = own_key + back_key
        value_above = own_value + back_value
    return (key_above, value_above)


def per_device(
    inputs,
    cotangent,
    seq_lengths,
    unit_slot,
    masters,
    first_moment,
    second_moment,
    bases,
    stats,
    vec_master,
    vec_first,
    vec_second,
):
    seq_count = lax.axis_size("seq")
    opt_count = lax.axis_size("opt")
    seq_index = lax.axis_index("seq")
    tok_count = inputs.shape[1]
    model_width = inputs.shape[2]
    own_slots = masters.shape[0]
    row_count = masters.shape[1]
    head_count = HEADS
    head_size = model_width // head_count
    score_scale = head_size ** (-0.5)
    ff_blocks = FF // model_width
    per_layer = 4 + 2 * ff_blocks
    vec_width = 5 * model_width + FF
    local_levels = (tok_count // BLOCK).bit_length() - 1
    long_devs = min(max(MAX_LEN // tok_count, 1), seq_count)
    tree_bits = long_devs.bit_length() - 1
    size = seq_count * row_count
    by_permutes = seq_count <= 8
    if by_permutes:
        relative = jnp.arange(seq_count, dtype=jnp.int32) ^ seq_index
        offsets = relative * row_count
        slot_at = relative
    else:
        offsets = jnp.zeros((1,), jnp.int32)
        slot_at = jnp.arange(own_slots, dtype=jnp.int32)
    packed_pieces = call_kernel(
        pack_body,
        [
            jax.ShapeDtypeStruct((6, row_count, model_width), jnp.bfloat16)
            for _ in range(slot_at.shape[0])
        ],
        [],
        "pack_slots",
        jnp.minimum(slot_at, own_slots - 1),
        stats,
        bases,
        first_moment,
        second_moment,
        smem_count=1,
    )
    owner_pieces = to_owners(packed_pieces, "seq", by_permutes)
    packed_units, packed_vecs = (
        lax.all_gather(masters.astype(jnp.bfloat16)[None], ("seq", "opt"), axis=0, tiled=True),
        lax.all_gather(vec_master.astype(jnp.bfloat16)[None], ("seq", "opt"), axis=0, tiled=True),
    )
    slot_weights = (
        packed_units.reshape(seq_count, opt_count, own_slots, row_count, model_width)
        .transpose(1, 2, 0, 3, 4)
        .reshape(opt_count * own_slots, seq_count * row_count, model_width)
    )
    units = jnp.take(slot_weights, unit_slot, axis=0)
    vectors = packed_vecs.reshape(-1).astype(jnp.float32)
    span_bits = jnp.zeros((), jnp.int32)
    for bit_at in range(tree_bits + 1):
        start_dev = seq_index >> bit_at << bit_at
        span_bits = jnp.where(
            seq_lengths[0, start_dev] == tok_count * (1 << bit_at), bit_at, span_bits
        )

    def layer_weights(layer_at):
        block_units = units[layer_at * per_layer : (layer_at + 1) * per_layer]
        w_qkv = block_units[0:3].transpose(1, 0, 2).reshape(model_width, 3 * model_width)
        w_up = block_units[4 : 4 + ff_blocks].transpose(1, 0, 2).reshape(model_width, FF)
        w_down = block_units[4 + ff_blocks :].reshape(FF, model_width)
        layer_vec = vectors[layer_at * vec_width : (layer_at + 1) * vec_width]
        vec_parts = (
            layer_vec[0:model_width],
            layer_vec[model_width : 2 * model_width],
            layer_vec[2 * model_width : 3 * model_width],
            layer_vec[3 * model_width : 4 * model_width],
            layer_vec[4 * model_width : 4 * model_width + FF],
            layer_vec[4 * model_width + FF :],
        )
        return (w_qkv, block_units[3], w_up, w_down, vec_parts)

    hidden = inputs[0].astype(jnp.float32)
    saved = []
    for layer_at in range(LAYERS):
        w_qkv, w_out, w_up, w_down, vec_parts = layer_weights(layer_at)
        gain_one, bias_one, gain_two, bias_two, bias_up, bias_down = vec_parts
        normed = layer_norm(hidden, gain_one, bias_one).astype(jnp.bfloat16)
        qkv = jnp.dot(normed, w_qkv, preferred_element_type=jnp.float32).astype(jnp.bfloat16)
        queries = qkv[:, :model_width].reshape(tok_count, head_count, head_size)
        key_levels = [qkv[:, model_width : 2 * model_width]]
        value_levels = [qkv[:, 2 * model_width :]]
        for height in range(local_levels):
            key_levels.append(pair_mean(key_levels[-1].astype(jnp.float32)).astype(jnp.bfloat16))
            value_levels.append(
                pair_mean(value_levels[-1].astype(jnp.float32)).astype(jnp.bfloat16)
            )
        far_list = coarse_up(
            key_levels[local_levels], value_levels[local_levels], seq_index, tree_bits, span_bits
        )
        groups = make_groups(
            key_levels, value_levels, far_list, head_count, head_size, local_levels
        )
        attended, log_total = attend(queries, groups, score_scale)
        mixed = attended.reshape(tok_count, model_width).astype(jnp.bfloat16)
        middle = hidden + jnp.dot(mixed, w_out, preferred_element_type=jnp.float32)
        normed_two = layer_norm(middle, gain_two, bias_two).astype(jnp.bfloat16)
        pre_act = jnp.dot(normed_two, w_up, preferred_element_type=jnp.float32) + bias_up
        activated = gelu_exact(pre_act).astype(jnp.bfloat16)
        saved.append(
            (
                hidden,
                normed,
                queries,
                key_levels,
                groups,
                log_total,
                mixed,
                middle,
                normed_two,
                pre_act,
                activated,
            )
        )
        hidden = middle + jnp.dot(activated, w_down, preferred_element_type=jnp.float32) + bias_down
    grad = cotangent[0].astype(jnp.float32)
    unit_grads = [None] * LAYERS
    vec_grads = [None] * LAYERS
    for layer_at in reversed(range(LAYERS)):
        w_qkv, w_out, w_up, w_down, vec_parts = layer_weights(layer_at)
        gain_one, bias_one, gain_two, bias_two, bias_up, bias_down = vec_parts
        (
            layer_in,
            normed,
            queries,
            key_levels,
            groups,
            log_total,
            mixed,
            middle,
            normed_two,
            pre_act,
            activated,
        ) = saved[layer_at]
        down_grad = grad.astype(jnp.bfloat16)
        grad_down_w = jnp.einsum(
            "tf,td->fd", activated, down_grad, preferred_element_type=jnp.float32
        )
        grad_bias_down = jnp.sum(grad, axis=0)
        act_grad = jnp.einsum("td,fd->tf", down_grad, w_down, preferred_element_type=jnp.float32)
        unused, gelu_back = jax.vjp(gelu_exact, pre_act)
        pre_grad = gelu_back(act_grad)[0].astype(jnp.bfloat16)
        grad_up_w = jnp.einsum(
            "td,tf->df", normed_two, pre_grad, preferred_element_type=jnp.float32
        )
        grad_bias_up = jnp.sum(pre_grad.astype(jnp.float32), axis=0)
        normed_grad = jnp.einsum("tf,df->td", pre_grad, w_up, preferred_element_type=jnp.float32)
        unused, norm_back = jax.vjp(layer_norm, middle, gain_two, bias_two)
        middle_grad, grad_gain_two, grad_bias_two = norm_back(normed_grad)
        middle_grad = middle_grad + grad
        branch_grad = middle_grad.astype(jnp.bfloat16)
        grad_out_w = jnp.einsum("td,te->de", mixed, branch_grad, preferred_element_type=jnp.float32)
        mixed_grad = (
            jnp.einsum("te,de->td", branch_grad, w_out, preferred_element_type=jnp.float32)
            .astype(jnp.bfloat16)
            .reshape(tok_count, head_count, head_size)
        )
        query_grad, key_grads, value_grads = attend_back(
            queries, groups, score_scale, log_total, mixed_grad
        )
        key_acc = [jnp.zeros(level_keys.shape, jnp.float32) for level_keys in key_levels]
        value_acc = [jnp.zeros(level_keys.shape, jnp.float32) for level_keys in key_levels]
        key_acc[0] = key_grads[0].reshape(tok_count, model_width)
        value_acc[0] = value_grads[0].reshape(tok_count, model_width)
        for height in range(local_levels):
            key_acc[height] = key_acc[height] + flip_pairs(key_grads[1 + height]).reshape(
                -1, model_width
            )
            value_acc[height] = value_acc[height] + flip_pairs(value_grads[1 + height]).reshape(
                -1, model_width
            )
        far_grads = [
            (
                key_grads[1 + local_levels + bit_at].reshape(BLOCK, model_width),
                value_grads[1 + local_levels + bit_at].reshape(BLOCK, model_width),
            )
            for bit_at in range(tree_bits)
        ]
        near_key_grad, near_value_grad = coarse_down(far_grads, seq_index, tree_bits, model_width)
        key_acc[local_levels] = key_acc[local_levels] + near_key_grad
        value_acc[local_levels] = value_acc[local_levels] + near_value_grad
        for height in range(local_levels, 0, -1):
            key_acc[height - 1] = key_acc[height - 1] + pair_spread(key_acc[height])
            value_acc[height - 1] = value_acc[height - 1] + pair_spread(value_acc[height])
        qkv_grad = jnp.concatenate(
            [
                query_grad.reshape(tok_count, model_width).astype(jnp.bfloat16),
                key_acc[0].astype(jnp.bfloat16),
                value_acc[0].astype(jnp.bfloat16),
            ],
            axis=1,
        )
        grad_qkv_w = jnp.einsum("td,te->de", normed, qkv_grad, preferred_element_type=jnp.float32)
        normed_one_grad = jnp.einsum(
            "te,de->td", qkv_grad, w_qkv, preferred_element_type=jnp.float32
        )
        unused, norm_back_one = jax.vjp(layer_norm, layer_in, gain_one, bias_one)
        in_grad, grad_gain_one, grad_bias_one = norm_back_one(normed_one_grad)
        grad = in_grad + middle_grad
        unit_grads[layer_at] = jnp.concatenate(
            [
                grad_qkv_w.reshape(model_width, 3, model_width).transpose(1, 0, 2),
                grad_out_w[None],
                grad_up_w.reshape(model_width, ff_blocks, model_width).transpose(1, 0, 2),
                grad_down_w.reshape(ff_blocks, model_width, model_width),
            ],
            axis=0,
        )
        vec_grads[layer_at] = jnp.concatenate(
            [
                grad_gain_one,
                grad_bias_one,
                grad_gain_two,
                grad_bias_two,
                grad_bias_up,
                grad_bias_down,
            ]
        )
    all_units = jnp.concatenate(unit_grads, axis=0)
    all_vecs = jnp.concatenate(vec_grads)
    slot_grads = jnp.zeros_like(all_units).at[unit_slot].set(all_units)
    vec_device = all_vecs.reshape(seq_count * opt_count, -1)
    column_grads = lax.psum_scatter(
        slot_grads.astype(jnp.bfloat16), "opt", scatter_dimension=0, tiled=True
    )
    column_grads = jnp.pad(column_grads, [(0, seq_count - own_slots), (0, 0), (0, 0)])
    owner_grad = lax.psum_scatter(column_grads, "seq", scatter_dimension=0, tiled=True)[0]
    grad_vecs = lax.psum_scatter(vec_device, ("seq", "opt"), scatter_dimension=0, tiled=True)
    grad_vecs = grad_vecs.reshape(-1)
    *step_pieces, owner_stat, owner_basis = rotate_slot(offsets, owner_grad, owner_pieces)
    home_pieces = to_homes(step_pieces, "seq", by_permutes, own_slots)
    base_pieces = renew_bases(offsets, owner_stat, owner_basis)
    whole_shape = jax.ShapeDtypeStruct(masters.shape, jnp.float32)
    new_masters, new_first, new_second, new_stats = call_kernel(
        functools.partial(finish_body, own_slots, len(home_pieces)),
        [whole_shape, whole_shape, whole_shape, jax.ShapeDtypeStruct(stats.shape, jnp.float32)],
        [],
        "finish_slots",
        slot_at,
        masters,
        first_moment,
        second_moment,
        stats,
        *home_pieces,
        smem_count=1,
    )
    (new_bases,) = call_kernel(
        functools.partial(place_body, own_slots),
        [jax.ShapeDtypeStruct(bases.shape, jnp.float32)],
        [],
        "place_bases",
        slot_at,
        *to_homes(base_pieces, "seq", by_permutes, own_slots),
        smem_count=1,
    )
    new_vec_first = BETA_ONE * vec_first + (1.0 - BETA_ONE) * grad_vecs
    new_vec_second = BETA_TWO * vec_second + (1.0 - BETA_TWO) * grad_vecs * grad_vecs
    new_vectors = vec_master - RATE_VECTOR * (new_vec_first / (1.0 - BETA_ONE**STEP)) / (
        jnp.sqrt(new_vec_second / (1.0 - BETA_TWO**STEP)) + ADAM_EPS
    )
    return (
        hidden.astype(jnp.bfloat16)[None],
        grad[None],
        new_masters,
        new_first,
        new_second,
        new_bases,
        new_stats,
        new_vectors,
        new_vec_first,
        new_vec_second,
    )


def solution(mesh):
    placed = (
        P("opt", "seq", None),
        P("opt", "seq", None),
        P("opt", None),
        P(),
        P("opt", "seq", None),
        P("opt", "seq", None),
        P("opt", "seq", None),
        P("opt", None, "seq", None),
        P("opt", None, "seq", None),
        P(("seq", "opt")),
        P(("seq", "opt")),
        P(("seq", "opt")),
    )
    return jax.shard_map(
        per_device,
        mesh=mesh,
        in_specs=placed,
        out_specs=(
            P("opt", "seq", None),
            P("opt", "seq", None),
            P("opt", "seq", None),
            P("opt", "seq", None),
            P("opt", "seq", None),
            P("opt", None, "seq", None),
            P("opt", None, "seq", None),
            P(("seq", "opt")),
            P(("seq", "opt")),
            P(("seq", "opt")),
        ),
        check_vma=False,
    )
```

```python
import functools
import math

import jax
import jax.numpy as jnp
from jax import lax
from jax.experimental import pallas as pl
from jax.experimental.pallas import tpu as pltpu
from jax.sharding import PartitionSpec as P

HEADS = 8
FF = 2048
BLOCK = 16
LAYERS = 2
STEP = 10
MAX_LEN = 4096


HIGH = lax.Precision.HIGHEST
LN_TWO = math.log(2.0)
NEG_FILL = -1e30
NORM_EPS = 1e-05
ADAM_EPS = 1e-08
RATE_MATRIX = 0.03
RATE_VECTOR = 0.2
WEIGHT_DECAY = 0.01
BETA_ONE = 0.9
BETA_TWO = 0.95
BETA_STAT = 0.95

PANEL = 8
LANES = 128
UNIT_COUNT = 24
UNIT_OPT = 0
UNIT_ROW = UNIT_COUNT
UNIT_SLOT = 2 * UNIT_COUNT
DIAG = 128
VMEM_GRANT = 48 * 2**20
IN_VMEM = pl.BlockSpec(memory_space=pltpu.VMEM)
IN_SMEM = pl.BlockSpec(memory_space=pltpu.SMEM)
ANYWHERE = pl.BlockSpec(memory_space=pl.ANY)


def contract(left, right, left_dim, right_dim, precision=None):
    return lax.dot_general(
        left,
        right,
        (((left_dim,), (right_dim,)), ((), ())),
        precision=precision,
        preferred_element_type=jnp.float32,
    )


def split_two(values):
    high = values.astype(jnp.bfloat16)
    return (high, (values - high.astype(jnp.float32)).astype(jnp.bfloat16))


def wide_left(left, right_low, left_dim, right_dim):
    high, rest = split_two(left)
    return contract(high, right_low, left_dim, right_dim) + contract(
        rest, right_low, left_dim, right_dim
    )


def wide_right(left_low, right, left_dim, right_dim):
    high, rest = split_two(right)
    return contract(left_low, high, left_dim, right_dim) + contract(
        left_low, rest, left_dim, right_dim
    )


def call_kernel(
    body, out_shapes, scratch, name, *operands, smem_count=0, any_in=(), any_out=(), aliases=None
):
    def place(at, listed):
        return ANYWHERE if at in listed else IN_VMEM

    return pl.pallas_call(
        body,
        out_shape=out_shapes,
        in_specs=[
            IN_SMEM if at < smem_count else place(at, any_in) for at in range(len(operands))
        ],
        out_specs=[place(at, any_out) for at in range(len(out_shapes))],
        scratch_shapes=scratch,
        input_output_aliases=aliases or {},
        compiler_params=pltpu.CompilerParams(vmem_limit_bytes=VMEM_GRANT),
        name=name,
    )(*operands)


def eliminate(left_part, right_part, turn):
    width = left_part.shape[1]
    turned = pltpu.roll(left_part, turn, 1)
    row_at = lax.broadcasted_iota(jnp.int32, (PANEL, width), 0)
    columns = [
        jnp.broadcast_to(turned[:, i : i + 1], (PANEL, width)) for i in range(PANEL)
    ]
    pivots = jnp.ones((PANEL, width), jnp.float32)
    for i in range(PANEL):
        pivot = jnp.broadcast_to(columns[i][i : i + 1, :], (PANEL, width))
        factor = jnp.where(row_at > i, columns[i] * pltpu.reciprocal(pivot, approx=False), 0.0)
        pivots = jnp.where(row_at == i, pivot, pivots)
        left_part = left_part - factor * jnp.broadcast_to(left_part[i : i + 1, :], (PANEL, width))
        right_part = right_part - factor * jnp.broadcast_to(
            right_part[i : i + 1, :], (PANEL, width)
        )
        for j in range(i + 1, PANEL):
            columns[j] = columns[j] - factor * jnp.broadcast_to(
                columns[j][i : i + 1, :], (PANEL, width)
            )
    scale = lax.rsqrt(pivots)
    return (left_part * scale, right_part * scale)


def factorize(gram, upper, work, inverses):
    count, size, _ = gram.shape
    blocks = size // DIAG
    eye = (
        lax.broadcasted_iota(jnp.int32, (DIAG, DIAG), 0)
        == lax.broadcasted_iota(jnp.int32, (DIAG, DIAG), 1)
    ).astype(jnp.float32)
    for block_at in range(blocks):
        low, top = (block_at * DIAG, (block_at + 1) * DIAG)
        for m in range(count):
            work[m, :, 0:DIAG] = gram[m, low:top, low:top]
            work[m, :, DIAG:] = eye

        def panel(panel_at, carry):
            row = pl.multiple_of(panel_at * PANEL, PANEL)
            turn = lax.rem(DIAG - panel_at * PANEL, DIAG)
            for m in range(count):
                left_part, right_part = eliminate(
                    work[m, pl.ds(row, PANEL), 0:DIAG], work[m, pl.ds(row, PANEL), DIAG:], turn
                )
                inverses[m, block_at, pl.ds(row, PANEL), :] = right_part
                both = jnp.concatenate([left_part, right_part], axis=1)
                work[m] = work[m] - contract(left_part, both, 0, 0, HIGH)
            return carry

        lax.fori_loop(0, DIAG // PANEL, panel, 0)
        for m in range(count):
            if block_at + 1 < blocks:
                right_of = contract(inverses[m, block_at], gram[m, low:top, top:], 1, 0, HIGH)
                upper[m, low:top, top:] = right_of
                for other in range(block_at + 1, blocks):
                    skip = (other - block_at - 1) * DIAG
                    gram[m, other * DIAG : (other + 1) * DIAG, other * DIAG :] -= contract(
                        right_of[:, skip : skip + DIAG], right_of[:, skip:], 0, 0, HIGH
                    )


def renew_body(piece_count, *refs):
    offset_ref, stat_ref, basis_ref = refs[:3]
    piece_refs = refs[3 : 3 + piece_count]
    product, gram, upper, work, inverses = refs[3 + piece_count :]
    count, size, _ = stat_ref.shape
    for m in range(count):
        product[m] = wide_left(stat_ref[m], basis_ref[m], 1, 0)
        gram[m] = contract(product[m], product[m], 0, 0, HIGH)
    factorize(gram, upper, work, inverses)
    for low in range(0, size, DIAG):
        top = low + DIAG
        for m in range(count):
            rest = product[m, :, low:top]
            if low:
                rest = rest - contract(product[m, :, :low], upper[m, :low, low:top], 1, 0, HIGH)
            product[m, :, low:top] = contract(rest, inverses[m, low // DIAG], 1, 1, HIGH)
    rows = piece_refs[0].shape[1]
    for piece_at in range(piece_count):
        row = pl.multiple_of(offset_ref[piece_at], 8)
        piece_refs[piece_at][...] = product[:, pl.ds(row, rows), :].astype(jnp.bfloat16)


def renew_bases(offsets, new_stat, basis_low):
    count, size, _ = new_stat.shape
    piece_count = offsets.shape[0]
    square = pltpu.VMEM((count, size, size), jnp.float32)
    return call_kernel(
        functools.partial(renew_body, piece_count),
        [
            jax.ShapeDtypeStruct((count, size // piece_count, size), jnp.bfloat16)
            for _ in range(piece_count)
        ],
        [
            square,
            square,
            square,
            pltpu.VMEM((count, DIAG, 2 * DIAG), jnp.float32),
            pltpu.VMEM((count, size // DIAG, DIAG, DIAG), jnp.float32),
        ],
        "renew_bases",
        offsets,
        new_stat,
        basis_low,
        smem_count=1,
    )


def pack_body(slot_ref, stats, bases, first, second, *piece_refs):
    for piece_at, piece_ref in enumerate(piece_refs):
        slot = slot_ref[piece_at]
        piece_ref[0:2] = stats[slot].astype(jnp.bfloat16)
        piece_ref[2:4] = bases[slot].astype(jnp.bfloat16)
        piece_ref[4] = first[slot].astype(jnp.bfloat16)
        piece_ref[5] = second[slot].astype(jnp.bfloat16)


def rotate_body(piece_count, *refs):
    offset_ref, grad_ref = refs[:2]
    given = refs[2 : 2 + piece_count]
    sent = refs[2 + piece_count : 2 + 2 * piece_count]
    stat_ref, basis_ref, whole, results = refs[2 + 2 * piece_count :]
    rows = given[0].shape[1]
    for piece_at in range(piece_count):
        row = pl.multiple_of(offset_ref[piece_at], 8)
        whole[:, pl.ds(row, rows), :] = given[piece_at][...].astype(jnp.float32)
    grad = grad_ref[...]
    left = whole[2].astype(jnp.bfloat16)
    right = whole[3].astype(jnp.bfloat16)
    basis_ref[0] = left
    basis_ref[1] = right
    results[0] = contract(grad, grad, 1, 1)
    results[1] = contract(grad, grad, 0, 0)
    stat_ref[0] = BETA_STAT * whole[0] + (1.0 - BETA_STAT) * results[0]
    stat_ref[1] = BETA_STAT * whole[1] + (1.0 - BETA_STAT) * results[1]
    rotated = wide_left(contract(left, grad, 0, 0), right, 1, 0)
    results[2] = rotated
    new_first = BETA_ONE * whole[4] + (1.0 - BETA_ONE) * rotated
    new_second = BETA_TWO * whole[5] + (1.0 - BETA_TWO) * rotated * rotated
    direction = (
        new_first
        / (1.0 - BETA_ONE**STEP)
        / (jnp.sqrt(new_second / (1.0 - BETA_TWO**STEP)) + ADAM_EPS)
    )
    results[3] = wide_right(left, wide_left(direction, right, 1, 1), 1, 0)
    for piece_at in range(piece_count):
        row = pl.multiple_of(offset_ref[piece_at], 8)
        sent[piece_at][...] = results[:, pl.ds(row, rows), :].astype(jnp.bfloat16)


def rotate_slot(offsets, grad, pieces):
    size = grad.shape[0]
    piece_count = offsets.shape[0]
    return call_kernel(
        functools.partial(rotate_body, piece_count),
        [
            jax.ShapeDtypeStruct((4, size // piece_count, size), jnp.bfloat16)
            for _ in range(piece_count)
        ]
        + [
            jax.ShapeDtypeStruct((2, size, size), jnp.float32),
            jax.ShapeDtypeStruct((2, size, size), jnp.bfloat16),
        ],
        [
            pltpu.VMEM((6, size, size), jnp.float32),
            pltpu.VMEM((4, size, size), jnp.float32),
        ],
        "rotate_slot",
        offsets,
        grad,
        *pieces,
        smem_count=1,
    )


def finish_body(own_slots, piece_count, *refs):
    slot_ref, masters, first, second, stats = refs[:5]
    given = refs[5 : 5 + piece_count]
    new_masters, new_first, new_second, new_stats = refs[5 + piece_count :]
    for piece_at in range(piece_count):
        slot = slot_ref[piece_at]

        @pl.when(slot < own_slots)
        def _():
            piece = given[piece_at]
            rotated = piece[2].astype(jnp.float32)
            update = piece[3].astype(jnp.float32)
            new_first[slot] = BETA_ONE * first[slot] + (1.0 - BETA_ONE) * rotated
            new_second[slot] = BETA_TWO * second[slot] + (1.0 - BETA_TWO) * rotated * rotated
            new_masters[slot] = masters[slot] - RATE_MATRIX * (
                update + WEIGHT_DECAY * masters[slot]
            )
            new_stats[slot] = BETA_STAT * stats[slot] + (1.0 - BETA_STAT) * piece[
                0:2
            ].astype(jnp.float32)


def place_body(own_slots, slot_ref, *refs):
    new_bases = refs[-1]
    for piece_at, piece in enumerate(refs[:-1]):
        slot = slot_ref[piece_at]

        @pl.when(slot < own_slots)
        def _():
            new_bases[slot] = piece[...].astype(jnp.float32)


def swap_pieces(pieces, axis):
    device_count = lax.axis_size(axis)
    return [pieces[0]] + [
        lax.ppermute(pieces[k], axis, [(i, i ^ k) for i in range(device_count)])
        for k in range(1, device_count)
    ]


def to_owners(pieces, axis, by_permutes):
    if by_permutes:
        return swap_pieces(pieces, axis)
    stacked = jnp.stack(pieces)
    device_count = lax.axis_size(axis)
    padded = jnp.pad(stacked, [(0, device_count - len(pieces))] + [(0, 0)] * (stacked.ndim - 1))
    swapped = lax.all_to_all(padded, axis, 0, 0, tiled=True)
    kinds, _, width = pieces[0].shape
    return [jnp.swapaxes(swapped, 0, 1).reshape(kinds, -1, width)]


def to_homes(pieces, axis, by_permutes, own_slots):
    if by_permutes:
        return swap_pieces(pieces, axis)
    kinds, _, width = pieces[0].shape
    device_count = lax.axis_size(axis)
    shaped = jnp.swapaxes(pieces[0].reshape(kinds, device_count, -1, width), 0, 1)
    swapped = lax.all_to_all(shaped, axis, 0, 0, tiled=True)
    return [swapped[slot] for slot in range(own_slots)]


def partner(value, axis, apart):
    return lax.ppermute(value, axis, [(i, i ^ 1 << apart) for i in range(lax.axis_size(axis))])


def pair_mean(values):
    shaped = values.reshape((values.shape[0] // 2, 2) + values.shape[1:])
    return 0.5 * (shaped[:, 0] + shaped[:, 1])


def pair_spread(grads):
    return 0.5 * jnp.repeat(grads, 2, axis=0)


def sum_rows(values):
    return jnp.sum(values, axis=0, keepdims=True)


def norm_parts(values):
    centred = values - jnp.mean(values, axis=-1, keepdims=True)
    recip = lax.rsqrt(jnp.mean(centred * centred, axis=-1, keepdims=True) + NORM_EPS)
    return (centred * recip, recip)


def norm_back(grad, gain, normed, recip):
    scaled = grad * gain
    return recip * (
        scaled
        - jnp.mean(scaled, axis=-1, keepdims=True)
        - normed * jnp.mean(scaled * normed, axis=-1, keepdims=True)
    )


def half_matrix(shape, fine_dim):
    fine = lax.broadcasted_iota(jnp.int32, shape, fine_dim)
    coarse = lax.broadcasted_iota(jnp.int32, shape, 1 - fine_dim)
    return jnp.where(fine >> 1 == coarse, 0.5, 0.0).astype(jnp.bfloat16)


def pool(rows_low):
    count = rows_low.shape[0]
    return contract(half_matrix((count // 2, count), 1), rows_low, 1, 0).astype(jnp.bfloat16)


def spread(grads):
    count = grads.shape[0]
    return wide_right(half_matrix((2 * count, count), 0), grads, 1, 0)


def norm_cdf(values):
    return 0.5 * (1.0 + lax.erf(values * math.sqrt(0.5)))


def local_count(tok_count):
    return (tok_count // BLOCK).bit_length() - 1


def key_width(tok_count, tree_bits):
    rows = 2 * (tok_count - BLOCK) + BLOCK * tree_bits
    return -(-rows // LANES) * LANES


def score_offsets(tok_count, tree_bits, span_bits):
    token = jnp.arange(tok_count, dtype=jnp.int32)[:, None]
    parts = []
    for height in range(local_count(tok_count)):
        row = jnp.arange(tok_count >> height, dtype=jnp.int32)[None, :]
        apart = token // (BLOCK << height) ^ row // BLOCK
        counted = apart <= 1 if height == 0 else apart == 1
        parts.append(jnp.where(counted, height * LN_TWO, NEG_FILL))
    for bit_at in range(tree_bits):
        offset = (local_count(tok_count) + bit_at) * LN_TWO
        parts.append(
            jnp.broadcast_to(
                jnp.where(bit_at + 1 <= span_bits, offset, NEG_FILL), (tok_count, BLOCK)
            )
        )
    used = sum(part.shape[1] for part in parts)
    rest = key_width(tok_count, tree_bits) - used
    parts.append(jnp.full((tok_count, rest), NEG_FILL, jnp.float32))
    return jnp.concatenate(parts, axis=1).astype(jnp.float32)


def stack_keys(own_rows, far_rows):
    parts = [own_rows]
    for _ in range(local_count(own_rows.shape[0]) - 1):
        parts.append(pool(parts[-1]))
    parts = parts + far_rows
    rest = key_width(own_rows.shape[0], len(far_rows)) - sum(part.shape[0] for part in parts)
    if rest:
        parts.append(jnp.zeros((rest, own_rows.shape[1]), jnp.bfloat16))
    return jnp.concatenate(parts, axis=0)


def by_heads(pair):
    lane = lax.broadcasted_iota(jnp.int32, pair.shape, 1)
    zero = jnp.zeros_like(pair)
    first = lane < LANES // 2
    return jnp.concatenate([jnp.where(first, pair, zero), jnp.where(first, zero, pair)], axis=0)


def from_heads(both):
    count = both.shape[0] // 2
    lane = lax.broadcasted_iota(jnp.int32, (count, LANES), 1)
    return jnp.where(lane < LANES // 2, both[:count], both[count:])


def attend(qkv, far_rows, offsets, probs, mixed):
    width = qkv.shape[1] // 3
    score_scale = (width // HEADS) ** (-0.5)
    stack = stack_keys(qkv[:, width:], far_rows)
    both_offsets = jnp.concatenate([offsets, offsets], axis=0)
    for pair_at in range(width // LANES):
        low, top = (pair_at * LANES, (pair_at + 1) * LANES)
        scores = (
            contract(by_heads(qkv[:, low:top]), stack[:, low:top], 1, 1) * score_scale
            + both_offsets
        )
        expo = jnp.exp(scores - jnp.max(scores, axis=1, keepdims=True))
        weights = expo / jnp.sum(expo, axis=1, keepdims=True)
        probs[pair_at] = weights
        result = contract(
            weights.astype(jnp.bfloat16), stack[:, width + low : width + top], 1, 0
        )
        mixed[:, low:top] = from_heads(result).astype(jnp.bfloat16)


def attend_back(qkv, far_rows, probs, mixed_grad, query_grad, key_grads, far_grads):
    tok_count, width = mixed_grad.shape
    score_scale = (width // HEADS) ** (-0.5)
    stack = stack_keys(qkv[:, width:], far_rows)
    local_levels = local_count(tok_count)
    far_start = 2 * (tok_count - BLOCK)
    for pair_at in range(width // LANES):
        low, top = (pair_at * LANES, (pair_at + 1) * LANES)
        queries = by_heads(qkv[:, low:top])
        grads = by_heads(mixed_grad[:, low:top])
        weights = probs[pair_at]
        prob_grad = contract(grads, stack[:, width + low : width + top], 1, 1)
        inner = jnp.sum(weights * prob_grad, axis=1, keepdims=True)
        score_grad = (weights * (prob_grad - inner)).astype(jnp.bfloat16)
        query_grad[:, low:top] = (
            from_heads(contract(score_grad, stack[:, low:top], 1, 0)) * score_scale
        ).astype(jnp.bfloat16)
        for start, part in (
            (low, contract(score_grad, queries, 0, 0) * score_scale),
            (width + low, contract(weights.astype(jnp.bfloat16), grads, 0, 0)),
        ):
            for far_at, far_grad in enumerate(far_grads):
                row = far_start + BLOCK * far_at
                far_grad[:, start : start + LANES] = part[row : row + BLOCK]
            folded = None
            for height in reversed(range(local_levels)):
                row = 2 * (tok_count - (tok_count >> height))
                own = part[row : row + (tok_count >> height)]
                folded = own if folded is None else own + spread(folded)
            key_grads[:, start : start + LANES] = folded


class Units:
    def __init__(self, meta, packed, store, sems, units):
        self.store = store
        self.place = {unit: at for at, unit in enumerate(units)}
        self.waiting = {}
        rows = store.shape[2]
        for at, unit in enumerate(units):
            row = pl.multiple_of(meta[UNIT_ROW + unit], rows)
            copy = pltpu.make_async_copy(
                packed.at[:, meta[UNIT_OPT + unit], pl.ds(row, rows), :],
                store.at[at],
                sems.at[at],
            )
            copy.start()
            self.waiting[unit] = copy

    def __getitem__(self, unit):
        if unit in self.waiting:
            self.waiting.pop(unit).wait()
        width = self.store.shape[3]
        return self.store[self.place[unit]].reshape(width, width)


class Grads:
    def __init__(self, meta, slots, store, sems):
        self.meta, self.slots, self.store, self.sems = (meta, slots, store, sems)
        self.copies = []

    def put(self, unit, left_low, right_low):
        at = len(self.copies)
        self.store[at] = contract(left_low, right_low, 0, 0).astype(jnp.bfloat16)
        copy = pltpu.make_async_copy(
            self.store.at[at], self.slots.at[self.meta[UNIT_SLOT + unit]], self.sems.at[at]
        )
        copy.start()
        self.copies.append(copy)

    def finish(self):
        for copy in self.copies:
            copy.wait()


def project(hidden, units, first_unit, gain, bias, normed_ref, qkv_ref, near_ref):
    width = hidden.shape[1]
    normed, _ = norm_parts(hidden)
    normed_low = (normed * gain + bias).astype(jnp.bfloat16)
    normed_ref[...] = normed_low
    for part in range(3):
        qkv_ref[:, part * width : (part + 1) * width] = contract(
            normed_low, units[first_unit + part], 1, 0
        ).astype(jnp.bfloat16)
    near = qkv_ref[:, width:]
    for _ in range(local_count(near.shape[0])):
        near = pool(near)
    near_ref[...] = near


def feed_forward(middle, units, first_unit, vec, vec_at, normed_ref, pre_ref, act_ref):
    width = middle.shape[1]
    normed, _ = norm_parts(middle)
    normed_low = (normed * vec[vec_at + 2 : vec_at + 3] + vec[vec_at + 3 : vec_at + 4]).astype(
        jnp.bfloat16
    )
    normed_ref[...] = normed_low
    total = middle
    ff_blocks = FF // width
    for part in range(ff_blocks):
        low, top = (part * width, (part + 1) * width)
        row = vec_at + 4 + part
        pre = contract(normed_low, units[first_unit + 4 + part], 1, 0) + vec[row : row + 1]
        act = (pre * norm_cdf(pre)).astype(jnp.bfloat16)
        pre_ref[:, low:top] = pre
        act_ref[:, low:top] = act
        total = total + contract(act, units[first_unit + 4 + ff_blocks + part], 1, 0)
    row = vec_at + 4 + ff_blocks
    return total + vec[row : row + 1]


def feed_back(
    grad, middle, normed_low, pre_ref, act_ref, units, grads, first_unit, vec, vec_at, vec_grads, at
):
    width = middle.shape[1]
    ff_blocks = FF // width
    down_grad = grad.astype(jnp.bfloat16)
    normed_grad = jnp.zeros(middle.shape, jnp.float32)
    for part in range(ff_blocks):
        low, top = (part * width, (part + 1) * width)
        down_unit = first_unit + 4 + ff_blocks + part
        grads.put(down_unit, act_ref[:, low:top], down_grad)
        pre = pre_ref[:, low:top]
        slope = norm_cdf(pre) + pre * jnp.exp(-0.5 * pre * pre) * (1.0 / math.sqrt(2.0 * math.pi))
        pre_grad = (contract(down_grad, units[down_unit], 1, 1) * slope).astype(jnp.bfloat16)
        grads.put(first_unit + 4 + part, normed_low, pre_grad)
        vec_grads[at + 2 + part : at + 3 + part] = sum_rows(pre_grad.astype(jnp.float32))
        normed_grad = normed_grad + contract(pre_grad, units[first_unit + 4 + part], 1, 1)
    row = at + 2 + ff_blocks
    vec_grads[row : row + 1] = sum_rows(grad)
    normed, recip = norm_parts(middle)
    vec_grads[at : at + 1] = sum_rows(normed_grad * normed)
    vec_grads[at + 1 : at + 2] = sum_rows(normed_grad)
    return grad + norm_back(normed_grad, vec[vec_at + 2 : vec_at + 3], normed, recip)


def project_back(
    middle_grad, hidden, normed_low, query_grad, key_grads, near_grads, units, grads, first_unit,
    vec, vec_at, vec_grads,
):
    width = hidden.shape[1]
    near = near_grads[...]
    for _ in range(local_count(hidden.shape[0])):
        near = spread(near)
    rows_low = (key_grads[...] + near).astype(jnp.bfloat16)
    parts = (query_grad[...], rows_low[:, :width], rows_low[:, width:])
    normed_grad = jnp.zeros(hidden.shape, jnp.float32)
    for part, part_grad in enumerate(parts):
        grads.put(first_unit + part, normed_low, part_grad)
        normed_grad = normed_grad + contract(part_grad, units[first_unit + part], 1, 1)
    normed, recip = norm_parts(hidden)
    vec_grads[0:1] = sum_rows(normed_grad * normed)
    vec_grads[1:2] = sum_rows(normed_grad)
    return middle_grad + norm_back(normed_grad, vec[vec_at : vec_at + 1], normed, recip)


def first_body(per_layer, meta, vec, inputs, packed, normed, qkv, near, store, sems):
    units = Units(meta, packed, store, sems, range(3))
    project(inputs[...].astype(jnp.float32), units, 0, vec[0:1], vec[1:2], normed, qkv, near)


def middle_body(per_layer, vec_rows, tree_bits, meta, vec, offsets, inputs, qkv, *refs):
    far, refs = (refs[:tree_bits], refs[tree_bits:])
    packed, probs, mixed, middle, normed_two, pre, act, hidden, normed, next_qkv, near = refs[:11]
    store, sems = refs[11:]
    units = Units(meta, packed, store, sems, range(3, per_layer + 3))
    attend(qkv[...], [ref[...] for ref in far], offsets[...], probs, mixed)
    middle[...] = inputs[...].astype(jnp.float32) + contract(mixed[...], units[3], 1, 0)
    hidden[...] = feed_forward(middle[...], units, 0, vec, 0, normed_two, pre, act)
    project(
        hidden[...], units, per_layer, vec[vec_rows : vec_rows + 1],
        vec[vec_rows + 1 : vec_rows + 2], normed, next_qkv, near,
    )


def turn_body(per_layer, vec_rows, tree_bits, meta, vec, offsets, cotangent, hidden, qkv, *refs):
    far, refs = (refs[:tree_bits], refs[tree_bits:])
    packed, outputs, middle_grad, query_grad, key_grads, vec_grads, slots = refs[:7]
    far_grads, refs = (refs[7 : 7 + tree_bits], refs[7 + tree_bits :])
    store, sems, grad_store, grad_sems, probs, mixed, normed_two, pre, act = refs
    units = Units(meta, packed, store, sems, range(per_layer + 3, 2 * per_layer))
    grads = Grads(meta, slots, grad_store, grad_sems)
    far_rows = [ref[...] for ref in far]
    attend(qkv[...], far_rows, offsets[...], probs, mixed)
    middle = hidden[...] + contract(mixed[...], units[per_layer + 3], 1, 0)
    outputs[...] = feed_forward(
        middle, units, per_layer, vec, vec_rows, normed_two, pre, act
    ).astype(jnp.bfloat16)
    vec_grads[...] = jnp.zeros_like(vec_grads)
    grad = feed_back(
        cotangent[...].astype(jnp.float32), middle, normed_two[...], pre, act, units, grads,
        per_layer, vec, vec_rows, vec_grads, 2,
    )
    middle_grad[...] = grad
    branch_grad = grad.astype(jnp.bfloat16)
    grads.put(per_layer + 3, mixed[...], branch_grad)
    mixed_grad = contract(branch_grad, units[per_layer + 3], 1, 1).astype(jnp.bfloat16)
    attend_back(qkv[...], far_rows, probs, mixed_grad, query_grad, key_grads, far_grads)
    grads.finish()


def lower_body(per_layer, vec_rows, tree_bits, meta, vec, *refs):
    hidden, normed_one, query_in, key_in, near_in, middle_in = refs[:6]
    probs, mixed, middle, normed_two, pre, act, qkv = refs[6:13]
    far, refs = (refs[13 : 13 + tree_bits], refs[13 + tree_bits :])
    packed, _, middle_grad, query_grad, key_grads, vec_grads, slots = refs[:7]
    far_grads, refs = (refs[7 : 7 + tree_bits], refs[7 + tree_bits :])
    store, sems, grad_store, grad_sems = refs
    upper_units = list(range(per_layer, per_layer + 3))
    units = Units(
        meta, packed, store, sems, upper_units + list(range(3 + (per_layer - 4) // 2 + 1, per_layer))
        + list(range(3, 3 + (per_layer - 4) // 2 + 1)),
    )
    grads = Grads(meta, slots, grad_store, grad_sems)
    vec_grads[...] = jnp.zeros_like(vec_grads)
    grad = project_back(
        middle_in[...], hidden[...], normed_one[...], query_in, key_in, near_in, units, grads,
        per_layer, vec, vec_rows, vec_grads,
    )
    grad = feed_back(
        grad, middle[...], normed_two[...], pre, act, units, grads, 0, vec, 0, vec_grads, 2
    )
    middle_grad[...] = grad
    branch_grad = grad.astype(jnp.bfloat16)
    grads.put(3, mixed[...], branch_grad)
    mixed_grad = contract(branch_grad, units[3], 1, 1).astype(jnp.bfloat16)
    attend_back(
        qkv[...], [ref[...] for ref in far], probs, mixed_grad, query_grad, key_grads, far_grads
    )
    grads.finish()


def last_body(meta, vec, inputs, normed_one, query_in, key_in, near_in, middle_in, *refs):
    packed, _, input_grad, vec_grads, slots, store, sems, grad_store, grad_sems = refs
    units = Units(meta, packed, store, sems, range(3))
    grads = Grads(meta, slots, grad_store, grad_sems)
    vec_grads[...] = jnp.zeros_like(vec_grads)
    input_grad[...] = project_back(
        middle_in[...], inputs[...].astype(jnp.float32), normed_one[...], query_in, key_in,
        near_in, units, grads, 0, vec, 0, vec_grads,
    )
    grads.finish()


def coarse_up(own, seq_index, tree_bits):
    far_list = []
    for bit_at in range(tree_bits):
        far = partner(own, "seq", bit_at)
        far_list.append(far)
        if bit_at + 1 < tree_bits:
            upper = seq_index >> bit_at & 1 == 1
            joined = jnp.where(
                upper, jnp.concatenate([far, own]), jnp.concatenate([own, far])
            ).astype(jnp.float32)
            own = pair_mean(joined).astype(jnp.bfloat16)
    return far_list


def coarse_down(far_grads, seq_index):
    above = None
    for bit_at in reversed(range(len(far_grads))):
        upper = seq_index >> bit_at & 1 == 1
        sent = far_grads[bit_at]
        own = 0.0
        if above is not None:
            wide = pair_spread(above)
            own = jnp.where(upper, wide[BLOCK:], wide[:BLOCK])
            sent = sent + jnp.where(upper, wide[:BLOCK], wide[BLOCK:])
        above = own + partner(sent.astype(jnp.bfloat16), "seq", bit_at).astype(jnp.float32)
    return above


def per_device(
    inputs,
    cotangent,
    seq_lengths,
    unit_slot,
    masters,
    first_moment,
    second_moment,
    bases,
    stats,
    vec_master,
    vec_first,
    vec_second,
):
    seq_count = lax.axis_size("seq")
    opt_count = lax.axis_size("opt")
    seq_index = lax.axis_index("seq")
    tok_count = inputs.shape[1]
    model_width = inputs.shape[2]
    own_slots = masters.shape[0]
    row_count = masters.shape[1]
    ff_blocks = FF // model_width
    per_layer = 4 + 2 * ff_blocks
    vec_width = 5 * model_width + FF
    long_devs = min(max(MAX_LEN // tok_count, 1), seq_count)
    tree_bits = long_devs.bit_length() - 1
    size = seq_count * row_count
    by_permutes = seq_count <= 8
    if by_permutes:
        relative = jnp.arange(seq_count, dtype=jnp.int32) ^ seq_index
        offsets = relative * row_count
        slot_at = relative
    else:
        offsets = jnp.zeros((1,), jnp.int32)
        slot_at = jnp.arange(own_slots, dtype=jnp.int32)
    packed_pieces = call_kernel(
        pack_body,
        [
            jax.ShapeDtypeStruct((6, row_count, model_width), jnp.bfloat16)
            for _ in range(slot_at.shape[0])
        ],
        [],
        "pack_slots",
        jnp.minimum(slot_at, own_slots - 1),
        stats,
        bases,
        first_moment,
        second_moment,
        smem_count=1,
    )
    owner_pieces = to_owners(packed_pieces, "seq", by_permutes)
    vec_count = vec_master.shape[0]
    own_rows = own_slots * row_count
    vec_block = jnp.pad(
        vec_master.astype(jnp.bfloat16)[None], [(0, 15), (0, model_width - vec_count)]
    )
    gathered = lax.all_gather(
        jnp.concatenate(
            [masters.astype(jnp.bfloat16).reshape(own_rows, model_width), vec_block]
        )[None],
        ("seq", "opt"),
        axis=0,
        tiled=True,
    )
    vec = gathered[:, own_rows, :vec_count].reshape(-1, model_width).astype(jnp.float32)
    if row_count % 16 == 0:
        unit_rows = row_count
        packed = gathered.reshape(seq_count, opt_count, own_rows + 16, model_width)
    else:
        unit_rows = size
        packed = (
            gathered[:, :own_rows]
            .reshape(seq_count, opt_count, own_slots, row_count, model_width)
            .transpose(1, 2, 0, 3, 4)
            .reshape(1, opt_count, own_slots * size, model_width)
        )
    meta = jnp.concatenate(
        [unit_slot // own_slots, unit_slot % own_slots * unit_rows, unit_slot]
    ).astype(jnp.int32)
    span_bits = jnp.zeros((), jnp.int32)
    for bit_at in range(tree_bits + 1):
        start_dev = seq_index >> bit_at << bit_at
        span_bits = jnp.where(
            seq_lengths[0, start_dev] == tok_count * (1 << bit_at), bit_at, span_bits
        )
    offsets_in = score_offsets(tok_count, tree_bits, span_bits)
    width_in = offsets_in.shape[1]
    pair_count = model_width // LANES
    vec_rows = vec_width // model_width
    square = (model_width, model_width)

    def units_in(count):
        return [
            pltpu.VMEM((count, size // unit_rows, unit_rows, model_width), jnp.bfloat16),
            pltpu.SemaphoreType.DMA((count,)),
        ]

    def grads_out(count):
        return [pltpu.VMEM((count,) + square, jnp.bfloat16), pltpu.SemaphoreType.DMA((count,))]

    def low_of(*shape):
        return jax.ShapeDtypeStruct(shape, jnp.bfloat16)

    def full_of(*shape):
        return jax.ShapeDtypeStruct(shape, jnp.float32)

    projected = [
        low_of(tok_count, model_width),
        low_of(tok_count, 3 * model_width),
        low_of(BLOCK, 2 * model_width),
    ]
    attended = [
        full_of(pair_count, 2 * tok_count, width_in),
        low_of(tok_count, model_width),
    ]
    fed = [
        low_of(tok_count, model_width),
        full_of(tok_count, FF),
        low_of(tok_count, FF),
    ]
    back = [
        full_of(tok_count, model_width),
        low_of(tok_count, model_width),
        full_of(tok_count, 2 * model_width),
        full_of(16, model_width),
        low_of(UNIT_COUNT, *square),
    ] + [full_of(BLOCK, 2 * model_width)] * tree_bits
    normed_zero, qkv_zero, near_zero = call_kernel(
        functools.partial(first_body, per_layer),
        projected,
        units_in(3),
        "project_first",
        meta,
        vec,
        inputs[0],
        packed,
        smem_count=1,
        any_in=(3,),
    )
    far_zero = coarse_up(near_zero, seq_index, tree_bits)
    (
        probs, mixed, middle, normed_two, pre, act, hidden, normed_one, qkv_one, near_one,
    ) = call_kernel(
        functools.partial(middle_body, per_layer, vec_rows, tree_bits),
        attended + [full_of(tok_count, model_width)] + fed + [full_of(tok_count, model_width)]
        + projected,
        units_in(per_layer),
        "layer_first",
        meta,
        vec,
        offsets_in,
        inputs[0],
        qkv_zero,
        *far_zero,
        packed,
        smem_count=1,
        any_in=(5 + tree_bits,),
    )
    far_one = coarse_up(near_one, seq_index, tree_bits)
    outputs, middle_grad, query_grad, key_grads, vec_grads_up, slot_grads, *far_grads = call_kernel(
        functools.partial(turn_body, per_layer, vec_rows, tree_bits),
        [low_of(tok_count, model_width)] + back,
        units_in(per_layer - 3)
        + grads_out(per_layer - 3)
        + [pltpu.VMEM(shape.shape, shape.dtype) for shape in attended + fed],
        "layer_turn",
        meta,
        vec,
        offsets_in,
        cotangent[0],
        hidden,
        qkv_one,
        *far_one,
        packed,
        smem_count=1,
        any_in=(6 + tree_bits,),
        any_out=(5,),
    )
    near_grads = coarse_down(far_grads, seq_index)
    middle_grad, query_grad, key_grads, vec_grads_mid, slot_grads, *far_grads = call_kernel(
        functools.partial(lower_body, per_layer, vec_rows, tree_bits),
        back,
        units_in(per_layer) + grads_out(per_layer),
        "layer_back",
        meta,
        vec,
        hidden,
        normed_one,
        query_grad,
        key_grads,
        near_grads,
        middle_grad,
        probs,
        mixed,
        middle,
        normed_two,
        pre,
        act,
        qkv_zero,
        *far_zero,
        packed,
        slot_grads,
        smem_count=1,
        any_in=(15 + tree_bits, 16 + tree_bits),
        any_out=(4,),
        aliases={16 + tree_bits: 4},
    )
    near_grads = coarse_down(far_grads, seq_index)
    input_grad, vec_grads_low, slot_grads = call_kernel(
        last_body,
        [full_of(tok_count, model_width), full_of(16, model_width), low_of(UNIT_COUNT, *square)],
        units_in(3) + grads_out(3),
        "project_back",
        meta,
        vec,
        inputs[0],
        normed_zero,
        query_grad,
        key_grads,
        near_grads,
        middle_grad,
        packed,
        slot_grads,
        smem_count=1,
        any_in=(8, 9),
        any_out=(2,),
        aliases={9: 2},
    )
    vec_sum = jnp.concatenate(
        [vec_grads_low[0:2], vec_grads_mid[2:vec_rows], vec_grads_mid[0:2], vec_grads_up[2:vec_rows]]
    )
    for axis in ("opt", "seq"):
        for bit_at in range(lax.axis_size(axis).bit_length() - 1):
            vec_sum = vec_sum + partner(vec_sum, axis, bit_at)
    grad_vecs = lax.dynamic_slice_in_dim(
        vec_sum.reshape(-1), (seq_index * opt_count + lax.axis_index("opt")) * vec_count, vec_count
    )
    column_grads = lax.psum_scatter(
        slot_grads, "opt", scatter_dimension=0, tiled=True
    )
    column_grads = jnp.pad(column_grads, [(0, seq_count - own_slots), (0, 0), (0, 0)])
    owner_grad = lax.psum_scatter(column_grads, "seq", scatter_dimension=0, tiled=True)[0]
    *step_pieces, owner_stat, owner_basis = rotate_slot(offsets, owner_grad, owner_pieces)
    home_pieces = to_homes(step_pieces, "seq", by_permutes, own_slots)
    base_pieces = renew_bases(offsets, owner_stat, owner_basis)
    whole_shape = jax.ShapeDtypeStruct(masters.shape, jnp.float32)
    new_masters, new_first, new_second, new_stats = call_kernel(
        functools.partial(finish_body, own_slots, len(home_pieces)),
        [whole_shape, whole_shape, whole_shape, jax.ShapeDtypeStruct(stats.shape, jnp.float32)],
        [],
        "finish_slots",
        slot_at,
        masters,
        first_moment,
        second_moment,
        stats,
        *home_pieces,
        smem_count=1,
    )
    (new_bases,) = call_kernel(
        functools.partial(place_body, own_slots),
        [jax.ShapeDtypeStruct(bases.shape, jnp.float32)],
        [],
        "place_bases",
        slot_at,
        *to_homes(base_pieces, "seq", by_permutes, own_slots),
        smem_count=1,
    )
    new_vec_first = BETA_ONE * vec_first + (1.0 - BETA_ONE) * grad_vecs
    new_vec_second = BETA_TWO * vec_second + (1.0 - BETA_TWO) * grad_vecs * grad_vecs
    new_vectors = vec_master - RATE_VECTOR * (new_vec_first / (1.0 - BETA_ONE**STEP)) / (
        jnp.sqrt(new_vec_second / (1.0 - BETA_TWO**STEP)) + ADAM_EPS
    )
    return (
        outputs[None],
        input_grad[None],
        new_masters,
        new_first,
        new_second,
        new_bases,
        new_stats,
        new_vectors,
        new_vec_first,
        new_vec_second,
    )


def solution(mesh):
    placed = (
        P("opt", "seq", None),
        P("opt", "seq", None),
        P("opt", None),
        P(),
        P("opt", "seq", None),
        P("opt", "seq", None),
        P("opt", "seq", None),
        P("opt", None, "seq", None),
        P("opt", None, "seq", None),
        P(("seq", "opt")),
        P(("seq", "opt")),
        P(("seq", "opt")),
    )
    return jax.shard_map(
        per_device,
        mesh=mesh,
        in_specs=placed,
        out_specs=(
            P("opt", "seq", None),
            P("opt", "seq", None),
            P("opt", "seq", None),
            P("opt", "seq", None),
            P("opt", "seq", None),
            P("opt", None, "seq", None),
            P("opt", None, "seq", None),
            P(("seq", "opt")),
            P(("seq", "opt")),
            P(("seq", "opt")),
        ),
        check_vma=False,
    )
```

```python
import functools
import math

import jax
import jax.numpy as jnp
from jax import lax
from jax.experimental import pallas as pl
from jax.experimental.pallas import tpu as pltpu
from jax.sharding import PartitionSpec as P

HEADS = 8
FF = 2048
BLOCK = 16
LAYERS = 2
STEP = 10
MAX_LEN = 4096


HIGH = lax.Precision.HIGHEST
LN_TWO = math.log(2.0)
NEG_FILL = -1e30
NORM_EPS = 1e-05
ADAM_EPS = 1e-08
RATE_MATRIX = 0.03
RATE_VECTOR = 0.2
WEIGHT_DECAY = 0.01
BETA_ONE = 0.9
BETA_TWO = 0.95
BETA_STAT = 0.95

SUBLANES = 8
PANEL = 16
FLOPS_PER_US = 1_150_000_000
LANES = 128
UNIT_COUNT = 24
UNIT_OPT = 0
UNIT_ROW = UNIT_COUNT
UNIT_SLOT = 2 * UNIT_COUNT
DIAG = 128
VMEM_GRANT = 48 * 2**20
IN_VMEM = pl.BlockSpec(memory_space=pltpu.VMEM)
IN_SMEM = pl.BlockSpec(memory_space=pltpu.SMEM)
ANYWHERE = pl.BlockSpec(memory_space=pl.ANY)


def contract(left, right, left_dim, right_dim, precision=None):
    return lax.dot_general(
        left,
        right,
        (((left_dim,), (right_dim,)), ((), ())),
        precision=precision,
        preferred_element_type=jnp.float32,
    )


def split_two(values):
    high = values.astype(jnp.bfloat16)
    return (high, (values - high.astype(jnp.float32)).astype(jnp.bfloat16))


def wide_left(left, right_low, left_dim, right_dim):
    high, rest = split_two(left)
    return contract(high, right_low, left_dim, right_dim) + contract(
        rest, right_low, left_dim, right_dim
    )


def wide_right(left_low, right, left_dim, right_dim):
    high, rest = split_two(right)
    return contract(left_low, high, left_dim, right_dim) + contract(
        left_low, rest, left_dim, right_dim
    )


def call_kernel(
    body, out_shapes, scratch, name, *operands, smem_count=0, any_in=(), any_out=(), aliases=None,
    micros=2,
):
    def place(at, listed):
        return ANYWHERE if at in listed else IN_VMEM

    return pl.pallas_call(
        body,
        out_shape=out_shapes,
        in_specs=[
            IN_SMEM if at < smem_count else place(at, any_in) for at in range(len(operands))
        ],
        out_specs=[place(at, any_out) for at in range(len(out_shapes))],
        scratch_shapes=scratch,
        input_output_aliases=aliases or {},
        cost_estimate=pl.CostEstimate(
            flops=micros * FLOPS_PER_US, bytes_accessed=0, transcendentals=0
        ),
        compiler_params=pltpu.CompilerParams(vmem_limit_bytes=VMEM_GRANT),
        name=name,
    )(*operands)


def eliminate(panels, turn):
    rows, width = panels[0][0].shape
    row_at = lax.broadcasted_iota(jnp.int32, (SUBLANES, width), 0)

    def groups(values):
        return [values[low : low + SUBLANES] for low in range(0, rows, SUBLANES)]

    def spread_row(values, row):
        return jnp.broadcast_to(values[row : row + 1, :], values.shape)

    states = []
    for left, right in panels:
        turned = pltpu.roll(left, turn, 1)
        columns = [
            [jnp.broadcast_to(part, (SUBLANES, width)) for part in groups(turned[:, at : at + 1])]
            for at in range(rows)
        ]
        ones = [jnp.ones((SUBLANES, width), jnp.float32) for _ in range(rows // SUBLANES)]
        states.append((groups(left), groups(right), columns, ones))
    for at in range(rows):
        group_at, row = divmod(at, SUBLANES)
        for left, right, columns, pivots in states:
            pivot = spread_row(columns[at][group_at], row)
            inverse = pltpu.reciprocal(pivot, approx=False)
            pivots[group_at] = jnp.where(row_at == row, pivot, pivots[group_at])
            targets = [left, right] + columns[at + 1 :]
            given = [spread_row(target[group_at], row) for target in targets]
            for group in range(group_at, rows // SUBLANES):
                factor = columns[at][group] * inverse
                if group == group_at:
                    factor = jnp.where(row_at > row, factor, 0.0)
                for target, pivot_row in zip(targets, given):
                    target[group] = target[group] - factor * pivot_row
    results = []
    for left, right, _, pivots in states:
        scales = [lax.rsqrt(values) for values in pivots]
        results.append(
            tuple(
                jnp.concatenate([part * scale for part, scale in zip(parts, scales)], axis=0)
                for parts in (left, right)
            )
        )
    return results


def split_three(values):
    high = values.astype(jnp.bfloat16).astype(jnp.float32)
    rest = values - high
    middle = rest.astype(jnp.bfloat16).astype(jnp.float32)
    return (high, middle, rest - middle)


def thin_product(left, right):
    left_parts, right_parts = (split_three(left), split_three(right))
    pairs = ((0, 0), (0, 1), (1, 0), (1, 1), (0, 2), (2, 0))
    stacked_left = jnp.concatenate([left_parts[i] for i, _ in pairs], axis=0)
    stacked_right = jnp.concatenate([right_parts[j] for _, j in pairs], axis=0)
    return contract(stacked_left.astype(jnp.bfloat16), stacked_right.astype(jnp.bfloat16), 0, 0)


def factorize(grams, uppers, works, inverses):
    each = range(len(grams))
    size = grams[0].shape[0]
    eye = (
        lax.broadcasted_iota(jnp.int32, (DIAG, DIAG), 0)
        == lax.broadcasted_iota(jnp.int32, (DIAG, DIAG), 1)
    ).astype(jnp.float32)
    for low in range(0, size, DIAG):
        top = low + DIAG
        for m in each:
            works[m][:, 0:DIAG] = grams[m][low:top, low:top]
            works[m][:, DIAG:] = eye

        def panel(panel_at, carry):
            row = pl.multiple_of(panel_at * PANEL, PANEL)
            turn = lax.rem(DIAG - panel_at * PANEL, DIAG)
            panels = [
                (works[m][pl.ds(row, PANEL), 0:DIAG], works[m][pl.ds(row, PANEL), DIAG:])
                for m in each
            ]
            results = eliminate(panels, turn)
            updates = [
                thin_product(left, jnp.concatenate([left, right], axis=1))
                for left, right in results
            ]
            for m in each:
                inverses[m][low // DIAG, pl.ds(row, PANEL), :] = results[m][1]
            for m in each:
                works[m][...] = works[m][...] - updates[m]
            return carry

        lax.fori_loop(0, DIAG // PANEL, panel, 0)
        if top == size:
            break
        right_of = [contract(inverses[m][low // DIAG], grams[m][low:top, top:], 1, 0, HIGH) for m in each]
        for m in each:
            uppers[m][low:top, top:] = right_of[m]
        for other in range(top, size, DIAG):
            skip = other - top
            rest = [
                grams[m][other : other + DIAG, other:]
                - contract(right_of[m][:, skip : skip + DIAG], right_of[m][:, skip:], 0, 0, HIGH)
                for m in each
            ]
            for m in each:
                grams[m][other : other + DIAG, other:] = rest[m]


def renew_body(piece_count, *refs):
    offset_ref, stat_ref, basis_ref = refs[:3]
    piece_refs = refs[3 : 3 + piece_count]
    scratch = refs[3 + piece_count :]
    count, size, _ = stat_ref.shape
    each = range(count)
    products, grams, uppers, works, inverses = (
        scratch[at : at + count] for at in range(0, 5 * count, count)
    )
    values = [wide_left(stat_ref[m], basis_ref[m], 1, 0) for m in each]
    for m in each:
        products[m][...] = values[m]
    for low in range(0, size, DIAG):
        values = [
            contract(products[m][:, low : low + DIAG], products[m][:, low:], 0, 0, HIGH)
            for m in each
        ]
        for m in each:
            grams[m][low : low + DIAG, low:] = values[m]
    factorize(grams, uppers, works, inverses)
    for low in range(0, size, DIAG):
        top = low + DIAG
        values = [products[m][:, low:top] for m in each]
        if low:
            values = [
                values[m]
                - contract(products[m][:, :low], uppers[m][:low, low:top], 1, 0, HIGH)
                for m in each
            ]
        values = [contract(values[m], inverses[m][low // DIAG], 1, 1, HIGH) for m in each]
        for m in each:
            products[m][:, low:top] = values[m]
    rows = piece_refs[0].shape[1]
    for piece_at in range(piece_count):
        row = pl.multiple_of(offset_ref[piece_at], 8)
        for m in each:
            piece_refs[piece_at][m] = products[m][pl.ds(row, rows), :].astype(jnp.bfloat16)


def renew_bases(offsets, new_stat, basis_low):
    count, size, _ = new_stat.shape
    piece_count = offsets.shape[0]
    return call_kernel(
        functools.partial(renew_body, piece_count),
        [
            jax.ShapeDtypeStruct((count, size // piece_count, size), jnp.bfloat16)
            for _ in range(piece_count)
        ],
        [pltpu.VMEM((size, size), jnp.float32)] * (3 * count)
        + [pltpu.VMEM((DIAG, 2 * DIAG), jnp.float32)] * count
        + [pltpu.VMEM((size // DIAG, DIAG, DIAG), jnp.float32)] * count,
        "renew_bases",
        offsets,
        new_stat,
        basis_low,
        smem_count=1,
        micros=40,
    )


def pack_body(own_slots, stats, bases, first, second, packed):
    for target in range(packed.shape[0]):
        slot = min(target, own_slots - 1)
        packed[target, 0:2] = stats[slot].astype(jnp.bfloat16)
        packed[target, 2:4] = bases[slot].astype(jnp.bfloat16)
        packed[target, 4] = first[slot].astype(jnp.bfloat16)
        packed[target, 5] = second[slot].astype(jnp.bfloat16)


def rotate_body(piece_count, *refs):
    offset_ref, grad_ref, given = refs[:3]
    sent, stat_ref, basis_ref, whole, results = refs[3:]
    rows = given.shape[2]
    for source in range(given.shape[0]):
        whole[:, source * rows : (source + 1) * rows, :] = given[source].astype(jnp.float32)
    grad = grad_ref[...]
    left = whole[2].astype(jnp.bfloat16)
    right = whole[3].astype(jnp.bfloat16)
    basis_ref[0] = left
    basis_ref[1] = right
    results[0] = contract(grad, grad, 1, 1)
    results[1] = contract(grad, grad, 0, 0)
    stat_ref[0] = BETA_STAT * whole[0] + (1.0 - BETA_STAT) * results[0]
    stat_ref[1] = BETA_STAT * whole[1] + (1.0 - BETA_STAT) * results[1]
    rotated = wide_left(contract(left, grad, 0, 0), right, 1, 0)
    results[2] = rotated
    new_first = BETA_ONE * whole[4] + (1.0 - BETA_ONE) * rotated
    new_second = BETA_TWO * whole[5] + (1.0 - BETA_TWO) * rotated * rotated
    direction = (
        new_first
        / (1.0 - BETA_ONE**STEP)
        / (jnp.sqrt(new_second / (1.0 - BETA_TWO**STEP)) + ADAM_EPS)
    )
    results[3] = wide_right(left, wide_left(direction, right, 1, 1), 1, 0)
    for target in range(sent.shape[0]):
        sent[target] = results[:, target * rows : (target + 1) * rows, :].astype(jnp.bfloat16)


def rotate_slot(offsets, grad, owner_rows):
    size = grad.shape[0]
    piece_count = offsets.shape[0]
    return call_kernel(
        functools.partial(rotate_body, piece_count),
        [
            jax.ShapeDtypeStruct((owner_rows.shape[0], 4) + owner_rows.shape[2:], jnp.bfloat16),
            jax.ShapeDtypeStruct((2, size, size), jnp.float32),
            jax.ShapeDtypeStruct((2, size, size), jnp.bfloat16),
        ],
        [
            pltpu.VMEM((6, size, size), jnp.float32),
            pltpu.VMEM((4, size, size), jnp.float32),
        ],
        "rotate_slot",
        offsets,
        grad,
        owner_rows,
        smem_count=1,
        micros=6,
    )


def finish_body(
    own_slots, masters, first, second, stats, given, new_masters, new_first, new_second, new_stats
):
    for slot in range(own_slots):
        rotated = given[slot, 2].astype(jnp.float32)
        update = given[slot, 3].astype(jnp.float32)
        new_first[slot] = BETA_ONE * first[slot] + (1.0 - BETA_ONE) * rotated
        new_second[slot] = BETA_TWO * second[slot] + (1.0 - BETA_TWO) * rotated * rotated
        new_masters[slot] = masters[slot] - RATE_MATRIX * (update + WEIGHT_DECAY * masters[slot])
        new_stats[slot] = BETA_STAT * stats[slot] + (1.0 - BETA_STAT) * given[slot, 0:2].astype(
            jnp.float32
        )


def place_body(own_slots, slot_ref, *refs):
    new_bases = refs[-1]
    for piece_at, piece in enumerate(refs[:-1]):
        slot = slot_ref[piece_at]

        @pl.when(slot < own_slots)
        def _():
            new_bases[slot] = piece[...].astype(jnp.float32)


def swap_pieces(pieces, axis, wanted):
    device_count = lax.axis_size(axis)
    return [pieces[0]] + [
        lax.ppermute(
            pieces[k], axis, [(i, i ^ k) for i in range(device_count) if wanted(i, i ^ k)]
        )
        for k in range(1, device_count)
    ]


def add_low(left, right):
    return (left.astype(jnp.float32) + right.astype(jnp.float32)).astype(jnp.bfloat16)


def sum_to_owner(kept, sent, seq_index, vec_sum):
    def beside(values, vec_sum, axis, bit_at):
        return lax.optimization_barrier((values, vec_sum + partner(vec_sum, axis, bit_at)))

    size = kept.shape[-1]
    z_count = kept.shape[0] // 4
    shape = (2, 2, z_count, size, size)
    kept = kept.reshape(shape)
    came, vec_sum = beside(partner(sent, "opt", 0), vec_sum, "opt", 0)
    came = came.reshape(shape)
    half = size // 2

    def part(x_at, y_at, rows):
        return add_low(kept[x_at, y_at, :, rows], came[x_at, y_at, :, rows])

    upper, lower = (slice(0, half), slice(half, size))
    by_x = partner(part(1, slice(0, 2), upper), "opt", 1)
    by_y = partner(part(slice(0, 2), 1, lower), "seq", 0)
    by_x, vec_sum = beside(by_x, vec_sum, "opt", 1)
    stay_x = part(0, slice(0, 2), upper)
    stay_y = part(slice(0, 2), 0, lower)
    then_y = partner(add_low(stay_x[1], by_x[1]), "seq", 0)
    then_x = partner(add_low(stay_y[1], by_y[1]), "opt", 1)
    then_y, vec_sum = beside(then_y, vec_sum, "seq", 0)
    z_index = seq_index >> 1

    def both(apart):
        at = jnp.minimum(z_index ^ apart, z_count - 1)

        def pick(values):
            return lax.dynamic_index_in_dim(values, at, 0, keepdims=False)

        total_upper = (
            pick(stay_x[0]).astype(jnp.float32)
            + pick(by_x[0]).astype(jnp.float32)
            + pick(then_y).astype(jnp.float32)
        )
        total_lower = (
            pick(stay_y[0]).astype(jnp.float32)
            + pick(by_y[0]).astype(jnp.float32)
            + pick(then_x).astype(jnp.float32)
        )
        return jnp.concatenate([total_upper, total_lower]).astype(jnp.bfloat16)

    near_one = partner(both(1), "seq", 1)
    near_far = partner(both(3), "seq", 1)
    near_one, vec_sum = beside(near_one, vec_sum, "seq", 1)
    last = partner(add_low(both(2), near_far), "seq", 2)
    last, vec_sum = beside(last, vec_sum, "seq", 2)
    total = both(0).astype(jnp.float32) + near_one.astype(jnp.float32) + last.astype(jnp.float32)
    return (total.astype(jnp.bfloat16), vec_sum)


def to_homes(pieces, axis, by_permutes, own_slots):
    if by_permutes:
        return swap_pieces(pieces, axis, lambda source, target: source < own_slots)
    kinds, _, width = pieces[0].shape
    device_count = lax.axis_size(axis)
    shaped = jnp.swapaxes(pieces[0].reshape(kinds, device_count, -1, width), 0, 1)
    swapped = lax.all_to_all(shaped, axis, 0, 0, tiled=True)
    return [swapped[slot] for slot in range(own_slots)]


def partner(value, axis, apart):
    return lax.ppermute(value, axis, [(i, i ^ 1 << apart) for i in range(lax.axis_size(axis))])


def pair_mean(values):
    shaped = values.reshape((values.shape[0] // 2, 2) + values.shape[1:])
    return 0.5 * (shaped[:, 0] + shaped[:, 1])


def pair_spread(grads):
    return 0.5 * jnp.repeat(grads, 2, axis=0)


def sum_rows(values):
    return jnp.sum(values, axis=0, keepdims=True)


def norm_parts(values):
    centred = values - jnp.mean(values, axis=-1, keepdims=True)
    recip = lax.rsqrt(jnp.mean(centred * centred, axis=-1, keepdims=True) + NORM_EPS)
    return (centred * recip, recip)


def norm_back(grad, gain, normed, recip):
    scaled = grad * gain
    return recip * (
        scaled
        - jnp.mean(scaled, axis=-1, keepdims=True)
        - normed * jnp.mean(scaled * normed, axis=-1, keepdims=True)
    )


def half_matrix(shape, fine_dim):
    fine = lax.broadcasted_iota(jnp.int32, shape, fine_dim)
    coarse = lax.broadcasted_iota(jnp.int32, shape, 1 - fine_dim)
    return jnp.where(fine >> 1 == coarse, 0.5, 0.0).astype(jnp.bfloat16)


def pool(rows_low):
    count = rows_low.shape[0]
    return contract(half_matrix((count // 2, count), 1), rows_low, 1, 0).astype(jnp.bfloat16)


def spread(grads):
    count = grads.shape[0]
    return wide_right(half_matrix((2 * count, count), 0), grads, 1, 0)


def norm_cdf(values):
    return 0.5 * (1.0 + lax.erf(values * math.sqrt(0.5)))


def local_count(tok_count):
    return (tok_count // BLOCK).bit_length() - 1


def key_width(tok_count, tree_bits):
    rows = 2 * (tok_count - BLOCK) + BLOCK * tree_bits
    return -(-rows // LANES) * LANES


def score_offsets(tok_count, tree_bits, span_bits):
    token = jnp.arange(tok_count, dtype=jnp.int32)[:, None]
    parts = []
    for height in range(local_count(tok_count)):
        row = jnp.arange(tok_count >> height, dtype=jnp.int32)[None, :]
        apart = token // (BLOCK << height) ^ row // BLOCK
        counted = apart <= 1 if height == 0 else apart == 1
        parts.append(jnp.where(counted, height * LN_TWO, NEG_FILL))
    for bit_at in range(tree_bits):
        offset = (local_count(tok_count) + bit_at) * LN_TWO
        parts.append(
            jnp.broadcast_to(
                jnp.where(bit_at + 1 <= span_bits, offset, NEG_FILL), (tok_count, BLOCK)
            )
        )
    used = sum(part.shape[1] for part in parts)
    rest = key_width(tok_count, tree_bits) - used
    parts.append(jnp.full((tok_count, rest), NEG_FILL, jnp.float32))
    return jnp.concatenate(parts, axis=1).astype(jnp.float32)


def stack_keys(own_rows, far_rows):
    parts = [own_rows]
    for _ in range(local_count(own_rows.shape[0]) - 1):
        parts.append(pool(parts[-1]))
    parts = parts + far_rows
    rest = key_width(own_rows.shape[0], len(far_rows)) - sum(part.shape[0] for part in parts)
    if rest:
        parts.append(jnp.zeros((rest, own_rows.shape[1]), jnp.bfloat16))
    return jnp.concatenate(parts, axis=0)


def by_heads(pair):
    lane = lax.broadcasted_iota(jnp.int32, pair.shape, 1)
    zero = jnp.zeros_like(pair)
    first = lane < LANES // 2
    return jnp.concatenate([jnp.where(first, pair, zero), jnp.where(first, zero, pair)], axis=0)


def from_heads(both):
    count = both.shape[0] // 2
    lane = lax.broadcasted_iota(jnp.int32, (count, LANES), 1)
    return jnp.where(lane < LANES // 2, both[:count], both[count:])


def attend(qkv, far_rows, offsets, probs, mixed):
    width = qkv.shape[1] // 3
    score_scale = (width // HEADS) ** (-0.5)
    stack = stack_keys(qkv[:, width:], far_rows)
    both_offsets = jnp.concatenate([offsets, offsets], axis=0)
    for pair_at in range(width // LANES):
        low, top = (pair_at * LANES, (pair_at + 1) * LANES)
        scores = (
            contract(by_heads(qkv[:, low:top]), stack[:, low:top], 1, 1) * score_scale
            + both_offsets
        )
        expo = jnp.exp(scores - jnp.max(scores, axis=1, keepdims=True))
        weights = expo / jnp.sum(expo, axis=1, keepdims=True)
        probs[pair_at] = weights
        result = contract(
            weights.astype(jnp.bfloat16), stack[:, width + low : width + top], 1, 0
        )
        mixed[:, low:top] = from_heads(result).astype(jnp.bfloat16)


def attend_back(qkv, far_rows, probs, mixed_grad, query_grad, key_grads, far_grads):
    tok_count, width = mixed_grad.shape
    score_scale = (width // HEADS) ** (-0.5)
    stack = stack_keys(qkv[:, width:], far_rows)
    local_levels = local_count(tok_count)
    far_start = 2 * (tok_count - BLOCK)
    for pair_at in range(width // LANES):
        low, top = (pair_at * LANES, (pair_at + 1) * LANES)
        queries = by_heads(qkv[:, low:top])
        grads = by_heads(mixed_grad[:, low:top])
        weights = probs[pair_at]
        prob_grad = contract(grads, stack[:, width + low : width + top], 1, 1)
        inner = jnp.sum(weights * prob_grad, axis=1, keepdims=True)
        score_grad = (weights * (prob_grad - inner)).astype(jnp.bfloat16)
        query_grad[:, low:top] = (
            from_heads(contract(score_grad, stack[:, low:top], 1, 0)) * score_scale
        ).astype(jnp.bfloat16)
        for start, part in (
            (low, contract(score_grad, queries, 0, 0) * score_scale),
            (width + low, contract(weights.astype(jnp.bfloat16), grads, 0, 0)),
        ):
            for far_at, far_grad in enumerate(far_grads):
                row = far_start + BLOCK * far_at
                far_grad[:, start : start + LANES] = part[row : row + BLOCK]
            folded = None
            for height in reversed(range(local_levels)):
                row = 2 * (tok_count - (tok_count >> height))
                own = part[row : row + (tok_count >> height)]
                folded = own if folded is None else own + spread(folded)
            key_grads[:, start : start + LANES] = folded


class Units:
    def __init__(self, meta, packed, store, sems, units):
        self.store = store
        self.place = {unit: at for at, unit in enumerate(units)}
        self.waiting = {}
        rows = store.shape[2]
        for at, unit in enumerate(units):
            row = pl.multiple_of(meta[UNIT_ROW + unit], rows)
            copy = pltpu.make_async_copy(
                packed.at[:, meta[UNIT_OPT + unit], pl.ds(row, rows), :],
                store.at[at],
                sems.at[at],
            )
            copy.start()
            self.waiting[unit] = copy

    def __getitem__(self, unit):
        if unit in self.waiting:
            self.waiting.pop(unit).wait()
        width = self.store.shape[3]
        return self.store[self.place[unit]].reshape(width, width)


class Grads:
    def __init__(self, meta, kept, sent, store, sems):
        self.meta, self.kept, self.sent, self.store, self.sems = (meta, kept, sent, store, sems)
        self.copies = []

    def put(self, unit, left_low, right_low):
        at = len(self.copies)
        self.store[at] = contract(left_low, right_low, 0, 0).astype(jnp.bfloat16)
        place = self.meta[UNIT_SLOT + unit]
        half = self.kept.shape[0]
        inner = jnp.where(place < half, place, place - half)
        keeping, sending = (
            pltpu.make_async_copy(self.store.at[at], target.at[inner], self.sems.at[at])
            for target in (self.kept, self.sent)
        )
        pl.when(place < half)(keeping.start)
        pl.when(place >= half)(sending.start)
        self.copies.append(keeping)

    def finish(self):
        for copy in self.copies:
            copy.wait()


def project(hidden, units, first_unit, gain, bias, normed_ref, qkv_ref, near_ref):
    width = hidden.shape[1]
    normed, _ = norm_parts(hidden)
    normed_low = (normed * gain + bias).astype(jnp.bfloat16)
    normed_ref[...] = normed_low
    for part in range(3):
        qkv_ref[:, part * width : (part + 1) * width] = contract(
            normed_low, units[first_unit + part], 1, 0
        ).astype(jnp.bfloat16)
    near = qkv_ref[:, width:]
    for _ in range(local_count(near.shape[0])):
        near = pool(near)
    near_ref[...] = near


def feed_forward(middle, units, first_unit, vec, vec_at, normed_ref, pre_ref, act_ref):
    width = middle.shape[1]
    normed, _ = norm_parts(middle)
    normed_low = (normed * vec[vec_at + 2 : vec_at + 3] + vec[vec_at + 3 : vec_at + 4]).astype(
        jnp.bfloat16
    )
    normed_ref[...] = normed_low
    total = middle
    ff_blocks = FF // width
    for part in range(ff_blocks):
        low, top = (part * width, (part + 1) * width)
        row = vec_at + 4 + part
        pre = contract(normed_low, units[first_unit + 4 + part], 1, 0) + vec[row : row + 1]
        act = (pre * norm_cdf(pre)).astype(jnp.bfloat16)
        pre_ref[:, low:top] = pre
        act_ref[:, low:top] = act
        total = total + contract(act, units[first_unit + 4 + ff_blocks + part], 1, 0)
    row = vec_at + 4 + ff_blocks
    return total + vec[row : row + 1]


def feed_back(
    grad, middle, normed_low, pre_ref, act_ref, units, grads, first_unit, vec, vec_at, vec_grads, at
):
    width = middle.shape[1]
    ff_blocks = FF // width
    down_grad = grad.astype(jnp.bfloat16)
    normed_grad = jnp.zeros(middle.shape, jnp.float32)
    for part in range(ff_blocks):
        low, top = (part * width, (part + 1) * width)
        down_unit = first_unit + 4 + ff_blocks + part
        grads.put(down_unit, act_ref[:, low:top], down_grad)
        pre = pre_ref[:, low:top]
        slope = norm_cdf(pre) + pre * jnp.exp(-0.5 * pre * pre) * (1.0 / math.sqrt(2.0 * math.pi))
        pre_grad = (contract(down_grad, units[down_unit], 1, 1) * slope).astype(jnp.bfloat16)
        grads.put(first_unit + 4 + part, normed_low, pre_grad)
        vec_grads[at + 2 + part : at + 3 + part] = sum_rows(pre_grad.astype(jnp.float32))
        normed_grad = normed_grad + contract(pre_grad, units[first_unit + 4 + part], 1, 1)
    row = at + 2 + ff_blocks
    vec_grads[row : row + 1] = sum_rows(grad)
    normed, recip = norm_parts(middle)
    vec_grads[at : at + 1] = sum_rows(normed_grad * normed)
    vec_grads[at + 1 : at + 2] = sum_rows(normed_grad)
    return grad + norm_back(normed_grad, vec[vec_at + 2 : vec_at + 3], normed, recip)


def project_back(
    middle_grad, hidden, normed_low, query_grad, key_grads, near_grads, units, grads, first_unit,
    vec, vec_at, vec_grads,
):
    width = hidden.shape[1]
    near = near_grads[...]
    for _ in range(local_count(hidden.shape[0])):
        near = spread(near)
    rows_low = (key_grads[...] + near).astype(jnp.bfloat16)
    parts = (query_grad[...], rows_low[:, :width], rows_low[:, width:])
    normed_grad = jnp.zeros(hidden.shape, jnp.float32)
    for part, part_grad in enumerate(parts):
        grads.put(first_unit + part, normed_low, part_grad)
        normed_grad = normed_grad + contract(part_grad, units[first_unit + part], 1, 1)
    normed, recip = norm_parts(hidden)
    vec_grads[0:1] = sum_rows(normed_grad * normed)
    vec_grads[1:2] = sum_rows(normed_grad)
    return middle_grad + norm_back(normed_grad, vec[vec_at : vec_at + 1], normed, recip)


def first_body(per_layer, meta, vec, inputs, packed, normed, qkv, near, store, sems):
    units = Units(meta, packed, store, sems, range(3))
    project(inputs[...].astype(jnp.float32), units, 0, vec[0:1], vec[1:2], normed, qkv, near)


def middle_body(per_layer, vec_rows, tree_bits, meta, vec, offsets, inputs, qkv, *refs):
    far, refs = (refs[:tree_bits], refs[tree_bits:])
    packed, probs, mixed, middle, normed_two, pre, act, hidden, normed, next_qkv, near = refs[:11]
    store, sems = refs[11:]
    units = Units(meta, packed, store, sems, range(3, per_layer + 3))
    attend(qkv[...], [ref[...] for ref in far], offsets[...], probs, mixed)
    middle[...] = inputs[...].astype(jnp.float32) + contract(mixed[...], units[3], 1, 0)
    hidden[...] = feed_forward(middle[...], units, 0, vec, 0, normed_two, pre, act)
    project(
        hidden[...], units, per_layer, vec[vec_rows : vec_rows + 1],
        vec[vec_rows + 1 : vec_rows + 2], normed, next_qkv, near,
    )


def turn_body(per_layer, vec_rows, tree_bits, meta, vec, offsets, cotangent, hidden, qkv, *refs):
    far, refs = (refs[:tree_bits], refs[tree_bits:])
    packed, outputs, middle_grad, query_grad, key_grads, vec_grads, kept, sent = refs[:8]
    far_grads, refs = (refs[8 : 8 + tree_bits], refs[8 + tree_bits :])
    store, sems, grad_store, grad_sems, probs, mixed, normed_two, pre, act = refs
    units = Units(meta, packed, store, sems, range(per_layer + 3, 2 * per_layer))
    grads = Grads(meta, kept, sent, grad_store, grad_sems)
    far_rows = [ref[...] for ref in far]
    attend(qkv[...], far_rows, offsets[...], probs, mixed)
    middle = hidden[...] + contract(mixed[...], units[per_layer + 3], 1, 0)
    outputs[...] = feed_forward(
        middle, units, per_layer, vec, vec_rows, normed_two, pre, act
    ).astype(jnp.bfloat16)
    vec_grads[...] = jnp.zeros_like(vec_grads)
    grad = feed_back(
        cotangent[...].astype(jnp.float32), middle, normed_two[...], pre, act, units, grads,
        per_layer, vec, vec_rows, vec_grads, 2,
    )
    middle_grad[...] = grad
    branch_grad = grad.astype(jnp.bfloat16)
    grads.put(per_layer + 3, mixed[...], branch_grad)
    mixed_grad = contract(branch_grad, units[per_layer + 3], 1, 1).astype(jnp.bfloat16)
    attend_back(qkv[...], far_rows, probs, mixed_grad, query_grad, key_grads, far_grads)
    grads.finish()


def lower_body(per_layer, vec_rows, tree_bits, meta, vec, *refs):
    hidden, normed_one, query_in, key_in, near_in, middle_in = refs[:6]
    probs, mixed, middle, normed_two, pre, act, qkv = refs[6:13]
    far, refs = (refs[13 : 13 + tree_bits], refs[13 + tree_bits :])
    packed, _, _, middle_grad, query_grad, key_grads, vec_grads, kept, sent = refs[:9]
    far_grads, refs = (refs[9 : 9 + tree_bits], refs[9 + tree_bits :])
    store, sems, grad_store, grad_sems = refs
    upper_units = list(range(per_layer, per_layer + 3))
    units = Units(
        meta, packed, store, sems, upper_units + list(range(3 + (per_layer - 4) // 2 + 1, per_layer))
        + list(range(3, 3 + (per_layer - 4) // 2 + 1)),
    )
    grads = Grads(meta, kept, sent, grad_store, grad_sems)
    vec_grads[...] = jnp.zeros_like(vec_grads)
    grad = project_back(
        middle_in[...], hidden[...], normed_one[...], query_in, key_in, near_in, units, grads,
        per_layer, vec, vec_rows, vec_grads,
    )
    grad = feed_back(
        grad, middle[...], normed_two[...], pre, act, units, grads, 0, vec, 0, vec_grads, 2
    )
    middle_grad[...] = grad
    branch_grad = grad.astype(jnp.bfloat16)
    grads.put(3, mixed[...], branch_grad)
    mixed_grad = contract(branch_grad, units[3], 1, 1).astype(jnp.bfloat16)
    attend_back(
        qkv[...], [ref[...] for ref in far], probs, mixed_grad, query_grad, key_grads, far_grads
    )
    grads.finish()


def last_body(meta, vec, inputs, normed_one, query_in, key_in, near_in, middle_in, *refs):
    packed, _, _, input_grad, vec_grads, kept, sent, store, sems, grad_store, grad_sems = refs
    units = Units(meta, packed, store, sems, range(3))
    grads = Grads(meta, kept, sent, grad_store, grad_sems)
    vec_grads[...] = jnp.zeros_like(vec_grads)
    input_grad[...] = project_back(
        middle_in[...], inputs[...].astype(jnp.float32), normed_one[...], query_in, key_in,
        near_in, units, grads, 0, vec, 0, vec_grads,
    )
    grads.finish()


def coarse_up(own, seq_index, tree_bits):
    far_list = []
    for bit_at in range(tree_bits):
        far = partner(own, "seq", bit_at)
        far_list.append(far)
        if bit_at + 1 < tree_bits:
            upper = seq_index >> bit_at & 1 == 1
            joined = jnp.where(
                upper, jnp.concatenate([far, own]), jnp.concatenate([own, far])
            ).astype(jnp.float32)
            own = pair_mean(joined).astype(jnp.bfloat16)
    return far_list


def coarse_down(far_grads, seq_index):
    above = None
    for bit_at in reversed(range(len(far_grads))):
        upper = seq_index >> bit_at & 1 == 1
        sent = far_grads[bit_at]
        own = 0.0
        if above is not None:
            wide = pair_spread(above)
            own = jnp.where(upper, wide[BLOCK:], wide[:BLOCK])
            sent = sent + jnp.where(upper, wide[:BLOCK], wide[BLOCK:])
        above = own + partner(sent.astype(jnp.bfloat16), "seq", bit_at).astype(jnp.float32)
    return above


def per_device(
    inputs,
    cotangent,
    seq_lengths,
    unit_slot,
    masters,
    first_moment,
    second_moment,
    bases,
    stats,
    vec_master,
    vec_first,
    vec_second,
):
    seq_count = lax.axis_size("seq")
    opt_count = lax.axis_size("opt")
    seq_index = lax.axis_index("seq")
    tok_count = inputs.shape[1]
    model_width = inputs.shape[2]
    own_slots = masters.shape[0]
    row_count = masters.shape[1]
    ff_blocks = FF // model_width
    per_layer = 4 + 2 * ff_blocks
    vec_width = 5 * model_width + FF
    long_devs = min(max(MAX_LEN // tok_count, 1), seq_count)
    tree_bits = long_devs.bit_length() - 1
    size = seq_count * row_count
    by_permutes = seq_count == 8 and opt_count == 4 and own_slots == 6
    if by_permutes:
        relative = jnp.arange(seq_count, dtype=jnp.int32) ^ seq_index
        offsets = relative * row_count
        slot_at = relative
    else:
        offsets = jnp.zeros((1,), jnp.int32)
        slot_at = jnp.arange(own_slots, dtype=jnp.int32)
    (packed_slots,) = call_kernel(
        functools.partial(pack_body, own_slots),
        [jax.ShapeDtypeStruct((seq_count, 6, row_count, model_width), jnp.bfloat16)],
        [],
        "pack_slots",
        stats,
        bases,
        first_moment,
        second_moment,
        micros=3,
    )
    owner_rows = lax.all_to_all(packed_slots, "seq", 0, 0, tiled=True)
    vec_count = vec_master.shape[0]
    own_rows = own_slots * row_count
    vec_block = jnp.pad(
        vec_master.astype(jnp.bfloat16)[None], [(0, 15), (0, model_width - vec_count)]
    )
    gathered = lax.all_gather(
        jnp.concatenate(
            [masters.astype(jnp.bfloat16).reshape(own_rows, model_width), vec_block]
        )[None],
        ("seq", "opt"),
        axis=0,
        tiled=True,
    )
    vec = gathered[:, own_rows, :vec_count].reshape(-1, model_width).astype(jnp.float32)
    if row_count % 16 == 0:
        unit_rows = row_count
        packed = gathered.reshape(seq_count, opt_count, own_rows + 16, model_width)
    else:
        unit_rows = size
        packed = (
            gathered[:, :own_rows]
            .reshape(seq_count, opt_count, own_slots, row_count, model_width)
            .transpose(1, 2, 0, 3, 4)
            .reshape(1, opt_count, own_slots * size, model_width)
        )
    opt_index = lax.axis_index("opt")
    opt_at, slot_in = (unit_slot // own_slots, unit_slot % own_slots)
    if by_permutes:
        apart = opt_at ^ opt_index
        other = (apart & 1) * 4 + (apart >> 1) * 2 + ((slot_in ^ seq_index) & 1)
        place = other * (own_slots // 2) + (slot_in >> 1)
    else:
        place = unit_slot
    meta = jnp.concatenate([opt_at, slot_in * unit_rows, place]).astype(jnp.int32)
    span_bits = jnp.zeros((), jnp.int32)
    for bit_at in range(tree_bits + 1):
        start_dev = seq_index >> bit_at << bit_at
        span_bits = jnp.where(
            seq_lengths[0, start_dev] == tok_count * (1 << bit_at), bit_at, span_bits
        )
    offsets_in = score_offsets(tok_count, tree_bits, span_bits)
    width_in = offsets_in.shape[1]
    pair_count = model_width // LANES
    vec_rows = vec_width // model_width
    square = (model_width, model_width)

    def units_in(count):
        return [
            pltpu.VMEM((count, size // unit_rows, unit_rows, model_width), jnp.bfloat16),
            pltpu.SemaphoreType.DMA((count,)),
        ]

    def grads_out(count):
        return [pltpu.VMEM((count,) + square, jnp.bfloat16), pltpu.SemaphoreType.DMA((count,))]

    def low_of(*shape):
        return jax.ShapeDtypeStruct(shape, jnp.bfloat16)

    def full_of(*shape):
        return jax.ShapeDtypeStruct(shape, jnp.float32)

    projected = [
        low_of(tok_count, model_width),
        low_of(tok_count, 3 * model_width),
        low_of(BLOCK, 2 * model_width),
    ]
    attended = [
        full_of(pair_count, 2 * tok_count, width_in),
        low_of(tok_count, model_width),
    ]
    fed = [
        low_of(tok_count, model_width),
        full_of(tok_count, FF),
        low_of(tok_count, FF),
    ]
    back = [
        full_of(tok_count, model_width),
        low_of(tok_count, model_width),
        full_of(tok_count, 2 * model_width),
        full_of(16, model_width),
        low_of(UNIT_COUNT // 2, *square),
        low_of(UNIT_COUNT // 2, *square),
    ] + [full_of(BLOCK, 2 * model_width)] * tree_bits
    normed_zero, qkv_zero, near_zero = call_kernel(
        functools.partial(first_body, per_layer),
        projected,
        units_in(3),
        "project_first",
        meta,
        vec,
        inputs[0],
        packed,
        smem_count=1,
        micros=3,
        any_in=(3,),
    )
    far_zero = coarse_up(near_zero, seq_index, tree_bits)
    (
        probs, mixed, middle, normed_two, pre, act, hidden, normed_one, qkv_one, near_one,
    ) = call_kernel(
        functools.partial(middle_body, per_layer, vec_rows, tree_bits),
        attended + [full_of(tok_count, model_width)] + fed + [full_of(tok_count, model_width)]
        + projected,
        units_in(per_layer),
        "layer_first",
        meta,
        vec,
        offsets_in,
        inputs[0],
        qkv_zero,
        *far_zero,
        packed,
        smem_count=1,
        micros=7,
        any_in=(5 + tree_bits,),
    )
    far_one = coarse_up(near_one, seq_index, tree_bits)
    (
        outputs, middle_grad, query_grad, key_grads, vec_grads_up, kept, sent, *far_grads
    ) = call_kernel(
        functools.partial(turn_body, per_layer, vec_rows, tree_bits),
        [low_of(tok_count, model_width)] + back,
        units_in(per_layer - 3)
        + grads_out(per_layer - 3)
        + [pltpu.VMEM(shape.shape, shape.dtype) for shape in attended + fed],
        "layer_turn",
        meta,
        vec,
        offsets_in,
        cotangent[0],
        hidden,
        qkv_one,
        *far_one,
        packed,
        smem_count=1,
        micros=13,
        any_in=(6 + tree_bits,),
        any_out=(5, 6),
    )
    near_grads = coarse_down(far_grads, seq_index)
    middle_grad, query_grad, key_grads, vec_grads_mid, kept, sent, *far_grads = call_kernel(
        functools.partial(lower_body, per_layer, vec_rows, tree_bits),
        back,
        units_in(per_layer) + grads_out(per_layer),
        "layer_back",
        meta,
        vec,
        hidden,
        normed_one,
        query_grad,
        key_grads,
        near_grads,
        middle_grad,
        probs,
        mixed,
        middle,
        normed_two,
        pre,
        act,
        qkv_zero,
        *far_zero,
        packed,
        kept,
        sent,
        smem_count=1,
        micros=13,
        any_in=(15 + tree_bits, 16 + tree_bits, 17 + tree_bits),
        any_out=(4, 5),
        aliases={16 + tree_bits: 4, 17 + tree_bits: 5},
    )
    near_grads = coarse_down(far_grads, seq_index)
    input_grad, vec_grads_low, kept, sent = call_kernel(
        last_body,
        [full_of(tok_count, model_width), full_of(16, model_width)]
        + [low_of(UNIT_COUNT // 2, *square)] * 2,
        units_in(3) + grads_out(3),
        "project_back",
        meta,
        vec,
        inputs[0],
        normed_zero,
        query_grad,
        key_grads,
        near_grads,
        middle_grad,
        packed,
        kept,
        sent,
        smem_count=1,
        micros=5,
        any_in=(8, 9, 10),
        any_out=(2, 3),
        aliases={9: 2, 10: 3},
    )
    vec_sum = jnp.concatenate(
        [vec_grads_low[0:2], vec_grads_mid[2:vec_rows], vec_grads_mid[0:2], vec_grads_up[2:vec_rows]]
    )
    if by_permutes:
        owner_grad, vec_sum = sum_to_owner(kept, sent, seq_index, vec_sum)
    else:
        for axis in ("opt", "seq"):
            for bit_at in range(lax.axis_size(axis).bit_length() - 1):
                vec_sum = vec_sum + partner(vec_sum, axis, bit_at)
        column_grads = lax.psum_scatter(
            jnp.concatenate([kept, sent]), "opt", scatter_dimension=0, tiled=True
        )
        column_grads = jnp.pad(column_grads, [(0, seq_count - own_slots), (0, 0), (0, 0)])
        owner_grad = lax.psum_scatter(column_grads, "seq", scatter_dimension=0, tiled=True)[0]
    grad_vecs = lax.dynamic_slice_in_dim(
        vec_sum.reshape(-1), (seq_index * opt_count + lax.axis_index("opt")) * vec_count, vec_count
    )
    step_rows, owner_stat, owner_basis = rotate_slot(offsets, owner_grad, owner_rows)
    home_rows = lax.all_to_all(step_rows, "seq", 0, 0, tiled=True)
    base_pieces = renew_bases(offsets, owner_stat, owner_basis)
    base_pieces, home_rows = lax.optimization_barrier((base_pieces, home_rows))
    whole_shape = jax.ShapeDtypeStruct(masters.shape, jnp.float32)
    new_masters, new_first, new_second, new_stats = call_kernel(
        functools.partial(finish_body, own_slots),
        [whole_shape, whole_shape, whole_shape, jax.ShapeDtypeStruct(stats.shape, jnp.float32)],
        [],
        "finish_slots",
        masters,
        first_moment,
        second_moment,
        stats,
        home_rows,
        micros=4,
    )
    (new_bases,) = call_kernel(
        functools.partial(place_body, own_slots),
        [jax.ShapeDtypeStruct(bases.shape, jnp.float32)],
        [],
        "place_bases",
        slot_at,
        *to_homes(base_pieces, "seq", by_permutes, own_slots),
        smem_count=1,
    )
    new_vec_first = BETA_ONE * vec_first + (1.0 - BETA_ONE) * grad_vecs
    new_vec_second = BETA_TWO * vec_second + (1.0 - BETA_TWO) * grad_vecs * grad_vecs
    new_vectors = vec_master - RATE_VECTOR * (new_vec_first / (1.0 - BETA_ONE**STEP)) / (
        jnp.sqrt(new_vec_second / (1.0 - BETA_TWO**STEP)) + ADAM_EPS
    )
    return (
        outputs[None],
        input_grad[None],
        new_masters,
        new_first,
        new_second,
        new_bases,
        new_stats,
        new_vectors,
        new_vec_first,
        new_vec_second,
    )


def solution(mesh):
    placed = (
        P("opt", "seq", None),
        P("opt", "seq", None),
        P("opt", None),
        P(),
        P("opt", "seq", None),
        P("opt", "seq", None),
        P("opt", "seq", None),
        P("opt", None, "seq", None),
        P("opt", None, "seq", None),
        P(("seq", "opt")),
        P(("seq", "opt")),
        P(("seq", "opt")),
    )
    return jax.shard_map(
        per_device,
        mesh=mesh,
        in_specs=placed,
        out_specs=(
            P("opt", "seq", None),
            P("opt", "seq", None),
            P("opt", "seq", None),
            P("opt", "seq", None),
            P("opt", "seq", None),
            P("opt", None, "seq", None),
            P("opt", None, "seq", None),
            P(("seq", "opt")),
            P(("seq", "opt")),
            P(("seq", "opt")),
        ),
        check_vma=False,
    )
```

```python
import functools
import math

import jax
import jax.numpy as jnp
from jax import lax
from jax.experimental import pallas as pl
from jax.experimental.pallas import tpu as pltpu
from jax.sharding import PartitionSpec as P

HEADS = 8
FF = 2048
BLOCK = 16
LAYERS = 2
STEP = 10
MAX_LEN = 4096


HIGH = lax.Precision.HIGHEST
LN_TWO = math.log(2.0)
NEG_FILL = -1e30
NORM_EPS = 1e-05
ADAM_EPS = 1e-08
RATE_MATRIX = 0.03
RATE_VECTOR = 0.2
WEIGHT_DECAY = 0.01
BETA_ONE = 0.9
BETA_TWO = 0.95
BETA_STAT = 0.95

SUBLANES = 8
PANEL = 16
FLOPS_PER_US = 1_150_000_000
LANES = 128
UNIT_COUNT = 24
UNIT_OPT = 0
UNIT_ROW = UNIT_COUNT
UNIT_SLOT = 2 * UNIT_COUNT
DIAG = 128
VMEM_GRANT = 60 * 2**20
IN_VMEM = pl.BlockSpec(memory_space=pltpu.VMEM)
IN_SMEM = pl.BlockSpec(memory_space=pltpu.SMEM)
ANYWHERE = pl.BlockSpec(memory_space=pl.ANY)


def contract(left, right, left_dim, right_dim, precision=None):
    return lax.dot_general(
        left,
        right,
        (((left_dim,), (right_dim,)), ((), ())),
        precision=precision,
        preferred_element_type=jnp.float32,
    )


def split_two(values):
    high = values.astype(jnp.bfloat16)
    return (high, (values - high.astype(jnp.float32)).astype(jnp.bfloat16))


def wide_left(left, right_low, left_dim, right_dim):
    high, rest = split_two(left)
    return contract(high, right_low, left_dim, right_dim) + contract(
        rest, right_low, left_dim, right_dim
    )


def wide_right(left_low, right, left_dim, right_dim):
    high, rest = split_two(right)
    return contract(left_low, high, left_dim, right_dim) + contract(
        left_low, rest, left_dim, right_dim
    )


def call_kernel(
    body, out_shapes, scratch, name, *operands, smem_count=0, any_in=(), any_out=(), aliases=None,
    micros=2,
):
    def place(at, listed):
        return ANYWHERE if at in listed else IN_VMEM

    return pl.pallas_call(
        body,
        out_shape=out_shapes,
        in_specs=[
            IN_SMEM if at < smem_count else place(at, any_in) for at in range(len(operands))
        ],
        out_specs=[place(at, any_out) for at in range(len(out_shapes))],
        scratch_shapes=scratch,
        input_output_aliases=aliases or {},
        cost_estimate=pl.CostEstimate(
            flops=micros * FLOPS_PER_US, bytes_accessed=0, transcendentals=0
        ),
        compiler_params=pltpu.CompilerParams(vmem_limit_bytes=VMEM_GRANT),
        name=name,
    )(*operands)


def eliminate(panels, turn):
    rows, width = panels[0][0].shape
    row_at = lax.broadcasted_iota(jnp.int32, (SUBLANES, width), 0)

    def groups(values):
        return [values[low : low + SUBLANES] for low in range(0, rows, SUBLANES)]

    def spread_row(values, row):
        return jnp.broadcast_to(values[row : row + 1, :], values.shape)

    states = []
    for left, right in panels:
        turned = pltpu.roll(left, turn, 1)
        columns = [
            [jnp.broadcast_to(part, (SUBLANES, width)) for part in groups(turned[:, at : at + 1])]
            for at in range(rows)
        ]
        ones = [jnp.ones((SUBLANES, width), jnp.float32) for _ in range(rows // SUBLANES)]
        states.append((groups(left), groups(right), columns, ones))
    for at in range(rows):
        group_at, row = divmod(at, SUBLANES)
        for left, right, columns, pivots in states:
            pivot = spread_row(columns[at][group_at], row)
            inverse = pltpu.reciprocal(pivot, approx=False)
            pivots[group_at] = jnp.where(row_at == row, pivot, pivots[group_at])
            targets = [left, right] + columns[at + 1 :]
            given = [spread_row(target[group_at], row) for target in targets]
            for group in range(group_at, rows // SUBLANES):
                factor = columns[at][group] * inverse
                if group == group_at:
                    factor = jnp.where(row_at > row, factor, 0.0)
                for target, pivot_row in zip(targets, given):
                    target[group] = target[group] - factor * pivot_row
    results = []
    for left, right, _, pivots in states:
        scales = [lax.rsqrt(values) for values in pivots]
        results.append(
            tuple(
                jnp.concatenate([part * scale for part, scale in zip(parts, scales)], axis=0)
                for parts in (left, right)
            )
        )
    return results


def split_three(values):
    high = values.astype(jnp.bfloat16).astype(jnp.float32)
    rest = values - high
    middle = rest.astype(jnp.bfloat16).astype(jnp.float32)
    return (high, middle, rest - middle)


def thin_product(left, right):
    left_parts, right_parts = (split_three(left), split_three(right))
    pairs = ((0, 0), (0, 1), (1, 0), (1, 1), (0, 2), (2, 0))
    stacked_left = jnp.concatenate([left_parts[i] for i, _ in pairs], axis=0)
    stacked_right = jnp.concatenate([right_parts[j] for _, j in pairs], axis=0)
    return contract(stacked_left.astype(jnp.bfloat16), stacked_right.astype(jnp.bfloat16), 0, 0)


def factorize(grams, uppers, works, inverses):
    each = range(len(grams))
    size = grams[0].shape[0]
    eye = (
        lax.broadcasted_iota(jnp.int32, (DIAG, DIAG), 0)
        == lax.broadcasted_iota(jnp.int32, (DIAG, DIAG), 1)
    ).astype(jnp.float32)
    for low in range(0, size, DIAG):
        top = low + DIAG
        for m in each:
            works[m][:, 0:DIAG] = grams[m][low:top, low:top]
            works[m][:, DIAG:] = eye

        def panel(panel_at, carry):
            row = pl.multiple_of(panel_at * PANEL, PANEL)
            turn = lax.rem(DIAG - panel_at * PANEL, DIAG)
            panels = [
                (works[m][pl.ds(row, PANEL), 0:DIAG], works[m][pl.ds(row, PANEL), DIAG:])
                for m in each
            ]
            results = eliminate(panels, turn)
            updates = [
                thin_product(left, jnp.concatenate([left, right], axis=1))
                for left, right in results
            ]
            for m in each:
                inverses[m][low // DIAG, pl.ds(row, PANEL), :] = results[m][1]
            for m in each:
                works[m][...] = works[m][...] - updates[m]
            return carry

        lax.fori_loop(0, DIAG // PANEL, panel, 0)
        if top == size:
            break
        right_of = [contract(inverses[m][low // DIAG], grams[m][low:top, top:], 1, 0, HIGH) for m in each]
        for m in each:
            uppers[m][low:top, top:] = right_of[m]
        for other in range(top, size, DIAG):
            skip = other - top
            rest = [
                grams[m][other : other + DIAG, other:]
                - contract(right_of[m][:, skip : skip + DIAG], right_of[m][:, skip:], 0, 0, HIGH)
                for m in each
            ]
            for m in each:
                grams[m][other : other + DIAG, other:] = rest[m]


def renew_body(*refs):
    stat_ref, basis_ref, sent = refs[:3]
    scratch = refs[3:]
    count, size, _ = stat_ref.shape
    each = range(count)
    products, grams, uppers, works, inverses = (
        scratch[at : at + count] for at in range(0, 5 * count, count)
    )
    values = [wide_left(stat_ref[m], basis_ref[m], 1, 0) for m in each]
    for m in each:
        products[m][...] = values[m]
    for low in range(0, size, DIAG):
        values = [
            contract(products[m][:, low : low + DIAG], products[m][:, low:], 0, 0, HIGH)
            for m in each
        ]
        for m in each:
            grams[m][low : low + DIAG, low:] = values[m]
    factorize(grams, uppers, works, inverses)
    for low in range(0, size, DIAG):
        top = low + DIAG
        values = [products[m][:, low:top] for m in each]
        if low:
            values = [
                values[m]
                - contract(products[m][:, :low], uppers[m][:low, low:top], 1, 0, HIGH)
                for m in each
            ]
        values = [contract(values[m], inverses[m][low // DIAG], 1, 1, HIGH) for m in each]
        for m in each:
            products[m][:, low:top] = values[m]
    rows = sent.shape[2]
    for target in range(sent.shape[0]):
        for m in each:
            sent[target, m] = products[m][target * rows : (target + 1) * rows, :].astype(
                jnp.bfloat16
            )


def renew_bases(device_count, new_stat, basis_low):
    count, size, _ = new_stat.shape
    return call_kernel(
        renew_body,
        [jax.ShapeDtypeStruct((device_count, count, size // device_count, size), jnp.bfloat16)],
        [pltpu.VMEM((size, size), jnp.float32)] * (3 * count)
        + [pltpu.VMEM((DIAG, 2 * DIAG), jnp.float32)] * count
        + [pltpu.VMEM((size // DIAG, DIAG, DIAG), jnp.float32)] * count,
        "renew_bases",
        new_stat,
        basis_low,
        micros=40,
    )[0]


def owner_devices(own_slots, by_permutes):
    if not by_permutes:
        return list(range(own_slots))
    return [2 * (slot // 2 + slot % 2) + slot % 2 for slot in range(own_slots)]


def pack_body(slot_ref, stats, bases, first, second, *packed):
    at = 0
    for part in packed:
        for target in range(part.shape[0]):
            slot = slot_ref[at]
            part[target, 0:2] = stats[slot].astype(jnp.bfloat16)
            part[target, 2:4] = bases[slot].astype(jnp.bfloat16)
            part[target, 4] = first[slot].astype(jnp.bfloat16)
            part[target, 5] = second[slot].astype(jnp.bfloat16)
            at += 1


def rotate_body(turn_ref, grad_ref, given, sent, stat_ref, basis_ref, whole, results):
    sources, sides, _, rows, _ = given.shape
    for source in range(sources):
        for side in range(sides):
            row = source * sides * rows + (side ^ turn_ref[0]) * rows
            whole[:, pl.ds(pl.multiple_of(row, rows), rows), :] = given[source, side].astype(
                jnp.float32
            )
    grad = grad_ref[...]
    left = whole[2].astype(jnp.bfloat16)
    right = whole[3].astype(jnp.bfloat16)
    basis_ref[0] = left
    basis_ref[1] = right
    results[0] = contract(grad, grad, 1, 1)
    results[1] = contract(grad, grad, 0, 0)
    stat_ref[0] = BETA_STAT * whole[0] + (1.0 - BETA_STAT) * results[0]
    stat_ref[1] = BETA_STAT * whole[1] + (1.0 - BETA_STAT) * results[1]
    rotated = wide_left(contract(left, grad, 0, 0), right, 1, 0)
    results[2] = rotated
    new_first = BETA_ONE * whole[4] + (1.0 - BETA_ONE) * rotated
    new_second = BETA_TWO * whole[5] + (1.0 - BETA_TWO) * rotated * rotated
    direction = (
        new_first
        / (1.0 - BETA_ONE**STEP)
        / (jnp.sqrt(new_second / (1.0 - BETA_TWO**STEP)) + ADAM_EPS)
    )
    results[3] = wide_right(left, wide_left(direction, right, 1, 1), 1, 0)
    for target in range(sent.shape[0]):
        sent[target] = results[:, target * rows : (target + 1) * rows, :].astype(jnp.bfloat16)


def rotate_slot(turn, grad, owner_rows):
    size = grad.shape[0]
    return call_kernel(
        rotate_body,
        [
            jax.ShapeDtypeStruct(
                (size // owner_rows.shape[3], 4) + owner_rows.shape[3:], jnp.bfloat16
            ),
            jax.ShapeDtypeStruct((2, size, size), jnp.float32),
            jax.ShapeDtypeStruct((2, size, size), jnp.bfloat16),
        ],
        [
            pltpu.VMEM((6, size, size), jnp.float32),
            pltpu.VMEM((4, size, size), jnp.float32),
        ],
        "rotate_slot",
        turn,
        grad,
        owner_rows,
        smem_count=1,
        micros=6,
    )


def finish_body(
    owners, masters, first, second, stats, given, new_masters, new_first, new_second, new_stats
):
    for slot, owner in enumerate(owners):
        rotated = given[owner, 2].astype(jnp.float32)
        update = given[owner, 3].astype(jnp.float32)
        new_first[slot] = BETA_ONE * first[slot] + (1.0 - BETA_ONE) * rotated
        new_second[slot] = BETA_TWO * second[slot] + (1.0 - BETA_TWO) * rotated * rotated
        new_masters[slot] = masters[slot] - RATE_MATRIX * (update + WEIGHT_DECAY * masters[slot])
        new_stats[slot] = BETA_STAT * stats[slot] + (1.0 - BETA_STAT) * given[owner, 0:2].astype(
            jnp.float32
        )


def place_body(owners, given, new_bases):
    for slot, owner in enumerate(owners):
        new_bases[slot] = given[owner].astype(jnp.float32)


def add_low(left, right):
    return (left.astype(jnp.float32) + right.astype(jnp.float32)).astype(jnp.bfloat16)


def sum_to_owner(kept, sent, seq_index, vec_sum):
    def beside(values, vec_sum, axis, bit_at):
        return lax.optimization_barrier((values, vec_sum + partner(vec_sum, axis, bit_at)))

    size = kept.shape[-1]
    z_count = kept.shape[0] // 4
    shape = (2, 2, z_count, size, size)
    kept = kept.reshape(shape)
    came, vec_sum = beside(partner(sent, "opt", 0), vec_sum, "opt", 0)
    came = came.reshape(shape)
    half = size // 2

    def part(x_at, y_at, rows):
        return add_low(kept[x_at, y_at, :, rows], came[x_at, y_at, :, rows])

    upper, lower = (slice(0, half), slice(half, size))
    by_x = partner(part(1, slice(0, 2), upper), "opt", 1)
    by_y = partner(part(slice(0, 2), 1, lower), "seq", 0)
    by_x, vec_sum = beside(by_x, vec_sum, "opt", 1)
    stay_x = part(0, slice(0, 2), upper)
    stay_y = part(slice(0, 2), 0, lower)
    then_y = partner(add_low(stay_x[1], by_x[1]), "seq", 0)
    then_x = partner(add_low(stay_y[1], by_y[1]), "opt", 1)
    then_y, vec_sum = beside(then_y, vec_sum, "seq", 0)
    z_index = seq_index >> 1

    def both(apart):
        at = jnp.clip((z_index ^ apart) - (seq_index & 1), 0, z_count - 1)

        def pick(values):
            return lax.dynamic_index_in_dim(values, at, 0, keepdims=False)

        total_upper = (
            pick(stay_x[0]).astype(jnp.float32)
            + pick(by_x[0]).astype(jnp.float32)
            + pick(then_y).astype(jnp.float32)
        )
        total_lower = (
            pick(stay_y[0]).astype(jnp.float32)
            + pick(by_y[0]).astype(jnp.float32)
            + pick(then_x).astype(jnp.float32)
        )
        return jnp.concatenate([total_upper, total_lower]).astype(jnp.bfloat16)

    near_one = partner(both(1), "seq", 1)
    near_far = partner(both(3), "seq", 1)
    near_one, vec_sum = beside(near_one, vec_sum, "seq", 1)
    last = partner(add_low(both(2), near_far), "seq", 2)
    last, vec_sum = beside(last, vec_sum, "seq", 2)
    total = both(0).astype(jnp.float32) + near_one.astype(jnp.float32) + last.astype(jnp.float32)
    return (total.astype(jnp.bfloat16), vec_sum)


def partner(value, axis, apart):
    return lax.ppermute(value, axis, [(i, i ^ 1 << apart) for i in range(lax.axis_size(axis))])


def pair_mean(values):
    shaped = values.reshape((values.shape[0] // 2, 2) + values.shape[1:])
    return 0.5 * (shaped[:, 0] + shaped[:, 1])


def pair_spread(grads):
    return 0.5 * jnp.repeat(grads, 2, axis=0)


def sum_rows(values):
    return jnp.sum(values, axis=0, keepdims=True)


def norm_parts(values):
    centred = values - jnp.mean(values, axis=-1, keepdims=True)
    recip = lax.rsqrt(jnp.mean(centred * centred, axis=-1, keepdims=True) + NORM_EPS)
    return (centred * recip, recip)


def norm_back(grad, gain, normed, recip):
    scaled = grad * gain
    return recip * (
        scaled
        - jnp.mean(scaled, axis=-1, keepdims=True)
        - normed * jnp.mean(scaled * normed, axis=-1, keepdims=True)
    )


def half_matrix(shape, fine_dim):
    fine = lax.broadcasted_iota(jnp.int32, shape, fine_dim)
    coarse = lax.broadcasted_iota(jnp.int32, shape, 1 - fine_dim)
    return jnp.where(fine >> 1 == coarse, 0.5, 0.0).astype(jnp.bfloat16)


def pool(rows_low):
    count = rows_low.shape[0]
    return contract(half_matrix((count // 2, count), 1), rows_low, 1, 0).astype(jnp.bfloat16)


def spread(grads):
    count = grads.shape[0]
    return wide_right(half_matrix((2 * count, count), 0), grads, 1, 0)


def norm_cdf(values):
    return 0.5 * (1.0 + lax.erf(values * math.sqrt(0.5)))


def local_count(tok_count):
    return (tok_count // BLOCK).bit_length() - 1


def key_width(tok_count, tree_bits):
    rows = 2 * (tok_count - BLOCK) + BLOCK * tree_bits
    return -(-rows // LANES) * LANES


def score_offsets(tok_count, tree_bits, span_bits):
    token = jnp.arange(tok_count, dtype=jnp.int32)[:, None]
    parts = []
    for height in range(local_count(tok_count)):
        row = jnp.arange(tok_count >> height, dtype=jnp.int32)[None, :]
        apart = token // (BLOCK << height) ^ row // BLOCK
        counted = apart <= 1 if height == 0 else apart == 1
        parts.append(jnp.where(counted, height * LN_TWO, NEG_FILL))
    for bit_at in range(tree_bits):
        offset = (local_count(tok_count) + bit_at) * LN_TWO
        parts.append(
            jnp.broadcast_to(
                jnp.where(bit_at + 1 <= span_bits, offset, NEG_FILL), (tok_count, BLOCK)
            )
        )
    used = sum(part.shape[1] for part in parts)
    rest = key_width(tok_count, tree_bits) - used
    parts.append(jnp.full((tok_count, rest), NEG_FILL, jnp.float32))
    return jnp.concatenate(parts, axis=1).astype(jnp.float32)


def stack_keys(own_rows, far_rows):
    parts = [own_rows]
    for _ in range(local_count(own_rows.shape[0]) - 1):
        parts.append(pool(parts[-1]))
    parts = parts + far_rows
    rest = key_width(own_rows.shape[0], len(far_rows)) - sum(part.shape[0] for part in parts)
    if rest:
        parts.append(jnp.zeros((rest, own_rows.shape[1]), jnp.bfloat16))
    return jnp.concatenate(parts, axis=0)


def by_heads(pair):
    lane = lax.broadcasted_iota(jnp.int32, pair.shape, 1)
    zero = jnp.zeros_like(pair)
    first = lane < LANES // 2
    return jnp.concatenate([jnp.where(first, pair, zero), jnp.where(first, zero, pair)], axis=0)


def from_heads(both):
    count = both.shape[0] // 2
    lane = lax.broadcasted_iota(jnp.int32, (count, LANES), 1)
    return jnp.where(lane < LANES // 2, both[:count], both[count:])


def attend(qkv, far_rows, offsets, probs, mixed):
    width = qkv.shape[1] // 3
    score_scale = (width // HEADS) ** (-0.5)
    stack = stack_keys(qkv[:, width:], far_rows)
    both_offsets = jnp.concatenate([offsets, offsets], axis=0)
    for pair_at in range(width // LANES):
        low, top = (pair_at * LANES, (pair_at + 1) * LANES)
        scores = (
            contract(by_heads(qkv[:, low:top]), stack[:, low:top], 1, 1) * score_scale
            + both_offsets
        )
        expo = jnp.exp(scores - jnp.max(scores, axis=1, keepdims=True))
        weights = expo / jnp.sum(expo, axis=1, keepdims=True)
        probs[pair_at] = weights
        result = contract(
            weights.astype(jnp.bfloat16), stack[:, width + low : width + top], 1, 0
        )
        mixed[:, low:top] = from_heads(result).astype(jnp.bfloat16)


def attend_back(qkv, far_rows, probs, mixed_grad, query_grad, key_grads, far_grads):
    tok_count, width = mixed_grad.shape
    score_scale = (width // HEADS) ** (-0.5)
    stack = stack_keys(qkv[:, width:], far_rows)
    local_levels = local_count(tok_count)
    far_start = 2 * (tok_count - BLOCK)
    for pair_at in range(width // LANES):
        low, top = (pair_at * LANES, (pair_at + 1) * LANES)
        queries = by_heads(qkv[:, low:top])
        grads = by_heads(mixed_grad[:, low:top])
        weights = probs[pair_at]
        prob_grad = contract(grads, stack[:, width + low : width + top], 1, 1)
        inner = jnp.sum(weights * prob_grad, axis=1, keepdims=True)
        score_grad = (weights * (prob_grad - inner)).astype(jnp.bfloat16)
        query_grad[:, low:top] = (
            from_heads(contract(score_grad, stack[:, low:top], 1, 0)) * score_scale
        ).astype(jnp.bfloat16)
        for start, part in (
            (low, contract(score_grad, queries, 0, 0) * score_scale),
            (width + low, contract(weights.astype(jnp.bfloat16), grads, 0, 0)),
        ):
            for far_at, far_grad in enumerate(far_grads):
                row = far_start + BLOCK * far_at
                far_grad[:, start : start + LANES] = part[row : row + BLOCK]
            folded = None
            for height in reversed(range(local_levels)):
                row = 2 * (tok_count - (tok_count >> height))
                own = part[row : row + (tok_count >> height)]
                folded = own if folded is None else own + spread(folded)
            key_grads[:, start : start + LANES] = folded


class Units:
    def __init__(self, meta, packed, store, sems, units):
        self.store = store
        self.place = {unit: at for at, unit in enumerate(units)}
        self.waiting = {}
        rows = store.shape[2]
        for at, unit in enumerate(units):
            row = pl.multiple_of(meta[UNIT_ROW + unit], rows)
            copy = pltpu.make_async_copy(
                packed.at[:, meta[UNIT_OPT + unit], pl.ds(row, rows), :],
                store.at[at],
                sems.at[at],
            )
            copy.start()
            self.waiting[unit] = copy

    def __getitem__(self, unit):
        if unit in self.waiting:
            self.waiting.pop(unit).wait()
        width = self.store.shape[3]
        return self.store[self.place[unit]].reshape(width, width)


class Grads:
    def __init__(self, meta, kept, sent, store, sems):
        self.meta, self.kept, self.sent, self.store, self.sems = (meta, kept, sent, store, sems)
        self.copies = []

    def put(self, unit, left_low, right_low):
        at = len(self.copies)
        self.store[at] = contract(left_low, right_low, 0, 0).astype(jnp.bfloat16)
        place = self.meta[UNIT_SLOT + unit]
        half = self.kept.shape[0]
        inner = jnp.where(place < half, place, place - half)
        keeping, sending = (
            pltpu.make_async_copy(self.store.at[at], target.at[inner], self.sems.at[at])
            for target in (self.kept, self.sent)
        )
        pl.when(place < half)(keeping.start)
        pl.when(place >= half)(sending.start)
        self.copies.append(keeping)

    def finish(self):
        for copy in self.copies:
            copy.wait()


def project(hidden, units, first_unit, gain, bias, normed_ref, qkv_ref, near_ref):
    width = hidden.shape[1]
    normed, _ = norm_parts(hidden)
    normed_low = (normed * gain + bias).astype(jnp.bfloat16)
    normed_ref[...] = normed_low
    for part in range(3):
        qkv_ref[:, part * width : (part + 1) * width] = contract(
            normed_low, units[first_unit + part], 1, 0
        ).astype(jnp.bfloat16)
    near = qkv_ref[:, width:]
    for _ in range(local_count(near.shape[0])):
        near = pool(near)
    near_ref[...] = near


def feed_forward(middle, units, first_unit, vec, vec_at, normed_ref, pre_ref, act_ref):
    width = middle.shape[1]
    normed, _ = norm_parts(middle)
    normed_low = (normed * vec[vec_at + 2 : vec_at + 3] + vec[vec_at + 3 : vec_at + 4]).astype(
        jnp.bfloat16
    )
    normed_ref[...] = normed_low
    total = middle
    ff_blocks = FF // width
    for part in range(ff_blocks):
        low, top = (part * width, (part + 1) * width)
        row = vec_at + 4 + part
        pre = contract(normed_low, units[first_unit + 4 + part], 1, 0) + vec[row : row + 1]
        act = (pre * norm_cdf(pre)).astype(jnp.bfloat16)
        pre_ref[:, low:top] = pre
        act_ref[:, low:top] = act
        total = total + contract(act, units[first_unit + 4 + ff_blocks + part], 1, 0)
    row = vec_at + 4 + ff_blocks
    return total + vec[row : row + 1]


def feed_back(
    grad, middle, normed_low, pre_ref, act_ref, units, grads, first_unit, vec, vec_at, vec_grads, at
):
    width = middle.shape[1]
    ff_blocks = FF // width
    down_grad = grad.astype(jnp.bfloat16)
    normed_grad = jnp.zeros(middle.shape, jnp.float32)
    for part in range(ff_blocks):
        low, top = (part * width, (part + 1) * width)
        down_unit = first_unit + 4 + ff_blocks + part
        grads.put(down_unit, act_ref[:, low:top], down_grad)
        pre = pre_ref[:, low:top]
        slope = norm_cdf(pre) + pre * jnp.exp(-0.5 * pre * pre) * (1.0 / math.sqrt(2.0 * math.pi))
        pre_grad = (contract(down_grad, units[down_unit], 1, 1) * slope).astype(jnp.bfloat16)
        grads.put(first_unit + 4 + part, normed_low, pre_grad)
        vec_grads[at + 2 + part : at + 3 + part] = sum_rows(pre_grad.astype(jnp.float32))
        normed_grad = normed_grad + contract(pre_grad, units[first_unit + 4 + part], 1, 1)
    row = at + 2 + ff_blocks
    vec_grads[row : row + 1] = sum_rows(grad)
    normed, recip = norm_parts(middle)
    vec_grads[at : at + 1] = sum_rows(normed_grad * normed)
    vec_grads[at + 1 : at + 2] = sum_rows(normed_grad)
    return grad + norm_back(normed_grad, vec[vec_at + 2 : vec_at + 3], normed, recip)


def project_back(
    middle_grad, hidden, normed_low, query_grad, key_grads, near_grads, units, grads, first_unit,
    vec, vec_at, vec_grads,
):
    width = hidden.shape[1]
    near = near_grads[...]
    for _ in range(local_count(hidden.shape[0])):
        near = spread(near)
    rows_low = (key_grads[...] + near).astype(jnp.bfloat16)
    parts = (query_grad[...], rows_low[:, :width], rows_low[:, width:])
    normed_grad = jnp.zeros(hidden.shape, jnp.float32)
    for part, part_grad in enumerate(parts):
        grads.put(first_unit + part, normed_low, part_grad)
        normed_grad = normed_grad + contract(part_grad, units[first_unit + part], 1, 1)
    normed, recip = norm_parts(hidden)
    vec_grads[0:1] = sum_rows(normed_grad * normed)
    vec_grads[1:2] = sum_rows(normed_grad)
    return middle_grad + norm_back(normed_grad, vec[vec_at : vec_at + 1], normed, recip)


def first_body(per_layer, meta, vec, inputs, packed, normed, qkv, near, store, sems):
    units = Units(meta, packed, store, sems, range(3))
    project(inputs[...].astype(jnp.float32), units, 0, vec[0:1], vec[1:2], normed, qkv, near)


def middle_body(per_layer, vec_rows, tree_bits, meta, vec, offsets, inputs, qkv, *refs):
    far, refs = (refs[:tree_bits], refs[tree_bits:])
    packed, probs, mixed, middle, normed_two, pre, act, hidden, normed, next_qkv, near = refs[:11]
    store, sems = refs[11:]
    units = Units(meta, packed, store, sems, range(3, per_layer + 3))
    attend(qkv[...], [ref[...] for ref in far], offsets[...], probs, mixed)
    middle[...] = inputs[...].astype(jnp.float32) + contract(mixed[...], units[3], 1, 0)
    hidden[...] = feed_forward(middle[...], units, 0, vec, 0, normed_two, pre, act)
    project(
        hidden[...], units, per_layer, vec[vec_rows : vec_rows + 1],
        vec[vec_rows + 1 : vec_rows + 2], normed, next_qkv, near,
    )


def turn_body(per_layer, vec_rows, tree_bits, meta, vec, offsets, cotangent, hidden, qkv, *refs):
    far, refs = (refs[:tree_bits], refs[tree_bits:])
    packed, outputs, middle_grad, query_grad, key_grads, vec_grads, kept, sent = refs[:8]
    far_grads, refs = (refs[8 : 8 + tree_bits], refs[8 + tree_bits :])
    store, sems, grad_store, grad_sems, probs, mixed, normed_two, pre, act = refs
    units = Units(meta, packed, store, sems, range(per_layer + 3, 2 * per_layer))
    grads = Grads(meta, kept, sent, grad_store, grad_sems)
    far_rows = [ref[...] for ref in far]
    attend(qkv[...], far_rows, offsets[...], probs, mixed)
    middle = hidden[...] + contract(mixed[...], units[per_layer + 3], 1, 0)
    outputs[...] = feed_forward(
        middle, units, per_layer, vec, vec_rows, normed_two, pre, act
    ).astype(jnp.bfloat16)
    vec_grads[...] = jnp.zeros_like(vec_grads)
    grad = feed_back(
        cotangent[...].astype(jnp.float32), middle, normed_two[...], pre, act, units, grads,
        per_layer, vec, vec_rows, vec_grads, 2,
    )
    middle_grad[...] = grad
    branch_grad = grad.astype(jnp.bfloat16)
    grads.put(per_layer + 3, mixed[...], branch_grad)
    mixed_grad = contract(branch_grad, units[per_layer + 3], 1, 1).astype(jnp.bfloat16)
    attend_back(qkv[...], far_rows, probs, mixed_grad, query_grad, key_grads, far_grads)
    grads.finish()


def lower_body(per_layer, vec_rows, tree_bits, meta, vec, *refs):
    hidden, normed_one, query_in, key_in, near_in, middle_in = refs[:6]
    probs, mixed, middle, normed_two, pre, act, qkv = refs[6:13]
    far, refs = (refs[13 : 13 + tree_bits], refs[13 + tree_bits :])
    packed, _, _, middle_grad, query_grad, key_grads, vec_grads, kept, sent = refs[:9]
    far_grads, refs = (refs[9 : 9 + tree_bits], refs[9 + tree_bits :])
    store, sems, grad_store, grad_sems = refs
    upper_units = list(range(per_layer, per_layer + 3))
    units = Units(
        meta, packed, store, sems, upper_units + list(range(3 + (per_layer - 4) // 2 + 1, per_layer))
        + list(range(3, 3 + (per_layer - 4) // 2 + 1)),
    )
    grads = Grads(meta, kept, sent, grad_store, grad_sems)
    vec_grads[...] = jnp.zeros_like(vec_grads)
    grad = project_back(
        middle_in[...], hidden[...], normed_one[...], query_in, key_in, near_in, units, grads,
        per_layer, vec, vec_rows, vec_grads,
    )
    grad = feed_back(
        grad, middle[...], normed_two[...], pre, act, units, grads, 0, vec, 0, vec_grads, 2
    )
    middle_grad[...] = grad
    branch_grad = grad.astype(jnp.bfloat16)
    grads.put(3, mixed[...], branch_grad)
    mixed_grad = contract(branch_grad, units[3], 1, 1).astype(jnp.bfloat16)
    attend_back(
        qkv[...], [ref[...] for ref in far], probs, mixed_grad, query_grad, key_grads, far_grads
    )
    grads.finish()


def last_body(meta, vec, inputs, normed_one, query_in, key_in, near_in, middle_in, *refs):
    packed, _, _, input_grad, vec_grads, kept, sent, store, sems, grad_store, grad_sems = refs
    units = Units(meta, packed, store, sems, range(3))
    grads = Grads(meta, kept, sent, grad_store, grad_sems)
    vec_grads[...] = jnp.zeros_like(vec_grads)
    input_grad[...] = project_back(
        middle_in[...], inputs[...].astype(jnp.float32), normed_one[...], query_in, key_in,
        near_in, units, grads, 0, vec, 0, vec_grads,
    )
    grads.finish()


def coarse_up(own, seq_index, tree_bits):
    far_list = []
    for bit_at in range(tree_bits):
        far = partner(own, "seq", bit_at)
        far_list.append(far)
        if bit_at + 1 < tree_bits:
            upper = seq_index >> bit_at & 1 == 1
            joined = jnp.where(
                upper, jnp.concatenate([far, own]), jnp.concatenate([own, far])
            ).astype(jnp.float32)
            own = pair_mean(joined).astype(jnp.bfloat16)
    return far_list


def coarse_down(far_grads, seq_index):
    above = None
    for bit_at in reversed(range(len(far_grads))):
        upper = seq_index >> bit_at & 1 == 1
        sent = far_grads[bit_at]
        own = 0.0
        if above is not None:
            wide = pair_spread(above)
            own = jnp.where(upper, wide[BLOCK:], wide[:BLOCK])
            sent = sent + jnp.where(upper, wide[:BLOCK], wide[BLOCK:])
        above = own + partner(sent.astype(jnp.bfloat16), "seq", bit_at).astype(jnp.float32)
    return above


def per_device(
    inputs,
    cotangent,
    seq_lengths,
    unit_slot,
    masters,
    first_moment,
    second_moment,
    bases,
    stats,
    vec_master,
    vec_first,
    vec_second,
):
    seq_count = lax.axis_size("seq")
    opt_count = lax.axis_size("opt")
    seq_index = lax.axis_index("seq")
    tok_count = inputs.shape[1]
    model_width = inputs.shape[2]
    own_slots = masters.shape[0]
    row_count = masters.shape[1]
    ff_blocks = FF // model_width
    per_layer = 4 + 2 * ff_blocks
    vec_width = 5 * model_width + FF
    long_devs = min(max(MAX_LEN // tok_count, 1), seq_count)
    tree_bits = long_devs.bit_length() - 1
    size = seq_count * row_count
    by_permutes = seq_count == 8 and opt_count == 4 and own_slots == 6
    owners = owner_devices(own_slots, by_permutes)
    def pack_slots(slots, counts):
        return call_kernel(
            pack_body,
            [
                jax.ShapeDtypeStruct((count, 6, row_count, model_width), jnp.bfloat16)
                for count in counts
            ],
            [],
            "pack_slots",
            slots,
            stats,
            bases,
            first_moment,
            second_moment,
            smem_count=1,
            micros=3,
        )

    if by_permutes:
        parity = seq_index & 1
        half_slots = own_slots // 2
        pairs = 2 * jnp.arange(half_slots, dtype=jnp.int32)
        near, away = pack_slots(
            jnp.concatenate([pairs + parity, pairs + 1 - parity]), (half_slots, half_slots)
        )
        met = jnp.stack([near, partner(away, "seq", 0)], axis=1)
        to_owner = jnp.where(
            parity == 0,
            jnp.concatenate([met, met[-1:]]),
            jnp.concatenate([met[:1], met]),
        )
        turn = parity.reshape(1)
    else:
        (to_owner,) = pack_slots(
            jnp.asarray(
                [owners.index(at) if at in owners else 0 for at in range(seq_count)], jnp.int32
            ),
            (seq_count,),
        )
        to_owner = to_owner[:, None]
        turn = jnp.zeros((1,), jnp.int32)
    vec_count = vec_master.shape[0]
    own_rows = own_slots * row_count
    vec_block = jnp.pad(
        vec_master.astype(jnp.bfloat16)[None], [(0, 15), (0, model_width - vec_count)]
    )
    gathered = lax.all_gather(
        jnp.concatenate(
            [masters.astype(jnp.bfloat16).reshape(own_rows, model_width), vec_block]
        )[None],
        ("seq", "opt"),
        axis=0,
        tiled=True,
    )
    vec = gathered[:, own_rows, :vec_count].reshape(-1, model_width).astype(jnp.float32)
    if row_count % 16 == 0:
        unit_rows = row_count
        packed = gathered.reshape(seq_count, opt_count, own_rows + 16, model_width)
    else:
        unit_rows = size
        packed = (
            gathered[:, :own_rows]
            .reshape(seq_count, opt_count, own_slots, row_count, model_width)
            .transpose(1, 2, 0, 3, 4)
            .reshape(1, opt_count, own_slots * size, model_width)
        )
    opt_index = lax.axis_index("opt")
    opt_at, slot_in = (unit_slot // own_slots, unit_slot % own_slots)
    if by_permutes:
        apart = opt_at ^ opt_index
        other = (apart & 1) * 4 + (apart >> 1) * 2 + ((slot_in ^ seq_index) & 1)
        place = other * (own_slots // 2) + (slot_in >> 1)
    else:
        place = unit_slot
    meta = jnp.concatenate([opt_at, slot_in * unit_rows, place]).astype(jnp.int32)
    span_bits = jnp.zeros((), jnp.int32)
    for bit_at in range(tree_bits + 1):
        start_dev = seq_index >> bit_at << bit_at
        span_bits = jnp.where(
            seq_lengths[0, start_dev] == tok_count * (1 << bit_at), bit_at, span_bits
        )
    offsets_in = score_offsets(tok_count, tree_bits, span_bits)
    width_in = offsets_in.shape[1]
    pair_count = model_width // LANES
    vec_rows = vec_width // model_width
    square = (model_width, model_width)

    def units_in(count):
        return [
            pltpu.VMEM((count, size // unit_rows, unit_rows, model_width), jnp.bfloat16),
            pltpu.SemaphoreType.DMA((count,)),
        ]

    def grads_out(count):
        return [pltpu.VMEM((count,) + square, jnp.bfloat16), pltpu.SemaphoreType.DMA((count,))]

    def low_of(*shape):
        return jax.ShapeDtypeStruct(shape, jnp.bfloat16)

    def full_of(*shape):
        return jax.ShapeDtypeStruct(shape, jnp.float32)

    projected = [
        low_of(tok_count, model_width),
        low_of(tok_count, 3 * model_width),
        low_of(BLOCK, 2 * model_width),
    ]
    attended = [
        full_of(pair_count, 2 * tok_count, width_in),
        low_of(tok_count, model_width),
    ]
    fed = [
        low_of(tok_count, model_width),
        full_of(tok_count, FF),
        low_of(tok_count, FF),
    ]
    back = [
        full_of(tok_count, model_width),
        low_of(tok_count, model_width),
        full_of(tok_count, 2 * model_width),
        full_of(16, model_width),
        low_of(UNIT_COUNT // 2, *square),
        low_of(UNIT_COUNT // 2, *square),
    ] + [full_of(BLOCK, 2 * model_width)] * tree_bits
    packed, to_owner = lax.optimization_barrier((packed, to_owner))
    normed_zero, qkv_zero, near_zero = call_kernel(
        functools.partial(first_body, per_layer),
        projected,
        units_in(3),
        "project_first",
        meta,
        vec,
        inputs[0],
        packed,
        smem_count=1,
        micros=3,
        any_in=(3,),
    )
    far_zero = coarse_up(near_zero, seq_index, tree_bits)
    (
        probs, mixed, middle, normed_two, pre, act, hidden, normed_one, qkv_one, near_one,
    ) = call_kernel(
        functools.partial(middle_body, per_layer, vec_rows, tree_bits),
        attended + [full_of(tok_count, model_width)] + fed + [full_of(tok_count, model_width)]
        + projected,
        units_in(per_layer),
        "layer_first",
        meta,
        vec,
        offsets_in,
        inputs[0],
        qkv_zero,
        *far_zero,
        packed,
        smem_count=1,
        micros=7,
        any_in=(5 + tree_bits,),
    )
    far_one = coarse_up(near_one, seq_index, tree_bits)
    (
        outputs, middle_grad, query_grad, key_grads, vec_grads_up, kept, sent, *far_grads
    ) = call_kernel(
        functools.partial(turn_body, per_layer, vec_rows, tree_bits),
        [low_of(tok_count, model_width)] + back,
        units_in(per_layer - 3)
        + grads_out(per_layer - 3)
        + [pltpu.VMEM(shape.shape, shape.dtype) for shape in attended + fed],
        "layer_turn",
        meta,
        vec,
        offsets_in,
        cotangent[0],
        hidden,
        qkv_one,
        *far_one,
        packed,
        smem_count=1,
        micros=13,
        any_in=(6 + tree_bits,),
        any_out=(5, 6),
    )
    near_grads = coarse_down(far_grads, seq_index)
    middle_grad, query_grad, key_grads, vec_grads_mid, kept, sent, *far_grads = call_kernel(
        functools.partial(lower_body, per_layer, vec_rows, tree_bits),
        back,
        units_in(per_layer) + grads_out(per_layer),
        "layer_back",
        meta,
        vec,
        hidden,
        normed_one,
        query_grad,
        key_grads,
        near_grads,
        middle_grad,
        probs,
        mixed,
        middle,
        normed_two,
        pre,
        act,
        qkv_zero,
        *far_zero,
        packed,
        kept,
        sent,
        smem_count=1,
        micros=13,
        any_in=(15 + tree_bits, 16 + tree_bits, 17 + tree_bits),
        any_out=(4, 5),
        aliases={16 + tree_bits: 4, 17 + tree_bits: 5},
    )
    near_grads = coarse_down(far_grads, seq_index)
    input_grad, vec_grads_low, kept, sent = call_kernel(
        last_body,
        [full_of(tok_count, model_width), full_of(16, model_width)]
        + [low_of(UNIT_COUNT // 2, *square)] * 2,
        units_in(3) + grads_out(3),
        "project_back",
        meta,
        vec,
        inputs[0],
        normed_zero,
        query_grad,
        key_grads,
        near_grads,
        middle_grad,
        packed,
        kept,
        sent,
        smem_count=1,
        micros=5,
        any_in=(8, 9, 10),
        any_out=(2, 3),
        aliases={9: 2, 10: 3},
    )
    vec_sum = jnp.concatenate(
        [vec_grads_low[0:2], vec_grads_mid[2:vec_rows], vec_grads_mid[0:2], vec_grads_up[2:vec_rows]]
    )
    if by_permutes:
        sent, to_owner = lax.optimization_barrier((sent, to_owner))
        owner_rows = lax.all_to_all(
            to_owner,
            "seq",
            0,
            0,
            tiled=True,
            axis_index_groups=[list(range(at, seq_count, 2)) for at in range(2)],
        )
        owner_grad, vec_sum = sum_to_owner(kept, sent, seq_index, vec_sum)
    else:
        owner_rows = lax.all_to_all(to_owner, "seq", 0, 0, tiled=True)
        for axis in ("opt", "seq"):
            for bit_at in range(lax.axis_size(axis).bit_length() - 1):
                vec_sum = vec_sum + partner(vec_sum, axis, bit_at)
        column_grads = lax.psum_scatter(
            jnp.concatenate([kept, sent]), "opt", scatter_dimension=0, tiled=True
        )
        column_grads = jnp.pad(column_grads, [(0, seq_count - own_slots), (0, 0), (0, 0)])
        owner_grad = lax.psum_scatter(column_grads, "seq", scatter_dimension=0, tiled=True)[0]
    grad_vecs = lax.dynamic_slice_in_dim(
        vec_sum.reshape(-1), (seq_index * opt_count + lax.axis_index("opt")) * vec_count, vec_count
    )
    step_rows, owner_stat, owner_basis = rotate_slot(turn, owner_grad, owner_rows)
    home_rows = lax.all_to_all(step_rows, "seq", 0, 0, tiled=True)
    base_rows = renew_bases(seq_count, owner_stat, owner_basis)
    base_rows, home_rows = lax.optimization_barrier((base_rows, home_rows))
    base_rows = lax.all_to_all(base_rows, "seq", 0, 0, tiled=True)
    whole_shape = jax.ShapeDtypeStruct(masters.shape, jnp.float32)
    new_masters, new_first, new_second, new_stats = call_kernel(
        functools.partial(finish_body, owners),
        [whole_shape, whole_shape, whole_shape, jax.ShapeDtypeStruct(stats.shape, jnp.float32)],
        [],
        "finish_slots",
        masters,
        first_moment,
        second_moment,
        stats,
        home_rows,
        micros=4,
    )
    (new_bases,) = call_kernel(
        functools.partial(place_body, owners),
        [jax.ShapeDtypeStruct(bases.shape, jnp.float32)],
        [],
        "place_bases",
        base_rows,
    )
    new_vec_first = BETA_ONE * vec_first + (1.0 - BETA_ONE) * grad_vecs
    new_vec_second = BETA_TWO * vec_second + (1.0 - BETA_TWO) * grad_vecs * grad_vecs
    new_vectors = vec_master - RATE_VECTOR * (new_vec_first / (1.0 - BETA_ONE**STEP)) / (
        jnp.sqrt(new_vec_second / (1.0 - BETA_TWO**STEP)) + ADAM_EPS
    )
    return (
        outputs[None],
        input_grad[None],
        new_masters,
        new_first,
        new_second,
        new_bases,
        new_stats,
        new_vectors,
        new_vec_first,
        new_vec_second,
    )


def solution(mesh):
    placed = (
        P("opt", "seq", None),
        P("opt", "seq", None),
        P("opt", None),
        P(),
        P("opt", "seq", None),
        P("opt", "seq", None),
        P("opt", "seq", None),
        P("opt", None, "seq", None),
        P("opt", None, "seq", None),
        P(("seq", "opt")),
        P(("seq", "opt")),
        P(("seq", "opt")),
    )
    return jax.shard_map(
        per_device,
        mesh=mesh,
        in_specs=placed,
        out_specs=(
            P("opt", "seq", None),
            P("opt", "seq", None),
            P("opt", "seq", None),
            P("opt", "seq", None),
            P("opt", "seq", None),
            P("opt", None, "seq", None),
            P("opt", None, "seq", None),
            P(("seq", "opt")),
            P(("seq", "opt")),
            P(("seq", "opt")),
        ),
        check_vma=False,
    )
```

```python
import functools
import math

import jax
import jax.numpy as jnp
from jax import lax
from jax.experimental import pallas as pl
from jax.experimental.pallas import tpu as pltpu
from jax.sharding import PartitionSpec as P

HEADS = 8
FF = 2048
BLOCK = 16
LAYERS = 2
STEP = 10
MAX_LEN = 4096


HIGH = lax.Precision.HIGHEST
LN_TWO = math.log(2.0)
NEG_FILL = -1e30
NORM_EPS = 1e-05
ADAM_EPS = 1e-08
RATE_MATRIX = 0.03
RATE_VECTOR = 0.2
WEIGHT_DECAY = 0.01
BETA_ONE = 0.9
BETA_TWO = 0.95
BETA_STAT = 0.95

SUBLANES = 8
PANEL = 16
FLOPS_PER_US = 1_150_000_000
LANES = 128
UNIT_COUNT = 24
UNIT_OPT = 0
UNIT_ROW = UNIT_COUNT
UNIT_SLOT = 2 * UNIT_COUNT
DIAG = 128
VMEM_GRANT = 60 * 2**20
IN_VMEM = pl.BlockSpec(memory_space=pltpu.VMEM)
IN_SMEM = pl.BlockSpec(memory_space=pltpu.SMEM)
ANYWHERE = pl.BlockSpec(memory_space=pl.ANY)


def contract(left, right, left_dim, right_dim, precision=None):
    return lax.dot_general(
        left,
        right,
        (((left_dim,), (right_dim,)), ((), ())),
        precision=precision,
        preferred_element_type=jnp.float32,
    )


def split_two(values):
    high = values.astype(jnp.bfloat16)
    return (high, (values - high.astype(jnp.float32)).astype(jnp.bfloat16))


def wide_left(left, right_low, left_dim, right_dim):
    high, rest = split_two(left)
    return contract(high, right_low, left_dim, right_dim) + contract(
        rest, right_low, left_dim, right_dim
    )


def wide_right(left_low, right, left_dim, right_dim):
    high, rest = split_two(right)
    return contract(left_low, high, left_dim, right_dim) + contract(
        left_low, rest, left_dim, right_dim
    )


def call_kernel(
    body, out_shapes, scratch, name, *operands, smem_count=0, any_in=(), any_out=(), aliases=None,
    micros=2,
):
    def place(at, listed):
        return ANYWHERE if at in listed else IN_VMEM

    return pl.pallas_call(
        body,
        out_shape=out_shapes,
        in_specs=[
            IN_SMEM if at < smem_count else place(at, any_in) for at in range(len(operands))
        ],
        out_specs=[place(at, any_out) for at in range(len(out_shapes))],
        scratch_shapes=scratch,
        input_output_aliases=aliases or {},
        cost_estimate=pl.CostEstimate(
            flops=micros * FLOPS_PER_US, bytes_accessed=0, transcendentals=0
        ),
        compiler_params=pltpu.CompilerParams(vmem_limit_bytes=VMEM_GRANT),
        name=name,
    )(*operands)


def eliminate(panels, turn):
    rows, width = panels[0][0].shape
    row_at = lax.broadcasted_iota(jnp.int32, (SUBLANES, width), 0)

    def groups(values):
        return [values[low : low + SUBLANES] for low in range(0, rows, SUBLANES)]

    def spread_row(values, row):
        return jnp.broadcast_to(values[row : row + 1, :], values.shape)

    states = []
    for left, right in panels:
        turned = pltpu.roll(left, turn, 1)
        columns = [
            [jnp.broadcast_to(part, (SUBLANES, width)) for part in groups(turned[:, at : at + 1])]
            for at in range(rows)
        ]
        ones = [jnp.ones((SUBLANES, width), jnp.float32) for _ in range(rows // SUBLANES)]
        states.append((groups(left), groups(right), columns, ones))
    for at in range(rows):
        group_at, row = divmod(at, SUBLANES)
        for left, right, columns, pivots in states:
            pivot = spread_row(columns[at][group_at], row)
            inverse = pltpu.reciprocal(pivot, approx=False)
            pivots[group_at] = jnp.where(row_at == row, pivot, pivots[group_at])
            targets = [left, right] + columns[at + 1 :]
            given = [spread_row(target[group_at], row) for target in targets]
            for group in range(group_at, rows // SUBLANES):
                factor = columns[at][group] * inverse
                if group == group_at:
                    factor = jnp.where(row_at > row, factor, 0.0)
                for target, pivot_row in zip(targets, given):
                    target[group] = target[group] - factor * pivot_row
    results = []
    for left, right, _, pivots in states:
        scales = [lax.rsqrt(values) for values in pivots]
        results.append(
            tuple(
                jnp.concatenate([part * scale for part, scale in zip(parts, scales)], axis=0)
                for parts in (left, right)
            )
        )
    return results


def split_three(values):
    high = values.astype(jnp.bfloat16).astype(jnp.float32)
    rest = values - high
    middle = rest.astype(jnp.bfloat16).astype(jnp.float32)
    return (high, middle, rest - middle)


def thin_product(left, right):
    left_parts, right_parts = (split_three(left), split_three(right))
    pairs = ((0, 0), (0, 1), (1, 0), (1, 1), (0, 2), (2, 0))
    stacked_left = jnp.concatenate([left_parts[i] for i, _ in pairs], axis=0)
    stacked_right = jnp.concatenate([right_parts[j] for _, j in pairs], axis=0)
    return contract(stacked_left.astype(jnp.bfloat16), stacked_right.astype(jnp.bfloat16), 0, 0)


def factorize(grams, uppers, works, inverses):
    each = range(len(grams))
    size = grams[0].shape[0]
    eye = (
        lax.broadcasted_iota(jnp.int32, (DIAG, DIAG), 0)
        == lax.broadcasted_iota(jnp.int32, (DIAG, DIAG), 1)
    ).astype(jnp.float32)
    for low in range(0, size, DIAG):
        top = low + DIAG
        for m in each:
            works[m][:, 0:DIAG] = grams[m][low:top, low:top]
            works[m][:, DIAG:] = eye

        def panel(panel_at, carry):
            row = pl.multiple_of(panel_at * PANEL, PANEL)
            turn = lax.rem(DIAG - panel_at * PANEL, DIAG)
            panels = [
                (works[m][pl.ds(row, PANEL), 0:DIAG], works[m][pl.ds(row, PANEL), DIAG:])
                for m in each
            ]
            results = eliminate(panels, turn)
            updates = [
                thin_product(left, jnp.concatenate([left, right], axis=1))
                for left, right in results
            ]
            for m in each:
                inverses[m][low // DIAG, pl.ds(row, PANEL), :] = results[m][1]
            for m in each:
                works[m][...] = works[m][...] - updates[m]
            return carry

        lax.fori_loop(0, DIAG // PANEL, panel, 0)
        if top == size:
            break
        right_of = [contract(inverses[m][low // DIAG], grams[m][low:top, top:], 1, 0, HIGH) for m in each]
        for m in each:
            uppers[m][low:top, top:] = right_of[m]
        for other in range(top, size, DIAG):
            skip = other - top
            rest = [
                grams[m][other : other + DIAG, other:]
                - contract(right_of[m][:, skip : skip + DIAG], right_of[m][:, skip:], 0, 0, HIGH)
                for m in each
            ]
            for m in each:
                grams[m][other : other + DIAG, other:] = rest[m]


def renew_body(*refs):
    stat_ref, basis_ref, sent = refs[:3]
    scratch = refs[3:]
    count, size, _ = stat_ref.shape
    each = range(count)
    products, grams, uppers, works, inverses = (
        scratch[at : at + count] for at in range(0, 5 * count, count)
    )
    values = [wide_left(stat_ref[m], basis_ref[m], 1, 0) for m in each]
    for m in each:
        products[m][...] = values[m]
    for low in range(0, size, DIAG):
        values = [
            contract(products[m][:, low : low + DIAG], products[m][:, low:], 0, 0, HIGH)
            for m in each
        ]
        for m in each:
            grams[m][low : low + DIAG, low:] = values[m]
    factorize(grams, uppers, works, inverses)
    for low in range(0, size, DIAG):
        top = low + DIAG
        values = [products[m][:, low:top] for m in each]
        if low:
            values = [
                values[m]
                - contract(products[m][:, :low], uppers[m][:low, low:top], 1, 0, HIGH)
                for m in each
            ]
        values = [contract(values[m], inverses[m][low // DIAG], 1, 1, HIGH) for m in each]
        for m in each:
            products[m][:, low:top] = values[m]
    rows = sent.shape[2]
    for target in range(sent.shape[0]):
        for m in each:
            sent[target, m] = products[m][target * rows : (target + 1) * rows, :].astype(
                jnp.bfloat16
            )


def renew_bases(device_count, new_stat, basis_low):
    count, size, _ = new_stat.shape
    return call_kernel(
        renew_body,
        [jax.ShapeDtypeStruct((device_count, count, size // device_count, size), jnp.bfloat16)],
        [pltpu.VMEM((size, size), jnp.float32)] * (3 * count)
        + [pltpu.VMEM((DIAG, 2 * DIAG), jnp.float32)] * count
        + [pltpu.VMEM((size // DIAG, DIAG, DIAG), jnp.float32)] * count,
        "renew_bases",
        new_stat,
        basis_low,
        micros=40,
    )[0]


def owner_devices(own_slots, by_permutes):
    if not by_permutes:
        return list(range(own_slots))
    return [2 * (slot // 2 + slot % 2) + slot % 2 for slot in range(own_slots)]


def pack_body(slot_ref, stats, bases, first, second, *packed):
    at = 0
    for part in packed:
        for target in range(part.shape[0]):
            slot = slot_ref[at]
            part[target, 0:2] = stats[slot].astype(jnp.bfloat16)
            part[target, 2:4] = bases[slot].astype(jnp.bfloat16)
            part[target, 4] = first[slot].astype(jnp.bfloat16)
            part[target, 5] = second[slot].astype(jnp.bfloat16)
            at += 1


def rotate_body(count, turn_ref, grad_ref, *refs):
    given, (sent, stat_ref, basis_ref, whole, results) = (refs[:count], refs[count:])
    kind = 0
    for part in given:
        sources, sides, kinds, rows, _ = part.shape
        for source in range(sources):
            for side in range(sides):
                row = source * sides * rows + (side ^ turn_ref[0]) * rows
                whole[kind : kind + kinds, pl.ds(pl.multiple_of(row, rows), rows), :] = part[
                    source, side
                ].astype(jnp.float32)
        kind += kinds
    grad = grad_ref[...]
    left = whole[2].astype(jnp.bfloat16)
    right = whole[3].astype(jnp.bfloat16)
    basis_ref[0] = left
    basis_ref[1] = right
    results[0] = contract(grad, grad, 1, 1)
    results[1] = contract(grad, grad, 0, 0)
    stat_ref[0] = BETA_STAT * whole[0] + (1.0 - BETA_STAT) * results[0]
    stat_ref[1] = BETA_STAT * whole[1] + (1.0 - BETA_STAT) * results[1]
    rotated = wide_left(contract(left, grad, 0, 0), right, 1, 0)
    results[2] = rotated
    new_first = BETA_ONE * whole[4] + (1.0 - BETA_ONE) * rotated
    new_second = BETA_TWO * whole[5] + (1.0 - BETA_TWO) * rotated * rotated
    direction = (
        new_first
        / (1.0 - BETA_ONE**STEP)
        / (jnp.sqrt(new_second / (1.0 - BETA_TWO**STEP)) + ADAM_EPS)
    )
    results[3] = wide_right(left, wide_left(direction, right, 1, 1), 1, 0)
    for target in range(sent.shape[0]):
        sent[target] = results[:, target * rows : (target + 1) * rows, :].astype(jnp.bfloat16)


def rotate_slot(turn, grad, owner_rows):
    size = grad.shape[0]
    return call_kernel(
        functools.partial(rotate_body, len(owner_rows)),
        [
            jax.ShapeDtypeStruct(
                (size // owner_rows[0].shape[3], 4) + owner_rows[0].shape[3:], jnp.bfloat16
            ),
            jax.ShapeDtypeStruct((2, size, size), jnp.float32),
            jax.ShapeDtypeStruct((2, size, size), jnp.bfloat16),
        ],
        [
            pltpu.VMEM((6, size, size), jnp.float32),
            pltpu.VMEM((4, size, size), jnp.float32),
        ],
        "rotate_slot",
        turn,
        grad,
        *owner_rows,
        smem_count=1,
        micros=6,
    )


def finish_body(
    owners, masters, first, second, stats, given, new_masters, new_first, new_second, new_stats
):
    for slot, owner in enumerate(owners):
        rotated = given[owner, 2].astype(jnp.float32)
        update = given[owner, 3].astype(jnp.float32)
        new_first[slot] = BETA_ONE * first[slot] + (1.0 - BETA_ONE) * rotated
        new_second[slot] = BETA_TWO * second[slot] + (1.0 - BETA_TWO) * rotated * rotated
        new_masters[slot] = masters[slot] - RATE_MATRIX * (update + WEIGHT_DECAY * masters[slot])
        new_stats[slot] = BETA_STAT * stats[slot] + (1.0 - BETA_STAT) * given[owner, 0:2].astype(
            jnp.float32
        )


def place_body(owners, given, new_bases):
    for slot, owner in enumerate(owners):
        new_bases[slot] = given[owner].astype(jnp.float32)


def add_low(left, right):
    return (left.astype(jnp.float32) + right.astype(jnp.float32)).astype(jnp.bfloat16)


def sum_to_owner(kept_upper, kept_lower, sent_upper, sent_lower, seq_index, vec_sum):
    def beside(values, vec_sum, *exchanges):
        for axis, bit_at in exchanges:
            vec_sum = vec_sum + partner(vec_sum, axis, bit_at)
        return lax.optimization_barrier((values, vec_sum))

    _, rows, width = kept_upper.shape
    z_count = kept_upper.shape[0] // 4
    shape = (2, 2, z_count, rows, width)
    upper, came_upper = (kept_upper.reshape(shape), partner(sent_upper, "opt", 0).reshape(shape))
    lower, came_lower = (kept_lower.reshape(shape), partner(sent_lower, "opt", 0).reshape(shape))
    send_x = add_low(upper[1], came_upper[1])
    send_x, upper, came_upper = lax.optimization_barrier((send_x, upper, came_upper))
    by_x = partner(send_x, "opt", 1)
    send_y = add_low(lower[:, 1], came_lower[:, 1])
    send_y, lower, came_lower = lax.optimization_barrier((send_y, lower, came_lower))
    by_y = partner(send_y, "seq", 0)
    by_x, vec_sum = beside(by_x, vec_sum, ("opt", 0))
    stay_x = add_low(upper[0], came_upper[0])
    stay_y = add_low(lower[:, 0], came_lower[:, 0])
    then_y = partner(add_low(stay_x[1], by_x[1]), "seq", 0)
    then_x = partner(add_low(stay_y[1], by_y[1]), "opt", 1)
    then_y, vec_sum = beside(then_y, vec_sum, ("seq", 1))
    z_index = seq_index >> 1

    def both(apart):
        at = jnp.clip((z_index ^ apart) - (seq_index & 1), 0, z_count - 1)

        def pick(values):
            return lax.dynamic_index_in_dim(values, at, 0, keepdims=False)

        total_upper = (
            pick(stay_x[0]).astype(jnp.float32)
            + pick(by_x[0]).astype(jnp.float32)
            + pick(then_y).astype(jnp.float32)
        )
        total_lower = (
            pick(stay_y[0]).astype(jnp.float32)
            + pick(by_y[0]).astype(jnp.float32)
            + pick(then_x).astype(jnp.float32)
        )
        return jnp.concatenate([total_upper, total_lower]).astype(jnp.bfloat16)

    near_one = partner(both(1), "seq", 1)
    near_far = partner(both(3), "seq", 1)
    near_far, vec_sum = beside(near_far, vec_sum, ("seq", 2))
    last = partner(add_low(both(2), near_far), "seq", 2)
    last, vec_sum = beside(last, vec_sum, ("opt", 1), ("seq", 0))
    total = both(0).astype(jnp.float32) + near_one.astype(jnp.float32) + last.astype(jnp.float32)
    return (total.astype(jnp.bfloat16), vec_sum)


def partner(value, axis, apart):
    return lax.ppermute(value, axis, [(i, i ^ 1 << apart) for i in range(lax.axis_size(axis))])


def pair_mean(values):
    shaped = values.reshape((values.shape[0] // 2, 2) + values.shape[1:])
    return 0.5 * (shaped[:, 0] + shaped[:, 1])


def pair_spread(grads):
    return 0.5 * jnp.repeat(grads, 2, axis=0)


def sum_rows(values):
    return jnp.sum(values, axis=0, keepdims=True)


def norm_parts(values):
    centred = values - jnp.mean(values, axis=-1, keepdims=True)
    recip = lax.rsqrt(jnp.mean(centred * centred, axis=-1, keepdims=True) + NORM_EPS)
    return (centred * recip, recip)


def norm_back(grad, gain, normed, recip):
    scaled = grad * gain
    return recip * (
        scaled
        - jnp.mean(scaled, axis=-1, keepdims=True)
        - normed * jnp.mean(scaled * normed, axis=-1, keepdims=True)
    )


def half_matrix(shape, fine_dim):
    fine = lax.broadcasted_iota(jnp.int32, shape, fine_dim)
    coarse = lax.broadcasted_iota(jnp.int32, shape, 1 - fine_dim)
    return jnp.where(fine >> 1 == coarse, 0.5, 0.0).astype(jnp.bfloat16)


def pool(rows_low):
    count = rows_low.shape[0]
    return contract(half_matrix((count // 2, count), 1), rows_low, 1, 0).astype(jnp.bfloat16)


def spread(grads):
    count = grads.shape[0]
    return wide_right(half_matrix((2 * count, count), 0), grads, 1, 0)


def norm_cdf(values):
    return 0.5 * (1.0 + lax.erf(values * math.sqrt(0.5)))


def local_count(tok_count):
    return (tok_count // BLOCK).bit_length() - 1


def key_width(tok_count, tree_bits):
    rows = 2 * (tok_count - BLOCK) + BLOCK * tree_bits
    return -(-rows // LANES) * LANES


def score_offsets(tok_count, tree_bits, span_bits):
    token = jnp.arange(tok_count, dtype=jnp.int32)[:, None]
    parts = []
    for height in range(local_count(tok_count)):
        row = jnp.arange(tok_count >> height, dtype=jnp.int32)[None, :]
        apart = token // (BLOCK << height) ^ row // BLOCK
        counted = apart <= 1 if height == 0 else apart == 1
        parts.append(jnp.where(counted, height * LN_TWO, NEG_FILL))
    for bit_at in range(tree_bits):
        offset = (local_count(tok_count) + bit_at) * LN_TWO
        parts.append(
            jnp.broadcast_to(
                jnp.where(bit_at + 1 <= span_bits, offset, NEG_FILL), (tok_count, BLOCK)
            )
        )
    used = sum(part.shape[1] for part in parts)
    rest = key_width(tok_count, tree_bits) - used
    parts.append(jnp.full((tok_count, rest), NEG_FILL, jnp.float32))
    return jnp.concatenate(parts, axis=1).astype(jnp.float32)


def stack_keys(own_rows, far_rows):
    parts = [own_rows]
    for _ in range(local_count(own_rows.shape[0]) - 1):
        parts.append(pool(parts[-1]))
    parts = parts + far_rows
    rest = key_width(own_rows.shape[0], len(far_rows)) - sum(part.shape[0] for part in parts)
    if rest:
        parts.append(jnp.zeros((rest, own_rows.shape[1]), jnp.bfloat16))
    return jnp.concatenate(parts, axis=0)


def by_heads(pair):
    lane = lax.broadcasted_iota(jnp.int32, pair.shape, 1)
    zero = jnp.zeros_like(pair)
    first = lane < LANES // 2
    return jnp.concatenate([jnp.where(first, pair, zero), jnp.where(first, zero, pair)], axis=0)


def from_heads(both):
    count = both.shape[0] // 2
    lane = lax.broadcasted_iota(jnp.int32, (count, LANES), 1)
    return jnp.where(lane < LANES // 2, both[:count], both[count:])


def attend(qkv, far_rows, offsets, probs, mixed):
    width = qkv.shape[1] // 3
    score_scale = (width // HEADS) ** (-0.5)
    stack = stack_keys(qkv[:, width:], far_rows)
    both_offsets = jnp.concatenate([offsets, offsets], axis=0)
    for pair_at in range(width // LANES):
        low, top = (pair_at * LANES, (pair_at + 1) * LANES)
        scores = (
            contract(by_heads(qkv[:, low:top]), stack[:, low:top], 1, 1) * score_scale
            + both_offsets
        )
        expo = jnp.exp(scores - jnp.max(scores, axis=1, keepdims=True))
        weights = expo / jnp.sum(expo, axis=1, keepdims=True)
        probs[pair_at] = weights
        result = contract(
            weights.astype(jnp.bfloat16), stack[:, width + low : width + top], 1, 0
        )
        mixed[:, low:top] = from_heads(result).astype(jnp.bfloat16)


def attend_back(qkv, far_rows, probs, mixed_grad, query_grad, key_grads, far_grads):
    tok_count, width = mixed_grad.shape
    score_scale = (width // HEADS) ** (-0.5)
    stack = stack_keys(qkv[:, width:], far_rows)
    local_levels = local_count(tok_count)
    far_start = 2 * (tok_count - BLOCK)
    for pair_at in range(width // LANES):
        low, top = (pair_at * LANES, (pair_at + 1) * LANES)
        queries = by_heads(qkv[:, low:top])
        grads = by_heads(mixed_grad[:, low:top])
        weights = probs[pair_at]
        prob_grad = contract(grads, stack[:, width + low : width + top], 1, 1)
        inner = jnp.sum(weights * prob_grad, axis=1, keepdims=True)
        score_grad = (weights * (prob_grad - inner)).astype(jnp.bfloat16)
        query_grad[:, low:top] = (
            from_heads(contract(score_grad, stack[:, low:top], 1, 0)) * score_scale
        ).astype(jnp.bfloat16)
        for start, part in (
            (low, contract(score_grad, queries, 0, 0) * score_scale),
            (width + low, contract(weights.astype(jnp.bfloat16), grads, 0, 0)),
        ):
            for far_at, far_grad in enumerate(far_grads):
                row = far_start + BLOCK * far_at
                far_grad[:, start : start + LANES] = part[row : row + BLOCK]
            folded = None
            for height in reversed(range(local_levels)):
                row = 2 * (tok_count - (tok_count >> height))
                own = part[row : row + (tok_count >> height)]
                folded = own if folded is None else own + spread(folded)
            key_grads[:, start : start + LANES] = folded


class Units:
    def __init__(self, meta, packed, store, sems, units):
        self.store = store
        self.place = {unit: at for at, unit in enumerate(units)}
        self.waiting = {}
        rows = store.shape[2]
        for at, unit in enumerate(units):
            row = pl.multiple_of(meta[UNIT_ROW + unit], rows)
            copy = pltpu.make_async_copy(
                packed.at[:, meta[UNIT_OPT + unit], pl.ds(row, rows), :],
                store.at[at],
                sems.at[at],
            )
            copy.start()
            self.waiting[unit] = copy

    def __getitem__(self, unit):
        if unit in self.waiting:
            self.waiting.pop(unit).wait()
        width = self.store.shape[3]
        return self.store[self.place[unit]].reshape(width, width)


class Grads:
    def __init__(self, meta, *refs):
        self.meta, self.buffers, self.store, self.sems = (meta, refs[:4], refs[4], refs[5])
        self.copies = []

    def put(self, first_unit, left_low, right_low):
        product = contract(left_low, right_low, 0, 0).astype(jnp.bfloat16)
        width = self.store.shape[2]
        slots, rows, _ = self.buffers[0].shape
        for low in range(0, product.shape[0], width):
            for side in range(0, product.shape[1], width):
                at = len(self.copies) // 2
                self.store[at] = product[low : low + width, side : side + width]
                place = self.meta[UNIT_SLOT + first_unit + low // width + side // width]
                inner = jnp.where(place < slots, place, place - slots)
                for half in range(2):
                    keeping, sending = (
                        pltpu.make_async_copy(
                            self.store.at[at, pl.ds(half * rows, rows)],
                            target.at[inner],
                            self.sems.at[at, half],
                        )
                        for target in (self.buffers[half], self.buffers[2 + half])
                    )
                    pl.when(place < slots)(keeping.start)
                    pl.when(place >= slots)(sending.start)
                    self.copies.append(keeping)

    def finish(self):
        for copy in self.copies:
            copy.wait()


def project(hidden, units, first_unit, gain, bias, normed_ref, qkv_ref, near_ref):
    width = hidden.shape[1]
    normed, _ = norm_parts(hidden)
    normed_low = (normed * gain + bias).astype(jnp.bfloat16)
    normed_ref[...] = normed_low
    for part in range(3):
        qkv_ref[:, part * width : (part + 1) * width] = contract(
            normed_low, units[first_unit + part], 1, 0
        ).astype(jnp.bfloat16)
    near = qkv_ref[:, width:]
    for _ in range(local_count(near.shape[0])):
        near = pool(near)
    near_ref[...] = near


def feed_forward(middle, units, first_unit, vec, vec_at, normed_ref, pre_ref, act_ref):
    width = middle.shape[1]
    normed, _ = norm_parts(middle)
    normed_low = (normed * vec[vec_at + 2 : vec_at + 3] + vec[vec_at + 3 : vec_at + 4]).astype(
        jnp.bfloat16
    )
    normed_ref[...] = normed_low
    total = middle
    ff_blocks = FF // width
    for part in range(ff_blocks):
        low, top = (part * width, (part + 1) * width)
        row = vec_at + 4 + part
        pre = contract(normed_low, units[first_unit + 4 + part], 1, 0) + vec[row : row + 1]
        act = (pre * norm_cdf(pre)).astype(jnp.bfloat16)
        pre_ref[:, low:top] = pre
        act_ref[:, low:top] = act
        total = total + contract(act, units[first_unit + 4 + ff_blocks + part], 1, 0)
    row = vec_at + 4 + ff_blocks
    return total + vec[row : row + 1]


def feed_back(
    grad, middle, pre_ref, units, first_unit, vec, vec_at, vec_grads, at, pre_grad_ref
):
    width = middle.shape[1]
    ff_blocks = FF // width
    down_grad = grad.astype(jnp.bfloat16)
    normed_grad = jnp.zeros(middle.shape, jnp.float32)
    for part in range(ff_blocks):
        low, top = (part * width, (part + 1) * width)
        pre = pre_ref[:, low:top]
        slope = norm_cdf(pre) + pre * jnp.exp(-0.5 * pre * pre) * (1.0 / math.sqrt(2.0 * math.pi))
        pre_grad = (
            contract(down_grad, units[first_unit + 4 + ff_blocks + part], 1, 1) * slope
        ).astype(jnp.bfloat16)
        pre_grad_ref[:, low:top] = pre_grad
        vec_grads[at + 2 + part : at + 3 + part] = sum_rows(pre_grad.astype(jnp.float32))
        normed_grad = normed_grad + contract(pre_grad, units[first_unit + 4 + part], 1, 1)
    row = at + 2 + ff_blocks
    vec_grads[row : row + 1] = sum_rows(grad)
    normed, recip = norm_parts(middle)
    vec_grads[at : at + 1] = sum_rows(normed_grad * normed)
    vec_grads[at + 1 : at + 2] = sum_rows(normed_grad)
    return grad + norm_back(normed_grad, vec[vec_at + 2 : vec_at + 3], normed, recip)


def with_near(key_grads, near):
    for _ in range(local_count(key_grads.shape[0])):
        near = spread(near)
    return (key_grads + near).astype(jnp.bfloat16)


def project_back(
    middle_grad, hidden, query_grad, rows_low, units, first_unit, vec, vec_at, vec_grads
):
    width = hidden.shape[1]
    normed_grad = contract(query_grad, units[first_unit], 1, 1)
    for part in range(2):
        normed_grad = normed_grad + contract(
            rows_low[:, part * width : (part + 1) * width], units[first_unit + 1 + part], 1, 1
        )
    normed, recip = norm_parts(hidden)
    vec_grads[0:1] = sum_rows(normed_grad * normed)
    vec_grads[1:2] = sum_rows(normed_grad)
    return middle_grad + norm_back(normed_grad, vec[vec_at : vec_at + 1], normed, recip)


def first_body(per_layer, meta, vec, inputs, packed, normed, qkv, near, store, sems):
    units = Units(meta, packed, store, sems, range(3))
    project(inputs[...].astype(jnp.float32), units, 0, vec[0:1], vec[1:2], normed, qkv, near)


def middle_body(per_layer, vec_rows, tree_bits, meta, vec, offsets, inputs, qkv, *refs):
    far, refs = (refs[:tree_bits], refs[tree_bits:])
    packed, probs_out, mixed, middle, normed_two, pre_out, act = refs[:7]
    hidden, normed, next_qkv, near, store, sems, probs, pre, out_sems = refs[7:]
    units = Units(meta, packed, store, sems, range(3, per_layer + 3))
    attend(qkv[...], [ref[...] for ref in far], offsets[...], probs, mixed)
    probs_copy = pltpu.make_async_copy(probs, probs_out, out_sems.at[0])
    probs_copy.start()
    middle[...] = inputs[...].astype(jnp.float32) + contract(mixed[...], units[3], 1, 0)
    hidden[...] = feed_forward(middle[...], units, 0, vec, 0, normed_two, pre, act)
    pre_copy = pltpu.make_async_copy(pre, pre_out, out_sems.at[1])
    pre_copy.start()
    project(
        hidden[...], units, per_layer, vec[vec_rows : vec_rows + 1],
        vec[vec_rows + 1 : vec_rows + 2], normed, next_qkv, near,
    )
    probs_copy.wait()
    pre_copy.wait()


def turn_body(per_layer, vec_rows, tree_bits, meta, vec, offsets, cotangent, hidden, qkv, *refs):
    far, refs = (refs[:tree_bits], refs[tree_bits:])
    packed, outputs, mixed, normed_two, act = refs[:5]
    middle_grad, query_grad, key_grads, vec_grads, pre_grad, branch_low = refs[5:11]
    far_grads, refs = (refs[11 : 11 + tree_bits], refs[11 + tree_bits :])
    store, sems, probs, pre = refs
    units = Units(meta, packed, store, sems, range(per_layer + 3, 2 * per_layer))
    far_rows = [ref[...] for ref in far]
    attend(qkv[...], far_rows, offsets[...], probs, mixed)
    middle = hidden[...] + contract(mixed[...], units[per_layer + 3], 1, 0)
    outputs[...] = feed_forward(
        middle, units, per_layer, vec, vec_rows, normed_two, pre, act
    ).astype(jnp.bfloat16)
    vec_grads[...] = jnp.zeros_like(vec_grads)
    grad = feed_back(
        cotangent[...].astype(jnp.float32), middle, pre, units, per_layer, vec, vec_rows,
        vec_grads, 2, pre_grad,
    )
    middle_grad[...] = grad
    branch_grad = grad.astype(jnp.bfloat16)
    branch_low[...] = branch_grad
    mixed_grad = contract(branch_grad, units[per_layer + 3], 1, 1).astype(jnp.bfloat16)
    attend_back(qkv[...], far_rows, probs, mixed_grad, query_grad, key_grads, far_grads)


def lower_body(per_layer, vec_rows, tree_bits, meta, vec, *refs):
    hidden, query_in, key_in, near_in, middle_in, middle, qkv = refs[:7]
    far, refs = (refs[7 : 7 + tree_bits], refs[7 + tree_bits :])
    probs_in, pre_in, packed, down_low, rows_low = refs[:5]
    middle_grad, query_grad, key_grads, vec_grads, pre_grad, branch_low = refs[5:11]
    far_grads, refs = (refs[11 : 11 + tree_bits], refs[11 + tree_bits :])
    store, sems, probs, pre, in_sems = refs
    split = 4 + (per_layer - 4) // 2
    units = Units(
        meta, packed, store, sems,
        list(range(per_layer, per_layer + 3)) + list(range(split, per_layer))
        + list(range(3, split)),
    )
    pre_copy = pltpu.make_async_copy(pre_in, pre, in_sems.at[0])
    probs_copy = pltpu.make_async_copy(probs_in, probs, in_sems.at[1])
    pre_copy.start()
    probs_copy.start()
    vec_grads[...] = jnp.zeros_like(vec_grads)
    rows_low[...] = with_near(key_in[...], near_in[...])
    grad = project_back(
        middle_in[...], hidden[...], query_in[...], rows_low[...], units, per_layer, vec,
        vec_rows, vec_grads,
    )
    down_low[...] = grad.astype(jnp.bfloat16)
    pre_copy.wait()
    grad = feed_back(grad, middle[...], pre, units, 0, vec, 0, vec_grads, 2, pre_grad)
    middle_grad[...] = grad
    branch_grad = grad.astype(jnp.bfloat16)
    branch_low[...] = branch_grad
    mixed_grad = contract(branch_grad, units[3], 1, 1).astype(jnp.bfloat16)
    probs_copy.wait()
    attend_back(
        qkv[...], [ref[...] for ref in far], probs, mixed_grad, query_grad, key_grads, far_grads
    )


def last_body(meta, vec, inputs, query_grad, rows_low, middle_in, packed, *refs):
    input_grad, vec_grads, store, sems = refs
    units = Units(meta, packed, store, sems, range(3))
    vec_grads[...] = jnp.zeros_like(vec_grads)
    input_grad[...] = project_back(
        middle_in[...], inputs[...].astype(jnp.float32), query_grad[...], rows_low[...], units, 0,
        vec, 0, vec_grads,
    )


def grads_body(pairs, array_count, held, meta, *refs):
    arrays, refs = (refs[:array_count], refs[array_count + held :])
    grads = Grads(meta, *refs)
    for first_unit, left, right in pairs:
        grads.put(first_unit, arrays[left][...], arrays[right][...])
    grads.finish()


def last_grads_body(meta, normed, query_grad, key_grads, near_grads, *refs):
    rows_low, *refs = refs[4:]
    grads = Grads(meta, *refs)
    grads.put(0, normed[...], query_grad[...])
    rows_low[...] = with_near(key_grads[...], near_grads[...])
    grads.put(1, normed[...], rows_low[...])
    grads.finish()


def coarse_up(own, seq_index, tree_bits):
    far_list = []
    for bit_at in range(tree_bits):
        far = partner(own, "seq", bit_at)
        far_list.append(far)
        if bit_at + 1 < tree_bits:
            upper = seq_index >> bit_at & 1 == 1
            joined = jnp.where(
                upper, jnp.concatenate([far, own]), jnp.concatenate([own, far])
            ).astype(jnp.float32)
            own = pair_mean(joined).astype(jnp.bfloat16)
    return far_list


def coarse_down(far_grads, seq_index):
    above = None
    for bit_at in reversed(range(len(far_grads))):
        upper = seq_index >> bit_at & 1 == 1
        sent = far_grads[bit_at]
        own = 0.0
        if above is not None:
            wide = pair_spread(above)
            own = jnp.where(upper, wide[BLOCK:], wide[:BLOCK])
            sent = sent + jnp.where(upper, wide[:BLOCK], wide[BLOCK:])
        above = own + partner(sent.astype(jnp.bfloat16), "seq", bit_at).astype(jnp.float32)
    return above


def per_device(
    inputs,
    cotangent,
    seq_lengths,
    unit_slot,
    masters,
    first_moment,
    second_moment,
    bases,
    stats,
    vec_master,
    vec_first,
    vec_second,
):
    seq_count = lax.axis_size("seq")
    opt_count = lax.axis_size("opt")
    seq_index = lax.axis_index("seq")
    tok_count = inputs.shape[1]
    model_width = inputs.shape[2]
    own_slots = masters.shape[0]
    row_count = masters.shape[1]
    ff_blocks = FF // model_width
    per_layer = 4 + 2 * ff_blocks
    vec_width = 5 * model_width + FF
    long_devs = min(max(MAX_LEN // tok_count, 1), seq_count)
    tree_bits = long_devs.bit_length() - 1
    size = seq_count * row_count
    by_permutes = seq_count == 8 and opt_count == 4 and own_slots == 6
    owners = owner_devices(own_slots, by_permutes)
    def pack_slots(slots, counts):
        return call_kernel(
            pack_body,
            [
                jax.ShapeDtypeStruct((count, 6, row_count, model_width), jnp.bfloat16)
                for count in counts
            ],
            [],
            "pack_slots",
            slots,
            stats,
            bases,
            first_moment,
            second_moment,
            smem_count=1,
            micros=3,
        )

    if by_permutes:
        parity = seq_index & 1
        half_slots = own_slots // 2
        pairs = 2 * jnp.arange(half_slots, dtype=jnp.int32)
        near, away = pack_slots(
            jnp.concatenate([pairs + parity, pairs + 1 - parity]), (half_slots, half_slots)
        )
        met = jnp.stack([near, partner(away, "seq", 0)], axis=1)
        to_owner = jnp.where(
            parity == 0,
            jnp.concatenate([met, met[-1:]]),
            jnp.concatenate([met[:1], met]),
        )
        turn = parity.reshape(1)
    else:
        (to_owner,) = pack_slots(
            jnp.asarray(
                [owners.index(at) if at in owners else 0 for at in range(seq_count)], jnp.int32
            ),
            (seq_count,),
        )
        to_owner = to_owner[:, None]
        turn = jnp.zeros((1,), jnp.int32)
    vec_count = vec_master.shape[0]
    own_rows = own_slots * row_count
    vec_low = vec_master.astype(jnp.bfloat16)
    for axis in ("opt", "seq"):
        for bit_at in range(lax.axis_size(axis).bit_length() - 1):
            other = partner(vec_low, axis, bit_at)
            vec_low = jnp.where(
                lax.axis_index(axis) >> bit_at & 1 == 1,
                jnp.concatenate([other, vec_low]),
                jnp.concatenate([vec_low, other]),
            )
    vec = vec_low.reshape(-1, model_width).astype(jnp.float32)
    gathered = lax.all_gather(
        masters.astype(jnp.bfloat16).reshape(1, own_rows, model_width),
        ("seq", "opt"),
        axis=0,
        tiled=True,
    )
    if row_count % 16 == 0:
        unit_rows = row_count
        packed = gathered.reshape(seq_count, opt_count, own_rows, model_width)
    else:
        unit_rows = size
        packed = (
            gathered.reshape(seq_count, opt_count, own_slots, row_count, model_width)
            .transpose(1, 2, 0, 3, 4)
            .reshape(1, opt_count, own_slots * size, model_width)
        )
    opt_index = lax.axis_index("opt")
    opt_at, slot_in = (unit_slot // own_slots, unit_slot % own_slots)
    if by_permutes:
        apart = opt_at ^ opt_index
        other = (apart & 1) * 4 + (apart >> 1) * 2 + ((slot_in ^ seq_index) & 1)
        place = other * (own_slots // 2) + (slot_in >> 1)
    else:
        place = unit_slot
    meta = jnp.concatenate([opt_at, slot_in * unit_rows, place]).astype(jnp.int32)
    span_bits = jnp.zeros((), jnp.int32)
    for bit_at in range(tree_bits + 1):
        start_dev = seq_index >> bit_at << bit_at
        span_bits = jnp.where(
            seq_lengths[0, start_dev] == tok_count * (1 << bit_at), bit_at, span_bits
        )
    offsets_in = score_offsets(tok_count, tree_bits, span_bits)
    width_in = offsets_in.shape[1]
    pair_count = model_width // LANES
    vec_rows = vec_width // model_width
    square = (model_width, model_width)

    def units_in(count):
        return [
            pltpu.VMEM((count, size // unit_rows, unit_rows, model_width), jnp.bfloat16),
            pltpu.SemaphoreType.DMA((count,)),
        ]

    def grads_out(count):
        return [pltpu.VMEM((count,) + square, jnp.bfloat16), pltpu.SemaphoreType.DMA((count, 2))]

    def low_of(*shape):
        return jax.ShapeDtypeStruct(shape, jnp.bfloat16)

    def full_of(*shape):
        return jax.ShapeDtypeStruct(shape, jnp.float32)

    projected = [
        low_of(tok_count, model_width),
        low_of(tok_count, 3 * model_width),
        low_of(BLOCK, 2 * model_width),
    ]
    attended = [
        full_of(pair_count, 2 * tok_count, width_in),
        low_of(tok_count, model_width),
    ]
    fed = [
        low_of(tok_count, model_width),
        full_of(tok_count, FF),
        low_of(tok_count, FF),
    ]
    back = [
        full_of(tok_count, model_width),
        low_of(tok_count, model_width),
        full_of(tok_count, 2 * model_width),
        full_of(16, model_width),
        low_of(tok_count, FF),
        low_of(tok_count, model_width),
    ] + [full_of(BLOCK, 2 * model_width)] * tree_bits
    buffers = [low_of(UNIT_COUNT // 2, size // 2, model_width)] * 4
    ff_blocks = FF // model_width

    def in_vmem(shapes):
        return [pltpu.VMEM(shape.shape, shape.dtype) for shape in shapes]

    def unit_grads(name, held, pairs):
        arrays = []
        for _, *factors in pairs:
            arrays += [factor for factor in factors if not any(factor is one for one in arrays)]
        index = {id(array): at for at, array in enumerate(arrays)}
        count = sum(left.shape[1] * right.shape[1] for _, left, right in pairs) // model_width**2
        first = 1 + len(arrays)
        return call_kernel(
            functools.partial(
                grads_body,
                [(unit, index[id(left)], index[id(right)]) for unit, left, right in pairs],
                len(arrays),
                len(held),
            ),
            buffers,
            grads_out(count),
            name,
            meta,
            *arrays,
            *held,
            smem_count=1,
            micros=2,
            any_in=range(first, first + len(held)),
            any_out=range(4),
            aliases={first + at: at for at in range(len(held))},
        )

    packed, to_owner, offsets_in, vec, meta = lax.optimization_barrier(
        (packed, to_owner, offsets_in, vec, meta)
    )
    normed_zero, qkv_zero, near_zero = call_kernel(
        functools.partial(first_body, per_layer),
        projected,
        units_in(3),
        "project_first",
        meta,
        vec,
        inputs[0],
        packed,
        smem_count=1,
        micros=3,
        any_in=(3,),
    )
    far_zero = coarse_up(near_zero, seq_index, tree_bits)
    (
        probs, mixed, middle, normed_two, pre, act, hidden, normed_one, qkv_one, near_one,
    ) = call_kernel(
        functools.partial(middle_body, per_layer, vec_rows, tree_bits),
        attended + [full_of(tok_count, model_width)] + fed + [full_of(tok_count, model_width)]
        + projected,
        units_in(per_layer) + in_vmem([attended[0], fed[1]]) + [pltpu.SemaphoreType.DMA((2,))],
        "layer_first",
        meta,
        vec,
        offsets_in,
        inputs[0],
        qkv_zero,
        *far_zero,
        packed,
        smem_count=1,
        micros=7,
        any_in=(5 + tree_bits,),
        any_out=(0, 4),
    )
    far_one = coarse_up(near_one, seq_index, tree_bits)
    (
        outputs, mixed_one, normed_up, act_one, middle_grad, query_grad, key_grads, vec_grads_up,
        pre_grad, branch_low, *far_grads,
    ) = call_kernel(
        functools.partial(turn_body, per_layer, vec_rows, tree_bits),
        [low_of(tok_count, model_width), attended[1], fed[0], fed[2]] + back,
        units_in(per_layer - 3) + in_vmem([attended[0], fed[1]]),
        "layer_turn",
        meta,
        vec,
        offsets_in,
        cotangent[0],
        hidden,
        qkv_one,
        *far_one,
        packed,
        smem_count=1,
        micros=13,
        any_in=(6 + tree_bits,),
    )
    near_grads = coarse_down(far_grads, seq_index)
    held = unit_grads("down_grads", (), [(per_layer + 4 + ff_blocks, act_one, cotangent[0])])
    held = unit_grads(
        "up_grads",
        held,
        [(per_layer + 4, normed_up, pre_grad), (per_layer + 3, mixed_one, branch_low)],
    )
    (
        down_low, rows_low, middle_grad, query_zero, key_grads, vec_grads_mid, pre_grad,
        branch_low, *far_grads,
    ) = call_kernel(
        functools.partial(lower_body, per_layer, vec_rows, tree_bits),
        [low_of(tok_count, model_width), low_of(tok_count, 2 * model_width)] + back,
        units_in(per_layer) + in_vmem([attended[0], fed[1]]) + [pltpu.SemaphoreType.DMA((2,))],
        "layer_back",
        meta,
        vec,
        hidden,
        query_grad,
        key_grads,
        near_grads,
        middle_grad,
        middle,
        qkv_zero,
        *far_zero,
        probs,
        pre,
        packed,
        smem_count=1,
        micros=13,
        any_in=range(9 + tree_bits, 12 + tree_bits),
    )
    near_grads = coarse_down(far_grads, seq_index)
    held = unit_grads("down_grads_low", held, [(4 + ff_blocks, act, down_low)])
    held = unit_grads(
        "up_grads_low", held, [(4, normed_two, pre_grad), (3, mixed, branch_low)]
    )
    held = unit_grads(
        "project_grads",
        held,
        [(per_layer, normed_one, query_grad), (per_layer + 1, normed_one, rows_low)],
    )
    rows_zero, *held = call_kernel(
        last_grads_body,
        [low_of(tok_count, 2 * model_width)] + buffers,
        grads_out(3),
        "project_grads_low",
        meta,
        normed_zero,
        query_zero,
        key_grads,
        near_grads,
        *held,
        smem_count=1,
        micros=3,
        any_in=range(5, 9),
        any_out=range(1, 5),
        aliases={5 + at: 1 + at for at in range(4)},
    )
    input_grad, vec_grads_low = call_kernel(
        last_body,
        [full_of(tok_count, model_width), full_of(16, model_width)],
        units_in(3),
        "project_back",
        meta,
        vec,
        inputs[0],
        query_zero,
        rows_zero,
        middle_grad,
        packed,
        smem_count=1,
        micros=4,
        any_in=(6,),
    )
    vec_sum = jnp.concatenate(
        [vec_grads_low[0:2], vec_grads_mid[2:vec_rows], vec_grads_mid[0:2], vec_grads_up[2:vec_rows]]
    )
    def over_z(rows):
        groups = [list(range(at, seq_count, 2)) for at in range(2)]
        return lax.all_to_all(rows, "seq", 0, 0, tiled=True, axis_index_groups=groups)

    if by_permutes:
        held[2], to_owner = lax.optimization_barrier((held[2], to_owner))
        owner_rows = (over_z(to_owner),)
        owner_grad, vec_sum = sum_to_owner(*held, seq_index, vec_sum)
    else:
        owner_rows = (lax.all_to_all(to_owner, "seq", 0, 0, tiled=True),)
        for axis in ("opt", "seq"):
            for bit_at in range(lax.axis_size(axis).bit_length() - 1):
                vec_sum = vec_sum + partner(vec_sum, axis, bit_at)
        column_grads = lax.psum_scatter(
            jnp.concatenate(
                [jnp.concatenate(held[at : at + 2], axis=1) for at in (0, 2)]
            ),
            "opt",
            scatter_dimension=0,
            tiled=True,
        )
        column_grads = jnp.pad(column_grads, [(0, seq_count - own_slots), (0, 0), (0, 0)])
        owner_grad = lax.psum_scatter(column_grads, "seq", scatter_dimension=0, tiled=True)[0]
    step_rows, owner_stat, owner_basis = rotate_slot(turn, owner_grad, owner_rows)
    home_rows = lax.all_to_all(step_rows, "seq", 0, 0, tiled=True)
    base_rows = renew_bases(seq_count, owner_stat, owner_basis)
    base_rows, home_rows = lax.optimization_barrier((base_rows, home_rows))
    base_rows = lax.all_to_all(base_rows, "seq", 0, 0, tiled=True)
    whole_shape = jax.ShapeDtypeStruct(masters.shape, jnp.float32)
    new_masters, new_first, new_second, new_stats = call_kernel(
        functools.partial(finish_body, owners),
        [whole_shape, whole_shape, whole_shape, jax.ShapeDtypeStruct(stats.shape, jnp.float32)],
        [],
        "finish_slots",
        masters,
        first_moment,
        second_moment,
        stats,
        home_rows,
        micros=4,
    )
    (new_bases,) = call_kernel(
        functools.partial(place_body, owners),
        [jax.ShapeDtypeStruct(bases.shape, jnp.float32)],
        [],
        "place_bases",
        base_rows,
    )
    grad_vecs = lax.dynamic_slice_in_dim(
        vec_sum.reshape(-1), (seq_index * opt_count + lax.axis_index("opt")) * vec_count, vec_count
    )
    new_vec_first = BETA_ONE * vec_first + (1.0 - BETA_ONE) * grad_vecs
    new_vec_second = BETA_TWO * vec_second + (1.0 - BETA_TWO) * grad_vecs * grad_vecs
    new_vectors = vec_master - RATE_VECTOR * (new_vec_first / (1.0 - BETA_ONE**STEP)) / (
        jnp.sqrt(new_vec_second / (1.0 - BETA_TWO**STEP)) + ADAM_EPS
    )
    return (
        outputs[None],
        input_grad[None],
        new_masters,
        new_first,
        new_second,
        new_bases,
        new_stats,
        new_vectors,
        new_vec_first,
        new_vec_second,
    )


def solution(mesh):
    placed = (
        P("opt", "seq", None),
        P("opt", "seq", None),
        P("opt", None),
        P(),
        P("opt", "seq", None),
        P("opt", "seq", None),
        P("opt", "seq", None),
        P("opt", None, "seq", None),
        P("opt", None, "seq", None),
        P(("seq", "opt")),
        P(("seq", "opt")),
        P(("seq", "opt")),
    )
    return jax.shard_map(
        per_device,
        mesh=mesh,
        in_specs=placed,
        out_specs=(
            P("opt", "seq", None),
            P("opt", "seq", None),
            P("opt", "seq", None),
            P("opt", "seq", None),
            P("opt", "seq", None),
            P("opt", None, "seq", None),
            P("opt", None, "seq", None),
            P(("seq", "opt")),
            P(("seq", "opt")),
            P(("seq", "opt")),
        ),
        check_vma=False,
    )
```

```python
import functools
import math

import jax
import jax.numpy as jnp
from jax import lax
from jax.experimental import pallas as pl
from jax.experimental.pallas import tpu as pltpu
from jax.sharding import PartitionSpec as P

HEADS = 8
FF = 2048
BLOCK = 16
LAYERS = 2
STEP = 10
MAX_LEN = 4096


HIGH = lax.Precision.HIGHEST
LN_TWO = math.log(2.0)
NEG_FILL = -1e30
NORM_EPS = 1e-05
ADAM_EPS = 1e-08
RATE_MATRIX = 0.03
RATE_VECTOR = 0.2
WEIGHT_DECAY = 0.01
BETA_ONE = 0.9
BETA_TWO = 0.95
BETA_STAT = 0.95

SUBLANES = 8
PANEL = 16
FLOPS_PER_US = 1_150_000_000
LANES = 128
UNIT_COUNT = 24
UNIT_OPT = 0
UNIT_ROW = UNIT_COUNT
UNIT_SLOT = 2 * UNIT_COUNT
DIAG = 128
VMEM_GRANT = 60 * 2**20
IN_VMEM = pl.BlockSpec(memory_space=pltpu.VMEM)
IN_SMEM = pl.BlockSpec(memory_space=pltpu.SMEM)
ANYWHERE = pl.BlockSpec(memory_space=pl.ANY)


def contract(left, right, left_dim, right_dim, precision=None):
    return lax.dot_general(
        left,
        right,
        (((left_dim,), (right_dim,)), ((), ())),
        precision=precision,
        preferred_element_type=jnp.float32,
    )


def split_two(values):
    high = values.astype(jnp.bfloat16)
    return (high, (values - high.astype(jnp.float32)).astype(jnp.bfloat16))


def wide_left(left, right_low, left_dim, right_dim):
    high, rest = split_two(left)
    return contract(high, right_low, left_dim, right_dim) + contract(
        rest, right_low, left_dim, right_dim
    )


def wide_right(left_low, right, left_dim, right_dim):
    high, rest = split_two(right)
    return contract(left_low, high, left_dim, right_dim) + contract(
        left_low, rest, left_dim, right_dim
    )


def call_kernel(
    body, out_shapes, scratch, name, *operands, smem_count=0, any_in=(), any_out=(), aliases=None,
    micros=2,
):
    def place(at, listed):
        return ANYWHERE if at in listed else IN_VMEM

    return pl.pallas_call(
        body,
        out_shape=out_shapes,
        in_specs=[
            IN_SMEM if at < smem_count else place(at, any_in) for at in range(len(operands))
        ],
        out_specs=[place(at, any_out) for at in range(len(out_shapes))],
        scratch_shapes=scratch,
        input_output_aliases=aliases or {},
        cost_estimate=pl.CostEstimate(
            flops=micros * FLOPS_PER_US, bytes_accessed=0, transcendentals=0
        ),
        compiler_params=pltpu.CompilerParams(vmem_limit_bytes=VMEM_GRANT),
        name=name,
    )(*operands)


def eliminate(panels, turn):
    rows, width = panels[0][0].shape
    row_at = lax.broadcasted_iota(jnp.int32, (SUBLANES, width), 0)

    def groups(values):
        return [values[low : low + SUBLANES] for low in range(0, rows, SUBLANES)]

    def spread_row(values, row):
        return jnp.broadcast_to(values[row : row + 1, :], values.shape)

    states = []
    for left, right in panels:
        turned = pltpu.roll(left, turn, 1)
        columns = [
            [jnp.broadcast_to(part, (SUBLANES, width)) for part in groups(turned[:, at : at + 1])]
            for at in range(rows)
        ]
        ones = [jnp.ones((SUBLANES, width), jnp.float32) for _ in range(rows // SUBLANES)]
        states.append((groups(left), groups(right), columns, ones))
    for at in range(rows):
        group_at, row = divmod(at, SUBLANES)
        for left, right, columns, pivots in states:
            pivot = spread_row(columns[at][group_at], row)
            inverse = pltpu.reciprocal(pivot, approx=False)
            pivots[group_at] = jnp.where(row_at == row, pivot, pivots[group_at])
            targets = [left, right] + columns[at + 1 :]
            given = [spread_row(target[group_at], row) for target in targets]
            for group in range(group_at, rows // SUBLANES):
                factor = columns[at][group] * inverse
                if group == group_at:
                    factor = jnp.where(row_at > row, factor, 0.0)
                for target, pivot_row in zip(targets, given):
                    target[group] = target[group] - factor * pivot_row
    results = []
    for left, right, _, pivots in states:
        scales = [lax.rsqrt(values) for values in pivots]
        results.append(
            tuple(
                jnp.concatenate([part * scale for part, scale in zip(parts, scales)], axis=0)
                for parts in (left, right)
            )
        )
    return results


def split_three(values):
    high = values.astype(jnp.bfloat16).astype(jnp.float32)
    rest = values - high
    middle = rest.astype(jnp.bfloat16).astype(jnp.float32)
    return (high, middle, rest - middle)


def thin_product(left, right):
    left_parts, right_parts = (split_three(left), split_three(right))
    pairs = ((0, 0), (0, 1), (1, 0), (1, 1), (0, 2), (2, 0))
    stacked_left = jnp.concatenate([left_parts[i] for i, _ in pairs], axis=0)
    stacked_right = jnp.concatenate([right_parts[j] for _, j in pairs], axis=0)
    return contract(stacked_left.astype(jnp.bfloat16), stacked_right.astype(jnp.bfloat16), 0, 0)


def factorize(grams, uppers, works, inverses):
    each = range(len(grams))
    size = grams[0].shape[0]
    eye = (
        lax.broadcasted_iota(jnp.int32, (DIAG, DIAG), 0)
        == lax.broadcasted_iota(jnp.int32, (DIAG, DIAG), 1)
    ).astype(jnp.float32)
    for low in range(0, size, DIAG):
        top = low + DIAG
        for m in each:
            works[m][:, 0:DIAG] = grams[m][low:top, low:top]
            works[m][:, DIAG:] = eye

        def panel(panel_at, carry):
            row = pl.multiple_of(panel_at * PANEL, PANEL)
            turn = lax.rem(DIAG - panel_at * PANEL, DIAG)
            panels = [
                (works[m][pl.ds(row, PANEL), 0:DIAG], works[m][pl.ds(row, PANEL), DIAG:])
                for m in each
            ]
            results = eliminate(panels, turn)
            updates = [
                thin_product(left, jnp.concatenate([left, right], axis=1))
                for left, right in results
            ]
            for m in each:
                inverses[m][low // DIAG, pl.ds(row, PANEL), :] = results[m][1]
            for m in each:
                works[m][...] = works[m][...] - updates[m]
            return carry

        lax.fori_loop(0, DIAG // PANEL, panel, 0)
        if top == size:
            break
        right_of = [contract(inverses[m][low // DIAG], grams[m][low:top, top:], 1, 0, HIGH) for m in each]
        for m in each:
            uppers[m][low:top, top:] = right_of[m]
        for other in range(top, size, DIAG):
            skip = other - top
            rest = [
                grams[m][other : other + DIAG, other:]
                - contract(right_of[m][:, skip : skip + DIAG], right_of[m][:, skip:], 0, 0, HIGH)
                for m in each
            ]
            for m in each:
                grams[m][other : other + DIAG, other:] = rest[m]


def renew_body(*refs):
    stat_ref, basis_ref, sent = refs[:3]
    scratch = refs[3:]
    count, size, _ = stat_ref.shape
    each = range(count)
    products, grams, uppers, works, inverses = (
        scratch[at : at + count] for at in range(0, 5 * count, count)
    )
    values = [wide_left(stat_ref[m], basis_ref[m], 1, 0) for m in each]
    for m in each:
        products[m][...] = values[m]
    for low in range(0, size, DIAG):
        values = [
            contract(products[m][:, low : low + DIAG], products[m][:, low:], 0, 0, HIGH)
            for m in each
        ]
        for m in each:
            grams[m][low : low + DIAG, low:] = values[m]
    factorize(grams, uppers, works, inverses)
    for low in range(0, size, DIAG):
        top = low + DIAG
        values = [products[m][:, low:top] for m in each]
        if low:
            values = [
                values[m]
                - contract(products[m][:, :low], uppers[m][:low, low:top], 1, 0, HIGH)
                for m in each
            ]
        values = [contract(values[m], inverses[m][low // DIAG], 1, 1, HIGH) for m in each]
        for m in each:
            products[m][:, low:top] = values[m]
    rows = sent.shape[2]
    for target in range(sent.shape[0]):
        for m in each:
            sent[target, m] = products[m][target * rows : (target + 1) * rows, :].astype(
                jnp.bfloat16
            )


def renew_bases(device_count, new_stat, basis_low):
    count, size, _ = new_stat.shape
    return call_kernel(
        renew_body,
        [jax.ShapeDtypeStruct((device_count, count, size // device_count, size), jnp.bfloat16)],
        [pltpu.VMEM((size, size), jnp.float32)] * (3 * count)
        + [pltpu.VMEM((DIAG, 2 * DIAG), jnp.float32)] * count
        + [pltpu.VMEM((size // DIAG, DIAG, DIAG), jnp.float32)] * count,
        "renew_bases",
        new_stat,
        basis_low,
        micros=40,
    )[0]


def pack_body(slot_ref, stats, bases, first, second, *packed):
    at = 0
    for part in packed:
        for target in range(part.shape[0]):
            slot = slot_ref[at]
            part[target, 0:2] = stats[slot].astype(jnp.bfloat16)
            part[target, 2:4] = bases[slot].astype(jnp.bfloat16)
            part[target, 4] = first[slot].astype(jnp.bfloat16)
            part[target, 5] = second[slot].astype(jnp.bfloat16)
            at += 1


def rotate_body(count, row_ref, grad_ref, *refs):
    given, (sent, stat_ref, basis_ref, whole, results) = (refs[:count], refs[count:])
    at = 0
    for part in given:
        pieces, _, rows, _ = part.shape
        for piece in range(pieces):
            row = pl.multiple_of(row_ref[at], 8)
            whole[:, pl.ds(row, rows), :] = part[piece].astype(jnp.float32)
            at += 1
    grad = grad_ref[...]
    left = whole[2].astype(jnp.bfloat16)
    right = whole[3].astype(jnp.bfloat16)
    basis_ref[0] = left
    basis_ref[1] = right
    results[0] = contract(grad, grad, 1, 1)
    results[1] = contract(grad, grad, 0, 0)
    stat_ref[0] = BETA_STAT * whole[0] + (1.0 - BETA_STAT) * results[0]
    stat_ref[1] = BETA_STAT * whole[1] + (1.0 - BETA_STAT) * results[1]
    rotated = wide_left(contract(left, grad, 0, 0), right, 1, 0)
    results[2] = rotated
    new_first = BETA_ONE * whole[4] + (1.0 - BETA_ONE) * rotated
    new_second = BETA_TWO * whole[5] + (1.0 - BETA_TWO) * rotated * rotated
    direction = (
        new_first
        / (1.0 - BETA_ONE**STEP)
        / (jnp.sqrt(new_second / (1.0 - BETA_TWO**STEP)) + ADAM_EPS)
    )
    results[3] = wide_right(left, wide_left(direction, right, 1, 1), 1, 0)
    for target in range(sent.shape[0]):
        sent[target] = results[:, target * rows : (target + 1) * rows, :].astype(jnp.bfloat16)


def rotate_slot(row_at, grad, owner_rows):
    size = grad.shape[0]
    return call_kernel(
        functools.partial(rotate_body, len(owner_rows)),
        [
            jax.ShapeDtypeStruct(
                (size // owner_rows[0].shape[2], 4) + owner_rows[0].shape[2:], jnp.bfloat16
            ),
            jax.ShapeDtypeStruct((2, size, size), jnp.float32),
            jax.ShapeDtypeStruct((2, size, size), jnp.bfloat16),
        ],
        [
            pltpu.VMEM((6, size, size), jnp.float32),
            pltpu.VMEM((4, size, size), jnp.float32),
        ],
        "rotate_slot",
        row_at,
        grad,
        *owner_rows,
        smem_count=1,
        micros=6,
    )


def finish_body(
    owner_ref, masters, first, second, stats, given, new_masters, new_first, new_second, new_stats
):
    for slot in range(masters.shape[0]):
        owner = owner_ref[slot]
        rotated = given[owner, 2].astype(jnp.float32)
        update = given[owner, 3].astype(jnp.float32)
        new_first[slot] = BETA_ONE * first[slot] + (1.0 - BETA_ONE) * rotated
        new_second[slot] = BETA_TWO * second[slot] + (1.0 - BETA_TWO) * rotated * rotated
        new_masters[slot] = masters[slot] - RATE_MATRIX * (update + WEIGHT_DECAY * masters[slot])
        new_stats[slot] = BETA_STAT * stats[slot] + (1.0 - BETA_STAT) * given[owner, 0:2].astype(
            jnp.float32
        )


def place_body(owner_ref, given, new_bases):
    for slot in range(new_bases.shape[0]):
        new_bases[slot] = given[owner_ref[slot]].astype(jnp.float32)


def add_low(left, right):
    return (left.astype(jnp.float32) + right.astype(jnp.float32)).astype(jnp.bfloat16)


def over_z(value, apart, owner_apart):
    pairs = []
    for at in range(32):
        z, y, core = (at >> 3, at >> 2 & 1, at & 1)
        if z ^ owner_apart != (0 if y ^ core else 3):
            pairs.append((at, at ^ apart << 3))
    return lax.ppermute(value, ("seq", "opt"), pairs)


def sum_to_owner(
    kept_upper, kept_lower, sent_upper, sent_lower, seq_index, shift, vec_sum, to_owner
):
    def beside(values, vec_sum, *exchanges):
        for axis, bit_at in exchanges:
            vec_sum = vec_sum + partner(vec_sum, axis, bit_at)
        return lax.optimization_barrier((values, vec_sum))

    _, row_count, width = kept_upper.shape
    z_count = kept_upper.shape[0] // 4
    shape = (2, 2, z_count, row_count, width)
    upper, came_upper = (kept_upper.reshape(shape), partner(sent_upper, "opt", 0).reshape(shape))
    lower, came_lower = (kept_lower.reshape(shape), partner(sent_lower, "opt", 0).reshape(shape))
    send_x = add_low(upper[1], came_upper[1])
    send_x, upper, came_upper = lax.optimization_barrier((send_x, upper, came_upper))
    by_x = partner(send_x, "opt", 1)
    send_y = add_low(lower[:, 1], came_lower[:, 1])
    send_y, lower, came_lower = lax.optimization_barrier((send_y, lower, came_lower))
    by_y = partner(send_y, "seq", 0)
    rows = [to_owner[0]] + [over_z(to_owner[at], at, at) for at in range(1, 4)]
    (by_x, rows[1], rows[2]), vec_sum = beside((by_x, rows[1], rows[2]), vec_sum, ("opt", 0))
    stay_x = add_low(upper[0], came_upper[0])
    stay_y = add_low(lower[:, 0], came_lower[:, 0])
    then_y = partner(add_low(stay_x[1], by_x[1]), "seq", 0)
    then_x = partner(add_low(stay_y[1], by_y[1]), "opt", 1)
    (then_y, rows[3]), vec_sum = beside((then_y, rows[3]), vec_sum, ("seq", 1))
    z_index = seq_index >> 1

    def both(apart):
        at = jnp.clip((z_index ^ apart) - shift, 0, z_count - 1)

        def pick(values):
            return lax.dynamic_index_in_dim(values, at, 0, keepdims=False)

        total_upper = (
            pick(stay_x[0]).astype(jnp.float32)
            + pick(by_x[0]).astype(jnp.float32)
            + pick(then_y).astype(jnp.float32)
        )
        total_lower = (
            pick(stay_y[0]).astype(jnp.float32)
            + pick(by_y[0]).astype(jnp.float32)
            + pick(then_x).astype(jnp.float32)
        )
        return jnp.concatenate([total_upper, total_lower]).astype(jnp.bfloat16)

    near_one = over_z(both(1), 1, 1)
    near_far = over_z(both(3), 1, 3)
    near_far, vec_sum = beside(near_far, vec_sum, ("seq", 2))
    last = over_z(add_low(both(2), near_far), 2, 2)
    last, vec_sum = beside(last, vec_sum, ("opt", 1), ("seq", 0))
    total = both(0).astype(jnp.float32) + near_one.astype(jnp.float32) + last.astype(jnp.float32)
    return (total.astype(jnp.bfloat16), vec_sum, rows)


def partner(value, axis, apart):
    return lax.ppermute(value, axis, [(i, i ^ 1 << apart) for i in range(lax.axis_size(axis))])


def pair_mean(values):
    shaped = values.reshape((values.shape[0] // 2, 2) + values.shape[1:])
    return 0.5 * (shaped[:, 0] + shaped[:, 1])


def pair_spread(grads):
    return 0.5 * jnp.repeat(grads, 2, axis=0)


def sum_rows(values):
    return jnp.sum(values, axis=0, keepdims=True)


def norm_parts(values):
    centred = values - jnp.mean(values, axis=-1, keepdims=True)
    recip = lax.rsqrt(jnp.mean(centred * centred, axis=-1, keepdims=True) + NORM_EPS)
    return (centred * recip, recip)


def norm_back(grad, gain, normed, recip):
    scaled = grad * gain
    return recip * (
        scaled
        - jnp.mean(scaled, axis=-1, keepdims=True)
        - normed * jnp.mean(scaled * normed, axis=-1, keepdims=True)
    )


def half_matrix(shape, fine_dim):
    fine = lax.broadcasted_iota(jnp.int32, shape, fine_dim)
    coarse = lax.broadcasted_iota(jnp.int32, shape, 1 - fine_dim)
    return jnp.where(fine >> 1 == coarse, 0.5, 0.0).astype(jnp.bfloat16)


def pool(rows_low):
    count = rows_low.shape[0]
    return contract(half_matrix((count // 2, count), 1), rows_low, 1, 0).astype(jnp.bfloat16)


def spread(grads):
    count = grads.shape[0]
    return wide_right(half_matrix((2 * count, count), 0), grads, 1, 0)


def norm_cdf(values):
    return 0.5 * (1.0 + lax.erf(values * math.sqrt(0.5)))


def local_count(tok_count):
    return (tok_count // BLOCK).bit_length() - 1


def key_width(tok_count, tree_bits):
    rows = 2 * (tok_count - BLOCK) + BLOCK * tree_bits
    return -(-rows // LANES) * LANES


def score_offsets(tok_count, tree_bits, span_bits):
    token = jnp.arange(tok_count, dtype=jnp.int32)[:, None]
    parts = []
    for height in range(local_count(tok_count)):
        row = jnp.arange(tok_count >> height, dtype=jnp.int32)[None, :]
        apart = token // (BLOCK << height) ^ row // BLOCK
        counted = apart <= 1 if height == 0 else apart == 1
        parts.append(jnp.where(counted, height * LN_TWO, NEG_FILL))
    for bit_at in range(tree_bits):
        offset = (local_count(tok_count) + bit_at) * LN_TWO
        parts.append(
            jnp.broadcast_to(
                jnp.where(bit_at + 1 <= span_bits, offset, NEG_FILL), (tok_count, BLOCK)
            )
        )
    used = sum(part.shape[1] for part in parts)
    rest = key_width(tok_count, tree_bits) - used
    parts.append(jnp.full((tok_count, rest), NEG_FILL, jnp.float32))
    return jnp.concatenate(parts, axis=1).astype(jnp.float32)


def stack_keys(own_rows, far_rows):
    parts = [own_rows]
    for _ in range(local_count(own_rows.shape[0]) - 1):
        parts.append(pool(parts[-1]))
    parts = parts + far_rows
    rest = key_width(own_rows.shape[0], len(far_rows)) - sum(part.shape[0] for part in parts)
    if rest:
        parts.append(jnp.zeros((rest, own_rows.shape[1]), jnp.bfloat16))
    return jnp.concatenate(parts, axis=0)


def by_heads(pair):
    lane = lax.broadcasted_iota(jnp.int32, pair.shape, 1)
    zero = jnp.zeros_like(pair)
    first = lane < LANES // 2
    return jnp.concatenate([jnp.where(first, pair, zero), jnp.where(first, zero, pair)], axis=0)


def from_heads(both):
    count = both.shape[0] // 2
    lane = lax.broadcasted_iota(jnp.int32, (count, LANES), 1)
    return jnp.where(lane < LANES // 2, both[:count], both[count:])


def attend(qkv, far_rows, offsets, probs, mixed):
    width = qkv.shape[1] // 3
    score_scale = (width // HEADS) ** (-0.5)
    stack = stack_keys(qkv[:, width:], far_rows)
    both_offsets = jnp.concatenate([offsets, offsets], axis=0)
    for pair_at in range(width // LANES):
        low, top = (pair_at * LANES, (pair_at + 1) * LANES)
        scores = (
            contract(by_heads(qkv[:, low:top]), stack[:, low:top], 1, 1) * score_scale
            + both_offsets
        )
        expo = jnp.exp(scores - jnp.max(scores, axis=1, keepdims=True))
        weights = expo / jnp.sum(expo, axis=1, keepdims=True)
        probs[pair_at] = weights
        result = contract(
            weights.astype(jnp.bfloat16), stack[:, width + low : width + top], 1, 0
        )
        mixed[:, low:top] = from_heads(result).astype(jnp.bfloat16)


def attend_back(qkv, far_rows, probs, mixed_grad, query_grad, key_grads, far_grads):
    tok_count, width = mixed_grad.shape
    score_scale = (width // HEADS) ** (-0.5)
    stack = stack_keys(qkv[:, width:], far_rows)
    local_levels = local_count(tok_count)
    far_start = 2 * (tok_count - BLOCK)
    for pair_at in range(width // LANES):
        low, top = (pair_at * LANES, (pair_at + 1) * LANES)
        queries = by_heads(qkv[:, low:top])
        grads = by_heads(mixed_grad[:, low:top])
        weights = probs[pair_at]
        prob_grad = contract(grads, stack[:, width + low : width + top], 1, 1)
        inner = jnp.sum(weights * prob_grad, axis=1, keepdims=True)
        score_grad = (weights * (prob_grad - inner)).astype(jnp.bfloat16)
        query_grad[:, low:top] = (
            from_heads(contract(score_grad, stack[:, low:top], 1, 0)) * score_scale
        ).astype(jnp.bfloat16)
        for start, part in (
            (low, contract(score_grad, queries, 0, 0) * score_scale),
            (width + low, contract(weights.astype(jnp.bfloat16), grads, 0, 0)),
        ):
            for far_at, far_grad in enumerate(far_grads):
                row = far_start + BLOCK * far_at
                far_grad[:, start : start + LANES] = part[row : row + BLOCK]
            folded = None
            for height in reversed(range(local_levels)):
                row = 2 * (tok_count - (tok_count >> height))
                own = part[row : row + (tok_count >> height)]
                folded = own if folded is None else own + spread(folded)
            key_grads[:, start : start + LANES] = folded


class Units:
    def __init__(self, meta, packed, store, sems, units):
        self.store = store
        self.place = {unit: at for at, unit in enumerate(units)}
        self.waiting = {}
        rows = store.shape[2]
        for at, unit in enumerate(units):
            row = pl.multiple_of(meta[UNIT_ROW + unit], rows)
            copy = pltpu.make_async_copy(
                packed.at[:, meta[UNIT_OPT + unit], pl.ds(row, rows), :],
                store.at[at],
                sems.at[at],
            )
            copy.start()
            self.waiting[unit] = copy

    def __getitem__(self, unit):
        if unit in self.waiting:
            self.waiting.pop(unit).wait()
        width = self.store.shape[3]
        return self.store[self.place[unit]].reshape(width, width)


class Grads:
    def __init__(self, meta, *refs):
        self.meta, self.buffers, self.store, self.sems = (meta, refs[:4], refs[4], refs[5])
        self.copies = []

    def put(self, first_unit, left_low, right_low):
        product = contract(left_low, right_low, 0, 0).astype(jnp.bfloat16)
        width = self.store.shape[2]
        slots, rows, _ = self.buffers[0].shape
        for low in range(0, product.shape[0], width):
            for side in range(0, product.shape[1], width):
                at = len(self.copies) // 2
                self.store[at] = product[low : low + width, side : side + width]
                place = self.meta[UNIT_SLOT + first_unit + low // width + side // width]
                inner = jnp.where(place < slots, place, place - slots)
                for half in range(2):
                    keeping, sending = (
                        pltpu.make_async_copy(
                            self.store.at[at, pl.ds(half * rows, rows)],
                            target.at[inner],
                            self.sems.at[at, half],
                        )
                        for target in (self.buffers[half], self.buffers[2 + half])
                    )
                    pl.when(place < slots)(keeping.start)
                    pl.when(place >= slots)(sending.start)
                    self.copies.append(keeping)

    def finish(self):
        for copy in self.copies:
            copy.wait()


def project(hidden, units, first_unit, gain, bias, normed_ref, qkv_ref, near_ref):
    width = hidden.shape[1]
    normed, _ = norm_parts(hidden)
    normed_low = (normed * gain + bias).astype(jnp.bfloat16)
    normed_ref[...] = normed_low
    for part in range(3):
        qkv_ref[:, part * width : (part + 1) * width] = contract(
            normed_low, units[first_unit + part], 1, 0
        ).astype(jnp.bfloat16)
    near = qkv_ref[:, width:]
    for _ in range(local_count(near.shape[0])):
        near = pool(near)
    near_ref[...] = near


def feed_forward(middle, units, first_unit, vec, vec_at, normed_ref, pre_ref, act_ref):
    width = middle.shape[1]
    normed, _ = norm_parts(middle)
    normed_low = (normed * vec[vec_at + 2 : vec_at + 3] + vec[vec_at + 3 : vec_at + 4]).astype(
        jnp.bfloat16
    )
    normed_ref[...] = normed_low
    total = middle
    ff_blocks = FF // width
    for part in range(ff_blocks):
        low, top = (part * width, (part + 1) * width)
        row = vec_at + 4 + part
        pre = contract(normed_low, units[first_unit + 4 + part], 1, 0) + vec[row : row + 1]
        act = (pre * norm_cdf(pre)).astype(jnp.bfloat16)
        pre_ref[:, low:top] = pre
        act_ref[:, low:top] = act
        total = total + contract(act, units[first_unit + 4 + ff_blocks + part], 1, 0)
    row = vec_at + 4 + ff_blocks
    return total + vec[row : row + 1]


def feed_back(
    grad, middle, pre_ref, units, first_unit, vec, vec_at, vec_grads, at, pre_grad_ref
):
    width = middle.shape[1]
    ff_blocks = FF // width
    down_grad = grad.astype(jnp.bfloat16)
    normed_grad = jnp.zeros(middle.shape, jnp.float32)
    for part in range(ff_blocks):
        low, top = (part * width, (part + 1) * width)
        pre = pre_ref[:, low:top]
        slope = norm_cdf(pre) + pre * jnp.exp(-0.5 * pre * pre) * (1.0 / math.sqrt(2.0 * math.pi))
        pre_grad = (
            contract(down_grad, units[first_unit + 4 + ff_blocks + part], 1, 1) * slope
        ).astype(jnp.bfloat16)
        pre_grad_ref[:, low:top] = pre_grad
        vec_grads[at + 2 + part : at + 3 + part] = sum_rows(pre_grad.astype(jnp.float32))
        normed_grad = normed_grad + contract(pre_grad, units[first_unit + 4 + part], 1, 1)
    row = at + 2 + ff_blocks
    vec_grads[row : row + 1] = sum_rows(grad)
    normed, recip = norm_parts(middle)
    vec_grads[at : at + 1] = sum_rows(normed_grad * normed)
    vec_grads[at + 1 : at + 2] = sum_rows(normed_grad)
    return grad + norm_back(normed_grad, vec[vec_at + 2 : vec_at + 3], normed, recip)


def with_near(key_grads, near):
    for _ in range(local_count(key_grads.shape[0])):
        near = spread(near)
    return (key_grads + near).astype(jnp.bfloat16)


def project_back(
    middle_grad, hidden, query_grad, rows_low, units, first_unit, vec, vec_at, vec_grads
):
    width = hidden.shape[1]
    normed_grad = contract(query_grad, units[first_unit], 1, 1)
    for part in range(2):
        normed_grad = normed_grad + contract(
            rows_low[:, part * width : (part + 1) * width], units[first_unit + 1 + part], 1, 1
        )
    normed, recip = norm_parts(hidden)
    vec_grads[0:1] = sum_rows(normed_grad * normed)
    vec_grads[1:2] = sum_rows(normed_grad)
    return middle_grad + norm_back(normed_grad, vec[vec_at : vec_at + 1], normed, recip)


def first_body(per_layer, meta, vec, inputs, packed, normed, qkv, near, store, sems):
    units = Units(meta, packed, store, sems, range(3))
    project(inputs[...].astype(jnp.float32), units, 0, vec[0:1], vec[1:2], normed, qkv, near)


def middle_body(per_layer, vec_rows, tree_bits, meta, vec, offsets, inputs, qkv, *refs):
    far, refs = (refs[:tree_bits], refs[tree_bits:])
    packed, probs_out, mixed, middle, normed_two, pre_out, act = refs[:7]
    hidden, normed, next_qkv, near, store, sems, probs, pre, out_sems = refs[7:]
    units = Units(meta, packed, store, sems, range(3, per_layer + 3))
    attend(qkv[...], [ref[...] for ref in far], offsets[...], probs, mixed)
    probs_copy = pltpu.make_async_copy(probs, probs_out, out_sems.at[0])
    probs_copy.start()
    middle[...] = inputs[...].astype(jnp.float32) + contract(mixed[...], units[3], 1, 0)
    hidden[...] = feed_forward(middle[...], units, 0, vec, 0, normed_two, pre, act)
    pre_copy = pltpu.make_async_copy(pre, pre_out, out_sems.at[1])
    pre_copy.start()
    project(
        hidden[...], units, per_layer, vec[vec_rows : vec_rows + 1],
        vec[vec_rows + 1 : vec_rows + 2], normed, next_qkv, near,
    )
    probs_copy.wait()
    pre_copy.wait()


def turn_body(per_layer, vec_rows, tree_bits, meta, vec, offsets, cotangent, hidden, qkv, *refs):
    far, refs = (refs[:tree_bits], refs[tree_bits:])
    packed, outputs, mixed, normed_two, act = refs[:5]
    middle_grad, query_grad, key_grads, vec_grads, pre_grad, branch_low = refs[5:11]
    far_grads, refs = (refs[11 : 11 + tree_bits], refs[11 + tree_bits :])
    store, sems, probs, pre = refs
    units = Units(meta, packed, store, sems, range(per_layer + 3, 2 * per_layer))
    far_rows = [ref[...] for ref in far]
    attend(qkv[...], far_rows, offsets[...], probs, mixed)
    middle = hidden[...] + contract(mixed[...], units[per_layer + 3], 1, 0)
    outputs[...] = feed_forward(
        middle, units, per_layer, vec, vec_rows, normed_two, pre, act
    ).astype(jnp.bfloat16)
    vec_grads[...] = jnp.zeros_like(vec_grads)
    grad = feed_back(
        cotangent[...].astype(jnp.float32), middle, pre, units, per_layer, vec, vec_rows,
        vec_grads, 2, pre_grad,
    )
    middle_grad[...] = grad
    branch_grad = grad.astype(jnp.bfloat16)
    branch_low[...] = branch_grad
    mixed_grad = contract(branch_grad, units[per_layer + 3], 1, 1).astype(jnp.bfloat16)
    attend_back(qkv[...], far_rows, probs, mixed_grad, query_grad, key_grads, far_grads)


def lower_body(per_layer, vec_rows, tree_bits, meta, vec, *refs):
    hidden, query_in, key_in, near_in, middle_in, middle, qkv = refs[:7]
    far, refs = (refs[7 : 7 + tree_bits], refs[7 + tree_bits :])
    probs_in, pre_in, packed, down_low, rows_low = refs[:5]
    middle_grad, query_grad, key_grads, vec_grads, pre_grad, branch_low = refs[5:11]
    far_grads, refs = (refs[11 : 11 + tree_bits], refs[11 + tree_bits :])
    store, sems, probs, pre, in_sems = refs
    split = 4 + (per_layer - 4) // 2
    units = Units(
        meta, packed, store, sems,
        list(range(per_layer, per_layer + 3)) + list(range(split, per_layer))
        + list(range(3, split)),
    )
    pre_copy = pltpu.make_async_copy(pre_in, pre, in_sems.at[0])
    probs_copy = pltpu.make_async_copy(probs_in, probs, in_sems.at[1])
    pre_copy.start()
    probs_copy.start()
    vec_grads[...] = jnp.zeros_like(vec_grads)
    rows_low[...] = with_near(key_in[...], near_in[...])
    grad = project_back(
        middle_in[...], hidden[...], query_in[...], rows_low[...], units, per_layer, vec,
        vec_rows, vec_grads,
    )
    down_low[...] = grad.astype(jnp.bfloat16)
    pre_copy.wait()
    grad = feed_back(grad, middle[...], pre, units, 0, vec, 0, vec_grads, 2, pre_grad)
    middle_grad[...] = grad
    branch_grad = grad.astype(jnp.bfloat16)
    branch_low[...] = branch_grad
    mixed_grad = contract(branch_grad, units[3], 1, 1).astype(jnp.bfloat16)
    probs_copy.wait()
    attend_back(
        qkv[...], [ref[...] for ref in far], probs, mixed_grad, query_grad, key_grads, far_grads
    )


def last_body(meta, vec, inputs, query_grad, rows_low, middle_in, packed, *refs):
    input_grad, vec_grads, store, sems = refs
    units = Units(meta, packed, store, sems, range(3))
    vec_grads[...] = jnp.zeros_like(vec_grads)
    input_grad[...] = project_back(
        middle_in[...], inputs[...].astype(jnp.float32), query_grad[...], rows_low[...], units, 0,
        vec, 0, vec_grads,
    )


def grads_body(pairs, array_count, held, meta, *refs):
    arrays, refs = (refs[:array_count], refs[array_count + held :])
    grads = Grads(meta, *refs)
    for first_unit, left, right in pairs:
        grads.put(first_unit, arrays[left][...], arrays[right][...])
    grads.finish()


def last_grads_body(meta, normed, query_grad, key_grads, near_grads, *refs):
    rows_low, *refs = refs[4:]
    grads = Grads(meta, *refs)
    grads.put(0, normed[...], query_grad[...])
    rows_low[...] = with_near(key_grads[...], near_grads[...])
    grads.put(1, normed[...], rows_low[...])
    grads.finish()


def coarse_up(own, seq_index, tree_bits):
    far_list = []
    for bit_at in range(tree_bits):
        far = partner(own, "seq", bit_at)
        far_list.append(far)
        if bit_at + 1 < tree_bits:
            upper = seq_index >> bit_at & 1 == 1
            joined = jnp.where(
                upper, jnp.concatenate([far, own]), jnp.concatenate([own, far])
            ).astype(jnp.float32)
            own = pair_mean(joined).astype(jnp.bfloat16)
    return far_list


def coarse_down(far_grads, seq_index):
    above = None
    for bit_at in reversed(range(len(far_grads))):
        upper = seq_index >> bit_at & 1 == 1
        sent = far_grads[bit_at]
        own = 0.0
        if above is not None:
            wide = pair_spread(above)
            own = jnp.where(upper, wide[BLOCK:], wide[:BLOCK])
            sent = sent + jnp.where(upper, wide[:BLOCK], wide[BLOCK:])
        above = own + partner(sent.astype(jnp.bfloat16), "seq", bit_at).astype(jnp.float32)
    return above


def per_device(
    inputs,
    cotangent,
    seq_lengths,
    unit_slot,
    masters,
    first_moment,
    second_moment,
    bases,
    stats,
    vec_master,
    vec_first,
    vec_second,
):
    seq_count = lax.axis_size("seq")
    opt_count = lax.axis_size("opt")
    seq_index = lax.axis_index("seq")
    tok_count = inputs.shape[1]
    model_width = inputs.shape[2]
    own_slots = masters.shape[0]
    row_count = masters.shape[1]
    ff_blocks = FF // model_width
    per_layer = 4 + 2 * ff_blocks
    vec_width = 5 * model_width + FF
    long_devs = min(max(MAX_LEN // tok_count, 1), seq_count)
    tree_bits = long_devs.bit_length() - 1
    size = seq_count * row_count
    by_permutes = seq_count == 8 and opt_count == 4 and own_slots == 6
    slots = jnp.arange(own_slots, dtype=jnp.int32)
    def pack_slots(slots, counts):
        return call_kernel(
            pack_body,
            [
                jax.ShapeDtypeStruct((count, 6, row_count, model_width), jnp.bfloat16)
                for count in counts
            ],
            [],
            "pack_slots",
            slots,
            stats,
            bases,
            first_moment,
            second_moment,
            smem_count=1,
            micros=3,
        )

    if by_permutes:
        parity, core = (seq_index & 1, lax.axis_index("opt") & 1)
        shift = parity ^ core
        owners = 2 * ((slots >> 1) + ((slots & 1) ^ core)) + (slots & 1)
        half_slots = own_slots // 2
        pairs = 2 * jnp.arange(half_slots, dtype=jnp.int32)
        near, away = pack_slots(
            jnp.concatenate([pairs + parity, pairs + 1 - parity]), (half_slots, half_slots)
        )
        met = jnp.stack([near, partner(away, "seq", 0)], axis=1)
        z_index = seq_index >> 1
        to_owner = [
            lax.dynamic_index_in_dim(
                met, jnp.clip((z_index ^ apart) - shift, 0, half_slots - 1), 0, keepdims=False
            )
            for apart in range(4)
        ]
        row_at = jnp.stack(
            [
                (2 * (z_index ^ apart) + (parity ^ side)) * row_count
                for apart in range(4)
                for side in range(2)
            ]
        )
    else:
        owners = slots
        (to_owner,) = pack_slots(
            jnp.minimum(jnp.arange(seq_count, dtype=jnp.int32), own_slots - 1), (seq_count,)
        )
        row_at = jnp.arange(seq_count, dtype=jnp.int32) * row_count
    vec_count = vec_master.shape[0]
    own_rows = own_slots * row_count
    vec_low = vec_master.astype(jnp.bfloat16)
    for axis in ("opt", "seq"):
        for bit_at in range(lax.axis_size(axis).bit_length() - 1):
            other = partner(vec_low, axis, bit_at)
            vec_low = jnp.where(
                lax.axis_index(axis) >> bit_at & 1 == 1,
                jnp.concatenate([other, vec_low]),
                jnp.concatenate([vec_low, other]),
            )
    vec = vec_low.reshape(-1, model_width).astype(jnp.float32)
    gathered = lax.all_gather(
        masters.astype(jnp.bfloat16).reshape(1, own_rows, model_width),
        ("seq", "opt"),
        axis=0,
        tiled=True,
    )
    if row_count % 16 == 0:
        unit_rows = row_count
        packed = gathered.reshape(seq_count, opt_count, own_rows, model_width)
    else:
        unit_rows = size
        packed = (
            gathered.reshape(seq_count, opt_count, own_slots, row_count, model_width)
            .transpose(1, 2, 0, 3, 4)
            .reshape(1, opt_count, own_slots * size, model_width)
        )
    opt_index = lax.axis_index("opt")
    opt_at, slot_in = (unit_slot // own_slots, unit_slot % own_slots)
    if by_permutes:
        apart = opt_at ^ opt_index
        other = (apart & 1) * 4 + (apart >> 1) * 2 + ((slot_in ^ seq_index) & 1)
        place = other * (own_slots // 2) + (slot_in >> 1)
    else:
        place = unit_slot
    meta = jnp.concatenate([opt_at, slot_in * unit_rows, place]).astype(jnp.int32)
    span_bits = jnp.zeros((), jnp.int32)
    for bit_at in range(tree_bits + 1):
        start_dev = seq_index >> bit_at << bit_at
        span_bits = jnp.where(
            seq_lengths[0, start_dev] == tok_count * (1 << bit_at), bit_at, span_bits
        )
    offsets_in = score_offsets(tok_count, tree_bits, span_bits)
    width_in = offsets_in.shape[1]
    pair_count = model_width // LANES
    vec_rows = vec_width // model_width
    square = (model_width, model_width)

    def units_in(count):
        return [
            pltpu.VMEM((count, size // unit_rows, unit_rows, model_width), jnp.bfloat16),
            pltpu.SemaphoreType.DMA((count,)),
        ]

    def grads_out(count):
        return [pltpu.VMEM((count,) + square, jnp.bfloat16), pltpu.SemaphoreType.DMA((count, 2))]

    def low_of(*shape):
        return jax.ShapeDtypeStruct(shape, jnp.bfloat16)

    def full_of(*shape):
        return jax.ShapeDtypeStruct(shape, jnp.float32)

    projected = [
        low_of(tok_count, model_width),
        low_of(tok_count, 3 * model_width),
        low_of(BLOCK, 2 * model_width),
    ]
    attended = [
        full_of(pair_count, 2 * tok_count, width_in),
        low_of(tok_count, model_width),
    ]
    fed = [
        low_of(tok_count, model_width),
        full_of(tok_count, FF),
        low_of(tok_count, FF),
    ]
    back = [
        full_of(tok_count, model_width),
        low_of(tok_count, model_width),
        full_of(tok_count, 2 * model_width),
        full_of(16, model_width),
        low_of(tok_count, FF),
        low_of(tok_count, model_width),
    ] + [full_of(BLOCK, 2 * model_width)] * tree_bits
    buffers = [low_of(UNIT_COUNT // 2, size // 2, model_width)] * 4
    ff_blocks = FF // model_width

    def in_vmem(shapes):
        return [pltpu.VMEM(shape.shape, shape.dtype) for shape in shapes]

    def unit_grads(name, held, pairs):
        arrays = []
        for _, *factors in pairs:
            arrays += [factor for factor in factors if not any(factor is one for one in arrays)]
        index = {id(array): at for at, array in enumerate(arrays)}
        count = sum(left.shape[1] * right.shape[1] for _, left, right in pairs) // model_width**2
        first = 1 + len(arrays)
        return call_kernel(
            functools.partial(
                grads_body,
                [(unit, index[id(left)], index[id(right)]) for unit, left, right in pairs],
                len(arrays),
                len(held),
            ),
            buffers,
            grads_out(count),
            name,
            meta,
            *arrays,
            *held,
            smem_count=1,
            micros=2,
            any_in=range(first, first + len(held)),
            any_out=range(4),
            aliases={first + at: at for at in range(len(held))},
        )

    packed, to_owner, offsets_in, vec, meta = lax.optimization_barrier(
        (packed, to_owner, offsets_in, vec, meta)
    )
    normed_zero, qkv_zero, near_zero = call_kernel(
        functools.partial(first_body, per_layer),
        projected,
        units_in(3),
        "project_first",
        meta,
        vec,
        inputs[0],
        packed,
        smem_count=1,
        micros=3,
        any_in=(3,),
    )
    far_zero = coarse_up(near_zero, seq_index, tree_bits)
    (
        probs, mixed, middle, normed_two, pre, act, hidden, normed_one, qkv_one, near_one,
    ) = call_kernel(
        functools.partial(middle_body, per_layer, vec_rows, tree_bits),
        attended + [full_of(tok_count, model_width)] + fed + [full_of(tok_count, model_width)]
        + projected,
        units_in(per_layer) + in_vmem([attended[0], fed[1]]) + [pltpu.SemaphoreType.DMA((2,))],
        "layer_first",
        meta,
        vec,
        offsets_in,
        inputs[0],
        qkv_zero,
        *far_zero,
        packed,
        smem_count=1,
        micros=7,
        any_in=(5 + tree_bits,),
        any_out=(0, 4),
    )
    far_one = coarse_up(near_one, seq_index, tree_bits)
    (
        outputs, mixed_one, normed_up, act_one, middle_grad, query_grad, key_grads, vec_grads_up,
        pre_grad, branch_low, *far_grads,
    ) = call_kernel(
        functools.partial(turn_body, per_layer, vec_rows, tree_bits),
        [low_of(tok_count, model_width), attended[1], fed[0], fed[2]] + back,
        units_in(per_layer - 3) + in_vmem([attended[0], fed[1]]),
        "layer_turn",
        meta,
        vec,
        offsets_in,
        cotangent[0],
        hidden,
        qkv_one,
        *far_one,
        packed,
        smem_count=1,
        micros=13,
        any_in=(6 + tree_bits,),
    )
    near_grads = coarse_down(far_grads, seq_index)
    held = unit_grads("down_grads", (), [(per_layer + 4 + ff_blocks, act_one, cotangent[0])])
    held = unit_grads(
        "up_grads",
        held,
        [(per_layer + 4, normed_up, pre_grad), (per_layer + 3, mixed_one, branch_low)],
    )
    (
        down_low, rows_low, middle_grad, query_zero, key_grads, vec_grads_mid, pre_grad,
        branch_low, *far_grads,
    ) = call_kernel(
        functools.partial(lower_body, per_layer, vec_rows, tree_bits),
        [low_of(tok_count, model_width), low_of(tok_count, 2 * model_width)] + back,
        units_in(per_layer) + in_vmem([attended[0], fed[1]]) + [pltpu.SemaphoreType.DMA((2,))],
        "layer_back",
        meta,
        vec,
        hidden,
        query_grad,
        key_grads,
        near_grads,
        middle_grad,
        middle,
        qkv_zero,
        *far_zero,
        probs,
        pre,
        packed,
        smem_count=1,
        micros=13,
        any_in=range(9 + tree_bits, 12 + tree_bits),
    )
    near_grads = coarse_down(far_grads, seq_index)
    held = unit_grads("down_grads_low", held, [(4 + ff_blocks, act, down_low)])
    held = unit_grads(
        "up_grads_low", held, [(4, normed_two, pre_grad), (3, mixed, branch_low)]
    )
    held = unit_grads(
        "project_grads",
        held,
        [(per_layer, normed_one, query_grad), (per_layer + 1, normed_one, rows_low)],
    )
    rows_zero, *held = call_kernel(
        last_grads_body,
        [low_of(tok_count, 2 * model_width)] + buffers,
        grads_out(3),
        "project_grads_low",
        meta,
        normed_zero,
        query_zero,
        key_grads,
        near_grads,
        *held,
        smem_count=1,
        micros=3,
        any_in=range(5, 9),
        any_out=range(1, 5),
        aliases={5 + at: 1 + at for at in range(4)},
    )
    input_grad, vec_grads_low = call_kernel(
        last_body,
        [full_of(tok_count, model_width), full_of(16, model_width)],
        units_in(3),
        "project_back",
        meta,
        vec,
        inputs[0],
        query_zero,
        rows_zero,
        middle_grad,
        packed,
        smem_count=1,
        micros=4,
        any_in=(6,),
    )
    vec_sum = jnp.concatenate(
        [vec_grads_low[0:2], vec_grads_mid[2:vec_rows], vec_grads_mid[0:2], vec_grads_up[2:vec_rows]]
    )
    if by_permutes:
        held[2], to_owner = lax.optimization_barrier((held[2], to_owner))
        owner_grad, vec_sum, owner_rows = sum_to_owner(
            *held, seq_index, shift, vec_sum, to_owner
        )
    else:
        owner_rows = [lax.all_to_all(to_owner, "seq", 0, 0, tiled=True)]
        for axis in ("opt", "seq"):
            for bit_at in range(lax.axis_size(axis).bit_length() - 1):
                vec_sum = vec_sum + partner(vec_sum, axis, bit_at)
        column_grads = lax.psum_scatter(
            jnp.concatenate(
                [jnp.concatenate(held[at : at + 2], axis=1) for at in (0, 2)]
            ),
            "opt",
            scatter_dimension=0,
            tiled=True,
        )
        column_grads = jnp.pad(column_grads, [(0, seq_count - own_slots), (0, 0), (0, 0)])
        owner_grad = lax.psum_scatter(column_grads, "seq", scatter_dimension=0, tiled=True)[0]
    step_rows, owner_stat, owner_basis = rotate_slot(row_at, owner_grad, owner_rows)
    home_rows = lax.all_to_all(step_rows, "seq", 0, 0, tiled=True)
    base_rows = renew_bases(seq_count, owner_stat, owner_basis)
    base_rows, home_rows = lax.optimization_barrier((base_rows, home_rows))
    base_rows = lax.all_to_all(base_rows, "seq", 0, 0, tiled=True)
    whole_shape = jax.ShapeDtypeStruct(masters.shape, jnp.float32)
    new_masters, new_first, new_second, new_stats = call_kernel(
        finish_body,
        [whole_shape, whole_shape, whole_shape, jax.ShapeDtypeStruct(stats.shape, jnp.float32)],
        [],
        "finish_slots",
        owners,
        masters,
        first_moment,
        second_moment,
        stats,
        home_rows,
        smem_count=1,
        micros=4,
    )
    (new_bases,) = call_kernel(
        place_body,
        [jax.ShapeDtypeStruct(bases.shape, jnp.float32)],
        [],
        "place_bases",
        owners,
        base_rows,
        smem_count=1,
    )
    grad_vecs = lax.dynamic_slice_in_dim(
        vec_sum.reshape(-1), (seq_index * opt_count + lax.axis_index("opt")) * vec_count, vec_count
    )
    new_vec_first = BETA_ONE * vec_first + (1.0 - BETA_ONE) * grad_vecs
    new_vec_second = BETA_TWO * vec_second + (1.0 - BETA_TWO) * grad_vecs * grad_vecs
    new_vectors = vec_master - RATE_VECTOR * (new_vec_first / (1.0 - BETA_ONE**STEP)) / (
        jnp.sqrt(new_vec_second / (1.0 - BETA_TWO**STEP)) + ADAM_EPS
    )
    return (
        outputs[None],
        input_grad[None],
        new_masters,
        new_first,
        new_second,
        new_bases,
        new_stats,
        new_vectors,
        new_vec_first,
        new_vec_second,
    )


def solution(mesh):
    placed = (
        P("opt", "seq", None),
        P("opt", "seq", None),
        P("opt", None),
        P(),
        P("opt", "seq", None),
        P("opt", "seq", None),
        P("opt", "seq", None),
        P("opt", None, "seq", None),
        P("opt", None, "seq", None),
        P(("seq", "opt")),
        P(("seq", "opt")),
        P(("seq", "opt")),
    )
    return jax.shard_map(
        per_device,
        mesh=mesh,
        in_specs=placed,
        out_specs=(
            P("opt", "seq", None),
            P("opt", "seq", None),
            P("opt", "seq", None),
            P("opt", "seq", None),
            P("opt", "seq", None),
            P("opt", None, "seq", None),
            P("opt", None, "seq", None),
            P(("seq", "opt")),
            P(("seq", "opt")),
            P(("seq", "opt")),
        ),
        check_vma=False,
    )
```

```python
import functools
import math

import jax
import jax.numpy as jnp
from jax import lax
from jax.experimental import pallas as pl
from jax.experimental.pallas import tpu as pltpu
from jax.sharding import PartitionSpec as P

HEADS = 8
FF = 2048
BLOCK = 16
LAYERS = 2
STEP = 10
MAX_LEN = 4096


HIGH = lax.Precision.HIGHEST
LN_TWO = math.log(2.0)
NEG_FILL = -1e30
NORM_EPS = 1e-05
ADAM_EPS = 1e-08
RATE_MATRIX = 0.03
RATE_VECTOR = 0.2
WEIGHT_DECAY = 0.01
BETA_ONE = 0.9
BETA_TWO = 0.95
BETA_STAT = 0.95

SUBLANES = 8
PANEL = 16
FLOPS_PER_US = 1_150_000_000
LANES = 128
UNIT_COUNT = 24
UNIT_OPT = 0
UNIT_ROW = UNIT_COUNT
UNIT_SLOT = 2 * UNIT_COUNT
DIAG = 128
VMEM_GRANT = 60 * 2**20
IN_VMEM = pl.BlockSpec(memory_space=pltpu.VMEM)
IN_SMEM = pl.BlockSpec(memory_space=pltpu.SMEM)
ANYWHERE = pl.BlockSpec(memory_space=pl.ANY)


def contract(left, right, left_dim, right_dim, precision=None):
    return lax.dot_general(
        left,
        right,
        (((left_dim,), (right_dim,)), ((), ())),
        precision=precision,
        preferred_element_type=jnp.float32,
    )


def split_two(values):
    high = values.astype(jnp.bfloat16)
    return (high, (values - high.astype(jnp.float32)).astype(jnp.bfloat16))


def wide_left(left, right_low, left_dim, right_dim):
    high, rest = split_two(left)
    return contract(high, right_low, left_dim, right_dim) + contract(
        rest, right_low, left_dim, right_dim
    )


def wide_right(left_low, right, left_dim, right_dim):
    high, rest = split_two(right)
    return contract(left_low, high, left_dim, right_dim) + contract(
        left_low, rest, left_dim, right_dim
    )


def call_kernel(
    body, out_shapes, scratch, name, *operands, smem_count=0, any_in=(), any_out=(), aliases=None,
    micros=2,
):
    def place(at, listed):
        return ANYWHERE if at in listed else IN_VMEM

    return pl.pallas_call(
        body,
        out_shape=out_shapes,
        in_specs=[
            IN_SMEM if at < smem_count else place(at, any_in) for at in range(len(operands))
        ],
        out_specs=[place(at, any_out) for at in range(len(out_shapes))],
        scratch_shapes=scratch,
        input_output_aliases=aliases or {},
        cost_estimate=pl.CostEstimate(
            flops=micros * FLOPS_PER_US, bytes_accessed=0, transcendentals=0
        ),
        compiler_params=pltpu.CompilerParams(vmem_limit_bytes=VMEM_GRANT),
        name=name,
    )(*operands)


def eliminate(panels, turn):
    rows, width = panels[0][0].shape
    row_at = lax.broadcasted_iota(jnp.int32, (SUBLANES, width), 0)

    def groups(values):
        return [values[low : low + SUBLANES] for low in range(0, rows, SUBLANES)]

    def spread_row(values, row):
        return jnp.broadcast_to(values[row : row + 1, :], values.shape)

    states = []
    for left, right in panels:
        turned = pltpu.roll(left, turn, 1)
        columns = [
            [jnp.broadcast_to(part, (SUBLANES, width)) for part in groups(turned[:, at : at + 1])]
            for at in range(rows)
        ]
        ones = [jnp.ones((SUBLANES, width), jnp.float32) for _ in range(rows // SUBLANES)]
        states.append((groups(left), groups(right), columns, ones))
    for at in range(rows):
        group_at, row = divmod(at, SUBLANES)
        for left, right, columns, pivots in states:
            pivot = spread_row(columns[at][group_at], row)
            inverse = pltpu.reciprocal(pivot, approx=False)
            pivots[group_at] = jnp.where(row_at == row, pivot, pivots[group_at])
            targets = [left, right] + columns[at + 1 :]
            given = [spread_row(target[group_at], row) for target in targets]
            for group in range(group_at, rows // SUBLANES):
                factor = columns[at][group] * inverse
                if group == group_at:
                    factor = jnp.where(row_at > row, factor, 0.0)
                for target, pivot_row in zip(targets, given):
                    target[group] = target[group] - factor * pivot_row
    results = []
    for left, right, _, pivots in states:
        scales = [lax.rsqrt(values) for values in pivots]
        results.append(
            tuple(
                jnp.concatenate([part * scale for part, scale in zip(parts, scales)], axis=0)
                for parts in (left, right)
            )
        )
    return results


def split_three(values):
    high = values.astype(jnp.bfloat16).astype(jnp.float32)
    rest = values - high
    middle = rest.astype(jnp.bfloat16).astype(jnp.float32)
    return (high, middle, rest - middle)


def thin_product(left, right):
    left_parts, right_parts = (split_three(left), split_three(right))
    pairs = ((0, 0), (0, 1), (1, 0), (1, 1), (0, 2), (2, 0))
    stacked_left = jnp.concatenate([left_parts[i] for i, _ in pairs], axis=0)
    stacked_right = jnp.concatenate([right_parts[j] for _, j in pairs], axis=0)
    return contract(stacked_left.astype(jnp.bfloat16), stacked_right.astype(jnp.bfloat16), 0, 0)


def factorize(grams, uppers, works, inverses):
    each = range(len(grams))
    size = grams[0].shape[0]
    eye = (
        lax.broadcasted_iota(jnp.int32, (DIAG, DIAG), 0)
        == lax.broadcasted_iota(jnp.int32, (DIAG, DIAG), 1)
    ).astype(jnp.float32)
    for low in range(0, size, DIAG):
        top = low + DIAG
        for m in each:
            works[m][:, 0:DIAG] = grams[m][low:top, low:top]
            works[m][:, DIAG:] = eye

        def panel(panel_at, carry):
            row = pl.multiple_of(panel_at * PANEL, PANEL)
            turn = lax.rem(DIAG - panel_at * PANEL, DIAG)
            panels = [
                (works[m][pl.ds(row, PANEL), 0:DIAG], works[m][pl.ds(row, PANEL), DIAG:])
                for m in each
            ]
            results = eliminate(panels, turn)
            updates = [
                thin_product(left, jnp.concatenate([left, right], axis=1))
                for left, right in results
            ]
            for m in each:
                inverses[m][low // DIAG, pl.ds(row, PANEL), :] = results[m][1]
            for m in each:
                works[m][...] = works[m][...] - updates[m]
            return carry

        lax.fori_loop(0, DIAG // PANEL, panel, 0)
        if top == size:
            break
        right_of = [contract(inverses[m][low // DIAG], grams[m][low:top, top:], 1, 0, HIGH) for m in each]
        for m in each:
            uppers[m][low:top, top:] = right_of[m]
        for other in range(top, size, DIAG):
            skip = other - top
            rest = [
                grams[m][other : other + DIAG, other:]
                - contract(right_of[m][:, skip : skip + DIAG], right_of[m][:, skip:], 0, 0, HIGH)
                for m in each
            ]
            for m in each:
                grams[m][other : other + DIAG, other:] = rest[m]


def renew_body(*refs):
    stat_ref, basis_ref, sent = refs[:3]
    scratch = refs[3:]
    count, size, _ = stat_ref.shape
    each = range(count)
    products, grams, uppers, works, inverses = (
        scratch[at : at + count] for at in range(0, 5 * count, count)
    )
    values = [wide_left(stat_ref[m], basis_ref[m], 1, 0) for m in each]
    for m in each:
        products[m][...] = values[m]
    for low in range(0, size, DIAG):
        values = [
            contract(products[m][:, low : low + DIAG], products[m][:, low:], 0, 0, HIGH)
            for m in each
        ]
        for m in each:
            grams[m][low : low + DIAG, low:] = values[m]
    factorize(grams, uppers, works, inverses)
    for low in range(0, size, DIAG):
        top = low + DIAG
        values = [products[m][:, low:top] for m in each]
        if low:
            values = [
                values[m]
                - contract(products[m][:, :low], uppers[m][:low, low:top], 1, 0, HIGH)
                for m in each
            ]
        values = [contract(values[m], inverses[m][low // DIAG], 1, 1, HIGH) for m in each]
        for m in each:
            products[m][:, low:top] = values[m]
    rows = sent.shape[2]
    for target in range(sent.shape[0]):
        for m in each:
            sent[target, m] = products[m][target * rows : (target + 1) * rows, :].astype(
                jnp.bfloat16
            )


def renew_bases(device_count, new_stat, basis_low):
    count, size, _ = new_stat.shape
    return call_kernel(
        renew_body,
        [jax.ShapeDtypeStruct((device_count, count, size // device_count, size), jnp.bfloat16)],
        [pltpu.VMEM((size, size), jnp.float32)] * (3 * count)
        + [pltpu.VMEM((DIAG, 2 * DIAG), jnp.float32)] * count
        + [pltpu.VMEM((size // DIAG, DIAG, DIAG), jnp.float32)] * count,
        "renew_bases",
        new_stat,
        basis_low,
        micros=40,
    )[0]


def pack_body(slot_ref, stats, bases, first, second, *packed):
    at = 0
    for part in packed:
        for target in range(part.shape[0]):
            slot = slot_ref[at]
            part[target, 0:2] = stats[slot].astype(jnp.bfloat16)
            part[target, 2:4] = bases[slot].astype(jnp.bfloat16)
            part[target, 4] = first[slot].astype(jnp.bfloat16)
            part[target, 5] = second[slot].astype(jnp.bfloat16)
            at += 1


def rotate_body(count, row_ref, grad_ref, *refs):
    given, (sent, stat_ref, basis_ref, whole, results) = (refs[:count], refs[count:])
    at = 0
    for part in given:
        pieces, _, rows, _ = part.shape
        for piece in range(pieces):
            row = pl.multiple_of(row_ref[at], 8)
            whole[:, pl.ds(row, rows), :] = part[piece].astype(jnp.float32)
            at += 1
    grad = grad_ref[...]
    left = whole[2].astype(jnp.bfloat16)
    right = whole[3].astype(jnp.bfloat16)
    basis_ref[0] = left
    basis_ref[1] = right
    results[0] = contract(grad, grad, 1, 1)
    results[1] = contract(grad, grad, 0, 0)
    stat_ref[0] = BETA_STAT * whole[0] + (1.0 - BETA_STAT) * results[0]
    stat_ref[1] = BETA_STAT * whole[1] + (1.0 - BETA_STAT) * results[1]
    rotated = wide_left(contract(left, grad, 0, 0), right, 1, 0)
    results[2] = rotated
    new_first = BETA_ONE * whole[4] + (1.0 - BETA_ONE) * rotated
    new_second = BETA_TWO * whole[5] + (1.0 - BETA_TWO) * rotated * rotated
    direction = (
        new_first
        / (1.0 - BETA_ONE**STEP)
        / (jnp.sqrt(new_second / (1.0 - BETA_TWO**STEP)) + ADAM_EPS)
    )
    results[3] = wide_right(left, wide_left(direction, right, 1, 1), 1, 0)
    for target in range(sent.shape[0]):
        sent[target] = results[:, target * rows : (target + 1) * rows, :].astype(jnp.bfloat16)


def rotate_slot(row_at, grad, owner_rows):
    size = grad.shape[0]
    return call_kernel(
        functools.partial(rotate_body, len(owner_rows)),
        [
            jax.ShapeDtypeStruct(
                (size // owner_rows[0].shape[2], 4) + owner_rows[0].shape[2:], jnp.bfloat16
            ),
            jax.ShapeDtypeStruct((2, size, size), jnp.float32),
            jax.ShapeDtypeStruct((2, size, size), jnp.bfloat16),
        ],
        [
            pltpu.VMEM((6, size, size), jnp.float32),
            pltpu.VMEM((4, size, size), jnp.float32),
        ],
        "rotate_slot",
        row_at,
        grad,
        *owner_rows,
        smem_count=1,
        micros=6,
    )


def finish_body(
    owner_ref, masters, first, second, stats, given, new_masters, new_first, new_second, new_stats
):
    for slot in range(masters.shape[0]):
        owner = owner_ref[slot]
        rotated = given[owner, 2].astype(jnp.float32)
        update = given[owner, 3].astype(jnp.float32)
        new_first[slot] = BETA_ONE * first[slot] + (1.0 - BETA_ONE) * rotated
        new_second[slot] = BETA_TWO * second[slot] + (1.0 - BETA_TWO) * rotated * rotated
        new_masters[slot] = masters[slot] - RATE_MATRIX * (update + WEIGHT_DECAY * masters[slot])
        new_stats[slot] = BETA_STAT * stats[slot] + (1.0 - BETA_STAT) * given[owner, 0:2].astype(
            jnp.float32
        )


def place_body(owner_ref, given, new_bases):
    for slot in range(new_bases.shape[0]):
        new_bases[slot] = given[owner_ref[slot]].astype(jnp.float32)


def add_low(left, right):
    return (left.astype(jnp.float32) + right.astype(jnp.float32)).astype(jnp.bfloat16)


def over_z(value, apart, owner_apart):
    pairs = []
    for at in range(32):
        z, y, core = (at >> 3, at >> 2 & 1, at & 1)
        if z ^ owner_apart != (0 if y ^ core else 3):
            pairs.append((at, at ^ apart << 3))
    return lax.ppermute(value, ("seq", "opt"), pairs)


def sum_to_owner(
    kept_upper, kept_lower, sent_upper, sent_lower, seq_index, shift, vec_sum, to_owner
):
    def beside(values, vec_sum, *exchanges):
        for axis, bit_at in exchanges:
            vec_sum = vec_sum + partner(vec_sum, axis, bit_at)
        return lax.optimization_barrier((values, vec_sum))

    _, row_count, width = kept_upper.shape
    z_count = kept_upper.shape[0] // 4
    shape = (2, 2, z_count, row_count, width)
    upper, came_upper = (kept_upper.reshape(shape), partner(sent_upper, "opt", 0).reshape(shape))
    lower, came_lower = (kept_lower.reshape(shape), partner(sent_lower, "opt", 0).reshape(shape))
    send_x = add_low(upper[1], came_upper[1])
    send_x, upper, came_upper = lax.optimization_barrier((send_x, upper, came_upper))
    by_x = partner(send_x, "opt", 1)
    send_y = add_low(lower[:, 1], came_lower[:, 1])
    send_y, lower, came_lower = lax.optimization_barrier((send_y, lower, came_lower))
    by_y = partner(send_y, "seq", 0)
    rows = [to_owner[0]] + [over_z(to_owner[at], at, at) for at in range(1, 4)]
    (by_x, rows[1], rows[2]), vec_sum = beside((by_x, rows[1], rows[2]), vec_sum, ("opt", 0))
    stay_x = add_low(upper[0], came_upper[0])
    stay_y = add_low(lower[:, 0], came_lower[:, 0])
    then_y = partner(add_low(stay_x[1], by_x[1]), "seq", 0)
    then_x = partner(add_low(stay_y[1], by_y[1]), "opt", 1)
    (then_y, rows[3]), vec_sum = beside((then_y, rows[3]), vec_sum, ("seq", 1))
    z_index = seq_index >> 1

    def both(apart):
        at = jnp.clip((z_index ^ apart) - shift, 0, z_count - 1)

        def pick(values):
            return lax.dynamic_index_in_dim(values, at, 0, keepdims=False)

        total_upper = (
            pick(stay_x[0]).astype(jnp.float32)
            + pick(by_x[0]).astype(jnp.float32)
            + pick(then_y).astype(jnp.float32)
        )
        total_lower = (
            pick(stay_y[0]).astype(jnp.float32)
            + pick(by_y[0]).astype(jnp.float32)
            + pick(then_x).astype(jnp.float32)
        )
        return jnp.concatenate([total_upper, total_lower]).astype(jnp.bfloat16)

    near_one = over_z(both(1), 1, 1)
    near_far = over_z(both(3), 1, 3)
    near_far, vec_sum = beside(near_far, vec_sum, ("seq", 2))
    last = over_z(add_low(both(2), near_far), 2, 2)
    last, vec_sum = beside(last, vec_sum, ("opt", 1), ("seq", 0))
    total = both(0).astype(jnp.float32) + near_one.astype(jnp.float32) + last.astype(jnp.float32)
    return (total.astype(jnp.bfloat16), vec_sum, rows)


def across(value, axis, apart):
    return lax.ppermute(value, axis, [(i, i ^ apart) for i in range(lax.axis_size(axis))])


def partner(value, axis, bit_at):
    return across(value, axis, 1 << bit_at)


def pair_mean(values):
    shaped = values.reshape((values.shape[0] // 2, 2) + values.shape[1:])
    return 0.5 * (shaped[:, 0] + shaped[:, 1])


def pair_spread(grads):
    return 0.5 * jnp.repeat(grads, 2, axis=0)


def sum_rows(values):
    return jnp.sum(values, axis=0, keepdims=True)


def norm_parts(values):
    centred = values - jnp.mean(values, axis=-1, keepdims=True)
    recip = lax.rsqrt(jnp.mean(centred * centred, axis=-1, keepdims=True) + NORM_EPS)
    return (centred * recip, recip)


def norm_back(grad, gain, normed, recip):
    scaled = grad * gain
    return recip * (
        scaled
        - jnp.mean(scaled, axis=-1, keepdims=True)
        - normed * jnp.mean(scaled * normed, axis=-1, keepdims=True)
    )


def half_matrix(shape, fine_dim):
    fine = lax.broadcasted_iota(jnp.int32, shape, fine_dim)
    coarse = lax.broadcasted_iota(jnp.int32, shape, 1 - fine_dim)
    return jnp.where(fine >> 1 == coarse, 0.5, 0.0).astype(jnp.bfloat16)


def pool(rows_low):
    count = rows_low.shape[0]
    return contract(half_matrix((count // 2, count), 1), rows_low, 1, 0).astype(jnp.bfloat16)


def spread(grads):
    count = grads.shape[0]
    return wide_right(half_matrix((2 * count, count), 0), grads, 1, 0)


def norm_cdf(values):
    return 0.5 * (1.0 + lax.erf(values * math.sqrt(0.5)))


def local_count(tok_count):
    return (tok_count // BLOCK).bit_length() - 1


def key_width(tok_count, tree_bits):
    rows = 2 * (tok_count - BLOCK) + BLOCK * tree_bits
    return -(-rows // LANES) * LANES


def score_offsets(tok_count, tree_bits, span_bits):
    token = jnp.arange(tok_count, dtype=jnp.int32)[:, None]
    parts = []
    for height in range(local_count(tok_count)):
        row = jnp.arange(tok_count >> height, dtype=jnp.int32)[None, :]
        apart = token // (BLOCK << height) ^ row // BLOCK
        counted = apart <= 1 if height == 0 else apart == 1
        parts.append(jnp.where(counted, height * LN_TWO, NEG_FILL))
    for bit_at in range(tree_bits):
        offset = (local_count(tok_count) + bit_at) * LN_TWO
        parts.append(
            jnp.broadcast_to(
                jnp.where(bit_at + 1 <= span_bits, offset, NEG_FILL), (tok_count, BLOCK)
            )
        )
    used = sum(part.shape[1] for part in parts)
    rest = key_width(tok_count, tree_bits) - used
    parts.append(jnp.full((tok_count, rest), NEG_FILL, jnp.float32))
    return jnp.concatenate(parts, axis=1).astype(jnp.float32)


def stack_keys(own_rows, far_rows):
    parts = [own_rows]
    for _ in range(local_count(own_rows.shape[0]) - 1):
        parts.append(pool(parts[-1]))
    parts = parts + far_rows
    rest = key_width(own_rows.shape[0], len(far_rows)) - sum(part.shape[0] for part in parts)
    if rest:
        parts.append(jnp.zeros((rest, own_rows.shape[1]), jnp.bfloat16))
    return jnp.concatenate(parts, axis=0)


def by_heads(pair):
    lane = lax.broadcasted_iota(jnp.int32, pair.shape, 1)
    zero = jnp.zeros_like(pair)
    first = lane < LANES // 2
    return jnp.concatenate([jnp.where(first, pair, zero), jnp.where(first, zero, pair)], axis=0)


def from_heads(both):
    count = both.shape[0] // 2
    lane = lax.broadcasted_iota(jnp.int32, (count, LANES), 1)
    return jnp.where(lane < LANES // 2, both[:count], both[count:])


def attend(qkv, stack, offsets, probs, mixed):
    width = qkv.shape[1] // 3
    score_scale = (width // HEADS) ** (-0.5)
    both_offsets = jnp.concatenate([offsets, offsets], axis=0)
    for pair_at in range(width // LANES):
        low, top = (pair_at * LANES, (pair_at + 1) * LANES)
        scores = (
            contract(by_heads(qkv[:, low:top]), stack[:, low:top], 1, 1) * score_scale
            + both_offsets
        )
        expo = jnp.exp(scores - jnp.max(scores, axis=1, keepdims=True))
        weights = expo * (1.0 / jnp.sum(expo, axis=1, keepdims=True))
        probs[pair_at] = weights
        result = contract(
            weights.astype(jnp.bfloat16), stack[:, width + low : width + top], 1, 0
        )
        mixed[:, low:top] = from_heads(result).astype(jnp.bfloat16)


def attend_back(qkv, stack, probs, mixed_grad, query_grad, key_grads, far_grads, all_grads):
    tok_count, width = mixed_grad.shape
    score_scale = (width // HEADS) ** (-0.5)
    for pair_at in range(width // LANES):
        low, top = (pair_at * LANES, (pair_at + 1) * LANES)
        queries = by_heads(qkv[:, low:top])
        grads = by_heads(mixed_grad[:, low:top])
        weights = probs[pair_at]
        prob_grad = contract(grads, stack[:, width + low : width + top], 1, 1)
        inner = jnp.sum(weights * prob_grad, axis=1, keepdims=True)
        score_grad = (weights * (prob_grad - inner)).astype(jnp.bfloat16)
        query_grad[:, low:top] = (
            from_heads(contract(score_grad, stack[:, low:top], 1, 0)) * score_scale
        ).astype(jnp.bfloat16)
        all_grads[:, low:top] = contract(score_grad, queries, 0, 0) * score_scale
        all_grads[:, width + low : width + top] = contract(
            weights.astype(jnp.bfloat16), grads, 0, 0
        )
    for far_at, far_grad in enumerate(far_grads):
        row = 2 * (tok_count - BLOCK) + BLOCK * far_at
        far_grad[...] = all_grads[row : row + BLOCK]
    folded = None
    for height in reversed(range(local_count(tok_count))):
        row = 2 * (tok_count - (tok_count >> height))
        own = all_grads[row : row + (tok_count >> height)]
        folded = own if folded is None else own + spread(folded)
    key_grads[...] = folded


class Units:
    def __init__(self, meta, packed, store, sems, units):
        self.store = store
        self.place = {unit: at for at, unit in enumerate(units)}
        self.waiting = {}
        rows = store.shape[2]
        for at, unit in enumerate(units):
            row = pl.multiple_of(meta[UNIT_ROW + unit], rows)
            copy = pltpu.make_async_copy(
                packed.at[:, meta[UNIT_OPT + unit], pl.ds(row, rows), :],
                store.at[at],
                sems.at[at],
            )
            copy.start()
            self.waiting[unit] = copy

    def __getitem__(self, unit):
        if unit in self.waiting:
            self.waiting.pop(unit).wait()
        width = self.store.shape[3]
        return self.store[self.place[unit]].reshape(width, width)


class Grads:
    def __init__(self, meta, *refs):
        self.meta, self.buffers, self.store, self.sems = (meta, refs[:4], refs[4], refs[5])
        self.copies = []

    def put(self, first_unit, left_low, right_low):
        product = contract(left_low, right_low, 0, 0).astype(jnp.bfloat16)
        width = self.store.shape[2]
        slots, rows, _ = self.buffers[0].shape
        for low in range(0, product.shape[0], width):
            for side in range(0, product.shape[1], width):
                at = len(self.copies) // 2
                self.store[at] = product[low : low + width, side : side + width]
                place = self.meta[UNIT_SLOT + first_unit + low // width + side // width]
                inner = jnp.where(place < slots, place, place - slots)
                for half in range(2):
                    keeping, sending = (
                        pltpu.make_async_copy(
                            self.store.at[at, pl.ds(half * rows, rows)],
                            target.at[inner],
                            self.sems.at[at, half],
                        )
                        for target in (self.buffers[half], self.buffers[2 + half])
                    )
                    pl.when(place < slots)(keeping.start)
                    pl.when(place >= slots)(sending.start)
                    self.copies.append(keeping)

    def finish(self):
        for copy in self.copies:
            copy.wait()


def project(hidden, units, first_unit, gain, bias, normed_ref, qkv_ref, near_ref):
    width = hidden.shape[1]
    normed, _ = norm_parts(hidden)
    normed_low = (normed * gain + bias).astype(jnp.bfloat16)
    normed_ref[...] = normed_low
    for part in range(3):
        qkv_ref[:, part * width : (part + 1) * width] = contract(
            normed_low, units[first_unit + part], 1, 0
        ).astype(jnp.bfloat16)
    near = qkv_ref[:, width:]
    for _ in range(local_count(near.shape[0])):
        near = pool(near)
    near_ref[...] = near


def feed_forward(middle, units, first_unit, vec, vec_at, normed_ref, slope_ref, act_ref):
    width = middle.shape[1]
    normed, _ = norm_parts(middle)
    normed_low = (normed * vec[vec_at + 2 : vec_at + 3] + vec[vec_at + 3 : vec_at + 4]).astype(
        jnp.bfloat16
    )
    normed_ref[...] = normed_low
    total = middle
    ff_blocks = FF // width
    for part in range(ff_blocks):
        low, top = (part * width, (part + 1) * width)
        row = vec_at + 4 + part
        pre = contract(normed_low, units[first_unit + 4 + part], 1, 0) + vec[row : row + 1]
        share = norm_cdf(pre)
        act = (pre * share).astype(jnp.bfloat16)
        slope_ref[:, low:top] = share + pre * jnp.exp(-0.5 * pre * pre) * (
            1.0 / math.sqrt(2.0 * math.pi)
        )
        act_ref[:, low:top] = act
        total = total + contract(act, units[first_unit + 4 + ff_blocks + part], 1, 0)
    row = vec_at + 4 + ff_blocks
    return total + vec[row : row + 1]


def feed_back(
    grad, middle, slope_ref, units, first_unit, vec, vec_at, vec_grads, at, pre_grad_ref
):
    width = middle.shape[1]
    ff_blocks = FF // width
    down_grad = grad.astype(jnp.bfloat16)
    normed_grad = jnp.zeros(middle.shape, jnp.float32)
    for part in range(ff_blocks):
        low, top = (part * width, (part + 1) * width)
        pre_grad = (
            contract(down_grad, units[first_unit + 4 + ff_blocks + part], 1, 1)
            * slope_ref[:, low:top]
        ).astype(jnp.bfloat16)
        pre_grad_ref[:, low:top] = pre_grad
        vec_grads[at + 2 + part : at + 3 + part] = sum_rows(pre_grad.astype(jnp.float32))
        normed_grad = normed_grad + contract(pre_grad, units[first_unit + 4 + part], 1, 1)
    row = at + 2 + ff_blocks
    vec_grads[row : row + 1] = sum_rows(grad)
    normed, recip = norm_parts(middle)
    vec_grads[at : at + 1] = sum_rows(normed_grad * normed)
    vec_grads[at + 1 : at + 2] = sum_rows(normed_grad)
    return grad + norm_back(normed_grad, vec[vec_at + 2 : vec_at + 3], normed, recip)


def with_near(key_grads, near):
    for _ in range(local_count(key_grads.shape[0])):
        near = spread(near)
    return (key_grads + near).astype(jnp.bfloat16)


def project_back(
    middle_grad, hidden, query_grad, rows_low, units, first_unit, vec, vec_at, vec_grads
):
    width = hidden.shape[1]
    normed_grad = contract(query_grad, units[first_unit], 1, 1)
    for part in range(2):
        normed_grad = normed_grad + contract(
            rows_low[:, part * width : (part + 1) * width], units[first_unit + 1 + part], 1, 1
        )
    normed, recip = norm_parts(hidden)
    vec_grads[0:1] = sum_rows(normed_grad * normed)
    vec_grads[1:2] = sum_rows(normed_grad)
    return middle_grad + norm_back(normed_grad, vec[vec_at : vec_at + 1], normed, recip)


def first_body(per_layer, meta, vec, inputs, packed, normed, qkv, near, store, sems):
    units = Units(meta, packed, store, sems, range(3))
    project(inputs[...].astype(jnp.float32), units, 0, vec[0:1], vec[1:2], normed, qkv, near)


def middle_body(per_layer, vec_rows, tree_bits, meta, vec, offsets, inputs, qkv, *refs):
    far, refs = (refs[:tree_bits], refs[tree_bits:])
    packed, probs_out, mixed, middle, normed_two, slope_out, act = refs[:7]
    hidden, normed, next_qkv, near, store, sems, probs, slope, out_sems = refs[7:]
    units = Units(meta, packed, store, sems, range(3, per_layer + 3))
    stack = stack_keys(qkv[:, mixed.shape[1] :], [ref[...] for ref in far])
    attend(qkv[...], stack, offsets[...], probs, mixed)
    probs_copy = pltpu.make_async_copy(probs, probs_out, out_sems.at[0])
    probs_copy.start()
    middle[...] = inputs[...].astype(jnp.float32) + contract(mixed[...], units[3], 1, 0)
    hidden[...] = feed_forward(middle[...], units, 0, vec, 0, normed_two, slope, act)
    slope_copy = pltpu.make_async_copy(slope, slope_out, out_sems.at[1])
    slope_copy.start()
    project(
        hidden[...], units, per_layer, vec[vec_rows : vec_rows + 1],
        vec[vec_rows + 1 : vec_rows + 2], normed, next_qkv, near,
    )
    probs_copy.wait()
    slope_copy.wait()


def turn_body(per_layer, vec_rows, tree_bits, meta, vec, offsets, cotangent, hidden, qkv, *refs):
    far, refs = (refs[:tree_bits], refs[tree_bits:])
    packed, outputs, mixed, normed_two, act = refs[:5]
    middle_grad, query_grad, key_grads, vec_grads, pre_grad, branch_low = refs[5:11]
    far_grads, refs = (refs[11 : 11 + tree_bits], refs[11 + tree_bits :])
    store, sems, probs, slope, all_grads = refs
    units = Units(meta, packed, store, sems, range(per_layer + 3, 2 * per_layer))
    stack = stack_keys(qkv[:, mixed.shape[1] :], [ref[...] for ref in far])
    attend(qkv[...], stack, offsets[...], probs, mixed)
    middle = hidden[...] + contract(mixed[...], units[per_layer + 3], 1, 0)
    outputs[...] = feed_forward(
        middle, units, per_layer, vec, vec_rows, normed_two, slope, act
    ).astype(jnp.bfloat16)
    vec_grads[...] = jnp.zeros_like(vec_grads)
    grad = feed_back(
        cotangent[...].astype(jnp.float32), middle, slope, units, per_layer, vec, vec_rows,
        vec_grads, 2, pre_grad,
    )
    middle_grad[...] = grad
    branch_grad = grad.astype(jnp.bfloat16)
    branch_low[...] = branch_grad
    mixed_grad = contract(branch_grad, units[per_layer + 3], 1, 1).astype(jnp.bfloat16)
    attend_back(
        qkv[...], stack, probs, mixed_grad, query_grad, key_grads, far_grads, all_grads
    )


def lower_body(per_layer, vec_rows, tree_bits, meta, vec, *refs):
    hidden, query_in, key_in, near_in, middle_in, middle, qkv = refs[:7]
    far, refs = (refs[7 : 7 + tree_bits], refs[7 + tree_bits :])
    probs_in, slope_in, packed, down_low, rows_low = refs[:5]
    middle_grad, query_grad, key_grads, vec_grads, pre_grad, branch_low = refs[5:11]
    far_grads, refs = (refs[11 : 11 + tree_bits], refs[11 + tree_bits :])
    store, sems, probs, slope, in_sems, all_grads = refs
    split = 4 + (per_layer - 4) // 2
    units = Units(
        meta, packed, store, sems,
        list(range(per_layer, per_layer + 3)) + list(range(split, per_layer))
        + list(range(3, split)),
    )
    slope_copy = pltpu.make_async_copy(slope_in, slope, in_sems.at[0])
    probs_copy = pltpu.make_async_copy(probs_in, probs, in_sems.at[1])
    slope_copy.start()
    probs_copy.start()
    vec_grads[...] = jnp.zeros_like(vec_grads)
    rows_low[...] = with_near(key_in[...], near_in[...])
    grad = project_back(
        middle_in[...], hidden[...], query_in[...], rows_low[...], units, per_layer, vec,
        vec_rows, vec_grads,
    )
    down_low[...] = grad.astype(jnp.bfloat16)
    slope_copy.wait()
    grad = feed_back(grad, middle[...], slope, units, 0, vec, 0, vec_grads, 2, pre_grad)
    middle_grad[...] = grad
    branch_grad = grad.astype(jnp.bfloat16)
    branch_low[...] = branch_grad
    mixed_grad = contract(branch_grad, units[3], 1, 1).astype(jnp.bfloat16)
    probs_copy.wait()
    stack = stack_keys(qkv[:, mixed_grad.shape[1] :], [ref[...] for ref in far])
    attend_back(
        qkv[...], stack, probs, mixed_grad, query_grad, key_grads, far_grads, all_grads
    )


def last_body(meta, vec, inputs, query_grad, rows_low, middle_in, packed, *refs):
    input_grad, vec_grads, store, sems = refs
    units = Units(meta, packed, store, sems, range(3))
    vec_grads[...] = jnp.zeros_like(vec_grads)
    input_grad[...] = project_back(
        middle_in[...], inputs[...].astype(jnp.float32), query_grad[...], rows_low[...], units, 0,
        vec, 0, vec_grads,
    )


def grads_body(pairs, array_count, held, meta, *refs):
    arrays, refs = (refs[:array_count], refs[array_count + held :])
    grads = Grads(meta, *refs)
    for first_unit, left, right in pairs:
        grads.put(first_unit, arrays[left][...], arrays[right][...])
    grads.finish()


def last_grads_body(meta, normed, query_grad, key_grads, near_grads, *refs):
    rows_low, *refs = refs[4:]
    grads = Grads(meta, *refs)
    grads.put(0, normed[...], query_grad[...])
    rows_low[...] = with_near(key_grads[...], near_grads[...])
    grads.put(1, normed[...], rows_low[...])
    grads.finish()


def pooled(rows_low):
    return pair_mean(rows_low.astype(jnp.float32)).astype(jnp.bfloat16)


def in_order(first, own, other):
    return jnp.where(first, jnp.concatenate([own, other]), jnp.concatenate([other, own]))


def coarse_up(own, seq_index, tree_bits):
    far_list = []
    if tree_bits == 3:
        far_list.append(partner(own, "seq", 0))
        own = pooled(in_order(seq_index & 1 == 0, own, far_list[0]))
        near, same, cross = (across(own, "seq", apart) for apart in (2, 4, 6))
        return far_list + [near, pooled(in_order(seq_index & 2 == 0, same, cross))]
    for bit_at in range(tree_bits):
        far = partner(own, "seq", bit_at)
        far_list.append(far)
        if bit_at + 1 < tree_bits:
            own = pooled(in_order(seq_index >> bit_at & 1 == 0, own, far))
    return far_list


def coarse_down(far_grads, seq_index):
    above = None
    if len(far_grads) == 3:
        wide = pair_spread(far_grads[2])
        first = seq_index & 2 == 0
        same = jnp.where(first, wide[:BLOCK], wide[BLOCK:]).astype(jnp.bfloat16)
        cross = jnp.where(first, wide[BLOCK:], wide[:BLOCK]).astype(jnp.bfloat16)
        above = (
            across(same, "seq", 4).astype(jnp.float32)
            + across(cross, "seq", 6).astype(jnp.float32)
            + across(far_grads[1].astype(jnp.bfloat16), "seq", 2).astype(jnp.float32)
        )
        far_grads = far_grads[:1]
    for bit_at in reversed(range(len(far_grads))):
        upper = seq_index >> bit_at & 1 == 1
        sent = far_grads[bit_at]
        own = 0.0
        if above is not None:
            wide = pair_spread(above)
            own = jnp.where(upper, wide[BLOCK:], wide[:BLOCK])
            sent = sent + jnp.where(upper, wide[:BLOCK], wide[BLOCK:])
        above = own + partner(sent.astype(jnp.bfloat16), "seq", bit_at).astype(jnp.float32)
    return above


def per_device(
    inputs,
    cotangent,
    seq_lengths,
    unit_slot,
    masters,
    first_moment,
    second_moment,
    bases,
    stats,
    vec_master,
    vec_first,
    vec_second,
):
    seq_count = lax.axis_size("seq")
    opt_count = lax.axis_size("opt")
    seq_index = lax.axis_index("seq")
    tok_count = inputs.shape[1]
    model_width = inputs.shape[2]
    own_slots = masters.shape[0]
    row_count = masters.shape[1]
    ff_blocks = FF // model_width
    per_layer = 4 + 2 * ff_blocks
    vec_width = 5 * model_width + FF
    long_devs = min(max(MAX_LEN // tok_count, 1), seq_count)
    tree_bits = long_devs.bit_length() - 1
    size = seq_count * row_count
    by_permutes = seq_count == 8 and opt_count == 4 and own_slots == 6
    slots = jnp.arange(own_slots, dtype=jnp.int32)
    def pack_slots(slots, counts):
        return call_kernel(
            pack_body,
            [
                jax.ShapeDtypeStruct((count, 6, row_count, model_width), jnp.bfloat16)
                for count in counts
            ],
            [],
            "pack_slots",
            slots,
            stats,
            bases,
            first_moment,
            second_moment,
            smem_count=1,
            micros=3,
        )

    if by_permutes:
        parity, core = (seq_index & 1, lax.axis_index("opt") & 1)
        shift = parity ^ core
        owners = 2 * ((slots >> 1) + ((slots & 1) ^ core)) + (slots & 1)
        half_slots = own_slots // 2
        pairs = 2 * jnp.arange(half_slots, dtype=jnp.int32)
        near, away = pack_slots(
            jnp.concatenate([pairs + parity, pairs + 1 - parity]), (half_slots, half_slots)
        )
        met = jnp.stack([near, partner(away, "seq", 0)], axis=1)
        z_index = seq_index >> 1
        to_owner = [
            lax.dynamic_index_in_dim(
                met, jnp.clip((z_index ^ apart) - shift, 0, half_slots - 1), 0, keepdims=False
            )
            for apart in range(4)
        ]
        row_at = jnp.stack(
            [
                (2 * (z_index ^ apart) + (parity ^ side)) * row_count
                for apart in range(4)
                for side in range(2)
            ]
        )
    else:
        owners = slots
        (to_owner,) = pack_slots(
            jnp.minimum(jnp.arange(seq_count, dtype=jnp.int32), own_slots - 1), (seq_count,)
        )
        row_at = jnp.arange(seq_count, dtype=jnp.int32) * row_count
    vec_count = vec_master.shape[0]
    own_rows = own_slots * row_count
    vec_low = vec_master.astype(jnp.bfloat16)
    for axis in ("opt", "seq"):
        for bit_at in range(lax.axis_size(axis).bit_length() - 1):
            other = partner(vec_low, axis, bit_at)
            vec_low = jnp.where(
                lax.axis_index(axis) >> bit_at & 1 == 1,
                jnp.concatenate([other, vec_low]),
                jnp.concatenate([vec_low, other]),
            )
    vec = vec_low.reshape(-1, model_width).astype(jnp.float32)
    gathered = lax.all_gather(
        masters.astype(jnp.bfloat16).reshape(1, own_rows, model_width),
        ("seq", "opt"),
        axis=0,
        tiled=True,
    )
    if row_count % 16 == 0:
        unit_rows = row_count
        packed = gathered.reshape(seq_count, opt_count, own_rows, model_width)
    else:
        unit_rows = size
        packed = (
            gathered.reshape(seq_count, opt_count, own_slots, row_count, model_width)
            .transpose(1, 2, 0, 3, 4)
            .reshape(1, opt_count, own_slots * size, model_width)
        )
    opt_index = lax.axis_index("opt")
    opt_at, slot_in = (unit_slot // own_slots, unit_slot % own_slots)
    if by_permutes:
        apart = opt_at ^ opt_index
        other = (apart & 1) * 4 + (apart >> 1) * 2 + ((slot_in ^ seq_index) & 1)
        place = other * (own_slots // 2) + (slot_in >> 1)
    else:
        place = unit_slot
    meta = jnp.concatenate([opt_at, slot_in * unit_rows, place]).astype(jnp.int32)
    span_bits = jnp.zeros((), jnp.int32)
    for bit_at in range(tree_bits + 1):
        start_dev = seq_index >> bit_at << bit_at
        span_bits = jnp.where(
            seq_lengths[0, start_dev] == tok_count * (1 << bit_at), bit_at, span_bits
        )
    offsets_in = score_offsets(tok_count, tree_bits, span_bits)
    width_in = offsets_in.shape[1]
    pair_count = model_width // LANES
    vec_rows = vec_width // model_width
    square = (model_width, model_width)

    def units_in(count):
        return [
            pltpu.VMEM((count, size // unit_rows, unit_rows, model_width), jnp.bfloat16),
            pltpu.SemaphoreType.DMA((count,)),
        ]

    def grads_out(count):
        return [pltpu.VMEM((count,) + square, jnp.bfloat16), pltpu.SemaphoreType.DMA((count, 2))]

    def low_of(*shape):
        return jax.ShapeDtypeStruct(shape, jnp.bfloat16)

    def full_of(*shape):
        return jax.ShapeDtypeStruct(shape, jnp.float32)

    projected = [
        low_of(tok_count, model_width),
        low_of(tok_count, 3 * model_width),
        low_of(BLOCK, 2 * model_width),
    ]
    attended = [
        full_of(pair_count, 2 * tok_count, width_in),
        low_of(tok_count, model_width),
    ]
    fed = [
        low_of(tok_count, model_width),
        full_of(tok_count, FF),
        low_of(tok_count, FF),
    ]
    back = [
        full_of(tok_count, model_width),
        low_of(tok_count, model_width),
        full_of(tok_count, 2 * model_width),
        full_of(16, model_width),
        low_of(tok_count, FF),
        low_of(tok_count, model_width),
    ] + [full_of(BLOCK, 2 * model_width)] * tree_bits
    all_grads = full_of(width_in, 2 * model_width)
    buffers = [low_of(UNIT_COUNT // 2, size // 2, model_width)] * 4
    ff_blocks = FF // model_width

    def in_vmem(shapes):
        return [pltpu.VMEM(shape.shape, shape.dtype) for shape in shapes]

    def unit_grads(name, held, pairs):
        arrays = []
        for _, *factors in pairs:
            arrays += [factor for factor in factors if not any(factor is one for one in arrays)]
        index = {id(array): at for at, array in enumerate(arrays)}
        count = sum(left.shape[1] * right.shape[1] for _, left, right in pairs) // model_width**2
        first = 1 + len(arrays)
        return call_kernel(
            functools.partial(
                grads_body,
                [(unit, index[id(left)], index[id(right)]) for unit, left, right in pairs],
                len(arrays),
                len(held),
            ),
            buffers,
            grads_out(count),
            name,
            meta,
            *arrays,
            *held,
            smem_count=1,
            micros=2,
            any_in=range(first, first + len(held)),
            any_out=range(4),
            aliases={first + at: at for at in range(len(held))},
        )

    packed, to_owner, offsets_in, vec, meta = lax.optimization_barrier(
        (packed, to_owner, offsets_in, vec, meta)
    )
    normed_zero, qkv_zero, near_zero = call_kernel(
        functools.partial(first_body, per_layer),
        projected,
        units_in(3),
        "project_first",
        meta,
        vec,
        inputs[0],
        packed,
        smem_count=1,
        micros=3,
        any_in=(3,),
    )
    far_zero = coarse_up(near_zero, seq_index, tree_bits)
    (
        probs, mixed, middle, normed_two, slope, act, hidden, normed_one, qkv_one, near_one,
    ) = call_kernel(
        functools.partial(middle_body, per_layer, vec_rows, tree_bits),
        attended + [full_of(tok_count, model_width)] + fed + [full_of(tok_count, model_width)]
        + projected,
        units_in(per_layer) + in_vmem([attended[0], fed[1]]) + [pltpu.SemaphoreType.DMA((2,))],
        "layer_first",
        meta,
        vec,
        offsets_in,
        inputs[0],
        qkv_zero,
        *far_zero,
        packed,
        smem_count=1,
        micros=7,
        any_in=(5 + tree_bits,),
        any_out=(0, 4),
    )
    far_one = coarse_up(near_one, seq_index, tree_bits)
    (
        outputs, mixed_one, normed_up, act_one, middle_grad, query_grad, key_grads, vec_grads_up,
        pre_grad, branch_low, *far_grads,
    ) = call_kernel(
        functools.partial(turn_body, per_layer, vec_rows, tree_bits),
        [low_of(tok_count, model_width), attended[1], fed[0], fed[2]] + back,
        units_in(per_layer - 3) + in_vmem([attended[0], fed[1], all_grads]),
        "layer_turn",
        meta,
        vec,
        offsets_in,
        cotangent[0],
        hidden,
        qkv_one,
        *far_one,
        packed,
        smem_count=1,
        micros=13,
        any_in=(6 + tree_bits,),
    )
    near_grads = coarse_down(far_grads, seq_index)
    held = unit_grads("down_grads", (), [(per_layer + 4 + ff_blocks, act_one, cotangent[0])])
    held = unit_grads(
        "up_grads",
        held,
        [(per_layer + 4, normed_up, pre_grad), (per_layer + 3, mixed_one, branch_low)],
    )
    (
        down_low, rows_low, middle_grad, query_zero, key_grads, vec_grads_mid, pre_grad,
        branch_low, *far_grads,
    ) = call_kernel(
        functools.partial(lower_body, per_layer, vec_rows, tree_bits),
        [low_of(tok_count, model_width), low_of(tok_count, 2 * model_width)] + back,
        units_in(per_layer)
        + in_vmem([attended[0], fed[1]])
        + [pltpu.SemaphoreType.DMA((2,))]
        + in_vmem([all_grads]),
        "layer_back",
        meta,
        vec,
        hidden,
        query_grad,
        key_grads,
        near_grads,
        middle_grad,
        middle,
        qkv_zero,
        *far_zero,
        probs,
        slope,
        packed,
        smem_count=1,
        micros=13,
        any_in=range(9 + tree_bits, 12 + tree_bits),
    )
    near_grads = coarse_down(far_grads, seq_index)
    held = unit_grads("down_grads_low", held, [(4 + ff_blocks, act, down_low)])
    held = unit_grads(
        "up_grads_low", held, [(4, normed_two, pre_grad), (3, mixed, branch_low)]
    )
    held = unit_grads(
        "project_grads",
        held,
        [(per_layer, normed_one, query_grad), (per_layer + 1, normed_one, rows_low)],
    )
    rows_zero, *held = call_kernel(
        last_grads_body,
        [low_of(tok_count, 2 * model_width)] + buffers,
        grads_out(3),
        "project_grads_low",
        meta,
        normed_zero,
        query_zero,
        key_grads,
        near_grads,
        *held,
        smem_count=1,
        micros=3,
        any_in=range(5, 9),
        any_out=range(1, 5),
        aliases={5 + at: 1 + at for at in range(4)},
    )
    input_grad, vec_grads_low = call_kernel(
        last_body,
        [full_of(tok_count, model_width), full_of(16, model_width)],
        units_in(3),
        "project_back",
        meta,
        vec,
        inputs[0],
        query_zero,
        rows_zero,
        middle_grad,
        packed,
        smem_count=1,
        micros=4,
        any_in=(6,),
    )
    vec_sum = jnp.concatenate(
        [vec_grads_low[0:2], vec_grads_mid[2:vec_rows], vec_grads_mid[0:2], vec_grads_up[2:vec_rows]]
    )
    if by_permutes:
        held[2], to_owner = lax.optimization_barrier((held[2], to_owner))
        owner_grad, vec_sum, owner_rows = sum_to_owner(
            *held, seq_index, shift, vec_sum, to_owner
        )
    else:
        owner_rows = [lax.all_to_all(to_owner, "seq", 0, 0, tiled=True)]
        for axis in ("opt", "seq"):
            for bit_at in range(lax.axis_size(axis).bit_length() - 1):
                vec_sum = vec_sum + partner(vec_sum, axis, bit_at)
        column_grads = lax.psum_scatter(
            jnp.concatenate(
                [jnp.concatenate(held[at : at + 2], axis=1) for at in (0, 2)]
            ),
            "opt",
            scatter_dimension=0,
            tiled=True,
        )
        column_grads = jnp.pad(column_grads, [(0, seq_count - own_slots), (0, 0), (0, 0)])
        owner_grad = lax.psum_scatter(column_grads, "seq", scatter_dimension=0, tiled=True)[0]
    step_rows, owner_stat, owner_basis = rotate_slot(row_at, owner_grad, owner_rows)
    home_rows = lax.all_to_all(step_rows, "seq", 0, 0, tiled=True)
    base_rows = renew_bases(seq_count, owner_stat, owner_basis)
    base_rows, home_rows = lax.optimization_barrier((base_rows, home_rows))
    base_rows = lax.all_to_all(base_rows, "seq", 0, 0, tiled=True)
    whole_shape = jax.ShapeDtypeStruct(masters.shape, jnp.float32)
    new_masters, new_first, new_second, new_stats = call_kernel(
        finish_body,
        [whole_shape, whole_shape, whole_shape, jax.ShapeDtypeStruct(stats.shape, jnp.float32)],
        [],
        "finish_slots",
        owners,
        masters,
        first_moment,
        second_moment,
        stats,
        home_rows,
        smem_count=1,
        micros=4,
    )
    (new_bases,) = call_kernel(
        place_body,
        [jax.ShapeDtypeStruct(bases.shape, jnp.float32)],
        [],
        "place_bases",
        owners,
        base_rows,
        smem_count=1,
    )
    grad_vecs = lax.dynamic_slice_in_dim(
        vec_sum.reshape(-1), (seq_index * opt_count + lax.axis_index("opt")) * vec_count, vec_count
    )
    new_vec_first = BETA_ONE * vec_first + (1.0 - BETA_ONE) * grad_vecs
    new_vec_second = BETA_TWO * vec_second + (1.0 - BETA_TWO) * grad_vecs * grad_vecs
    new_vectors = vec_master - RATE_VECTOR * (new_vec_first / (1.0 - BETA_ONE**STEP)) / (
        jnp.sqrt(new_vec_second / (1.0 - BETA_TWO**STEP)) + ADAM_EPS
    )
    return (
        outputs[None],
        input_grad[None],
        new_masters,
        new_first,
        new_second,
        new_bases,
        new_stats,
        new_vectors,
        new_vec_first,
        new_vec_second,
    )


def solution(mesh):
    placed = (
        P("opt", "seq", None),
        P("opt", "seq", None),
        P("opt", None),
        P(),
        P("opt", "seq", None),
        P("opt", "seq", None),
        P("opt", "seq", None),
        P("opt", None, "seq", None),
        P("opt", None, "seq", None),
        P(("seq", "opt")),
        P(("seq", "opt")),
        P(("seq", "opt")),
    )
    return jax.shard_map(
        per_device,
        mesh=mesh,
        in_specs=placed,
        out_specs=(
            P("opt", "seq", None),
            P("opt", "seq", None),
            P("opt", "seq", None),
            P("opt", "seq", None),
            P("opt", "seq", None),
            P("opt", None, "seq", None),
            P("opt", None, "seq", None),
            P(("seq", "opt")),
            P(("seq", "opt")),
            P(("seq", "opt")),
        ),
        check_vma=False,
    )
```

```python
import functools
import math

import jax
import jax.numpy as jnp
from jax import lax
from jax.experimental import pallas as pl
from jax.experimental.pallas import tpu as pltpu
from jax.sharding import PartitionSpec as P

HEADS = 8
FF = 2048
BLOCK = 16
LAYERS = 2
STEP = 10
MAX_LEN = 4096


HIGH = lax.Precision.HIGHEST
LN_TWO = math.log(2.0)
NEG_FILL = -1e30
NORM_EPS = 1e-05
ADAM_EPS = 1e-08
RATE_MATRIX = 0.03
RATE_VECTOR = 0.2
WEIGHT_DECAY = 0.01
BETA_ONE = 0.9
BETA_TWO = 0.95
BETA_STAT = 0.95

SUBLANES = 8
PANEL = 16
FLOPS_PER_US = 1_150_000_000
LANES = 128
UNIT_COUNT = 24
UNIT_OPT = 0
UNIT_ROW = UNIT_COUNT
UNIT_SLOT = 2 * UNIT_COUNT
DIAG = 128
VMEM_GRANT = 60 * 2**20
IN_VMEM = pl.BlockSpec(memory_space=pltpu.VMEM)
IN_SMEM = pl.BlockSpec(memory_space=pltpu.SMEM)
ANYWHERE = pl.BlockSpec(memory_space=pl.ANY)


def contract(left, right, left_dim, right_dim, precision=None):
    return lax.dot_general(
        left,
        right,
        (((left_dim,), (right_dim,)), ((), ())),
        precision=precision,
        preferred_element_type=jnp.float32,
    )


def split_two(values):
    high = values.astype(jnp.bfloat16)
    return (high, (values - high.astype(jnp.float32)).astype(jnp.bfloat16))


def wide_left(left, right_low, left_dim, right_dim):
    high, rest = split_two(left)
    return contract(high, right_low, left_dim, right_dim) + contract(
        rest, right_low, left_dim, right_dim
    )


def wide_right(left_low, right, left_dim, right_dim):
    high, rest = split_two(right)
    return contract(left_low, high, left_dim, right_dim) + contract(
        left_low, rest, left_dim, right_dim
    )


def call_kernel(
    body, out_shapes, scratch, name, *operands, smem_count=0, any_in=(), any_out=(), aliases=None,
    micros=2,
):
    def place(at, listed):
        return ANYWHERE if at in listed else IN_VMEM

    return pl.pallas_call(
        body,
        out_shape=out_shapes,
        in_specs=[
            IN_SMEM if at < smem_count else place(at, any_in) for at in range(len(operands))
        ],
        out_specs=[place(at, any_out) for at in range(len(out_shapes))],
        scratch_shapes=scratch,
        input_output_aliases=aliases or {},
        cost_estimate=pl.CostEstimate(
            flops=micros * FLOPS_PER_US, bytes_accessed=0, transcendentals=0
        ),
        compiler_params=pltpu.CompilerParams(vmem_limit_bytes=VMEM_GRANT),
        name=name,
    )(*operands)


def eliminate(panels, turn):
    rows, width = panels[0][0].shape
    row_at = lax.broadcasted_iota(jnp.int32, (SUBLANES, width), 0)

    def groups(values):
        return [values[low : low + SUBLANES] for low in range(0, rows, SUBLANES)]

    def spread_row(values, row):
        return jnp.broadcast_to(values[row : row + 1, :], values.shape)

    states = []
    for left, right in panels:
        turned = pltpu.roll(left, turn, 1)
        columns = [
            [jnp.broadcast_to(part, (SUBLANES, width)) for part in groups(turned[:, at : at + 1])]
            for at in range(rows)
        ]
        ones = [jnp.ones((SUBLANES, width), jnp.float32) for _ in range(rows // SUBLANES)]
        states.append((groups(left), groups(right), columns, ones))
    for at in range(rows):
        group_at, row = divmod(at, SUBLANES)
        for left, right, columns, pivots in states:
            pivot = spread_row(columns[at][group_at], row)
            inverse = pltpu.reciprocal(pivot, approx=False)
            pivots[group_at] = jnp.where(row_at == row, pivot, pivots[group_at])
            targets = [left, right] + columns[at + 1 :]
            given = [spread_row(target[group_at], row) for target in targets]
            for group in range(group_at, rows // SUBLANES):
                factor = columns[at][group] * inverse
                if group == group_at:
                    factor = jnp.where(row_at > row, factor, 0.0)
                for target, pivot_row in zip(targets, given):
                    target[group] = target[group] - factor * pivot_row
    results = []
    for left, right, _, pivots in states:
        scales = [lax.rsqrt(values) for values in pivots]
        results.append(
            tuple(
                jnp.concatenate([part * scale for part, scale in zip(parts, scales)], axis=0)
                for parts in (left, right)
            )
        )
    return results


def split_three(values):
    high = values.astype(jnp.bfloat16).astype(jnp.float32)
    rest = values - high
    middle = rest.astype(jnp.bfloat16).astype(jnp.float32)
    return (high, middle, rest - middle)


def thin_product(left, right):
    left_parts, right_parts = (split_three(left), split_three(right))
    pairs = ((0, 0), (0, 1), (1, 0), (1, 1), (0, 2), (2, 0))
    stacked_left = jnp.concatenate([left_parts[i] for i, _ in pairs], axis=0)
    stacked_right = jnp.concatenate([right_parts[j] for _, j in pairs], axis=0)
    return contract(stacked_left.astype(jnp.bfloat16), stacked_right.astype(jnp.bfloat16), 0, 0)


def factorize(grams, uppers, works, inverses, solve):
    each = range(len(grams))
    size = grams[0].shape[0]
    eye = (
        lax.broadcasted_iota(jnp.int32, (DIAG, DIAG), 0)
        == lax.broadcasted_iota(jnp.int32, (DIAG, DIAG), 1)
    ).astype(jnp.float32)
    for low in range(0, size, DIAG):
        top = low + DIAG
        for m in each:
            works[m][:, 0:DIAG] = grams[m][low:top, low:top]
            works[m][:, DIAG:] = eye

        def panel(panel_at, carry):
            row = pl.multiple_of(panel_at * PANEL, PANEL)
            turn = lax.rem(DIAG - panel_at * PANEL, DIAG)
            panels = [
                (works[m][pl.ds(row, PANEL), 0:DIAG], works[m][pl.ds(row, PANEL), DIAG:])
                for m in each
            ]
            if low:
                share = size * PANEL // DIAG
                rows = pl.ds(pl.multiple_of(panel_at * share, share), share)
                store, solved = solve(low - DIAG, rows)
            results = eliminate(panels, turn)
            updates = [
                thin_product(left, jnp.concatenate([left, right], axis=1))
                for left, right in results
            ]
            for m in each:
                inverses[m][low // DIAG, pl.ds(row, PANEL), :] = results[m][1]
            for m in each:
                works[m][...] = works[m][...] - updates[m]
            if low:
                store(solved)
            return carry

        lax.fori_loop(0, DIAG // PANEL, panel, 0)
        if top == size:
            break
        right_of = [contract(inverses[m][low // DIAG], grams[m][low:top, top:], 1, 0, HIGH) for m in each]
        for m in each:
            uppers[m][low:top, top:] = right_of[m]
        for other in range(top, size, DIAG):
            skip = other - top
            rest = [
                grams[m][other : other + DIAG, other:]
                - contract(right_of[m][:, skip : skip + DIAG], right_of[m][:, skip:], 0, 0, HIGH)
                for m in each
            ]
            for m in each:
                grams[m][other : other + DIAG, other:] = rest[m]


def renew_body(*refs):
    stat_ref, basis_ref, sent = refs[:3]
    scratch = refs[3:]
    count, size, _ = stat_ref.shape
    each = range(count)
    products, grams, uppers, works, inverses = (
        scratch[at : at + count] for at in range(0, 5 * count, count)
    )
    values = [wide_left(stat_ref[m], basis_ref[m], 1, 0) for m in each]
    for m in each:
        products[m][...] = values[m]
    for low in range(0, size, DIAG):
        values = [
            contract(products[m][:, low : low + DIAG], products[m][:, low:], 0, 0, HIGH)
            for m in each
        ]
        for m in each:
            grams[m][low : low + DIAG, low:] = values[m]

    def solve(low, rows):
        top = low + DIAG
        values = [products[m][rows, low:top] for m in each]
        if low:
            values = [
                values[m]
                - contract(products[m][rows, :low], uppers[m][:low, low:top], 1, 0, HIGH)
                for m in each
            ]
        values = [contract(values[m], inverses[m][low // DIAG], 1, 1, HIGH) for m in each]

        def store(solved):
            for m in each:
                products[m][rows, low:top] = solved[m]

        return (store, values)

    factorize(grams, uppers, works, inverses, solve)
    store, solved = solve(size - DIAG, slice(None))
    store(solved)
    rows = sent.shape[2]
    for target in range(sent.shape[0]):
        for m in each:
            sent[target, m] = products[m][target * rows : (target + 1) * rows, :].astype(
                jnp.bfloat16
            )


def renew_bases(device_count, new_stat, basis_low):
    count, size, _ = new_stat.shape
    return call_kernel(
        renew_body,
        [jax.ShapeDtypeStruct((device_count, count, size // device_count, size), jnp.bfloat16)],
        [pltpu.VMEM((size, size), jnp.float32)] * (3 * count)
        + [pltpu.VMEM((DIAG, 2 * DIAG), jnp.float32)] * count
        + [pltpu.VMEM((size // DIAG, DIAG, DIAG), jnp.float32)] * count,
        "renew_bases",
        new_stat,
        basis_low,
        micros=40,
    )[0]


KINDS = 5
EXTRA = 16


def pack_body(slot_ref, base_ref, stats, bases, first, second, *packed):
    _, _, rows, width = stats.shape
    pad = (packed[0].shape[1] - EXTRA) // KINDS
    row = base_ref[0] + lax.broadcasted_iota(jnp.int32, (rows, width), 0)
    column = lax.broadcasted_iota(jnp.int32, (rows, width), 1)
    at = 0
    for part in packed:
        for target in range(part.shape[0]):
            slot = slot_ref[at]
            right = stats[slot, 1]
            both = jnp.where(column >= row, stats[slot, 0], right)
            parts = (both, bases[slot, 0], bases[slot, 1], first[slot], second[slot])
            for kind, values in enumerate(parts):
                part[target, kind * pad : kind * pad + rows] = values.astype(jnp.bfloat16)
            diagonal = sum_rows(jnp.where(column == row, right, 0.0))
            part[target, KINDS * pad :] = jnp.broadcast_to(diagonal, (EXTRA, width)).astype(
                jnp.bfloat16
            )
            at += 1


def rotate_body(count, row_ref, grad_ref, *refs):
    given, (sent, stat_ref, basis_ref, whole, results) = (refs[:count], refs[count:])
    rows = sent.shape[2]
    pad = (given[0].shape[1] - EXTRA) // KINDS
    diagonal = jnp.zeros((1, whole.shape[2]), jnp.float32)
    at = 0
    for part in given:
        for piece in range(part.shape[0]):
            row = pl.multiple_of(row_ref[at], 8)
            for kind in range(KINDS):
                whole[kind, pl.ds(row, rows), :] = part[
                    piece, kind * pad : kind * pad + rows
                ].astype(jnp.float32)
            diagonal = diagonal + part[piece, KINDS * pad :].astype(jnp.float32)[0:1]
            at += 1
    both = whole[0]
    turned = both.T
    row = lax.broadcasted_iota(jnp.int32, both.shape, 0)
    column = lax.broadcasted_iota(jnp.int32, both.shape, 1)
    left_stat = jnp.where(column >= row, both, turned)
    right_stat = jnp.where(column < row, both, jnp.where(column > row, turned, diagonal))
    grad = grad_ref[...]
    left = whole[1].astype(jnp.bfloat16)
    right = whole[2].astype(jnp.bfloat16)
    basis_ref[0] = left
    basis_ref[1] = right
    results[0] = contract(grad, grad, 1, 1)
    results[1] = contract(grad, grad, 0, 0)
    stat_ref[0] = BETA_STAT * left_stat + (1.0 - BETA_STAT) * results[0]
    stat_ref[1] = BETA_STAT * right_stat + (1.0 - BETA_STAT) * results[1]
    rotated = wide_left(contract(left, grad, 0, 0), right, 1, 0)
    results[2] = rotated
    new_first = BETA_ONE * whole[3] + (1.0 - BETA_ONE) * rotated
    new_second = BETA_TWO * whole[4] + (1.0 - BETA_TWO) * rotated * rotated
    direction = (
        new_first
        / (1.0 - BETA_ONE**STEP)
        / (jnp.sqrt(new_second / (1.0 - BETA_TWO**STEP)) + ADAM_EPS)
    )
    results[3] = wide_right(left, wide_left(direction, right, 1, 1), 1, 0)
    for target in range(sent.shape[0]):
        sent[target] = results[:, target * rows : (target + 1) * rows, :].astype(jnp.bfloat16)


def rotate_slot(row_at, grad, owner_rows):
    size = grad.shape[0]
    return call_kernel(
        functools.partial(rotate_body, len(owner_rows)),
        [
            jax.ShapeDtypeStruct(
                (row_at.shape[0], 4, size // row_at.shape[0], size), jnp.bfloat16
            ),
            jax.ShapeDtypeStruct((2, size, size), jnp.float32),
            jax.ShapeDtypeStruct((2, size, size), jnp.bfloat16),
        ],
        [
            pltpu.VMEM((KINDS, size, size), jnp.float32),
            pltpu.VMEM((4, size, size), jnp.float32),
        ],
        "rotate_slot",
        row_at,
        grad,
        *owner_rows,
        smem_count=1,
        micros=6,
    )


def finish_body(
    owner_ref, masters, first, second, stats, given, new_masters, new_first, new_second, new_stats
):
    for slot in range(masters.shape[0]):
        owner = owner_ref[slot]
        rotated = given[owner, 2].astype(jnp.float32)
        update = given[owner, 3].astype(jnp.float32)
        new_first[slot] = BETA_ONE * first[slot] + (1.0 - BETA_ONE) * rotated
        new_second[slot] = BETA_TWO * second[slot] + (1.0 - BETA_TWO) * rotated * rotated
        new_masters[slot] = masters[slot] - RATE_MATRIX * (update + WEIGHT_DECAY * masters[slot])
        new_stats[slot] = BETA_STAT * stats[slot] + (1.0 - BETA_STAT) * given[owner, 0:2].astype(
            jnp.float32
        )


def place_body(owner_ref, given, new_bases):
    for slot in range(new_bases.shape[0]):
        new_bases[slot] = given[owner_ref[slot]].astype(jnp.float32)


def add_low(left, right):
    return (left.astype(jnp.float32) + right.astype(jnp.float32)).astype(jnp.bfloat16)


def over_z(value, apart, owner_apart):
    pairs = []
    for at in range(32):
        z, y, core = (at >> 3, at >> 2 & 1, at & 1)
        if z ^ owner_apart != (0 if y ^ core else 3):
            pairs.append((at, at ^ apart << 3))
    return lax.ppermute(value, ("seq", "opt"), pairs)


def sum_to_owner(
    kept_upper, kept_lower, sent_upper, sent_lower, seq_index, shift, vec_sum, to_owner
):
    def beside(values, vec_sum, *exchanges):
        for axis, bit_at in exchanges:
            vec_sum = vec_sum + partner(vec_sum, axis, bit_at)
        return lax.optimization_barrier((values, vec_sum))

    _, row_count, width = kept_upper.shape
    z_count = kept_upper.shape[0] // 4
    shape = (2, 2, z_count, row_count, width)
    upper, came_upper = (kept_upper.reshape(shape), partner(sent_upper, "opt", 0).reshape(shape))
    lower, came_lower = (kept_lower.reshape(shape), partner(sent_lower, "opt", 0).reshape(shape))
    send_x = add_low(upper[1], came_upper[1])
    send_x, upper, came_upper = lax.optimization_barrier((send_x, upper, came_upper))
    by_x = partner(send_x, "opt", 1)
    send_y = add_low(lower[:, 1], came_lower[:, 1])
    send_y, lower, came_lower = lax.optimization_barrier((send_y, lower, came_lower))
    by_y = partner(send_y, "seq", 0)
    rows = [to_owner[0]] + [over_z(to_owner[at], at, at) for at in range(1, 4)]
    (by_x, rows[1], rows[2]), vec_sum = beside((by_x, rows[1], rows[2]), vec_sum, ("opt", 0))
    stay_x = add_low(upper[0], came_upper[0])
    stay_y = add_low(lower[:, 0], came_lower[:, 0])
    then_y = partner(add_low(stay_x[1], by_x[1]), "seq", 0)
    then_x = partner(add_low(stay_y[1], by_y[1]), "opt", 1)
    (then_y, rows[3]), vec_sum = beside((then_y, rows[3]), vec_sum, ("seq", 1))
    z_index = seq_index >> 1

    def both(apart):
        at = jnp.clip((z_index ^ apart) - shift, 0, z_count - 1)

        def pick(values):
            return lax.dynamic_index_in_dim(values, at, 0, keepdims=False)

        total_upper = (
            pick(stay_x[0]).astype(jnp.float32)
            + pick(by_x[0]).astype(jnp.float32)
            + pick(then_y).astype(jnp.float32)
        )
        total_lower = (
            pick(stay_y[0]).astype(jnp.float32)
            + pick(by_y[0]).astype(jnp.float32)
            + pick(then_x).astype(jnp.float32)
        )
        return jnp.concatenate([total_upper, total_lower]).astype(jnp.bfloat16)

    near_one = over_z(both(1), 1, 1)
    near_far = over_z(both(3), 1, 3)
    near_far, vec_sum = beside(near_far, vec_sum, ("seq", 2))
    last = over_z(add_low(both(2), near_far), 2, 2)
    last, vec_sum = beside(last, vec_sum, ("opt", 1), ("seq", 0))
    total = both(0).astype(jnp.float32) + near_one.astype(jnp.float32) + last.astype(jnp.float32)
    return (total.astype(jnp.bfloat16), vec_sum, rows)


def across(value, axis, apart):
    return lax.ppermute(value, axis, [(i, i ^ apart) for i in range(lax.axis_size(axis))])


def partner(value, axis, bit_at):
    return across(value, axis, 1 << bit_at)


def pair_mean(values):
    shaped = values.reshape((values.shape[0] // 2, 2) + values.shape[1:])
    return 0.5 * (shaped[:, 0] + shaped[:, 1])


def pair_spread(grads):
    return 0.5 * jnp.repeat(grads, 2, axis=0)


def sum_rows(values):
    return jnp.sum(values, axis=0, keepdims=True)


def norm_parts(values):
    centred = values - jnp.mean(values, axis=-1, keepdims=True)
    recip = lax.rsqrt(jnp.mean(centred * centred, axis=-1, keepdims=True) + NORM_EPS)
    return (centred * recip, recip)


def norm_back(grad, gain, normed, recip):
    scaled = grad * gain
    return recip * (
        scaled
        - jnp.mean(scaled, axis=-1, keepdims=True)
        - normed * jnp.mean(scaled * normed, axis=-1, keepdims=True)
    )


def half_matrix(shape, fine_dim):
    fine = lax.broadcasted_iota(jnp.int32, shape, fine_dim)
    coarse = lax.broadcasted_iota(jnp.int32, shape, 1 - fine_dim)
    return jnp.where(fine >> 1 == coarse, 0.5, 0.0).astype(jnp.bfloat16)


def pool(rows_low):
    count = rows_low.shape[0]
    return contract(half_matrix((count // 2, count), 1), rows_low, 1, 0).astype(jnp.bfloat16)


def spread(grads):
    count = grads.shape[0]
    return wide_right(half_matrix((2 * count, count), 0), grads, 1, 0)


def norm_cdf(values):
    return 0.5 * (1.0 + lax.erf(values * math.sqrt(0.5)))


def local_count(tok_count):
    return (tok_count // BLOCK).bit_length() - 1


def key_width(tok_count, tree_bits):
    rows = 2 * (tok_count - BLOCK) + BLOCK * tree_bits
    return -(-rows // LANES) * LANES


def score_offsets(tok_count, tree_bits, span_bits):
    token = jnp.arange(tok_count, dtype=jnp.int32)[:, None]
    parts = []
    for height in range(local_count(tok_count)):
        row = jnp.arange(tok_count >> height, dtype=jnp.int32)[None, :]
        apart = token // (BLOCK << height) ^ row // BLOCK
        counted = apart <= 1 if height == 0 else apart == 1
        parts.append(jnp.where(counted, height * LN_TWO, NEG_FILL))
    for bit_at in range(tree_bits):
        offset = (local_count(tok_count) + bit_at) * LN_TWO
        parts.append(
            jnp.broadcast_to(
                jnp.where(bit_at + 1 <= span_bits, offset, NEG_FILL), (tok_count, BLOCK)
            )
        )
    used = sum(part.shape[1] for part in parts)
    rest = key_width(tok_count, tree_bits) - used
    parts.append(jnp.full((tok_count, rest), NEG_FILL, jnp.float32))
    return jnp.concatenate(parts, axis=1).astype(jnp.float32)


def stack_keys(own_rows, far_rows):
    parts = [own_rows]
    for _ in range(local_count(own_rows.shape[0]) - 1):
        parts.append(pool(parts[-1]))
    parts = parts + far_rows
    rest = key_width(own_rows.shape[0], len(far_rows)) - sum(part.shape[0] for part in parts)
    if rest:
        parts.append(jnp.zeros((rest, own_rows.shape[1]), jnp.bfloat16))
    return jnp.concatenate(parts, axis=0)


def by_heads(pair):
    lane = lax.broadcasted_iota(jnp.int32, pair.shape, 1)
    zero = jnp.zeros_like(pair)
    first = lane < LANES // 2
    return jnp.concatenate([jnp.where(first, pair, zero), jnp.where(first, zero, pair)], axis=0)


def from_heads(both):
    count = both.shape[0] // 2
    lane = lax.broadcasted_iota(jnp.int32, (count, LANES), 1)
    return jnp.where(lane < LANES // 2, both[:count], both[count:])


def attend(qkv, stack, offsets, probs, mixed):
    width = qkv.shape[1] // 3
    score_scale = (width // HEADS) ** (-0.5)
    both_offsets = jnp.concatenate([offsets, offsets], axis=0)
    for pair_at in range(width // LANES):
        low, top = (pair_at * LANES, (pair_at + 1) * LANES)
        scores = (
            contract(by_heads(qkv[:, low:top]), stack[:, low:top], 1, 1) * score_scale
            + both_offsets
        )
        expo = jnp.exp(scores - jnp.max(scores, axis=1, keepdims=True))
        weights = expo * (1.0 / jnp.sum(expo, axis=1, keepdims=True))
        probs[pair_at] = weights
        result = contract(
            weights.astype(jnp.bfloat16), stack[:, width + low : width + top], 1, 0
        )
        mixed[:, low:top] = from_heads(result).astype(jnp.bfloat16)


def attend_back(qkv, stack, probs, mixed_grad, query_grad, key_grads, far_grads, all_grads):
    tok_count, width = mixed_grad.shape
    score_scale = (width // HEADS) ** (-0.5)
    for pair_at in range(width // LANES):
        low, top = (pair_at * LANES, (pair_at + 1) * LANES)
        queries = by_heads(qkv[:, low:top])
        grads = by_heads(mixed_grad[:, low:top])
        weights = probs[pair_at]
        prob_grad = contract(grads, stack[:, width + low : width + top], 1, 1)
        inner = jnp.sum(weights * prob_grad, axis=1, keepdims=True)
        score_grad = (weights * (prob_grad - inner)).astype(jnp.bfloat16)
        query_grad[:, low:top] = (
            from_heads(contract(score_grad, stack[:, low:top], 1, 0)) * score_scale
        ).astype(jnp.bfloat16)
        all_grads[:, low:top] = contract(score_grad, queries, 0, 0) * score_scale
        all_grads[:, width + low : width + top] = contract(
            weights.astype(jnp.bfloat16), grads, 0, 0
        )
    for far_at, far_grad in enumerate(far_grads):
        row = 2 * (tok_count - BLOCK) + BLOCK * far_at
        far_grad[...] = all_grads[row : row + BLOCK]
    folded = None
    for height in reversed(range(local_count(tok_count))):
        row = 2 * (tok_count - (tok_count >> height))
        own = all_grads[row : row + (tok_count >> height)]
        folded = own if folded is None else own + spread(folded)
    key_grads[...] = folded


class Units:
    def __init__(self, meta, packed, store, sems, units):
        self.store = store
        self.place = {unit: at for at, unit in enumerate(units)}
        self.waiting = {}
        rows = store.shape[2]
        for at, unit in enumerate(units):
            row = pl.multiple_of(meta[UNIT_ROW + unit], rows)
            copy = pltpu.make_async_copy(
                packed.at[:, meta[UNIT_OPT + unit], pl.ds(row, rows), :],
                store.at[at],
                sems.at[at],
            )
            copy.start()
            self.waiting[unit] = copy

    def __getitem__(self, unit):
        if unit in self.waiting:
            self.waiting.pop(unit).wait()
        width = self.store.shape[3]
        return self.store[self.place[unit]].reshape(width, width)


class Grads:
    def __init__(self, meta, *refs):
        self.meta, self.buffers, self.store, self.sems = (meta, refs[:4], refs[4], refs[5])
        self.copies = []

    def put(self, first_unit, left_low, right_low):
        product = contract(left_low, right_low, 0, 0).astype(jnp.bfloat16)
        width = self.store.shape[2]
        slots, rows, _ = self.buffers[0].shape
        for low in range(0, product.shape[0], width):
            for side in range(0, product.shape[1], width):
                at = len(self.copies) // 2
                self.store[at] = product[low : low + width, side : side + width]
                place = self.meta[UNIT_SLOT + first_unit + low // width + side // width]
                inner = jnp.where(place < slots, place, place - slots)
                for half in range(2):
                    keeping, sending = (
                        pltpu.make_async_copy(
                            self.store.at[at, pl.ds(half * rows, rows)],
                            target.at[inner],
                            self.sems.at[at, half],
                        )
                        for target in (self.buffers[half], self.buffers[2 + half])
                    )
                    pl.when(place < slots)(keeping.start)
                    pl.when(place >= slots)(sending.start)
                    self.copies.append(keeping)

    def finish(self):
        for copy in self.copies:
            copy.wait()


def project(hidden, units, first_unit, gain, bias, normed_ref, qkv_ref, near_ref):
    width = hidden.shape[1]
    normed, _ = norm_parts(hidden)
    normed_low = (normed * gain + bias).astype(jnp.bfloat16)
    normed_ref[...] = normed_low
    for part in range(3):
        qkv_ref[:, part * width : (part + 1) * width] = contract(
            normed_low, units[first_unit + part], 1, 0
        ).astype(jnp.bfloat16)
    near = qkv_ref[:, width:]
    for _ in range(local_count(near.shape[0])):
        near = pool(near)
    near_ref[...] = near


def feed_forward(middle, units, first_unit, vec, vec_at, normed_ref, slope_ref, act_ref):
    width = middle.shape[1]
    normed, _ = norm_parts(middle)
    normed_low = (normed * vec[vec_at + 2 : vec_at + 3] + vec[vec_at + 3 : vec_at + 4]).astype(
        jnp.bfloat16
    )
    normed_ref[...] = normed_low
    total = middle
    ff_blocks = FF // width
    for part in range(ff_blocks):
        low, top = (part * width, (part + 1) * width)
        row = vec_at + 4 + part
        pre = contract(normed_low, units[first_unit + 4 + part], 1, 0) + vec[row : row + 1]
        share = norm_cdf(pre)
        act = (pre * share).astype(jnp.bfloat16)
        slope_ref[:, low:top] = share + pre * jnp.exp(-0.5 * pre * pre) * (
            1.0 / math.sqrt(2.0 * math.pi)
        )
        act_ref[:, low:top] = act
        total = total + contract(act, units[first_unit + 4 + ff_blocks + part], 1, 0)
    row = vec_at + 4 + ff_blocks
    return total + vec[row : row + 1]


def feed_back(
    grad, middle, slope_ref, units, first_unit, vec, vec_at, vec_grads, at, pre_grad_ref
):
    width = middle.shape[1]
    ff_blocks = FF // width
    down_grad = grad.astype(jnp.bfloat16)
    normed_grad = jnp.zeros(middle.shape, jnp.float32)
    for part in range(ff_blocks):
        low, top = (part * width, (part + 1) * width)
        pre_grad = (
            contract(down_grad, units[first_unit + 4 + ff_blocks + part], 1, 1)
            * slope_ref[:, low:top]
        ).astype(jnp.bfloat16)
        pre_grad_ref[:, low:top] = pre_grad
        vec_grads[at + 2 + part : at + 3 + part] = sum_rows(pre_grad.astype(jnp.float32))
        normed_grad = normed_grad + contract(pre_grad, units[first_unit + 4 + part], 1, 1)
    row = at + 2 + ff_blocks
    vec_grads[row : row + 1] = sum_rows(grad)
    normed, recip = norm_parts(middle)
    vec_grads[at : at + 1] = sum_rows(normed_grad * normed)
    vec_grads[at + 1 : at + 2] = sum_rows(normed_grad)
    return grad + norm_back(normed_grad, vec[vec_at + 2 : vec_at + 3], normed, recip)


def with_near(key_grads, near):
    for _ in range(local_count(key_grads.shape[0])):
        near = spread(near)
    return (key_grads + near).astype(jnp.bfloat16)


def project_back(
    middle_grad, hidden, query_grad, rows_low, units, first_unit, vec, vec_at, vec_grads
):
    width = hidden.shape[1]
    normed_grad = contract(query_grad, units[first_unit], 1, 1)
    for part in range(2):
        normed_grad = normed_grad + contract(
            rows_low[:, part * width : (part + 1) * width], units[first_unit + 1 + part], 1, 1
        )
    normed, recip = norm_parts(hidden)
    vec_grads[0:1] = sum_rows(normed_grad * normed)
    vec_grads[1:2] = sum_rows(normed_grad)
    return middle_grad + norm_back(normed_grad, vec[vec_at : vec_at + 1], normed, recip)


def first_body(per_layer, meta, vec, inputs, packed, normed, qkv, near, store, sems):
    units = Units(meta, packed, store, sems, range(3))
    project(inputs[...].astype(jnp.float32), units, 0, vec[0:1], vec[1:2], normed, qkv, near)


def middle_body(per_layer, vec_rows, tree_bits, meta, vec, offsets, inputs, qkv, *refs):
    far, refs = (refs[:tree_bits], refs[tree_bits:])
    packed, probs_out, mixed, middle, normed_two, slope_out, act = refs[:7]
    hidden, normed, next_qkv, near, store, sems, probs, slope, out_sems = refs[7:]
    units = Units(meta, packed, store, sems, range(3, per_layer + 3))
    stack = stack_keys(qkv[:, mixed.shape[1] :], [ref[...] for ref in far])
    attend(qkv[...], stack, offsets[...], probs, mixed)
    probs_copy = pltpu.make_async_copy(probs, probs_out, out_sems.at[0])
    probs_copy.start()
    middle[...] = inputs[...].astype(jnp.float32) + contract(mixed[...], units[3], 1, 0)
    hidden[...] = feed_forward(middle[...], units, 0, vec, 0, normed_two, slope, act)
    slope_copy = pltpu.make_async_copy(slope, slope_out, out_sems.at[1])
    slope_copy.start()
    project(
        hidden[...], units, per_layer, vec[vec_rows : vec_rows + 1],
        vec[vec_rows + 1 : vec_rows + 2], normed, next_qkv, near,
    )
    probs_copy.wait()
    slope_copy.wait()


def turn_body(per_layer, vec_rows, tree_bits, meta, vec, offsets, cotangent, hidden, qkv, *refs):
    far, refs = (refs[:tree_bits], refs[tree_bits:])
    packed, outputs, mixed, normed_two, act = refs[:5]
    middle_grad, query_grad, key_grads, vec_grads, pre_grad, branch_low = refs[5:11]
    far_grads, refs = (refs[11 : 11 + tree_bits], refs[11 + tree_bits :])
    store, sems, probs, slope, all_grads = refs
    units = Units(meta, packed, store, sems, range(per_layer + 3, 2 * per_layer))
    stack = stack_keys(qkv[:, mixed.shape[1] :], [ref[...] for ref in far])
    attend(qkv[...], stack, offsets[...], probs, mixed)
    middle = hidden[...] + contract(mixed[...], units[per_layer + 3], 1, 0)
    outputs[...] = feed_forward(
        middle, units, per_layer, vec, vec_rows, normed_two, slope, act
    ).astype(jnp.bfloat16)
    vec_grads[...] = jnp.zeros_like(vec_grads)
    grad = feed_back(
        cotangent[...].astype(jnp.float32), middle, slope, units, per_layer, vec, vec_rows,
        vec_grads, 2, pre_grad,
    )
    middle_grad[...] = grad
    branch_grad = grad.astype(jnp.bfloat16)
    branch_low[...] = branch_grad
    mixed_grad = contract(branch_grad, units[per_layer + 3], 1, 1).astype(jnp.bfloat16)
    attend_back(
        qkv[...], stack, probs, mixed_grad, query_grad, key_grads, far_grads, all_grads
    )


def lower_body(per_layer, vec_rows, tree_bits, meta, vec, *refs):
    hidden, query_in, key_in, near_in, middle_in, middle, qkv = refs[:7]
    far, refs = (refs[7 : 7 + tree_bits], refs[7 + tree_bits :])
    probs_in, slope_in, packed, down_low, rows_low = refs[:5]
    middle_grad, query_grad, key_grads, vec_grads, pre_grad, branch_low = refs[5:11]
    far_grads, refs = (refs[11 : 11 + tree_bits], refs[11 + tree_bits :])
    store, sems, probs, slope, in_sems, all_grads = refs
    split = 4 + (per_layer - 4) // 2
    units = Units(
        meta, packed, store, sems,
        list(range(per_layer, per_layer + 3)) + list(range(split, per_layer))
        + list(range(3, split)),
    )
    slope_copy = pltpu.make_async_copy(slope_in, slope, in_sems.at[0])
    probs_copy = pltpu.make_async_copy(probs_in, probs, in_sems.at[1])
    slope_copy.start()
    probs_copy.start()
    vec_grads[...] = jnp.zeros_like(vec_grads)
    rows_low[...] = with_near(key_in[...], near_in[...])
    grad = project_back(
        middle_in[...], hidden[...], query_in[...], rows_low[...], units, per_layer, vec,
        vec_rows, vec_grads,
    )
    down_low[...] = grad.astype(jnp.bfloat16)
    slope_copy.wait()
    grad = feed_back(grad, middle[...], slope, units, 0, vec, 0, vec_grads, 2, pre_grad)
    middle_grad[...] = grad
    branch_grad = grad.astype(jnp.bfloat16)
    branch_low[...] = branch_grad
    mixed_grad = contract(branch_grad, units[3], 1, 1).astype(jnp.bfloat16)
    probs_copy.wait()
    stack = stack_keys(qkv[:, mixed_grad.shape[1] :], [ref[...] for ref in far])
    attend_back(
        qkv[...], stack, probs, mixed_grad, query_grad, key_grads, far_grads, all_grads
    )


def last_body(meta, vec, inputs, query_grad, rows_low, middle_in, packed, *refs):
    input_grad, vec_grads, store, sems = refs
    units = Units(meta, packed, store, sems, range(3))
    vec_grads[...] = jnp.zeros_like(vec_grads)
    input_grad[...] = project_back(
        middle_in[...], inputs[...].astype(jnp.float32), query_grad[...], rows_low[...], units, 0,
        vec, 0, vec_grads,
    )


def grads_body(pairs, array_count, held, meta, *refs):
    arrays, refs = (refs[:array_count], refs[array_count + held :])
    grads = Grads(meta, *refs)
    for first_unit, left, right in pairs:
        grads.put(first_unit, arrays[left][...], arrays[right][...])
    grads.finish()


def last_grads_body(meta, normed, query_grad, key_grads, near_grads, *refs):
    rows_low, *refs = refs[4:]
    grads = Grads(meta, *refs)
    grads.put(0, normed[...], query_grad[...])
    rows_low[...] = with_near(key_grads[...], near_grads[...])
    grads.put(1, normed[...], rows_low[...])
    grads.finish()


def pooled(rows_low):
    return pair_mean(rows_low.astype(jnp.float32)).astype(jnp.bfloat16)


def in_order(first, own, other):
    return jnp.where(first, jnp.concatenate([own, other]), jnp.concatenate([other, own]))


def coarse_up(own, seq_index, tree_bits):
    far_list = []
    if tree_bits == 3:
        far_list.append(partner(own, "seq", 0))
        own = pooled(in_order(seq_index & 1 == 0, own, far_list[0]))
        near, same, cross = (across(own, "seq", apart) for apart in (2, 4, 6))
        return far_list + [near, pooled(in_order(seq_index & 2 == 0, same, cross))]
    for bit_at in range(tree_bits):
        far = partner(own, "seq", bit_at)
        far_list.append(far)
        if bit_at + 1 < tree_bits:
            own = pooled(in_order(seq_index >> bit_at & 1 == 0, own, far))
    return far_list


def coarse_down(far_grads, seq_index):
    above = None
    if len(far_grads) == 3:
        wide = pair_spread(far_grads[2])
        first = seq_index & 2 == 0
        same = jnp.where(first, wide[:BLOCK], wide[BLOCK:]).astype(jnp.bfloat16)
        cross = jnp.where(first, wide[BLOCK:], wide[:BLOCK]).astype(jnp.bfloat16)
        above = (
            across(same, "seq", 4).astype(jnp.float32)
            + across(cross, "seq", 6).astype(jnp.float32)
            + across(far_grads[1].astype(jnp.bfloat16), "seq", 2).astype(jnp.float32)
        )
        far_grads = far_grads[:1]
    for bit_at in reversed(range(len(far_grads))):
        upper = seq_index >> bit_at & 1 == 1
        sent = far_grads[bit_at]
        own = 0.0
        if above is not None:
            wide = pair_spread(above)
            own = jnp.where(upper, wide[BLOCK:], wide[:BLOCK])
            sent = sent + jnp.where(upper, wide[:BLOCK], wide[BLOCK:])
        above = own + partner(sent.astype(jnp.bfloat16), "seq", bit_at).astype(jnp.float32)
    return above


def per_device(
    inputs,
    cotangent,
    seq_lengths,
    unit_slot,
    masters,
    first_moment,
    second_moment,
    bases,
    stats,
    vec_master,
    vec_first,
    vec_second,
):
    seq_count = lax.axis_size("seq")
    opt_count = lax.axis_size("opt")
    seq_index = lax.axis_index("seq")
    tok_count = inputs.shape[1]
    model_width = inputs.shape[2]
    own_slots = masters.shape[0]
    row_count = masters.shape[1]
    ff_blocks = FF // model_width
    per_layer = 4 + 2 * ff_blocks
    vec_width = 5 * model_width + FF
    long_devs = min(max(MAX_LEN // tok_count, 1), seq_count)
    tree_bits = long_devs.bit_length() - 1
    size = seq_count * row_count
    by_permutes = seq_count == 8 and opt_count == 4 and own_slots == 6
    slots = jnp.arange(own_slots, dtype=jnp.int32)
    packed_rows = KINDS * max(row_count, EXTRA) + EXTRA

    def pack_slots(slots, counts):
        return call_kernel(
            pack_body,
            [
                jax.ShapeDtypeStruct((count, packed_rows, model_width), jnp.bfloat16)
                for count in counts
            ],
            [],
            "pack_slots",
            slots,
            (seq_index * row_count).reshape(1),
            stats,
            bases,
            first_moment,
            second_moment,
            smem_count=2,
            micros=3,
        )

    if by_permutes:
        parity, core = (seq_index & 1, lax.axis_index("opt") & 1)
        shift = parity ^ core
        owners = 2 * ((slots >> 1) + ((slots & 1) ^ core)) + (slots & 1)
        half_slots = own_slots // 2
        pairs = 2 * jnp.arange(half_slots, dtype=jnp.int32)
        near, away = pack_slots(
            jnp.concatenate([pairs + parity, pairs + 1 - parity]), (half_slots, half_slots)
        )
        met = jnp.stack([near, partner(away, "seq", 0)], axis=1)
        z_index = seq_index >> 1
        to_owner = [
            lax.dynamic_index_in_dim(
                met, jnp.clip((z_index ^ apart) - shift, 0, half_slots - 1), 0, keepdims=False
            )
            for apart in range(4)
        ]
        row_at = jnp.stack(
            [
                (2 * (z_index ^ apart) + (parity ^ side)) * row_count
                for apart in range(4)
                for side in range(2)
            ]
        )
    else:
        owners = slots
        (to_owner,) = pack_slots(
            jnp.minimum(jnp.arange(seq_count, dtype=jnp.int32), own_slots - 1), (seq_count,)
        )
        row_at = jnp.arange(seq_count, dtype=jnp.int32) * row_count
    vec_count = vec_master.shape[0]
    own_rows = own_slots * row_count
    vec_low = vec_master.astype(jnp.bfloat16)
    for axis in ("opt", "seq"):
        for bit_at in range(lax.axis_size(axis).bit_length() - 1):
            other = partner(vec_low, axis, bit_at)
            vec_low = jnp.where(
                lax.axis_index(axis) >> bit_at & 1 == 1,
                jnp.concatenate([other, vec_low]),
                jnp.concatenate([vec_low, other]),
            )
    vec = vec_low.reshape(-1, model_width).astype(jnp.float32)
    gathered = lax.all_gather(
        masters.astype(jnp.bfloat16).reshape(1, own_rows, model_width),
        ("seq", "opt"),
        axis=0,
        tiled=True,
    )
    if row_count % 16 == 0:
        unit_rows = row_count
        packed = gathered.reshape(seq_count, opt_count, own_rows, model_width)
    else:
        unit_rows = size
        packed = (
            gathered.reshape(seq_count, opt_count, own_slots, row_count, model_width)
            .transpose(1, 2, 0, 3, 4)
            .reshape(1, opt_count, own_slots * size, model_width)
        )
    opt_index = lax.axis_index("opt")
    opt_at, slot_in = (unit_slot // own_slots, unit_slot % own_slots)
    if by_permutes:
        apart = opt_at ^ opt_index
        other = (apart & 1) * 4 + (apart >> 1) * 2 + ((slot_in ^ seq_index) & 1)
        place = other * (own_slots // 2) + (slot_in >> 1)
    else:
        place = unit_slot
    meta = jnp.concatenate([opt_at, slot_in * unit_rows, place]).astype(jnp.int32)
    span_bits = jnp.zeros((), jnp.int32)
    for bit_at in range(tree_bits + 1):
        start_dev = seq_index >> bit_at << bit_at
        span_bits = jnp.where(
            seq_lengths[0, start_dev] == tok_count * (1 << bit_at), bit_at, span_bits
        )
    offsets_in = score_offsets(tok_count, tree_bits, span_bits)
    width_in = offsets_in.shape[1]
    pair_count = model_width // LANES
    vec_rows = vec_width // model_width
    square = (model_width, model_width)

    def units_in(count):
        return [
            pltpu.VMEM((count, size // unit_rows, unit_rows, model_width), jnp.bfloat16),
            pltpu.SemaphoreType.DMA((count,)),
        ]

    def grads_out(count):
        return [pltpu.VMEM((count,) + square, jnp.bfloat16), pltpu.SemaphoreType.DMA((count, 2))]

    def low_of(*shape):
        return jax.ShapeDtypeStruct(shape, jnp.bfloat16)

    def full_of(*shape):
        return jax.ShapeDtypeStruct(shape, jnp.float32)

    projected = [
        low_of(tok_count, model_width),
        low_of(tok_count, 3 * model_width),
        low_of(BLOCK, 2 * model_width),
    ]
    attended = [
        full_of(pair_count, 2 * tok_count, width_in),
        low_of(tok_count, model_width),
    ]
    fed = [
        low_of(tok_count, model_width),
        full_of(tok_count, FF),
        low_of(tok_count, FF),
    ]
    back = [
        full_of(tok_count, model_width),
        low_of(tok_count, model_width),
        full_of(tok_count, 2 * model_width),
        full_of(16, model_width),
        low_of(tok_count, FF),
        low_of(tok_count, model_width),
    ] + [full_of(BLOCK, 2 * model_width)] * tree_bits
    all_grads = full_of(width_in, 2 * model_width)
    buffers = [low_of(UNIT_COUNT // 2, size // 2, model_width)] * 4
    ff_blocks = FF // model_width

    def in_vmem(shapes):
        return [pltpu.VMEM(shape.shape, shape.dtype) for shape in shapes]

    def unit_grads(name, held, pairs):
        arrays = []
        for _, *factors in pairs:
            arrays += [factor for factor in factors if not any(factor is one for one in arrays)]
        index = {id(array): at for at, array in enumerate(arrays)}
        count = sum(left.shape[1] * right.shape[1] for _, left, right in pairs) // model_width**2
        first = 1 + len(arrays)
        return call_kernel(
            functools.partial(
                grads_body,
                [(unit, index[id(left)], index[id(right)]) for unit, left, right in pairs],
                len(arrays),
                len(held),
            ),
            buffers,
            grads_out(count),
            name,
            meta,
            *arrays,
            *held,
            smem_count=1,
            micros=2,
            any_in=range(first, first + len(held)),
            any_out=range(4),
            aliases={first + at: at for at in range(len(held))},
        )

    packed, to_owner, offsets_in, vec, meta = lax.optimization_barrier(
        (packed, to_owner, offsets_in, vec, meta)
    )
    normed_zero, qkv_zero, near_zero = call_kernel(
        functools.partial(first_body, per_layer),
        projected,
        units_in(3),
        "project_first",
        meta,
        vec,
        inputs[0],
        packed,
        smem_count=1,
        micros=3,
        any_in=(3,),
    )
    far_zero = coarse_up(near_zero, seq_index, tree_bits)
    (
        probs, mixed, middle, normed_two, slope, act, hidden, normed_one, qkv_one, near_one,
    ) = call_kernel(
        functools.partial(middle_body, per_layer, vec_rows, tree_bits),
        attended + [full_of(tok_count, model_width)] + fed + [full_of(tok_count, model_width)]
        + projected,
        units_in(per_layer) + in_vmem([attended[0], fed[1]]) + [pltpu.SemaphoreType.DMA((2,))],
        "layer_first",
        meta,
        vec,
        offsets_in,
        inputs[0],
        qkv_zero,
        *far_zero,
        packed,
        smem_count=1,
        micros=7,
        any_in=(5 + tree_bits,),
        any_out=(0, 4),
    )
    far_one = coarse_up(near_one, seq_index, tree_bits)
    (
        outputs, mixed_one, normed_up, act_one, middle_grad, query_grad, key_grads, vec_grads_up,
        pre_grad, branch_low, *far_grads,
    ) = call_kernel(
        functools.partial(turn_body, per_layer, vec_rows, tree_bits),
        [low_of(tok_count, model_width), attended[1], fed[0], fed[2]] + back,
        units_in(per_layer - 3) + in_vmem([attended[0], fed[1], all_grads]),
        "layer_turn",
        meta,
        vec,
        offsets_in,
        cotangent[0],
        hidden,
        qkv_one,
        *far_one,
        packed,
        smem_count=1,
        micros=13,
        any_in=(6 + tree_bits,),
    )
    near_grads = coarse_down(far_grads, seq_index)
    held = unit_grads("down_grads", (), [(per_layer + 4 + ff_blocks, act_one, cotangent[0])])
    held = unit_grads(
        "up_grads",
        held,
        [(per_layer + 4, normed_up, pre_grad), (per_layer + 3, mixed_one, branch_low)],
    )
    (
        down_low, rows_low, middle_grad, query_zero, key_grads, vec_grads_mid, pre_grad,
        branch_low, *far_grads,
    ) = call_kernel(
        functools.partial(lower_body, per_layer, vec_rows, tree_bits),
        [low_of(tok_count, model_width), low_of(tok_count, 2 * model_width)] + back,
        units_in(per_layer)
        + in_vmem([attended[0], fed[1]])
        + [pltpu.SemaphoreType.DMA((2,))]
        + in_vmem([all_grads]),
        "layer_back",
        meta,
        vec,
        hidden,
        query_grad,
        key_grads,
        near_grads,
        middle_grad,
        middle,
        qkv_zero,
        *far_zero,
        probs,
        slope,
        packed,
        smem_count=1,
        micros=13,
        any_in=range(9 + tree_bits, 12 + tree_bits),
    )
    near_grads = coarse_down(far_grads, seq_index)
    held = unit_grads("down_grads_low", held, [(4 + ff_blocks, act, down_low)])
    held = unit_grads(
        "up_grads_low", held, [(4, normed_two, pre_grad), (3, mixed, branch_low)]
    )
    held = unit_grads(
        "project_grads",
        held,
        [(per_layer, normed_one, query_grad), (per_layer + 1, normed_one, rows_low)],
    )
    rows_zero, *held = call_kernel(
        last_grads_body,
        [low_of(tok_count, 2 * model_width)] + buffers,
        grads_out(3),
        "project_grads_low",
        meta,
        normed_zero,
        query_zero,
        key_grads,
        near_grads,
        *held,
        smem_count=1,
        micros=3,
        any_in=range(5, 9),
        any_out=range(1, 5),
        aliases={5 + at: 1 + at for at in range(4)},
    )
    input_grad, vec_grads_low = call_kernel(
        last_body,
        [full_of(tok_count, model_width), full_of(16, model_width)],
        units_in(3),
        "project_back",
        meta,
        vec,
        inputs[0],
        query_zero,
        rows_zero,
        middle_grad,
        packed,
        smem_count=1,
        micros=4,
        any_in=(6,),
    )
    vec_sum = jnp.concatenate(
        [vec_grads_low[0:2], vec_grads_mid[2:vec_rows], vec_grads_mid[0:2], vec_grads_up[2:vec_rows]]
    )
    if by_permutes:
        held[2], to_owner = lax.optimization_barrier((held[2], to_owner))
        owner_grad, vec_sum, owner_rows = sum_to_owner(
            *held, seq_index, shift, vec_sum, to_owner
        )
    else:
        owner_rows = [lax.all_to_all(to_owner, "seq", 0, 0, tiled=True)]
        for axis in ("opt", "seq"):
            for bit_at in range(lax.axis_size(axis).bit_length() - 1):
                vec_sum = vec_sum + partner(vec_sum, axis, bit_at)
        column_grads = lax.psum_scatter(
            jnp.concatenate(
                [jnp.concatenate(held[at : at + 2], axis=1) for at in (0, 2)]
            ),
            "opt",
            scatter_dimension=0,
            tiled=True,
        )
        column_grads = jnp.pad(column_grads, [(0, seq_count - own_slots), (0, 0), (0, 0)])
        owner_grad = lax.psum_scatter(column_grads, "seq", scatter_dimension=0, tiled=True)[0]
    step_rows, owner_stat, owner_basis = rotate_slot(row_at, owner_grad, owner_rows)
    home_rows = lax.all_to_all(step_rows, "seq", 0, 0, tiled=True)
    base_rows = renew_bases(seq_count, owner_stat, owner_basis)
    base_rows, home_rows = lax.optimization_barrier((base_rows, home_rows))
    base_rows = lax.all_to_all(base_rows, "seq", 0, 0, tiled=True)
    whole_shape = jax.ShapeDtypeStruct(masters.shape, jnp.float32)
    new_masters, new_first, new_second, new_stats = call_kernel(
        finish_body,
        [whole_shape, whole_shape, whole_shape, jax.ShapeDtypeStruct(stats.shape, jnp.float32)],
        [],
        "finish_slots",
        owners,
        masters,
        first_moment,
        second_moment,
        stats,
        home_rows,
        smem_count=1,
        micros=4,
    )
    (new_bases,) = call_kernel(
        place_body,
        [jax.ShapeDtypeStruct(bases.shape, jnp.float32)],
        [],
        "place_bases",
        owners,
        base_rows,
        smem_count=1,
    )
    grad_vecs = lax.dynamic_slice_in_dim(
        vec_sum.reshape(-1), (seq_index * opt_count + lax.axis_index("opt")) * vec_count, vec_count
    )
    new_vec_first = BETA_ONE * vec_first + (1.0 - BETA_ONE) * grad_vecs
    new_vec_second = BETA_TWO * vec_second + (1.0 - BETA_TWO) * grad_vecs * grad_vecs
    new_vectors = vec_master - RATE_VECTOR * (new_vec_first / (1.0 - BETA_ONE**STEP)) / (
        jnp.sqrt(new_vec_second / (1.0 - BETA_TWO**STEP)) + ADAM_EPS
    )
    return (
        outputs[None],
        input_grad[None],
        new_masters,
        new_first,
        new_second,
        new_bases,
        new_stats,
        new_vectors,
        new_vec_first,
        new_vec_second,
    )


def solution(mesh):
    placed = (
        P("opt", "seq", None),
        P("opt", "seq", None),
        P("opt", None),
        P(),
        P("opt", "seq", None),
        P("opt", "seq", None),
        P("opt", "seq", None),
        P("opt", None, "seq", None),
        P("opt", None, "seq", None),
        P(("seq", "opt")),
        P(("seq", "opt")),
        P(("seq", "opt")),
    )
    return jax.shard_map(
        per_device,
        mesh=mesh,
        in_specs=placed,
        out_specs=(
            P("opt", "seq", None),
            P("opt", "seq", None),
            P("opt", "seq", None),
            P("opt", "seq", None),
            P("opt", "seq", None),
            P("opt", None, "seq", None),
            P("opt", None, "seq", None),
            P(("seq", "opt")),
            P(("seq", "opt")),
            P(("seq", "opt")),
        ),
        check_vma=False,
    )
```

```python
import functools
import math

import jax
import jax.numpy as jnp
from jax import lax
from jax.experimental import pallas as pl
from jax.experimental.pallas import tpu as pltpu
from jax.sharding import PartitionSpec as P

HEADS = 8
FF = 2048
BLOCK = 16
LAYERS = 2
STEP = 10
MAX_LEN = 4096


HIGH = lax.Precision.HIGHEST
LN_TWO = math.log(2.0)
NEG_FILL = -1e30
NORM_EPS = 1e-05
ADAM_EPS = 1e-08
RATE_MATRIX = 0.03
RATE_VECTOR = 0.2
WEIGHT_DECAY = 0.01
BETA_ONE = 0.9
BETA_TWO = 0.95
BETA_STAT = 0.95

SUBLANES = 8
PANEL = 16
FLOPS_PER_US = 1_150_000_000
LANES = 128
UNIT_COUNT = 24
UNIT_OPT = 0
UNIT_ROW = UNIT_COUNT
UNIT_SLOT = 2 * UNIT_COUNT
DIAG = 128
VMEM_GRANT = 60 * 2**20
IN_VMEM = pl.BlockSpec(memory_space=pltpu.VMEM)
IN_SMEM = pl.BlockSpec(memory_space=pltpu.SMEM)
ANYWHERE = pl.BlockSpec(memory_space=pl.ANY)


def contract(left, right, left_dim, right_dim, precision=None):
    return lax.dot_general(
        left,
        right,
        (((left_dim,), (right_dim,)), ((), ())),
        precision=precision,
        preferred_element_type=jnp.float32,
    )


def split_two(values):
    high = values.astype(jnp.bfloat16)
    return (high, (values - high.astype(jnp.float32)).astype(jnp.bfloat16))


def wide_left(left, right_low, left_dim, right_dim):
    high, rest = split_two(left)
    return contract(high, right_low, left_dim, right_dim) + contract(
        rest, right_low, left_dim, right_dim
    )


def wide_right(left_low, right, left_dim, right_dim):
    high, rest = split_two(right)
    return contract(left_low, high, left_dim, right_dim) + contract(
        left_low, rest, left_dim, right_dim
    )


def call_kernel(
    body, out_shapes, scratch, name, *operands, smem_count=0, any_in=(), any_out=(), aliases=None,
    micros=2,
):
    def place(at, listed):
        return ANYWHERE if at in listed else IN_VMEM

    return pl.pallas_call(
        body,
        out_shape=out_shapes,
        in_specs=[
            IN_SMEM if at < smem_count else place(at, any_in) for at in range(len(operands))
        ],
        out_specs=[place(at, any_out) for at in range(len(out_shapes))],
        scratch_shapes=scratch,
        input_output_aliases=aliases or {},
        cost_estimate=pl.CostEstimate(
            flops=micros * FLOPS_PER_US, bytes_accessed=0, transcendentals=0
        ),
        compiler_params=pltpu.CompilerParams(vmem_limit_bytes=VMEM_GRANT),
        name=name,
    )(*operands)


def eliminate(panels, turn):
    rows, width = panels[0][0].shape
    row_at = lax.broadcasted_iota(jnp.int32, (SUBLANES, width), 0)

    def groups(values):
        return [values[low : low + SUBLANES] for low in range(0, rows, SUBLANES)]

    def spread_row(values, row):
        return jnp.broadcast_to(values[row : row + 1, :], values.shape)

    states = []
    for left, right in panels:
        turned = pltpu.roll(left, turn, 1)
        columns = [
            [jnp.broadcast_to(part, (SUBLANES, width)) for part in groups(turned[:, at : at + 1])]
            for at in range(rows)
        ]
        ones = [jnp.ones((SUBLANES, width), jnp.float32) for _ in range(rows // SUBLANES)]
        states.append((groups(left), groups(right), columns, ones))
    for at in range(rows):
        group_at, row = divmod(at, SUBLANES)
        for left, right, columns, pivots in states:
            pivot = spread_row(columns[at][group_at], row)
            inverse = pltpu.reciprocal(pivot, approx=False)
            pivots[group_at] = jnp.where(row_at == row, pivot, pivots[group_at])
            targets = [left, right] + columns[at + 1 :]
            given = [spread_row(target[group_at], row) for target in targets]
            for group in range(group_at, rows // SUBLANES):
                factor = columns[at][group] * inverse
                if group == group_at:
                    factor = jnp.where(row_at > row, factor, 0.0)
                for target, pivot_row in zip(targets, given):
                    target[group] = target[group] - factor * pivot_row
    results = []
    for left, right, _, pivots in states:
        scales = [lax.rsqrt(values) for values in pivots]
        results.append(
            tuple(
                jnp.concatenate([part * scale for part, scale in zip(parts, scales)], axis=0)
                for parts in (left, right)
            )
        )
    return results


def split_three(values):
    high = values.astype(jnp.bfloat16).astype(jnp.float32)
    rest = values - high
    middle = rest.astype(jnp.bfloat16).astype(jnp.float32)
    return (high, middle, rest - middle)


def thin_product(left, right):
    left_parts, right_parts = (split_three(left), split_three(right))
    pairs = ((0, 0), (0, 1), (1, 0), (1, 1), (0, 2), (2, 0))
    stacked_left = jnp.concatenate([left_parts[i] for i, _ in pairs], axis=0)
    stacked_right = jnp.concatenate([right_parts[j] for _, j in pairs], axis=0)
    return contract(stacked_left.astype(jnp.bfloat16), stacked_right.astype(jnp.bfloat16), 0, 0)


def factorize(grams, uppers, works, inverses, solve):
    each = range(len(grams))
    size = grams[0].shape[0]
    eye = (
        lax.broadcasted_iota(jnp.int32, (DIAG, DIAG), 0)
        == lax.broadcasted_iota(jnp.int32, (DIAG, DIAG), 1)
    ).astype(jnp.float32)
    for low in range(0, size, DIAG):
        top = low + DIAG
        for m in each:
            works[m][:, 0:DIAG] = grams[m][low:top, low:top]
            works[m][:, DIAG:] = eye

        def panel(panel_at, carry):
            row = pl.multiple_of(panel_at * PANEL, PANEL)
            turn = lax.rem(DIAG - panel_at * PANEL, DIAG)
            panels = [
                (works[m][pl.ds(row, PANEL), 0:DIAG], works[m][pl.ds(row, PANEL), DIAG:])
                for m in each
            ]
            if low:
                share = size * PANEL // DIAG
                rows = pl.ds(pl.multiple_of(panel_at * share, share), share)
                store, solved = solve(low - DIAG, rows)
            results = eliminate(panels, turn)
            updates = [
                thin_product(left, jnp.concatenate([left, right], axis=1))
                for left, right in results
            ]
            for m in each:
                inverses[m][low // DIAG, pl.ds(row, PANEL), :] = results[m][1]
            for m in each:
                works[m][...] = works[m][...] - updates[m]
            if low:
                store(solved)
            return carry

        lax.fori_loop(0, DIAG // PANEL, panel, 0)
        if top == size:
            break
        right_of = [contract(inverses[m][low // DIAG], grams[m][low:top, top:], 1, 0, HIGH) for m in each]
        for m in each:
            uppers[m][low:top, top:] = right_of[m]
        for other in range(top, size, DIAG):
            skip = other - top
            rest = [
                grams[m][other : other + DIAG, other:]
                - contract(right_of[m][:, skip : skip + DIAG], right_of[m][:, skip:], 0, 0, HIGH)
                for m in each
            ]
            for m in each:
                grams[m][other : other + DIAG, other:] = rest[m]


def renew_body(*refs):
    stat_ref, basis_ref, sent = refs[:3]
    scratch = refs[3:]
    count, size, _ = stat_ref.shape
    each = range(count)
    products, grams, uppers, works, inverses = (
        scratch[at : at + count] for at in range(0, 5 * count, count)
    )
    values = [wide_left(stat_ref[m], basis_ref[m], 1, 0) for m in each]
    for m in each:
        products[m][...] = values[m]
    for low in range(0, size, DIAG):
        values = [
            contract(products[m][:, low : low + DIAG], products[m][:, low:], 0, 0, HIGH)
            for m in each
        ]
        for m in each:
            grams[m][low : low + DIAG, low:] = values[m]

    def solve(low, rows):
        top = low + DIAG
        values = [products[m][rows, low:top] for m in each]
        if low:
            values = [
                values[m]
                - contract(products[m][rows, :low], uppers[m][:low, low:top], 1, 0, HIGH)
                for m in each
            ]
        values = [contract(values[m], inverses[m][low // DIAG], 1, 1, HIGH) for m in each]

        def store(solved):
            for m in each:
                products[m][rows, low:top] = solved[m]

        return (store, values)

    factorize(grams, uppers, works, inverses, solve)
    store, solved = solve(size - DIAG, slice(None))
    store(solved)
    rows = sent.shape[2]
    for target in range(sent.shape[0]):
        for m in each:
            sent[target, m] = products[m][target * rows : (target + 1) * rows, :].astype(
                jnp.bfloat16
            )


def renew_bases(device_count, new_stat, basis_low):
    count, size, _ = new_stat.shape
    return call_kernel(
        renew_body,
        [jax.ShapeDtypeStruct((device_count, count, size // device_count, size), jnp.bfloat16)],
        [pltpu.VMEM((size, size), jnp.float32)] * (3 * count)
        + [pltpu.VMEM((DIAG, 2 * DIAG), jnp.float32)] * count
        + [pltpu.VMEM((size // DIAG, DIAG, DIAG), jnp.float32)] * count,
        "renew_bases",
        new_stat,
        basis_low,
        micros=40,
    )[0]


KINDS = 5
EXTRA = 16


def pack_body(slot_ref, base_ref, stats, bases, first, second, *packed):
    _, _, rows, width = stats.shape
    pad = (packed[0].shape[1] - EXTRA) // KINDS
    row = base_ref[0] + lax.broadcasted_iota(jnp.int32, (rows, width), 0)
    column = lax.broadcasted_iota(jnp.int32, (rows, width), 1)
    at = 0
    for part in packed:
        for target in range(part.shape[0]):
            slot = slot_ref[at]
            right = stats[slot, 1]
            both = jnp.where(column >= row, stats[slot, 0], right)
            parts = (both, bases[slot, 0], bases[slot, 1], first[slot], second[slot])
            for kind, values in enumerate(parts):
                part[target, kind * pad : kind * pad + rows] = values.astype(jnp.bfloat16)
            diagonal = sum_rows(jnp.where(column == row, right, 0.0))
            part[target, KINDS * pad :] = jnp.broadcast_to(diagonal, (EXTRA, width)).astype(
                jnp.bfloat16
            )
            at += 1


def rotate_body(count, row_ref, grad_ref, *refs):
    given, (sent, stat_ref, basis_ref, whole, results) = (refs[:count], refs[count:])
    rows = sent.shape[2]
    pad = (given[0].shape[1] - EXTRA) // KINDS
    diagonal = jnp.zeros((1, whole.shape[2]), jnp.float32)
    at = 0
    for part in given:
        for piece in range(part.shape[0]):
            row = pl.multiple_of(row_ref[at], 8)
            for kind in range(KINDS):
                values = part[piece, kind * pad : kind * pad + rows]
                if kind in (1, 2) and rows % EXTRA == 0:
                    low_row = pl.multiple_of(row, EXTRA)
                    basis_ref[kind - 1, pl.ds(low_row, rows), :] = values
                else:
                    whole[kind, pl.ds(row, rows), :] = values.astype(jnp.float32)
            diagonal = diagonal + part[piece, KINDS * pad :].astype(jnp.float32)[0:1]
            at += 1
    both = whole[0]
    turned = both.T
    row = lax.broadcasted_iota(jnp.int32, both.shape, 0)
    column = lax.broadcasted_iota(jnp.int32, both.shape, 1)
    left_stat = jnp.where(column >= row, both, turned)
    right_stat = jnp.where(column < row, both, jnp.where(column > row, turned, diagonal))
    grad = grad_ref[...]
    if rows % EXTRA:
        basis_ref[...] = whole[1:3].astype(jnp.bfloat16)
    left = basis_ref[0]
    right = basis_ref[1]
    results[0] = contract(grad, grad, 1, 1)
    results[1] = contract(grad, grad, 0, 0)
    stat_ref[0] = BETA_STAT * left_stat + (1.0 - BETA_STAT) * results[0]
    stat_ref[1] = BETA_STAT * right_stat + (1.0 - BETA_STAT) * results[1]
    rotated = wide_left(contract(left, grad, 0, 0), right, 1, 0)
    results[2] = rotated
    new_first = BETA_ONE * whole[3] + (1.0 - BETA_ONE) * rotated
    new_second = BETA_TWO * whole[4] + (1.0 - BETA_TWO) * rotated * rotated
    direction = (
        new_first
        / (1.0 - BETA_ONE**STEP)
        / (jnp.sqrt(new_second / (1.0 - BETA_TWO**STEP)) + ADAM_EPS)
    )
    results[3] = wide_right(left, wide_left(direction, right, 1, 1), 1, 0)
    for target in range(sent.shape[0]):
        sent[target] = results[:, target * rows : (target + 1) * rows, :].astype(jnp.bfloat16)


def rotate_slot(row_at, grad, owner_rows):
    size = grad.shape[0]
    return call_kernel(
        functools.partial(rotate_body, len(owner_rows)),
        [
            jax.ShapeDtypeStruct(
                (row_at.shape[0], 4, size // row_at.shape[0], size), jnp.bfloat16
            ),
            jax.ShapeDtypeStruct((2, size, size), jnp.float32),
            jax.ShapeDtypeStruct((2, size, size), jnp.bfloat16),
        ],
        [
            pltpu.VMEM((KINDS, size, size), jnp.float32),
            pltpu.VMEM((4, size, size), jnp.float32),
        ],
        "rotate_slot",
        row_at,
        grad,
        *owner_rows,
        smem_count=1,
        micros=6,
    )


def finish_body(
    owner_ref, masters, first, second, stats, given, new_masters, new_first, new_second, new_stats
):
    for slot in range(masters.shape[0]):
        owner = owner_ref[slot]
        rotated = given[owner, 2].astype(jnp.float32)
        update = given[owner, 3].astype(jnp.float32)
        new_first[slot] = BETA_ONE * first[slot] + (1.0 - BETA_ONE) * rotated
        new_second[slot] = BETA_TWO * second[slot] + (1.0 - BETA_TWO) * rotated * rotated
        new_masters[slot] = masters[slot] - RATE_MATRIX * (update + WEIGHT_DECAY * masters[slot])
        new_stats[slot] = BETA_STAT * stats[slot] + (1.0 - BETA_STAT) * given[owner, 0:2].astype(
            jnp.float32
        )


def place_body(owner_ref, given, new_bases, low, full, in_sems, out_sems):
    slots = range(new_bases.shape[0])
    coming = [
        pltpu.make_async_copy(given.at[owner_ref[slot]], low.at[slot], in_sems.at[slot])
        for slot in slots
    ]
    going = [
        pltpu.make_async_copy(full.at[slot], new_bases.at[slot], out_sems.at[slot])
        for slot in slots
    ]
    for copy in coming:
        copy.start()
    for slot in slots:
        coming[slot].wait()
        full[slot] = low[slot].astype(jnp.float32)
        going[slot].start()
    for copy in going:
        copy.wait()


def add_low(left, right):
    return (left.astype(jnp.float32) + right.astype(jnp.float32)).astype(jnp.bfloat16)


def over_z(value, apart, owner_apart):
    pairs = []
    for at in range(32):
        z, y, core = (at >> 3, at >> 2 & 1, at & 1)
        if z ^ owner_apart != (0 if y ^ core else 3):
            pairs.append((at, at ^ apart << 3))
    return lax.ppermute(value, ("seq", "opt"), pairs)


def sum_to_owner(
    kept_upper, kept_lower, sent_upper, sent_lower, seq_index, shift, vec_sum, to_owner
):
    def beside(values, vec_sum, *exchanges):
        for axis, bit_at in exchanges:
            vec_sum = vec_sum + partner(vec_sum, axis, bit_at)
        return lax.optimization_barrier((values, vec_sum))

    _, row_count, width = kept_upper.shape
    z_count = kept_upper.shape[0] // 4
    shape = (2, 2, z_count, row_count, width)
    upper, came_upper = (kept_upper.reshape(shape), partner(sent_upper, "opt", 0).reshape(shape))
    lower, came_lower = (kept_lower.reshape(shape), partner(sent_lower, "opt", 0).reshape(shape))
    send_x = add_low(upper[1], came_upper[1])
    send_x, upper, came_upper = lax.optimization_barrier((send_x, upper, came_upper))
    by_x = partner(send_x, "opt", 1)
    send_y = add_low(lower[:, 1], came_lower[:, 1])
    send_y, lower, came_lower = lax.optimization_barrier((send_y, lower, came_lower))
    by_y = partner(send_y, "seq", 0)
    rows = [to_owner[0]] + [over_z(to_owner[at], at, at) for at in range(1, 4)]
    (by_x, rows[1], rows[2]), vec_sum = beside((by_x, rows[1], rows[2]), vec_sum, ("opt", 0))
    stay_x = add_low(upper[0], came_upper[0])
    stay_y = add_low(lower[:, 0], came_lower[:, 0])
    then_y = partner(add_low(stay_x[1], by_x[1]), "seq", 0)
    then_x = partner(add_low(stay_y[1], by_y[1]), "opt", 1)
    (then_y, rows[3]), vec_sum = beside((then_y, rows[3]), vec_sum, ("seq", 1))
    z_index = seq_index >> 1

    def both(apart):
        at = jnp.clip((z_index ^ apart) - shift, 0, z_count - 1)

        def pick(values):
            return lax.dynamic_index_in_dim(values, at, 0, keepdims=False)

        total_upper = (
            pick(stay_x[0]).astype(jnp.float32)
            + pick(by_x[0]).astype(jnp.float32)
            + pick(then_y).astype(jnp.float32)
        )
        total_lower = (
            pick(stay_y[0]).astype(jnp.float32)
            + pick(by_y[0]).astype(jnp.float32)
            + pick(then_x).astype(jnp.float32)
        )
        return jnp.concatenate([total_upper, total_lower]).astype(jnp.bfloat16)

    near_one = over_z(both(1), 1, 1)
    near_far = over_z(both(3), 1, 3)
    near_far, vec_sum = beside(near_far, vec_sum, ("seq", 2))
    last = over_z(add_low(both(2), near_far), 2, 2)
    last, vec_sum = beside(last, vec_sum, ("opt", 1), ("seq", 0))
    total = both(0).astype(jnp.float32) + near_one.astype(jnp.float32) + last.astype(jnp.float32)
    return (total.astype(jnp.bfloat16), vec_sum, rows)


def across(value, axis, apart):
    return lax.ppermute(value, axis, [(i, i ^ apart) for i in range(lax.axis_size(axis))])


def partner(value, axis, bit_at):
    return across(value, axis, 1 << bit_at)


def pair_mean(values):
    shaped = values.reshape((values.shape[0] // 2, 2) + values.shape[1:])
    return 0.5 * (shaped[:, 0] + shaped[:, 1])


def pair_spread(grads):
    return 0.5 * jnp.repeat(grads, 2, axis=0)


def sum_rows(values):
    return jnp.sum(values, axis=0, keepdims=True)


def norm_parts(values):
    centred = values - jnp.mean(values, axis=-1, keepdims=True)
    recip = lax.rsqrt(jnp.mean(centred * centred, axis=-1, keepdims=True) + NORM_EPS)
    return (centred * recip, recip)


def norm_back(grad, gain, normed, recip):
    scaled = grad * gain
    return recip * (
        scaled
        - jnp.mean(scaled, axis=-1, keepdims=True)
        - normed * jnp.mean(scaled * normed, axis=-1, keepdims=True)
    )


def half_matrix(shape, fine_dim):
    fine = lax.broadcasted_iota(jnp.int32, shape, fine_dim)
    coarse = lax.broadcasted_iota(jnp.int32, shape, 1 - fine_dim)
    return jnp.where(fine >> 1 == coarse, 0.5, 0.0).astype(jnp.bfloat16)


def pool(rows_low):
    count = rows_low.shape[0]
    return contract(half_matrix((count // 2, count), 1), rows_low, 1, 0).astype(jnp.bfloat16)


def spread(grads):
    count = grads.shape[0]
    return wide_right(half_matrix((2 * count, count), 0), grads, 1, 0)


def norm_cdf(values):
    return 0.5 * (1.0 + lax.erf(values * math.sqrt(0.5)))


def local_count(tok_count):
    return (tok_count // BLOCK).bit_length() - 1


def key_width(tok_count, tree_bits):
    rows = 2 * (tok_count - BLOCK) + BLOCK * tree_bits
    return -(-rows // LANES) * LANES


def score_offsets(tok_count, tree_bits, span_bits):
    token = jnp.arange(tok_count, dtype=jnp.int32)[:, None]
    parts = []
    for height in range(local_count(tok_count)):
        row = jnp.arange(tok_count >> height, dtype=jnp.int32)[None, :]
        apart = token // (BLOCK << height) ^ row // BLOCK
        counted = apart <= 1 if height == 0 else apart == 1
        parts.append(jnp.where(counted, height * LN_TWO, NEG_FILL))
    for bit_at in range(tree_bits):
        offset = (local_count(tok_count) + bit_at) * LN_TWO
        parts.append(
            jnp.broadcast_to(
                jnp.where(bit_at + 1 <= span_bits, offset, NEG_FILL), (tok_count, BLOCK)
            )
        )
    used = sum(part.shape[1] for part in parts)
    rest = key_width(tok_count, tree_bits) - used
    parts.append(jnp.full((tok_count, rest), NEG_FILL, jnp.float32))
    return jnp.concatenate(parts, axis=1).astype(jnp.float32)


def stack_keys(own_rows, far_rows):
    parts = [own_rows]
    for _ in range(local_count(own_rows.shape[0]) - 1):
        parts.append(pool(parts[-1]))
    parts = parts + far_rows
    rest = key_width(own_rows.shape[0], len(far_rows)) - sum(part.shape[0] for part in parts)
    if rest:
        parts.append(jnp.zeros((rest, own_rows.shape[1]), jnp.bfloat16))
    return jnp.concatenate(parts, axis=0)


def by_heads(pair):
    lane = lax.broadcasted_iota(jnp.int32, pair.shape, 1)
    zero = jnp.zeros_like(pair)
    first = lane < LANES // 2
    return jnp.concatenate([jnp.where(first, pair, zero), jnp.where(first, zero, pair)], axis=0)


def from_heads(both):
    count = both.shape[0] // 2
    lane = lax.broadcasted_iota(jnp.int32, (count, LANES), 1)
    return jnp.where(lane < LANES // 2, both[:count], both[count:])


def attend(qkv, stack, offsets, probs, mixed):
    width = qkv.shape[1] // 3
    score_scale = (width // HEADS) ** (-0.5)
    both_offsets = jnp.concatenate([offsets, offsets], axis=0)
    for pair_at in range(width // LANES):
        low, top = (pair_at * LANES, (pair_at + 1) * LANES)
        scores = (
            contract(by_heads(qkv[:, low:top]), stack[:, low:top], 1, 1) * score_scale
            + both_offsets
        )
        expo = jnp.exp(scores - jnp.max(scores, axis=1, keepdims=True))
        weights = expo * (1.0 / jnp.sum(expo, axis=1, keepdims=True))
        probs[pair_at] = weights
        result = contract(
            weights.astype(jnp.bfloat16), stack[:, width + low : width + top], 1, 0
        )
        mixed[:, low:top] = from_heads(result).astype(jnp.bfloat16)


def attend_back(qkv, stack, probs, mixed_grad, query_grad, key_grads, far_grads, all_grads):
    tok_count, width = mixed_grad.shape
    score_scale = (width // HEADS) ** (-0.5)
    for pair_at in range(width // LANES):
        low, top = (pair_at * LANES, (pair_at + 1) * LANES)
        queries = by_heads(qkv[:, low:top])
        grads = by_heads(mixed_grad[:, low:top])
        weights = probs[pair_at]
        prob_grad = contract(grads, stack[:, width + low : width + top], 1, 1)
        inner = jnp.sum(weights * prob_grad, axis=1, keepdims=True)
        score_grad = (weights * (prob_grad - inner)).astype(jnp.bfloat16)
        query_grad[:, low:top] = (
            from_heads(contract(score_grad, stack[:, low:top], 1, 0)) * score_scale
        ).astype(jnp.bfloat16)
        all_grads[:, low:top] = contract(score_grad, queries, 0, 0) * score_scale
        all_grads[:, width + low : width + top] = contract(
            weights.astype(jnp.bfloat16), grads, 0, 0
        )
    for far_at, far_grad in enumerate(far_grads):
        row = 2 * (tok_count - BLOCK) + BLOCK * far_at
        far_grad[...] = all_grads[row : row + BLOCK]
    folded = None
    for height in reversed(range(local_count(tok_count))):
        row = 2 * (tok_count - (tok_count >> height))
        own = all_grads[row : row + (tok_count >> height)]
        folded = own if folded is None else own + spread(folded)
    key_grads[...] = folded


class Units:
    def __init__(self, meta, packed, store, sems, units):
        self.store = store
        self.place = {unit: at for at, unit in enumerate(units)}
        self.waiting = {}
        rows = store.shape[2]
        for at, unit in enumerate(units):
            row = pl.multiple_of(meta[UNIT_ROW + unit], rows)
            copy = pltpu.make_async_copy(
                packed.at[:, meta[UNIT_OPT + unit], pl.ds(row, rows), :],
                store.at[at],
                sems.at[at],
            )
            copy.start()
            self.waiting[unit] = copy

    def __getitem__(self, unit):
        if unit in self.waiting:
            self.waiting.pop(unit).wait()
        width = self.store.shape[3]
        return self.store[self.place[unit]].reshape(width, width)


class Grads:
    def __init__(self, meta, *refs):
        self.meta, self.buffers, self.store, self.sems = (meta, refs[:4], refs[4], refs[5])
        self.copies = []

    def put(self, first_unit, left_low, right_low):
        product = contract(left_low, right_low, 0, 0).astype(jnp.bfloat16)
        width = self.store.shape[2]
        slots, rows, _ = self.buffers[0].shape
        for low in range(0, product.shape[0], width):
            for side in range(0, product.shape[1], width):
                at = len(self.copies) // 2
                self.store[at] = product[low : low + width, side : side + width]
                place = self.meta[UNIT_SLOT + first_unit + low // width + side // width]
                inner = jnp.where(place < slots, place, place - slots)
                for half in range(2):
                    keeping, sending = (
                        pltpu.make_async_copy(
                            self.store.at[at, pl.ds(half * rows, rows)],
                            target.at[inner],
                            self.sems.at[at, half],
                        )
                        for target in (self.buffers[half], self.buffers[2 + half])
                    )
                    pl.when(place < slots)(keeping.start)
                    pl.when(place >= slots)(sending.start)
                    self.copies.append(keeping)

    def finish(self):
        for copy in self.copies:
            copy.wait()


def project(hidden, units, first_unit, gain, bias, normed_ref, qkv_ref, near_ref):
    width = hidden.shape[1]
    normed, _ = norm_parts(hidden)
    normed_low = (normed * gain + bias).astype(jnp.bfloat16)
    normed_ref[...] = normed_low
    for part in range(3):
        qkv_ref[:, part * width : (part + 1) * width] = contract(
            normed_low, units[first_unit + part], 1, 0
        ).astype(jnp.bfloat16)
    near = qkv_ref[:, width:]
    for _ in range(local_count(near.shape[0])):
        near = pool(near)
    near_ref[...] = near


def feed_forward(middle, units, first_unit, vec, vec_at, normed_ref, slope_ref, act_ref):
    width = middle.shape[1]
    normed, _ = norm_parts(middle)
    normed_low = (normed * vec[vec_at + 2 : vec_at + 3] + vec[vec_at + 3 : vec_at + 4]).astype(
        jnp.bfloat16
    )
    normed_ref[...] = normed_low
    total = middle
    ff_blocks = FF // width
    for part in range(ff_blocks):
        low, top = (part * width, (part + 1) * width)
        row = vec_at + 4 + part
        pre = contract(normed_low, units[first_unit + 4 + part], 1, 0) + vec[row : row + 1]
        share = norm_cdf(pre)
        act = (pre * share).astype(jnp.bfloat16)
        slope_ref[:, low:top] = share + pre * jnp.exp(-0.5 * pre * pre) * (
            1.0 / math.sqrt(2.0 * math.pi)
        )
        act_ref[:, low:top] = act
        total = total + contract(act, units[first_unit + 4 + ff_blocks + part], 1, 0)
    row = vec_at + 4 + ff_blocks
    return total + vec[row : row + 1]


def feed_back(
    grad, middle, slope_ref, units, first_unit, vec, vec_at, vec_grads, at, pre_grad_ref
):
    width = middle.shape[1]
    ff_blocks = FF // width
    down_grad = grad.astype(jnp.bfloat16)
    normed_grad = jnp.zeros(middle.shape, jnp.float32)
    for part in range(ff_blocks):
        low, top = (part * width, (part + 1) * width)
        pre_grad = (
            contract(down_grad, units[first_unit + 4 + ff_blocks + part], 1, 1)
            * slope_ref[:, low:top]
        ).astype(jnp.bfloat16)
        pre_grad_ref[:, low:top] = pre_grad
        vec_grads[at + 2 + part : at + 3 + part] = sum_rows(pre_grad.astype(jnp.float32))
        normed_grad = normed_grad + contract(pre_grad, units[first_unit + 4 + part], 1, 1)
    row = at + 2 + ff_blocks
    vec_grads[row : row + 1] = sum_rows(grad)
    normed, recip = norm_parts(middle)
    vec_grads[at : at + 1] = sum_rows(normed_grad * normed)
    vec_grads[at + 1 : at + 2] = sum_rows(normed_grad)
    return grad + norm_back(normed_grad, vec[vec_at + 2 : vec_at + 3], normed, recip)


def with_near(key_grads, near):
    for _ in range(local_count(key_grads.shape[0])):
        near = spread(near)
    return (key_grads + near).astype(jnp.bfloat16)


def project_back(
    middle_grad, hidden, query_grad, rows_low, units, first_unit, vec, vec_at, vec_grads
):
    width = hidden.shape[1]
    normed_grad = contract(query_grad, units[first_unit], 1, 1)
    for part in range(2):
        normed_grad = normed_grad + contract(
            rows_low[:, part * width : (part + 1) * width], units[first_unit + 1 + part], 1, 1
        )
    normed, recip = norm_parts(hidden)
    vec_grads[0:1] = sum_rows(normed_grad * normed)
    vec_grads[1:2] = sum_rows(normed_grad)
    return middle_grad + norm_back(normed_grad, vec[vec_at : vec_at + 1], normed, recip)


def first_body(per_layer, meta, vec, inputs, packed, normed, qkv, near, store, sems):
    units = Units(meta, packed, store, sems, range(3))
    project(inputs[...].astype(jnp.float32), units, 0, vec[0:1], vec[1:2], normed, qkv, near)


def middle_body(per_layer, vec_rows, tree_bits, meta, vec, offsets, inputs, qkv, *refs):
    far, refs = (refs[:tree_bits], refs[tree_bits:])
    packed, probs_out, mixed, middle, normed_two, slope_out, act = refs[:7]
    hidden, normed, next_qkv, near, store, sems, probs, slope, out_sems = refs[7:]
    units = Units(meta, packed, store, sems, range(3, per_layer + 3))
    stack = stack_keys(qkv[:, mixed.shape[1] :], [ref[...] for ref in far])
    attend(qkv[...], stack, offsets[...], probs, mixed)
    probs_copy = pltpu.make_async_copy(probs, probs_out, out_sems.at[0])
    probs_copy.start()
    middle[...] = inputs[...].astype(jnp.float32) + contract(mixed[...], units[3], 1, 0)
    hidden[...] = feed_forward(middle[...], units, 0, vec, 0, normed_two, slope, act)
    slope_copy = pltpu.make_async_copy(slope, slope_out, out_sems.at[1])
    slope_copy.start()
    project(
        hidden[...], units, per_layer, vec[vec_rows : vec_rows + 1],
        vec[vec_rows + 1 : vec_rows + 2], normed, next_qkv, near,
    )
    probs_copy.wait()
    slope_copy.wait()


def turn_body(per_layer, vec_rows, tree_bits, meta, vec, offsets, cotangent, hidden, qkv, *refs):
    far, refs = (refs[:tree_bits], refs[tree_bits:])
    packed, outputs, mixed, normed_two, act = refs[:5]
    middle_grad, query_grad, key_grads, vec_grads, pre_grad, branch_low = refs[5:11]
    far_grads, refs = (refs[11 : 11 + tree_bits], refs[11 + tree_bits :])
    store, sems, probs, slope, all_grads = refs
    units = Units(meta, packed, store, sems, range(per_layer + 3, 2 * per_layer))
    stack = stack_keys(qkv[:, mixed.shape[1] :], [ref[...] for ref in far])
    attend(qkv[...], stack, offsets[...], probs, mixed)
    middle = hidden[...] + contract(mixed[...], units[per_layer + 3], 1, 0)
    outputs[...] = feed_forward(
        middle, units, per_layer, vec, vec_rows, normed_two, slope, act
    ).astype(jnp.bfloat16)
    vec_grads[...] = jnp.zeros_like(vec_grads)
    grad = feed_back(
        cotangent[...].astype(jnp.float32), middle, slope, units, per_layer, vec, vec_rows,
        vec_grads, 2, pre_grad,
    )
    middle_grad[...] = grad
    branch_grad = grad.astype(jnp.bfloat16)
    branch_low[...] = branch_grad
    mixed_grad = contract(branch_grad, units[per_layer + 3], 1, 1).astype(jnp.bfloat16)
    attend_back(
        qkv[...], stack, probs, mixed_grad, query_grad, key_grads, far_grads, all_grads
    )


def lower_body(per_layer, vec_rows, tree_bits, meta, vec, *refs):
    hidden, query_in, key_in, near_in, middle_in, middle, qkv = refs[:7]
    far, refs = (refs[7 : 7 + tree_bits], refs[7 + tree_bits :])
    probs_in, slope_in, packed, down_low, rows_low = refs[:5]
    middle_grad, query_grad, key_grads, vec_grads, pre_grad, branch_low = refs[5:11]
    far_grads, refs = (refs[11 : 11 + tree_bits], refs[11 + tree_bits :])
    store, sems, probs, slope, in_sems, all_grads = refs
    split = 4 + (per_layer - 4) // 2
    units = Units(
        meta, packed, store, sems,
        list(range(per_layer, per_layer + 3)) + list(range(split, per_layer))
        + list(range(3, split)),
    )
    slope_copy = pltpu.make_async_copy(slope_in, slope, in_sems.at[0])
    probs_copy = pltpu.make_async_copy(probs_in, probs, in_sems.at[1])
    slope_copy.start()
    probs_copy.start()
    vec_grads[...] = jnp.zeros_like(vec_grads)
    rows_low[...] = with_near(key_in[...], near_in[...])
    grad = project_back(
        middle_in[...], hidden[...], query_in[...], rows_low[...], units, per_layer, vec,
        vec_rows, vec_grads,
    )
    down_low[...] = grad.astype(jnp.bfloat16)
    slope_copy.wait()
    grad = feed_back(grad, middle[...], slope, units, 0, vec, 0, vec_grads, 2, pre_grad)
    middle_grad[...] = grad
    branch_grad = grad.astype(jnp.bfloat16)
    branch_low[...] = branch_grad
    mixed_grad = contract(branch_grad, units[3], 1, 1).astype(jnp.bfloat16)
    probs_copy.wait()
    stack = stack_keys(qkv[:, mixed_grad.shape[1] :], [ref[...] for ref in far])
    attend_back(
        qkv[...], stack, probs, mixed_grad, query_grad, key_grads, far_grads, all_grads
    )


def last_body(meta, vec, inputs, query_grad, rows_low, middle_in, packed, *refs):
    input_grad, vec_grads, store, sems = refs
    units = Units(meta, packed, store, sems, range(3))
    vec_grads[...] = jnp.zeros_like(vec_grads)
    input_grad[...] = project_back(
        middle_in[...], inputs[...].astype(jnp.float32), query_grad[...], rows_low[...], units, 0,
        vec, 0, vec_grads,
    )


def grads_body(pairs, array_count, held, meta, *refs):
    arrays, refs = (refs[:array_count], refs[array_count + held :])
    grads = Grads(meta, *refs)
    for first_unit, left, right in pairs:
        grads.put(first_unit, arrays[left][...], arrays[right][...])
    grads.finish()


def last_grads_body(meta, normed, query_grad, key_grads, near_grads, *refs):
    rows_low, *refs = refs[4:]
    grads = Grads(meta, *refs)
    grads.put(0, normed[...], query_grad[...])
    rows_low[...] = with_near(key_grads[...], near_grads[...])
    grads.put(1, normed[...], rows_low[...])
    grads.finish()


def pooled(rows_low):
    return pair_mean(rows_low.astype(jnp.float32)).astype(jnp.bfloat16)


def in_order(first, own, other):
    return jnp.where(first, jnp.concatenate([own, other]), jnp.concatenate([other, own]))


def coarse_up(own, seq_index, tree_bits):
    far_list = []
    if tree_bits == 3:
        far_list.append(partner(own, "seq", 0))
        own = pooled(in_order(seq_index & 1 == 0, own, far_list[0]))
        near, same, cross = (across(own, "seq", apart) for apart in (2, 4, 6))
        return far_list + [near, pooled(in_order(seq_index & 2 == 0, same, cross))]
    for bit_at in range(tree_bits):
        far = partner(own, "seq", bit_at)
        far_list.append(far)
        if bit_at + 1 < tree_bits:
            own = pooled(in_order(seq_index >> bit_at & 1 == 0, own, far))
    return far_list


def coarse_down(far_grads, seq_index):
    above = None
    if len(far_grads) == 3:
        wide = pair_spread(far_grads[2])
        first = seq_index & 2 == 0
        same = jnp.where(first, wide[:BLOCK], wide[BLOCK:]).astype(jnp.bfloat16)
        cross = jnp.where(first, wide[BLOCK:], wide[:BLOCK]).astype(jnp.bfloat16)
        above = (
            across(same, "seq", 4).astype(jnp.float32)
            + across(cross, "seq", 6).astype(jnp.float32)
            + across(far_grads[1].astype(jnp.bfloat16), "seq", 2).astype(jnp.float32)
        )
        far_grads = far_grads[:1]
    for bit_at in reversed(range(len(far_grads))):
        upper = seq_index >> bit_at & 1 == 1
        sent = far_grads[bit_at]
        own = 0.0
        if above is not None:
            wide = pair_spread(above)
            own = jnp.where(upper, wide[BLOCK:], wide[:BLOCK])
            sent = sent + jnp.where(upper, wide[:BLOCK], wide[BLOCK:])
        above = own + partner(sent.astype(jnp.bfloat16), "seq", bit_at).astype(jnp.float32)
    return above


def per_device(
    inputs,
    cotangent,
    seq_lengths,
    unit_slot,
    masters,
    first_moment,
    second_moment,
    bases,
    stats,
    vec_master,
    vec_first,
    vec_second,
):
    seq_count = lax.axis_size("seq")
    opt_count = lax.axis_size("opt")
    seq_index = lax.axis_index("seq")
    tok_count = inputs.shape[1]
    model_width = inputs.shape[2]
    own_slots = masters.shape[0]
    row_count = masters.shape[1]
    ff_blocks = FF // model_width
    per_layer = 4 + 2 * ff_blocks
    vec_width = 5 * model_width + FF
    long_devs = min(max(MAX_LEN // tok_count, 1), seq_count)
    tree_bits = long_devs.bit_length() - 1
    size = seq_count * row_count
    by_permutes = seq_count == 8 and opt_count == 4 and own_slots == 6
    slots = jnp.arange(own_slots, dtype=jnp.int32)
    packed_rows = KINDS * max(row_count, EXTRA) + EXTRA

    def pack_slots(slots, counts):
        return call_kernel(
            pack_body,
            [
                jax.ShapeDtypeStruct((count, packed_rows, model_width), jnp.bfloat16)
                for count in counts
            ],
            [],
            "pack_slots",
            slots,
            (seq_index * row_count).reshape(1),
            stats,
            bases,
            first_moment,
            second_moment,
            smem_count=2,
            micros=3,
        )

    if by_permutes:
        parity, core = (seq_index & 1, lax.axis_index("opt") & 1)
        shift = parity ^ core
        owners = 2 * ((slots >> 1) + ((slots & 1) ^ core)) + (slots & 1)
        half_slots = own_slots // 2
        pairs = 2 * jnp.arange(half_slots, dtype=jnp.int32)
        near, away = pack_slots(
            jnp.concatenate([pairs + parity, pairs + 1 - parity]), (half_slots, half_slots)
        )
        met = jnp.stack([near, partner(away, "seq", 0)], axis=1)
        z_index = seq_index >> 1
        to_owner = [
            lax.dynamic_index_in_dim(
                met, jnp.clip((z_index ^ apart) - shift, 0, half_slots - 1), 0, keepdims=False
            )
            for apart in range(4)
        ]
        row_at = jnp.stack(
            [
                (2 * (z_index ^ apart) + (parity ^ side)) * row_count
                for apart in range(4)
                for side in range(2)
            ]
        )
    else:
        owners = slots
        (to_owner,) = pack_slots(
            jnp.minimum(jnp.arange(seq_count, dtype=jnp.int32), own_slots - 1), (seq_count,)
        )
        row_at = jnp.arange(seq_count, dtype=jnp.int32) * row_count
    vec_count = vec_master.shape[0]
    own_rows = own_slots * row_count
    vec_low = vec_master.astype(jnp.bfloat16)
    for axis in ("opt", "seq"):
        for bit_at in range(lax.axis_size(axis).bit_length() - 1):
            other = partner(vec_low, axis, bit_at)
            vec_low = jnp.where(
                lax.axis_index(axis) >> bit_at & 1 == 1,
                jnp.concatenate([other, vec_low]),
                jnp.concatenate([vec_low, other]),
            )
    vec = vec_low.reshape(-1, model_width).astype(jnp.float32)
    gathered = lax.all_gather(
        masters.astype(jnp.bfloat16).reshape(1, own_rows, model_width),
        ("seq", "opt"),
        axis=0,
        tiled=True,
    )
    if row_count % 16 == 0:
        unit_rows = row_count
        packed = gathered.reshape(seq_count, opt_count, own_rows, model_width)
    else:
        unit_rows = size
        packed = (
            gathered.reshape(seq_count, opt_count, own_slots, row_count, model_width)
            .transpose(1, 2, 0, 3, 4)
            .reshape(1, opt_count, own_slots * size, model_width)
        )
    opt_index = lax.axis_index("opt")
    opt_at, slot_in = (unit_slot // own_slots, unit_slot % own_slots)
    if by_permutes:
        apart = opt_at ^ opt_index
        other = (apart & 1) * 4 + (apart >> 1) * 2 + ((slot_in ^ seq_index) & 1)
        place = other * (own_slots // 2) + (slot_in >> 1)
    else:
        place = unit_slot
    meta = jnp.concatenate([opt_at, slot_in * unit_rows, place]).astype(jnp.int32)
    span_bits = jnp.zeros((), jnp.int32)
    for bit_at in range(tree_bits + 1):
        start_dev = seq_index >> bit_at << bit_at
        span_bits = jnp.where(
            seq_lengths[0, start_dev] == tok_count * (1 << bit_at), bit_at, span_bits
        )
    offsets_in = score_offsets(tok_count, tree_bits, span_bits)
    width_in = offsets_in.shape[1]
    pair_count = model_width // LANES
    vec_rows = vec_width // model_width
    square = (model_width, model_width)

    def units_in(count):
        return [
            pltpu.VMEM((count, size // unit_rows, unit_rows, model_width), jnp.bfloat16),
            pltpu.SemaphoreType.DMA((count,)),
        ]

    def grads_out(count):
        return [pltpu.VMEM((count,) + square, jnp.bfloat16), pltpu.SemaphoreType.DMA((count, 2))]

    def low_of(*shape):
        return jax.ShapeDtypeStruct(shape, jnp.bfloat16)

    def full_of(*shape):
        return jax.ShapeDtypeStruct(shape, jnp.float32)

    projected = [
        low_of(tok_count, model_width),
        low_of(tok_count, 3 * model_width),
        low_of(BLOCK, 2 * model_width),
    ]
    attended = [
        full_of(pair_count, 2 * tok_count, width_in),
        low_of(tok_count, model_width),
    ]
    fed = [
        low_of(tok_count, model_width),
        full_of(tok_count, FF),
        low_of(tok_count, FF),
    ]
    back = [
        full_of(tok_count, model_width),
        low_of(tok_count, model_width),
        full_of(tok_count, 2 * model_width),
        full_of(16, model_width),
        low_of(tok_count, FF),
        low_of(tok_count, model_width),
    ] + [full_of(BLOCK, 2 * model_width)] * tree_bits
    all_grads = full_of(width_in, 2 * model_width)
    buffers = [low_of(UNIT_COUNT // 2, size // 2, model_width)] * 4
    ff_blocks = FF // model_width

    def in_vmem(shapes):
        return [pltpu.VMEM(shape.shape, shape.dtype) for shape in shapes]

    def unit_grads(name, held, pairs):
        arrays = []
        for _, *factors in pairs:
            arrays += [factor for factor in factors if not any(factor is one for one in arrays)]
        index = {id(array): at for at, array in enumerate(arrays)}
        count = sum(left.shape[1] * right.shape[1] for _, left, right in pairs) // model_width**2
        first = 1 + len(arrays)
        return call_kernel(
            functools.partial(
                grads_body,
                [(unit, index[id(left)], index[id(right)]) for unit, left, right in pairs],
                len(arrays),
                len(held),
            ),
            buffers,
            grads_out(count),
            name,
            meta,
            *arrays,
            *held,
            smem_count=1,
            micros=2,
            any_in=range(first, first + len(held)),
            any_out=range(4),
            aliases={first + at: at for at in range(len(held))},
        )

    packed, to_owner, offsets_in, vec, meta = lax.optimization_barrier(
        (packed, to_owner, offsets_in, vec, meta)
    )
    normed_zero, qkv_zero, near_zero = call_kernel(
        functools.partial(first_body, per_layer),
        projected,
        units_in(3),
        "project_first",
        meta,
        vec,
        inputs[0],
        packed,
        smem_count=1,
        micros=3,
        any_in=(3,),
    )
    far_zero = coarse_up(near_zero, seq_index, tree_bits)
    (
        probs, mixed, middle, normed_two, slope, act, hidden, normed_one, qkv_one, near_one,
    ) = call_kernel(
        functools.partial(middle_body, per_layer, vec_rows, tree_bits),
        attended + [full_of(tok_count, model_width)] + fed + [full_of(tok_count, model_width)]
        + projected,
        units_in(per_layer) + in_vmem([attended[0], fed[1]]) + [pltpu.SemaphoreType.DMA((2,))],
        "layer_first",
        meta,
        vec,
        offsets_in,
        inputs[0],
        qkv_zero,
        *far_zero,
        packed,
        smem_count=1,
        micros=7,
        any_in=(5 + tree_bits,),
        any_out=(0, 4),
    )
    far_one = coarse_up(near_one, seq_index, tree_bits)
    (
        outputs, mixed_one, normed_up, act_one, middle_grad, query_grad, key_grads, vec_grads_up,
        pre_grad, branch_low, *far_grads,
    ) = call_kernel(
        functools.partial(turn_body, per_layer, vec_rows, tree_bits),
        [low_of(tok_count, model_width), attended[1], fed[0], fed[2]] + back,
        units_in(per_layer - 3) + in_vmem([attended[0], fed[1], all_grads]),
        "layer_turn",
        meta,
        vec,
        offsets_in,
        cotangent[0],
        hidden,
        qkv_one,
        *far_one,
        packed,
        smem_count=1,
        micros=13,
        any_in=(6 + tree_bits,),
    )
    near_grads = coarse_down(far_grads, seq_index)
    held = unit_grads("down_grads", (), [(per_layer + 4 + ff_blocks, act_one, cotangent[0])])
    held = unit_grads(
        "up_grads",
        held,
        [(per_layer + 4, normed_up, pre_grad), (per_layer + 3, mixed_one, branch_low)],
    )
    (
        down_low, rows_low, middle_grad, query_zero, key_grads, vec_grads_mid, pre_grad,
        branch_low, *far_grads,
    ) = call_kernel(
        functools.partial(lower_body, per_layer, vec_rows, tree_bits),
        [low_of(tok_count, model_width), low_of(tok_count, 2 * model_width)] + back,
        units_in(per_layer)
        + in_vmem([attended[0], fed[1]])
        + [pltpu.SemaphoreType.DMA((2,))]
        + in_vmem([all_grads]),
        "layer_back",
        meta,
        vec,
        hidden,
        query_grad,
        key_grads,
        near_grads,
        middle_grad,
        middle,
        qkv_zero,
        *far_zero,
        probs,
        slope,
        packed,
        smem_count=1,
        micros=13,
        any_in=range(9 + tree_bits, 12 + tree_bits),
    )
    near_grads = coarse_down(far_grads, seq_index)
    held = unit_grads("down_grads_low", held, [(4 + ff_blocks, act, down_low)])
    held = unit_grads(
        "up_grads_low", held, [(4, normed_two, pre_grad), (3, mixed, branch_low)]
    )
    held = unit_grads(
        "project_grads",
        held,
        [(per_layer, normed_one, query_grad), (per_layer + 1, normed_one, rows_low)],
    )
    rows_zero, *held = call_kernel(
        last_grads_body,
        [low_of(tok_count, 2 * model_width)] + buffers,
        grads_out(3),
        "project_grads_low",
        meta,
        normed_zero,
        query_zero,
        key_grads,
        near_grads,
        *held,
        smem_count=1,
        micros=3,
        any_in=range(5, 9),
        any_out=range(1, 5),
        aliases={5 + at: 1 + at for at in range(4)},
    )
    input_grad, vec_grads_low = call_kernel(
        last_body,
        [full_of(tok_count, model_width), full_of(16, model_width)],
        units_in(3),
        "project_back",
        meta,
        vec,
        inputs[0],
        query_zero,
        rows_zero,
        middle_grad,
        packed,
        smem_count=1,
        micros=4,
        any_in=(6,),
    )
    vec_sum = jnp.concatenate(
        [vec_grads_low[0:2], vec_grads_mid[2:vec_rows], vec_grads_mid[0:2], vec_grads_up[2:vec_rows]]
    )
    if by_permutes:
        held[2], to_owner = lax.optimization_barrier((held[2], to_owner))
        owner_grad, vec_sum, owner_rows = sum_to_owner(
            *held, seq_index, shift, vec_sum, to_owner
        )
    else:
        owner_rows = [lax.all_to_all(to_owner, "seq", 0, 0, tiled=True)]
        for axis in ("opt", "seq"):
            for bit_at in range(lax.axis_size(axis).bit_length() - 1):
                vec_sum = vec_sum + partner(vec_sum, axis, bit_at)
        column_grads = lax.psum_scatter(
            jnp.concatenate(
                [jnp.concatenate(held[at : at + 2], axis=1) for at in (0, 2)]
            ),
            "opt",
            scatter_dimension=0,
            tiled=True,
        )
        column_grads = jnp.pad(column_grads, [(0, seq_count - own_slots), (0, 0), (0, 0)])
        owner_grad = lax.psum_scatter(column_grads, "seq", scatter_dimension=0, tiled=True)[0]
    step_rows, owner_stat, owner_basis = rotate_slot(row_at, owner_grad, owner_rows)
    home_rows = lax.all_to_all(step_rows, "seq", 0, 0, tiled=True)
    base_rows = renew_bases(seq_count, owner_stat, owner_basis)
    base_rows, home_rows = lax.optimization_barrier((base_rows, home_rows))
    base_rows = lax.all_to_all(base_rows, "seq", 0, 0, tiled=True)
    whole_shape = jax.ShapeDtypeStruct(masters.shape, jnp.float32)
    new_masters, new_first, new_second, new_stats = call_kernel(
        finish_body,
        [whole_shape, whole_shape, whole_shape, jax.ShapeDtypeStruct(stats.shape, jnp.float32)],
        [],
        "finish_slots",
        owners,
        masters,
        first_moment,
        second_moment,
        stats,
        home_rows,
        smem_count=1,
        micros=4,
    )
    (new_bases,) = call_kernel(
        place_body,
        [jax.ShapeDtypeStruct(bases.shape, jnp.float32)],
        [
            pltpu.VMEM(bases.shape, jnp.bfloat16),
            pltpu.VMEM(bases.shape, jnp.float32),
            pltpu.SemaphoreType.DMA((own_slots,)),
            pltpu.SemaphoreType.DMA((own_slots,)),
        ],
        "place_bases",
        owners,
        base_rows,
        smem_count=1,
        any_in=(1,),
        any_out=(0,),
    )
    grad_vecs = lax.dynamic_slice_in_dim(
        vec_sum.reshape(-1), (seq_index * opt_count + lax.axis_index("opt")) * vec_count, vec_count
    )
    new_vec_first = BETA_ONE * vec_first + (1.0 - BETA_ONE) * grad_vecs
    new_vec_second = BETA_TWO * vec_second + (1.0 - BETA_TWO) * grad_vecs * grad_vecs
    new_vectors = vec_master - RATE_VECTOR * (new_vec_first / (1.0 - BETA_ONE**STEP)) / (
        jnp.sqrt(new_vec_second / (1.0 - BETA_TWO**STEP)) + ADAM_EPS
    )
    return (
        outputs[None],
        input_grad[None],
        new_masters,
        new_first,
        new_second,
        new_bases,
        new_stats,
        new_vectors,
        new_vec_first,
        new_vec_second,
    )


def solution(mesh):
    placed = (
        P("opt", "seq", None),
        P("opt", "seq", None),
        P("opt", None),
        P(),
        P("opt", "seq", None),
        P("opt", "seq", None),
        P("opt", "seq", None),
        P("opt", None, "seq", None),
        P("opt", None, "seq", None),
        P(("seq", "opt")),
        P(("seq", "opt")),
        P(("seq", "opt")),
    )
    return jax.shard_map(
        per_device,
        mesh=mesh,
        in_specs=placed,
        out_specs=(
            P("opt", "seq", None),
            P("opt", "seq", None),
            P("opt", "seq", None),
            P("opt", "seq", None),
            P("opt", "seq", None),
            P("opt", None, "seq", None),
            P("opt", None, "seq", None),
            P(("seq", "opt")),
            P(("seq", "opt")),
            P(("seq", "opt")),
        ),
        check_vma=False,
    )
```
